32 devices in a mesh: expert: 8 (over z, y), tensor: 4 (over x, core).
Axes of the slice: x: 2, y: 2, z: 4, core: 2. Of those that a mesh axis runs over, the one named last changes fastest.
Arguments:
- block_in: bfloat16 [17336, 1024], P('expert'), may hold values from -6 to 6
- norm_one: float32 [1024], replicated, may hold values from 0.5 to 1.5
- head_in: bfloat16 [3, 1024, 1024], P(None, None, 'tensor'), may hold values from -0.1875 to 0.1875
- head_out: bfloat16 [1024, 1024], P('tensor'), may hold values from -0.5 to 0.5
- norm_two: float32 [1024], replicated, may hold values from 0.5 to 1.5
- router: bfloat16 [1024, 8], replicated, may hold values from -0.125 to 0.125
- expert_in: bfloat16 [8, 1024, 4096], P('expert', None, 'tensor'), may hold values from -0.1875 to 0.1875
- expert_out: bfloat16 [8, 4096, 1024], P('expert', 'tensor'), may hold values from -0.09375 to 0.09375
- expert_ids: int32 [17336, 2], P('expert'), may hold values from 0 to 7, all different within a row; in each aligned block of 2167 rows (0 to 2166, 2167 to 4333, ...) at most 880 rows name the same one
- route_noise: float32 [17336, 2], P('expert'), may hold values from -3 to 3
- cotangent: bfloat16 [17336, 1024], P('expert'), may hold values from -6 to 6
Outputs:
- block_out: bfloat16 [17336, 1024], P('expert')
- input_grad: float32 [17336, 1024], P('expert')
- norm_one_grad: float32 [1024], replicated
- head_in_grad: float32 [3, 1024, 1024], P(None, None, 'tensor')
- head_out_grad: float32 [1024, 1024], P('tensor')
- norm_two_grad: float32 [1024], replicated
- router_grad: float32 [1024, 8], replicated
- expert_in_grad: float32 [8, 1024, 4096], P('expert', None, 'tensor')
- expert_out_grad: float32 [8, 4096, 1024], P('expert', 'tensor')
The draws below stay inside these ranges and needn't reach their ends.
Inputs may be any that keep to these rules, and one draw needn't show every extreme that they name: `expert_ids`: each row names 2 different experts, and every expert is named somewhere. In each aligned block of 2167 rows no expert is named by more than 880 rows, and in every draw some block has an expert named by exactly 880 rows.
All inputs are finite; a program needn't handle non-finite values.
Results may differ from the reference program's by a relative error of at most 0.019.
Values may be sent and summed in bfloat16 or wider, within the bound.
No kernel may reach another device: no remote copies, remote signals or barrier semaphores. Data moves between devices by JAX's collectives and lax.ppermute only.
A program may use at most 320 MiB of HBM per device.

```python
import math
import jax
import jax.numpy as jnp
import numpy as np
from jax import lax

D = 1024
HEADS = 16
HD = 64
FF = 4096
SEQ = 197
TOP = 2
IMG_DEV = 11
TOK_DEV = 2167
TOKENS = 17336
EXPERTS = 8
CAP = 880
N_EXPERT = 8


def block_scale(stream_key, extent, pieces, low, high):
    def one(axis_at, blocks):
        heights = jax.random.uniform(jax.random.fold_in(jax.random.fold_in(stream_key, 6), axis_at), (blocks,), jnp.float32, low / len(pieces), high / len(pieces))
        return jnp.repeat(jnp.exp(heights), extent[axis_at] // blocks).reshape((-1,) + (1,) * (len(extent) - axis_at - 1))

    factor_of = one(*pieces[0])
    for cut in pieces[1:]:
        factor_of = factor_of * one(*cut)
    return factor_of


def routed_block(rng, own, number, rows, number_of, top, most, lean):
    sequence = jax.random.permutation(rng, number_of)
    packed, usual = load_shares(number_of, rows * top, most, lean, True), load_shares(number_of, rows * top, most, lean, False)
    places = jnp.arange(number_of)

    def named(sizes, rotation):
        used = int((sizes > 0).sum())
        fixed = max(1, used // 4)
        passed = fixed + (places - fixed + rotation * (used - fixed)) % max(1, number_of - fixed)
        return jnp.zeros((number_of,), jnp.int32).at[sequence[jnp.where(places < fixed, places, passed)]].set(jnp.asarray(sizes, jnp.int32))

    sizes = jnp.where(number % 4 == 0, named(packed, number // 4), named(usual, number - number // 4 - 1))
    mixed = jax.random.permutation(jax.random.fold_in(own, 3), number_of)
    giver, taker = mixed[0:number_of // 2 * 2:2], mixed[1:number_of // 2 * 2:2]
    margin = jnp.minimum(sizes[giver] - 1, most - sizes[taker]) // 2
    margin = jnp.where((giver == sequence[0]) | (taker == sequence[0]) | (sizes[taker] == 0), 0, jnp.maximum(margin, 0))
    passed = jax.random.randint(jax.random.fold_in(own, 4), (number_of // 2,), 0, 1 << 20) % (margin + 1)
    sizes = sizes.at[giver].add(-passed).at[taker].add(passed)
    members = jnp.searchsorted(jnp.cumsum(sizes), jnp.arange(rows * top), side="right").astype(jnp.int32)
    table = members.reshape(top, rows).T
    table = table[jax.random.permutation(jax.random.fold_in(own, 1), rows)]
    rotation = jax.random.randint(jax.random.fold_in(own, 2), (rows, 1), 0, top)
    return jnp.take_along_axis(table, (jnp.arange(top)[None, :] + rotation) % top, axis=1)


def load_shares(number_of, total, limit, slope, full):
    loads = [(1 << 20) // math.isqrt(grade ** slope) + 1 for grade in range(1, number_of + 1)]
    largest = limit if full else min(limit, max(-(-total // number_of), total * loads[0] // sum(loads)))
    least = 1 if total - largest >= number_of - 1 else 0
    holding, surplus = [largest] + [least] * (number_of - 1), total - largest - least * (number_of - 1)
    while surplus > 0:
        free = [i for i in range(1, number_of) if holding[i] < largest] or [i for i in range(1, number_of) if holding[i] < limit]
        pool, remaining = sum([loads[i] for i in free]), surplus
        for i in free:
            extra = min(limit - holding[i], max(1, remaining * loads[i] // pool), surplus)
            holding[i] = holding[i] + extra
            surplus = surplus - extra
    return np.array(holding)


def scatter_about(rng, shape, scale, most, shards=(), held_as=jnp.bfloat16):
    factor_of = block_scale(rng, shape, shards, -0.22, 0.18) if shards else 1.0
    values = jax.random.normal(rng, shape, jnp.float32) * scale * factor_of
    return jnp.minimum(jnp.maximum(values, -most), most).astype(held_as)


def setup_inputs(seed: int = 0) -> dict:
    seeds = jax.random.split(jax.random.key(seed), 12)
    block_in = scatter_about(seeds[0], (TOKENS, D), 1.0, 6.0, ((0, 8),))
    norm_one = jnp.clip(1.0 + 0.1 * jax.random.normal(seeds[1], (D,), jnp.float32), 0.5, 1.5)
    head_in = scatter_about(seeds[2], (3, D, D), D ** -0.5, 0.1875, ((2, 4),))
    head_out = scatter_about(seeds[3], (D, D), (D // 8) ** -0.5, 0.5, ((0, 4),))
    norm_two = jnp.clip(1.0 + 0.1 * jax.random.normal(seeds[4], (D,), jnp.float32), 0.5, 1.5)
    router = scatter_about(seeds[5], (D, EXPERTS), (2 * D) ** -0.5, 0.125)
    expert_in = scatter_about(seeds[6], (EXPERTS, D, FF), D ** -0.5, 0.1875, ((0, 8), (2, 4)))
    expert_out = scatter_about(seeds[7], (EXPERTS, FF, D), FF ** -0.5, 0.09375, ((0, 8), (1, 4)))
    expert_ids_keys = jax.random.split(jax.random.fold_in(seeds[8], 1), TOKENS // TOK_DEV)
    expert_ids_turns = jax.random.permutation(jax.random.fold_in(seeds[8], 3), TOKENS // TOK_DEV)
    expert_ids = jax.vmap(lambda own, number: routed_block(jax.random.fold_in(seeds[8], 2), own, number, TOK_DEV, EXPERTS, TOP, CAP, 1))(expert_ids_keys, expert_ids_turns).reshape((TOKENS, TOP))
    route_noise = scatter_about(seeds[9], (TOKENS, TOP), 0.5, 3.0, ((0, 8),), jnp.float32)
    cotangent = scatter_about(seeds[10], (TOKENS, D), 1.0, 6.0, ((0, 8),))
    return {"block_in": block_in, "norm_one": norm_one, "head_in": head_in, "head_out": head_out, "norm_two": norm_two, "router": router, "expert_in": expert_in, "expert_out": expert_out, "expert_ids": expert_ids, "route_noise": route_noise, "cotangent": cotangent}


EPSILON = 1e-06
EXACT = lax.Precision.HIGHEST

@jax.custom_vjp
def low(v):
    return lax.optimization_barrier(v.astype(jnp.bfloat16)).astype(jnp.float32)

@jax.custom_vjp
def low_back(v):
    return v

def low_keep(v):
    return (low(v), None)

def low_pass(kept, grad):
    return (grad,)

def back_keep(v):
    return (v, None)

def back_low(kept, grad):
    return (low(grad),)
low.defvjp(low_keep, low_pass)
low_back.defvjp(back_keep, back_low)

def layer_norm(field, gain_vec):
    centre = field - lax.optimization_barrier(jnp.mean(field, -1, keepdims=True))
    scaled = centre * lax.rsqrt(lax.optimization_barrier(jnp.mean(centre * centre, -1, keepdims=True)) + EPSILON)
    return scaled * gain_vec

def slot_positions(expert_ids):
    blocks = expert_ids.reshape(N_EXPERT, TOK_DEV * TOP)
    onehot = (blocks[:, :, None] == jnp.arange(EXPERTS, dtype=jnp.int32)).astype(jnp.int32)
    before = jnp.cumsum(onehot, axis=1) - onehot
    slots = lax.optimization_barrier(jnp.sum(before * onehot, axis=-1))
    source_index = jnp.arange(N_EXPERT, dtype=jnp.int32)[:, None]
    return ((source_index * EXPERTS + blocks) * CAP + slots).reshape(TOKENS * TOP).astype(jnp.int32)

def image_attention(token_block, head_in, head_out):
    pictures = token_block.reshape(IMG_DEV, SEQ, D)
    projected = jnp.einsum('isd,kdc->kisc', pictures, head_in, precision=EXACT)
    projected = low(low_back(projected)).reshape(3, IMG_DEV, SEQ, HEADS, HD)
    scores = jnp.einsum('ishd,ithd->ihst', projected[0], projected[1], precision=EXACT) * HD ** (-0.5)
    scores = low_back(scores)
    highest = lax.optimization_barrier(jnp.max(scores, -1, keepdims=True))
    weights = jnp.exp(scores - highest)
    probabilities = weights / lax.optimization_barrier(jnp.sum(weights, -1, keepdims=True))
    mixed_heads = jnp.einsum('ihst,ithd->ishd', low(probabilities), projected[2], precision=EXACT)
    mixed_heads = low(low_back(mixed_heads)).reshape(TOK_DEV, D)
    return jnp.dot(mixed_heads, head_out, precision=EXACT)

def attention(first_in, head_in, head_out):
    group_step = jax.checkpoint(lambda token_block: image_attention(token_block, head_in, head_out))
    unused_carry, outputs = lax.scan(lambda carry_in, token_block: (carry_in, group_step(token_block)), None, first_in.reshape(N_EXPERT, TOK_DEV, D))
    return outputs.reshape(TOKENS, D)

def expert_rows(token_rows, weight_in, weight_out):
    hidden = low_back(jnp.dot(token_rows, weight_in, precision=EXACT))
    active = low(jax.nn.gelu(hidden, approximate=False))
    return low(low_back(jnp.dot(active, weight_out, precision=EXACT)))

def forward(block_in, norm_one, head_in, head_out, norm_two, router, expert_in, expert_out, expert_ids, route_noise, positions):
    first_in = low(layer_norm(block_in, norm_one))
    middle = block_in + low_back(attention(first_in, head_in, head_out))
    second_in = low(layer_norm(middle, norm_two))
    logits = low_back(jnp.dot(second_in, router, precision=EXACT))
    selector = (expert_ids[:, :, None] == jnp.arange(EXPERTS, dtype=jnp.int32)).astype(logits.dtype)
    chosen = lax.optimization_barrier(jnp.sum(selector * logits[:, None, :], -1)) + route_noise.astype(logits.dtype)
    highest = lax.optimization_barrier(jnp.max(chosen, -1, keepdims=True))
    weights = jnp.exp(chosen - highest)
    gate_values = weights / lax.optimization_barrier(jnp.sum(weights, -1, keepdims=True))
    token_rows = jnp.broadcast_to(second_in[:, None, :], (TOKENS, TOP, D)).reshape(TOKENS * TOP, D)
    buffer = jnp.zeros((N_EXPERT * EXPERTS * CAP, D), second_in.dtype).at[positions].set(token_rows)
    buffer = low_back(buffer)
    per_expert = buffer.reshape(N_EXPERT, EXPERTS, CAP, D).transpose(1, 0, 2, 3).reshape(EXPERTS, N_EXPERT * CAP, D)
    outputs = lax.map(jax.checkpoint(lambda expert_item: expert_rows(expert_item[0], expert_item[1], expert_item[2])), (per_expert, expert_in, expert_out))
    outputs = outputs.reshape(EXPERTS, N_EXPERT, CAP, D).transpose(1, 0, 2, 3).reshape(N_EXPERT * EXPERTS * CAP, D)
    returned = outputs[positions].reshape(TOKENS, TOP, D)
    combined = lax.optimization_barrier(jnp.sum(gate_values[:, :, None] * returned, 1))
    return middle + combined

def reference(block_in, norm_one, head_in, head_out, norm_two, router, expert_in, expert_out, expert_ids, route_noise, cotangent):
    positions = slot_positions(expert_ids)

    def run(*floats):
        return forward(*floats, expert_ids, route_noise, positions)
    floats = [item.astype(jnp.float32) for item in (block_in, norm_one, head_in, head_out, norm_two, router, expert_in, expert_out)]
    result, pullback = jax.vjp(run, *floats)
    gradients = pullback(cotangent.astype(jnp.float32))
    return (result.astype(jnp.bfloat16), gradients[0], gradients[1], gradients[2], gradients[3], gradients[4], gradients[5], gradients[6], gradients[7])
```

```python
import functools

import jax
import jax.numpy as jnp
from jax import lax
from jax.experimental import pallas as pl
from jax.experimental.pallas import tpu as pltpu
from jax.sharding import PartitionSpec as P

HD = 64
SEQ = 197
LANES = 128
EPSILON = 1e-06
CHUNKS = 1
BF = jnp.bfloat16
F32 = jnp.float32


def up_to(value, unit):
    return -(-value // unit) * unit


def params(mib=48):
    return pltpu.CompilerParams(vmem_limit_bytes=mib * 1024 * 1024)


def dot(a, b, da=1, db=0):
    return lax.dot_general(a, b, (((da,), (db,)), ((), ())), preferred_element_type=F32)


def iota(rows, cols, dim):
    return lax.broadcasted_iota(jnp.int32, (rows, cols), dim)


def flag(mask):
    return jnp.where(mask, 1.0, 0.0)


def whole(shape, once=False):
    zeros = (0,) * len(shape)
    mode = pl.Buffered(1) if once else None
    return pl.BlockSpec(shape, lambda *_: zeros, pipeline_mode=mode)


def image(*shape):
    return pl.BlockSpec((1,) + shape, lambda i: (i,) + (0,) * len(shape))


def fill(x_ref, tail_ref, rows_ref):
    full = x_ref.shape[0] // 16 * 16
    rows_ref[0:full, :] = x_ref[0:full, :]
    rows_ref[full : full + 16, :] = tail_ref[...]
    rest = rows_ref.shape[0] - full - 16
    if rest:
        rows_ref[full + 16 :, :] = jnp.zeros((rest, rows_ref.shape[1]), BF)


def norm_parts(field):
    centre = field - jnp.mean(field, -1, keepdims=True)
    spread = lax.rsqrt(jnp.mean(centre * centre, -1, keepdims=True) + EPSILON)
    return centre * spread, spread


def norm_field_back(upstream, gain, scaled, spread):
    weighted = upstream * gain
    return spread * (
        weighted
        - jnp.mean(weighted, -1, keepdims=True)
        - scaled * jnp.mean(weighted * scaled, -1, keepdims=True)
    )


def head_masks():
    lane = iota(1, LANES, 1)
    return [(flag(lane // HD == h)).astype(BF) for h in range(2)]


def attend_kernel(images, x_ref, tail_ref, gain_ref, w_ref, mixed_ref, first_ref, qkv_ref, log_ref, rows):
    i = pl.program_id(0)

    @pl.when(i == 0)
    def _():
        fill(x_ref, tail_ref, rows)

    height = first_ref.shape[1]
    window = height + 16
    start = jnp.minimum(i, images - 1) * SEQ
    aligned = start // 16 * 16
    r, c = iota(height, window, 0), iota(height, window, 1)
    limit = jnp.where(i < images, SEQ, 0)
    shift = flag((c == r + (start - aligned)) & (r < limit)).astype(BF)
    field = dot(shift, rows[pl.ds(pl.multiple_of(aligned, 16), window), :])
    scaled, _ = norm_parts(field)
    first = (scaled * gain_ref[...]).astype(BF)
    first_ref[0] = first
    for k in range(3):
        qkv_ref[k, 0] = dot(first, w_ref[k]).astype(BF)
    masks = head_masks()
    lane = iota(1, LANES, 1)
    key_lane = iota(1, height, 1)
    logs = jnp.zeros((height, LANES), F32)
    for pair in range(mixed_ref.shape[2] // LANES):
        cols = slice(pair * LANES, (pair + 1) * LANES)
        queries, keys, values = (qkv_ref[k, 0, :, cols] for k in range(3))
        total = jnp.zeros((height, LANES), F32)
        for h in range(2):
            scores = dot(queries * masks[h], keys, 1, 1) * HD ** (-0.5)
            scores = jnp.where(key_lane < SEQ, scores, -1e30)
            highest = jnp.max(scores, -1, keepdims=True)
            weights = jnp.exp(scores - highest)
            sums = jnp.sum(weights, -1, keepdims=True)
            probs = (weights * (1.0 / sums)).astype(BF)
            total += dot(probs, values * masks[h])
            logs = jnp.where(lane == pair * 2 + h, highest + jnp.log(sums), logs)
        mixed_ref[0, :, cols] = total.astype(BF)
    log_ref[0] = logs


def attend(block_in, tail, gain, head_in, images, image_slots, height):
    rows, width = block_in.shape
    cols = head_in.shape[2]
    return pl.pallas_call(
        functools.partial(attend_kernel, images),
        grid=(image_slots,),
        in_specs=[whole((rows, width), True), whole((16, width)), whole((1, width)), whole(head_in.shape, True)],
        out_specs=[
            image(height, cols),
            image(height, width),
            pl.BlockSpec((3, 1, height, cols), lambda i: (0, i, 0, 0)),
            image(height, LANES),
        ],
        out_shape=[
            jax.ShapeDtypeStruct((image_slots, height, cols), BF),
            jax.ShapeDtypeStruct((image_slots, height, width), BF),
            jax.ShapeDtypeStruct((3, image_slots, height, cols), BF),
            jax.ShapeDtypeStruct((image_slots, height, LANES), F32),
        ],
        scratch_shapes=[pltpu.VMEM((rows // 16 * 16 + 48, width), BF)],
        compiler_params=params(),
        name="attend",
    )(block_in, tail, gain, head_in)


def attend_back_kernel(dmix_ref, qkv_ref, log_ref, first_ref, w_ref, fg_ref, hg_ref, acc, grads):
    i = pl.program_id(0)
    height = first_ref.shape[1]
    masks = head_masks()
    lane = iota(1, LANES, 1)
    key_lane = iota(1, height, 1)
    scale = HD ** (-0.5)
    logs = log_ref[0]
    for pair in range(dmix_ref.shape[2] // LANES):
        cols = slice(pair * LANES, (pair + 1) * LANES)
        queries, keys, values = (qkv_ref[k, 0, :, cols] for k in range(3))
        out_grad = dmix_ref[0, :, cols]
        dq = jnp.zeros((height, LANES), F32)
        dk = jnp.zeros((height, LANES), F32)
        dv = jnp.zeros((height, LANES), F32)
        for h in range(2):
            q_h = queries * masks[h]
            o_h = out_grad * masks[h]
            log_h = jnp.sum(jnp.where(lane == pair * 2 + h, logs, 0.0), -1, keepdims=True)
            probs = jnp.exp(dot(q_h, keys, 1, 1) * scale - log_h)
            probs = jnp.where(key_lane < SEQ, probs, 0.0)
            prob_grad = dot(o_h, values, 1, 1)
            dv += dot(probs.astype(BF), o_h, 0, 0)
            delta = jnp.sum(probs * prob_grad, -1, keepdims=True)
            score_grad = (probs * (prob_grad - delta)).astype(BF)
            dq += dot(score_grad, keys * masks[h])
            dk += dot(score_grad, q_h, 0, 0)
        grads[0, :, cols] = (dq * scale).astype(BF)
        grads[1, :, cols] = (dk * scale).astype(BF)
        grads[2, :, cols] = dv.astype(BF)

    @pl.when(i == 0)
    def _():
        acc[...] = jnp.zeros_like(acc)

    first = first_ref[0]
    total = None
    for k in range(3):
        part = dot(grads[k], w_ref[k], 1, 1)
        total = part if total is None else total + part
        acc[k] += dot(first, grads[k], 0, 0)
    fg_ref[0] = total.astype(BF)

    @pl.when(i == pl.num_programs(0) - 1)
    def _():
        hg_ref[...] = acc[...].astype(BF)


def attend_back(dmix, qkv, logs, first, head_in):
    image_slots, height, cols = dmix.shape
    width = first.shape[2]
    return pl.pallas_call(
        attend_back_kernel,
        grid=(image_slots,),
        in_specs=[
            image(height, cols),
            pl.BlockSpec((3, 1, height, cols), lambda i: (0, i, 0, 0)),
            image(height, LANES),
            image(height, width),
            whole(head_in.shape, True),
        ],
        out_specs=[image(height, width), whole(head_in.shape)],
        out_shape=[
            jax.ShapeDtypeStruct((image_slots, height, width), BF),
            jax.ShapeDtypeStruct(head_in.shape, BF),
        ],
        scratch_shapes=[pltpu.VMEM(head_in.shape, F32), pltpu.VMEM((3, height, cols), BF)],
        compiler_params=params(),
        name="attend_back",
    )(dmix, qkv, logs, first, head_in)


def pack_first_kernel(slots, base, x_ref, tail_ref, lp_ref, side_ref, out_ref, rows):
    e = pl.program_id(0)

    @pl.when(e == 0)
    def _():
        fill(x_ref, tail_ref, rows)

    j = base + e * slots + iota(slots, rows.shape[0], 0)
    picks = [flag(lp_ref[c : c + 1, :] == j) for c in range(2)]
    width = x_ref.shape[1]
    out_ref[0, :, 0:width] = dot((picks[0] + picks[1]).astype(BF), rows[...]).astype(BF)
    out_ref[0, :, width:] = (
        dot(picks[0].astype(BF), side_ref[0]) + dot(picks[1].astype(BF), side_ref[1])
    ).astype(BF)


def pack_first(x, tail, lp, side, experts, slots, base):
    rows, width = x.shape
    padded = lp.shape[1]
    return pl.pallas_call(
        functools.partial(pack_first_kernel, slots, base),
        grid=(experts,),
        in_specs=[whole((rows, width), True), whole((16, width)), whole(lp.shape), whole(side.shape)],
        out_specs=image(slots, width + LANES),
        out_shape=jax.ShapeDtypeStruct((experts, slots, width + LANES), BF),
        scratch_shapes=[pltpu.VMEM((padded, width), BF)],
        compiler_params=params(),
        name="pack_cotangent",
    )(x, tail, lp, side)


def pack_kernel(slots, base, x_ref, lp_ref, out_ref):
    j = base + pl.program_id(0) * slots + iota(slots, x_ref.shape[0], 0)
    picks = flag((lp_ref[0:1, :] == j) | (lp_ref[1:2, :] == j)).astype(BF)
    out_ref[0] = dot(picks, x_ref[...]).astype(BF)


def pack(x, lp, experts, slots, base):
    rows, width = x.shape
    return pl.pallas_call(
        functools.partial(pack_kernel, slots, base),
        grid=(experts,),
        in_specs=[whole((rows, width), True), whole(lp.shape)],
        out_specs=image(slots, width),
        out_shape=jax.ShapeDtypeStruct((experts, slots, width), BF),
        compiler_params=params(),
        name="pack_rows",
    )(x, lp)


def unpack_kernel(count, lp_ref, *refs):
    row_refs, gg_refs, out_ref = refs[:count], refs[count:-1], refs[-1]
    lp = lp_ref[0]
    height = lp.shape[0]
    width = row_refs[0].shape[1]
    total = jnp.zeros((height, width), F32)
    extra = [jnp.zeros((height, 1), F32) for _ in range(2)]
    for n in range(count):
        slots = row_refs[n].shape[0]
        j = n * slots + iota(1, slots, 1)
        hits = [lp[:, c : c + 1] == j for c in range(2)]
        total += dot(flag(hits[0] | hits[1]).astype(BF), row_refs[n][...])
        if gg_refs:
            for c in range(2):
                extra[c] += jnp.sum(jnp.where(hits[c], gg_refs[n][...], 0.0), -1, keepdims=True)
    out_ref[0, :, 0:width] = total.astype(BF)
    if gg_refs:
        lane = iota(1, LANES, 1)
        tail = jnp.zeros((height, LANES), F32)
        for c in range(2):
            high = extra[c].astype(BF).astype(F32)
            tail = jnp.where(lane == c, high, tail)
            tail = jnp.where(lane == 2 + c, extra[c] - high, tail)
        out_ref[0, :, width:] = tail.astype(BF)


def unpack(lp, rows, gate_grads=()):
    image_slots, height, _ = lp.shape
    count = len(rows)
    width = rows[0].shape[1]
    out_width = width + (LANES if gate_grads else 0)
    return pl.pallas_call(
        functools.partial(unpack_kernel, count),
        grid=(image_slots,),
        in_specs=[image(height, 2)]
        + [whole(item.shape, True) for item in rows]
        + [whole(item.shape) for item in gate_grads],
        out_specs=image(height, out_width),
        out_shape=jax.ShapeDtypeStruct((image_slots, height, out_width), BF),
        compiler_params=params(),
        name="unpack_rows",
    )(lp, *rows, *gate_grads)


def middle_kernel(mixed_ref, wo_ref, x_ref, gain_ref, router_ref, ids_ref, noise_ref, mid_ref, second_ref, gates_ref):
    middle = x_ref[0].astype(F32)
    for t in range(wo_ref.shape[0]):
        middle += dot(mixed_ref[t, 0], wo_ref[t])
    mid_ref[0] = middle
    scaled, _ = norm_parts(middle)
    second = (scaled * gain_ref[...]).astype(BF)
    second_ref[0] = second
    logits = dot(second, router_ref[...])
    lane = iota(1, LANES, 1)
    chosen = [
        jnp.sum(jnp.where(lane == ids_ref[0, :, c : c + 1], logits, 0.0), -1, keepdims=True)
        + noise_ref[0, :, c : c + 1]
        for c in range(2)
    ]
    top = jnp.maximum(chosen[0], chosen[1])
    raw = [jnp.exp(item - top) for item in chosen]
    inverse = 1.0 / (raw[0] + raw[1])
    gates_ref[0] = jnp.where(lane == 0, raw[0] * inverse, 0.0) + jnp.where(lane == 1, raw[1] * inverse, 0.0)


def middle_of(mixed, head_out, x_own, gain, router, ids, noise):
    parts, own, height, cols = mixed.shape
    width = x_own.shape[2]
    return pl.pallas_call(
        middle_kernel,
        grid=(own,),
        in_specs=[
            pl.BlockSpec((parts, 1, height, cols), lambda i: (0, i, 0, 0)),
            whole(head_out.shape, True),
            image(height, width),
            whole((1, width)),
            whole(router.shape),
            image(height, 2),
            image(height, 2),
        ],
        out_specs=[image(height, width), image(height, width), image(height, LANES)],
        out_shape=[
            jax.ShapeDtypeStruct((own, height, width), F32),
            jax.ShapeDtypeStruct((own, height, width), BF),
            jax.ShapeDtypeStruct((own, height, LANES), F32),
        ],
        compiler_params=params(),
        name="middle",
    )(mixed, head_out, x_own, gain, router, ids, noise)


def middle_back_kernel(
    rs_ref, mid_ref, second_ref, gates_ref, ids_ref, up_ref, mixed_ref, wo_ref, gain_ref, router_ref,
    mg_ref, dmix_ref, hog_ref, rg_ref, ng_ref, hog_acc,
):
    i = pl.program_id(0)

    @pl.when(i == 0)
    def _():
        hog_acc[...] = jnp.zeros_like(hog_acc)
        rg_ref[...] = jnp.zeros_like(rg_ref)
        ng_ref[...] = jnp.zeros_like(ng_ref)

    width = up_ref.shape[2]
    lane = iota(1, LANES, 1)
    tail = rs_ref[0, :, width:].astype(F32)
    gates = gates_ref[0]
    gate, grad = [], []
    for c in range(2):
        gate.append(jnp.sum(jnp.where(lane == c, gates, 0.0), -1, keepdims=True))
        grad.append(jnp.sum(jnp.where((lane == c) | (lane == 2 + c), tail, 0.0), -1, keepdims=True))
    mean_term = gate[0] * grad[0] + gate[1] * grad[1]
    logit_grad = jnp.zeros((up_ref.shape[1], LANES), F32)
    for c in range(2):
        logit_grad = jnp.where(lane == ids_ref[0, :, c : c + 1], gate[c] * (grad[c] - mean_term), logit_grad)
    logit_grad = logit_grad.astype(BF)
    second_grad = rs_ref[0, :, 0:width].astype(F32) + dot(logit_grad, router_ref[...], 1, 1)
    rg_ref[...] += dot(logit_grad, second_ref[0], 0, 0)
    scaled, spread = norm_parts(mid_ref[0])
    ng_ref[...] += jnp.sum(second_grad * scaled, 0, keepdims=True)
    middle_grad = up_ref[0].astype(F32) + norm_field_back(second_grad, gain_ref[...], scaled, spread)
    mg_ref[0] = middle_grad
    rounded = middle_grad.astype(BF)
    for t in range(wo_ref.shape[0]):
        dmix_ref[t, 0] = dot(rounded, wo_ref[t], 1, 1).astype(BF)
        hog_acc[t] += dot(mixed_ref[t, 0], rounded, 0, 0)

    @pl.when(i == pl.num_programs(0) - 1)
    def _():
        hog_ref[...] = hog_acc[...].astype(BF)


def middle_back(rs, middle, second, gates, ids, up, mixed, head_out, gain, router):
    parts, own, height, cols = mixed.shape
    width = up.shape[2]
    by_part = pl.BlockSpec((parts, 1, height, cols), lambda i: (0, i, 0, 0))
    return pl.pallas_call(
        middle_back_kernel,
        grid=(own,),
        in_specs=[
            image(height, rs.shape[2]),
            image(height, width),
            image(height, width),
            image(height, LANES),
            image(height, 2),
            image(height, width),
            by_part,
            whole(head_out.shape, True),
            whole((1, width)),
            whole(router.shape),
        ],
        out_specs=[image(height, width), by_part, whole(head_out.shape), whole((LANES, width)), whole((1, width))],
        out_shape=[
            jax.ShapeDtypeStruct((own, height, width), F32),
            jax.ShapeDtypeStruct((parts, own, height, cols), BF),
            jax.ShapeDtypeStruct(head_out.shape, BF),
            jax.ShapeDtypeStruct((LANES, width), F32),
            jax.ShapeDtypeStruct((1, width), F32),
        ],
        scratch_shapes=[pltpu.VMEM(head_out.shape, F32)],
        compiler_params=params(),
        name="middle_back",
    )(rs, middle, second, gates, ids, up, mixed, head_out, gain, router)


def input_back_kernel(fg_ref, x_ref, mg_ref, gain_ref, out_ref, ng_ref):
    @pl.when(pl.program_id(0) == 0)
    def _():
        ng_ref[...] = jnp.zeros_like(ng_ref)

    scaled, spread = norm_parts(x_ref[0].astype(F32))
    first_grad = fg_ref[0].astype(F32)
    ng_ref[...] += jnp.sum(first_grad * scaled, 0, keepdims=True)
    out_ref[0] = (mg_ref[0] + norm_field_back(first_grad, gain_ref[...], scaled, spread)).astype(BF)


def input_back(first_grad, x_own, middle_grad, gain):
    own, height, width = x_own.shape
    return pl.pallas_call(
        input_back_kernel,
        grid=(own,),
        in_specs=[image(height, width)] * 3 + [whole((1, width))],
        out_specs=[image(height, width), whole((1, width))],
        out_shape=[
            jax.ShapeDtypeStruct((own, height, width), BF),
            jax.ShapeDtypeStruct((1, width), F32),
        ],
        compiler_params=params(),
        name="input_back",
    )(first_grad, x_own, middle_grad, gain)


def gelu_parts(v):
    x = jnp.abs(v) * 0.7071067811865476
    t = 1.0 / (1.0 + 0.3275911 * x)
    bell = jnp.exp(-x * x)
    poly = ((((1.061405429 * t - 1.453152027) * t + 1.421413741) * t - 0.284496736) * t + 0.254829592) * t
    below = 0.5 * poly * bell
    share = jnp.where(v < 0.0, below, 1.0 - below)
    return v * share, share + v * bell * 0.3989422804014327


def expert_kernel(x_ref, g_ref, router_ref, w1_ref, w2_ref, back_ref, act_ref, hg_ref, rg_ref, dx_ref, gg_ref):
    width = x_ref.shape[1]
    rows = x_ref[...]
    lane = iota(1, LANES, 1)
    side = g_ref[:, width:].astype(F32)

    def column(*lanes):
        keep = lane == lanes[0]
        for other in lanes[1:]:
            keep = keep | (lane == other)
        return jnp.sum(jnp.where(keep, side, 0.0), -1, keepdims=True)

    logits = dot(rows, router_ref[...])
    lane_f = lane.astype(F32)
    mine = jnp.sum(jnp.where(lane_f == column(4), logits, 0.0), -1, keepdims=True)
    other = jnp.sum(jnp.where(lane_f == column(0), logits, 0.0), -1, keepdims=True)
    gate = 1.0 / (1.0 + jnp.exp(other - mine - column(1, 2, 3)))
    upstream = g_ref[:, 0:width].astype(F32)
    rows_grad = (gate * upstream).astype(BF)
    rg_ref[...] = rows_grad
    parts, _, hidden_here = w1_ref.shape
    step = min(512, hidden_here)
    for t in range(parts):
        for at in range(0, hidden_here, step):
            cols = slice(at, at + step)
            place = slice(t * hidden_here + at, t * hidden_here + at + step)
            hidden = dot(rows, w1_ref[t, :, cols])
            active_grad = dot(rows_grad, w2_ref[t, cols, :], 1, 1)
            active, slope = gelu_parts(hidden)
            act_ref[:, place] = active.astype(BF)
            hg_ref[:, place] = (active_grad * slope).astype(BF)
    out = None
    grad = None
    for t in range(parts):
        place = slice(t * hidden_here, (t + 1) * hidden_here)
        part = dot(act_ref[:, place], w2_ref[t])
        out = part if out is None else out + part
        part = dot(hg_ref[:, place], w1_ref[t], 1, 1)
        grad = part if grad is None else grad + part
    dx_ref[...] = grad.astype(BF)
    back_ref[...] = (gate * out).astype(BF)
    gate_grad = jnp.sum(upstream * out.astype(BF).astype(F32), -1, keepdims=True)
    gg_ref[...] = jnp.where(lane == 0, gate_grad, 0.0)


def expert(x, g, router, w1, w2):
    rows, width = x.shape
    total = w1.shape[0] * w1.shape[2]
    tile = next(size for size in (256, 224, 192, 128, 64, 32, 16) if rows % size == 0)

    def tiled(cols):
        return pl.BlockSpec((tile, cols), lambda i: (i, 0))

    flops = 8 * rows * width * total
    return pl.pallas_call(
        expert_kernel,
        grid=(rows // tile,),
        in_specs=[tiled(width), tiled(g.shape[1]), whole(router.shape), whole(w1.shape, True), whole(w2.shape, True)],
        out_specs=[tiled(width), tiled(total), tiled(total), tiled(width), tiled(width), tiled(LANES)],
        out_shape=[
            jax.ShapeDtypeStruct((rows, width), BF),
            jax.ShapeDtypeStruct((rows, total), BF),
            jax.ShapeDtypeStruct((rows, total), BF),
            jax.ShapeDtypeStruct((rows, width), BF),
            jax.ShapeDtypeStruct((rows, width), BF),
            jax.ShapeDtypeStruct((rows, LANES), F32),
        ],
        compiler_params=params(56),
        cost_estimate=pl.CostEstimate(flops=flops, bytes_accessed=rows * total * 6, transcendentals=rows * total * 2),
        name="expert",
    )(x, g, router, w1, w2)


def weight_kernel(count, *refs):
    ins, (out_ref,) = refs[:-1], refs[-1:]
    total = None
    for n in range(count):
        part = dot(ins[2 * n][...], ins[2 * n + 1][...], 0, 0)
        total = part if total is None else total + part
    out_ref[0] = total.astype(BF)


def weight_grad(columns, rows, parts):
    count = len(columns)
    total = columns[0].shape[1]
    width = rows[0].shape[1]
    here = total // parts
    step = min(512, here)
    per = here // step
    specs, args = [], []
    for a, b in zip(columns, rows):
        specs += [pl.BlockSpec((a.shape[0], step), lambda i: (0, i)), whole(b.shape, True)]
        args += [a, b]
    return pl.pallas_call(
        functools.partial(weight_kernel, count),
        grid=(total // step,),
        in_specs=specs,
        out_specs=pl.BlockSpec((1, step, width), lambda i: (i // per, i % per, 0)),
        out_shape=jax.ShapeDtypeStruct((parts, here, width), BF),
        compiler_params=params(),
        cost_estimate=pl.CostEstimate(
            flops=2 * sum(b.shape[0] for b in rows) * width * total, bytes_accessed=4 * total * width, transcendentals=0
        ),
        name="weight_grad",
    )(*args)


def shards(
    block_in,
    norm_one,
    head_in,
    head_out,
    norm_two,
    router,
    expert_in,
    expert_out,
    expert_ids,
    route_noise,
    cotangent,
):
    rows_here, width = block_in.shape
    parts = lax.axis_size("tensor")
    groups = lax.axis_size("expert")
    me = lax.axis_index("tensor")
    images = rows_here // SEQ
    own = -(-images // parts)
    image_slots = own * parts
    height = up_to(SEQ, 16)
    experts = router.shape[1]
    capacity = (rows_here * 2 * 8 // (5 * experts) + 15) // 16 * 16
    share = -(-capacity // parts)
    slots = up_to(share, 16 * CHUNKS) // CHUNKS
    chunk_rows = experts * slots
    full = rows_here // 16 * 16

    def tail_of(x):
        return jnp.pad(x[full:], ((0, 16 - (rows_here - full)), (0, 0)))

    def gathered(x):
        return lax.all_gather(x, "tensor", axis=0, tiled=False)

    def to_images(x, value):
        x = x.reshape(images, SEQ, x.shape[-1])
        return jnp.pad(
            x, ((0, image_slots - images), (0, height - SEQ), (0, 0)), constant_values=value
        )

    def own_images(x):
        pieces = []
        for n in range(own):
            at = jnp.minimum(me * own + n, images - 1) * SEQ
            piece = lax.dynamic_slice(x, (at, 0), (SEQ, x.shape[1]))
            pieces.append(jnp.pad(piece, ((0, height - SEQ), (0, 0))))
        return jnp.stack(pieces)

    def swap(x, axis):
        return lax.all_to_all(x, axis, split_axis=0, concat_axis=0, tiled=True)

    names = jnp.arange(experts, dtype=jnp.int32)
    member = [(expert_ids[:, c : c + 1] == names).astype(jnp.int32) for c in range(2)]
    both = member[0] + member[1]
    earlier = jnp.cumsum(both, 0) - both
    slot = jnp.stack([jnp.sum(earlier * item, -1) for item in member], 1)
    local = slot - me * share
    chunk = local // slots
    place = chunk * chunk_rows + expert_ids * slots + local % slots
    place = jnp.where((local >= 0) & (local < share), place, -1)
    place_flat = jnp.pad(place.T, ((0, 0), (0, full + 16 - rows_here)), constant_values=-1)
    place_images = to_images(place, -1)
    place_lanes = place_images.reshape(image_slots * height, 2).T
    ids_images = to_images(expert_ids, -1)
    noise_images = to_images(route_noise, 0.0)
    ids_own = lax.dynamic_slice_in_dim(ids_images, me * own, own, 0)
    noise_own = lax.dynamic_slice_in_dim(noise_images, me * own, own, 0)

    sides = []
    for c in range(2):
        gap = route_noise[:, c] - route_noise[:, 1 - c]
        high = gap.astype(BF)
        left = gap - high.astype(F32)
        mid = left.astype(BF)
        low = (left - mid.astype(F32)).astype(BF)
        columns = [expert_ids[:, 1 - c].astype(BF), high, mid, low, expert_ids[:, c].astype(BF)]
        sides.append(jnp.stack(columns, 1))
    side = jnp.pad(jnp.stack(sides), ((0, 0), (0, full + 16 - rows_here), (0, LANES - 5)))

    router_wide = jnp.pad(router, ((0, 0), (0, LANES - experts)))
    gain_one, gain_two = norm_one[None, :], norm_two[None, :]
    head_out_all = gathered(head_out)
    w1 = gathered(expert_in[0])

    tail = tail_of(cotangent)
    signals = [
        swap(pack_first(cotangent, tail, place_flat, side, experts, slots, n * chunk_rows), "expert")
        for n in range(CHUNKS)
    ]

    mixed, first_in, qkv, logs = attend(
        block_in, tail_of(block_in), gain_one, head_in, images, image_slots, height
    )
    mixed_rows = swap(mixed, "tensor").reshape(parts, own, height, mixed.shape[2])
    x_own = own_images(block_in)
    valid = (me * own + jnp.arange(own) < images)[:, None, None]
    up_own = jnp.where(valid, own_images(cotangent), 0)
    middle, second_in, gates = middle_of(
        mixed_rows, head_out_all, x_own, gain_two, router_wide, ids_own, noise_own
    )
    second_all = gathered(second_in).reshape(image_slots * height, width)
    second_all, late_out = lax.optimization_barrier((second_all, expert_out[0]))
    w2 = gathered(late_out)

    backs, actives, hidden_grads, rows_grads, arrived, returned, gate_grads = [], [], [], [], [], [], []
    for n in range(CHUNKS):
        x = swap(pack(second_all, place_lanes, experts, slots, n * chunk_rows), "expert")
        x = x.reshape(groups * slots, width)
        signal = signals[n].reshape(groups * slots, width + LANES)
        back, active, hidden_grad, rows_grad, row_grad, gate_grad = expert(x, signal, router_wide, w1, w2)
        arrived.append(x)
        actives.append(active)
        hidden_grads.append(hidden_grad)
        rows_grads.append(rows_grad)
        backs.append(back)
        returned.append(swap(row_grad.reshape(experts, slots, width), "expert").reshape(chunk_rows, width))
        gate_grads.append(swap(gate_grad[:, 0].reshape(experts, slots), "expert").reshape(1, chunk_rows))

    out_grad = lax.psum_scatter(weight_grad(actives, rows_grads, parts), "tensor", scatter_dimension=0)
    in_grad_parts = weight_grad(hidden_grads, arrived, parts)

    second_sum = lax.psum_scatter(
        unpack(place_images, returned, gate_grads), "tensor", scatter_dimension=0, tiled=True
    )
    middle_grad, mixed_grad, head_out_part, router_part, norm_two_part = middle_back(
        second_sum, middle, second_in, gates, ids_own, up_own, mixed_rows, head_out_all, gain_two, router_wide
    )
    mixed_grad = swap(mixed_grad.reshape(image_slots, height, mixed.shape[2]), "tensor")
    in_grad_parts, mixed_grad = lax.optimization_barrier((in_grad_parts, mixed_grad))
    in_grad = lax.psum_scatter(in_grad_parts, "tensor", scatter_dimension=0)
    mixed_grad, *backs = lax.optimization_barrier((mixed_grad, *backs))
    combined = [swap(item.reshape(experts, slots, width), "expert").reshape(chunk_rows, width) for item in backs]
    first_part, head_in_part = attend_back(mixed_grad, qkv, logs, first_in, head_in)
    first_grad = lax.psum_scatter(first_part, "tensor", scatter_dimension=0, tiled=True)
    input_part, norm_one_part = input_back(first_grad, x_own, middle_grad, gain_one)

    def to_rows(x):
        return x[:images, :SEQ].reshape(rows_here, width)

    input_grad = to_rows(gathered(input_part).reshape(image_slots, height, width)).astype(F32)
    out_sum = lax.psum_scatter(unpack(place_images, combined), "tensor", scatter_dimension=0, tiled=True)
    block_own = (middle + out_sum.astype(F32)).astype(BF)
    block_out = to_rows(gathered(block_own).reshape(image_slots, height, width))

    head_in_grad = lax.psum(head_in_part, "expert").astype(F32)
    head_out_grad = lax.psum(lax.psum_scatter(head_out_part, "tensor", scatter_dimension=0), "expert").astype(F32)
    small = lax.psum(
        jnp.concatenate([norm_one_part, norm_two_part, router_part[:experts]], 0), ("expert", "tensor")
    )
    return (
        block_out,
        input_grad,
        small[0],
        head_in_grad,
        head_out_grad,
        small[1],
        small[2:].T,
        in_grad.astype(F32).T[None],
        out_grad.astype(F32)[None],
    )


def solution(mesh):
    in_specs = (
        P("expert", None),
        P(),
        P(None, None, "tensor"),
        P("tensor", None),
        P(),
        P(),
        P("expert", None, "tensor"),
        P("expert", "tensor", None),
        P("expert", None),
        P("expert", None),
        P("expert", None),
    )
    out_specs = (
        P("expert", None),
        P("expert", None),
        P(),
        P(None, None, "tensor"),
        P("tensor", None),
        P(),
        P(),
        P("expert", None, "tensor"),
        P("expert", "tensor", None),
    )
    return jax.shard_map(shards, mesh=mesh, in_specs=in_specs, out_specs=out_specs, check_vma=False)
```

```python
import functools

import jax
import jax.numpy as jnp
from jax import lax
from jax.experimental import pallas as pl
from jax.experimental.pallas import tpu as pltpu
from jax.sharding import PartitionSpec as P

HD = 64
SEQ = 197
LANES = 128
EPSILON = 1e-06
CHUNKS = 2
BF = jnp.bfloat16
F32 = jnp.float32


def up_to(value, unit):
    return -(-value // unit) * unit


def params(mib=48):
    return pltpu.CompilerParams(vmem_limit_bytes=mib * 1024 * 1024)


def dot(a, b, da=1, db=0):
    return lax.dot_general(a, b, (((da,), (db,)), ((), ())), preferred_element_type=F32)


def iota(rows, cols, dim):
    return lax.broadcasted_iota(jnp.int32, (rows, cols), dim)


def flag(mask):
    return jnp.where(mask, 1.0, 0.0)


def whole(shape, once=False):
    zeros = (0,) * len(shape)
    mode = pl.Buffered(1) if once else None
    return pl.BlockSpec(shape, lambda *_: zeros, pipeline_mode=mode)


def image(*shape):
    return pl.BlockSpec((1,) + shape, lambda i, *_: (i,) + (0,) * len(shape))


def fill(x_ref, tail_ref, rows_ref):
    full = x_ref.shape[0] // 16 * 16
    rows_ref[0:full, :] = x_ref[0:full, :]
    rows_ref[full : full + 16, :] = tail_ref[...]
    rest = rows_ref.shape[0] - full - 16
    if rest:
        rows_ref[full + 16 :, :] = jnp.zeros((rest, rows_ref.shape[1]), BF)


def norm_parts(field):
    centre = field - jnp.mean(field, -1, keepdims=True)
    spread = lax.rsqrt(jnp.mean(centre * centre, -1, keepdims=True) + EPSILON)
    return centre * spread, spread


def norm_field_back(upstream, gain, scaled, spread):
    weighted = upstream * gain
    return spread * (
        weighted
        - jnp.mean(weighted, -1, keepdims=True)
        - scaled * jnp.mean(weighted * scaled, -1, keepdims=True)
    )


def cost(flops, size):
    return pl.CostEstimate(flops=flops, bytes_accessed=size, transcendentals=0)


def halves(steps, tail, dtype):
    half = steps // 2
    shape = jax.ShapeDtypeStruct((half,) + tail, dtype)
    zeros = (0,) * len(tail)
    specs = [
        pl.BlockSpec((1,) + tail, lambda i, *_: (jnp.minimum(i, half - 1),) + zeros),
        pl.BlockSpec((1,) + tail, lambda i, *_: (jnp.maximum(i - half, 0),) + zeros),
    ]
    return specs, [shape, shape]


def store_half(low_ref, high_ref, value):
    early = pl.program_id(0) < pl.num_programs(0) // 2

    @pl.when(early)
    def _():
        low_ref[0] = value

    @pl.when(jnp.logical_not(early))
    def _():
        high_ref[0] = value


def head_masks():
    lane = iota(1, LANES, 1)
    return [(flag(lane // HD == h)).astype(BF) for h in range(2)]


def attend_kernel(images, order_ref, x_ref, tail_ref, gain_ref, w_ref, mixed_ref, first_ref, qkv_ref, log_ref, rows):
    @pl.when(pl.program_id(0) == 0)
    def _():
        fill(x_ref, tail_ref, rows)

    i = order_ref[pl.program_id(0)]
    height = first_ref.shape[1]
    window = height + 16
    start = jnp.minimum(i, images - 1) * SEQ
    aligned = start // 16 * 16
    r, c = iota(height, window, 0), iota(height, window, 1)
    limit = jnp.where(i < images, SEQ, 0)
    shift = flag((c == r + (start - aligned)) & (r < limit)).astype(BF)
    field = dot(shift, rows[pl.ds(pl.multiple_of(aligned, 16), window), :])
    scaled, _ = norm_parts(field)
    first = (scaled * gain_ref[...]).astype(BF)
    first_ref[0] = first
    for k in range(3):
        qkv_ref[k, 0] = dot(first, w_ref[k]).astype(BF)
    masks = head_masks()
    lane = iota(1, LANES, 1)
    key_lane = iota(1, height, 1)
    logs = jnp.zeros((height, LANES), F32)
    for pair in range(mixed_ref.shape[2] // LANES):
        cols = slice(pair * LANES, (pair + 1) * LANES)
        queries, keys, values = (qkv_ref[k, 0, :, cols] for k in range(3))
        total = jnp.zeros((height, LANES), F32)
        for h in range(2):
            scores = dot(queries * masks[h], keys, 1, 1) * HD ** (-0.5)
            scores = jnp.where(key_lane < SEQ, scores, -1e30)
            highest = jnp.max(scores, -1, keepdims=True)
            weights = jnp.exp(scores - highest)
            sums = jnp.sum(weights, -1, keepdims=True)
            probs = (weights * (1.0 / sums)).astype(BF)
            total += dot(probs, values * masks[h])
            logs = jnp.where(lane == pair * 2 + h, highest + jnp.log(sums), logs)
        mixed_ref[0, :, cols] = total.astype(BF)
    log_ref[0] = logs


def attend(order, block_in, tail, gain, head_in, images, image_slots, height):
    rows, width = block_in.shape
    cols = head_in.shape[2]
    spec = pltpu.PrefetchScalarGridSpec(
        num_scalar_prefetch=1,
        grid=(image_slots,),
        in_specs=[whole((rows, width), True), whole((16, width)), whole((1, width)), whole(head_in.shape, True)],
        out_specs=[
            image(height, cols),
            image(height, width),
            pl.BlockSpec((3, 1, height, cols), lambda i, *_: (0, i, 0, 0)),
            image(height, LANES),
        ],
        scratch_shapes=[pltpu.VMEM((rows // 16 * 16 + 48, width), BF)],
    )
    return pl.pallas_call(
        functools.partial(attend_kernel, images),
        grid_spec=spec,
        out_shape=[
            jax.ShapeDtypeStruct((image_slots, height, cols), BF),
            jax.ShapeDtypeStruct((image_slots, height, width), BF),
            jax.ShapeDtypeStruct((3, image_slots, height, cols), BF),
            jax.ShapeDtypeStruct((image_slots, height, LANES), F32),
        ],
        compiler_params=params(),
        cost_estimate=cost(16 * image_slots * height * width * cols, 16 * rows * width),
        name="attend",
    )(order, block_in, tail, gain, head_in)


def attend_back_kernel(
    dmix_ref, qkv_ref, log_ref, first_ref, wt_ref, gain_ref, low_ref, high_ref, hg_ref, ng_ref, acc, grads
):
    i = pl.program_id(0)
    height = first_ref.shape[1]
    masks = head_masks()
    lane = iota(1, LANES, 1)
    key_lane = iota(1, height, 1)
    scale = HD ** (-0.5)
    logs = log_ref[0]
    for pair in range(dmix_ref.shape[2] // LANES):
        cols = slice(pair * LANES, (pair + 1) * LANES)
        queries, keys, values = (qkv_ref[k, 0, :, cols] for k in range(3))
        out_grad = dmix_ref[0, :, cols]
        dq = jnp.zeros((height, LANES), F32)
        dk = jnp.zeros((height, LANES), F32)
        dv = jnp.zeros((height, LANES), F32)
        for h in range(2):
            q_h = queries * masks[h]
            o_h = out_grad * masks[h]
            log_h = jnp.sum(jnp.where(lane == pair * 2 + h, logs, 0.0), -1, keepdims=True)
            probs = jnp.exp(dot(q_h, keys, 1, 1) * scale - log_h)
            probs = jnp.where(key_lane < SEQ, probs, 0.0)
            prob_grad = dot(o_h, values, 1, 1)
            dv += dot(probs.astype(BF), o_h, 0, 0)
            delta = jnp.sum(probs * prob_grad, -1, keepdims=True)
            score_grad = (probs * (prob_grad - delta)).astype(BF)
            dq += dot(score_grad, keys * masks[h])
            dk += dot(score_grad, q_h, 0, 0)
        grads[0, :, cols] = (dq * scale).astype(BF)
        grads[1, :, cols] = (dk * scale).astype(BF)
        grads[2, :, cols] = dv.astype(BF)

    @pl.when(i == 0)
    def _():
        acc[...] = jnp.zeros_like(acc)

    first = first_ref[0]
    total = None
    for k in range(3):
        part = dot(grads[k], wt_ref[k])
        total = part if total is None else total + part
        acc[k] += dot(grads[k], first, 0, 0)
    store_half(low_ref, high_ref, total.astype(BF))

    @pl.when(i == pl.num_programs(0) - 1)
    def _():
        hg_ref[...] = acc[...].astype(BF)
        gain_grad = jnp.zeros_like(ng_ref)
        for k in range(3):
            gain_grad += jnp.sum(acc[k] * wt_ref[k].astype(F32), 0, keepdims=True)
        ng_ref[...] = gain_grad / gain_ref[...]


def attend_back(dmix, qkv, logs, first, head_in_t, gain):
    image_slots, height, cols = dmix.shape
    width = first.shape[2]
    specs, shapes = halves(image_slots, (height, width), BF)
    return pl.pallas_call(
        attend_back_kernel,
        grid=(image_slots,),
        in_specs=[
            image(height, cols),
            pl.BlockSpec((3, 1, height, cols), lambda i: (0, i, 0, 0)),
            image(height, LANES),
            image(height, width),
            whole(head_in_t.shape, True),
            whole((1, width)),
        ],
        out_specs=specs + [whole(head_in_t.shape), whole((1, width))],
        out_shape=shapes
        + [jax.ShapeDtypeStruct(head_in_t.shape, BF), jax.ShapeDtypeStruct((1, width), F32)],
        scratch_shapes=[pltpu.VMEM(head_in_t.shape, F32), pltpu.VMEM((3, height, cols), BF)],
        compiler_params=params(),
        cost_estimate=cost(24 * image_slots * height * width * cols, 20 * image_slots * height * width),
        name="attend_back",
    )(dmix, qkv, logs, first, head_in_t, gain)


def pack_first_kernel(slots, base, x_ref, tail_ref, lp_ref, side_ref, out_ref, rows):
    e = pl.program_id(0)

    @pl.when(e == 0)
    def _():
        fill(x_ref, tail_ref, rows)

    j = base + e * slots + iota(slots, rows.shape[0], 0)
    picks = [flag(lp_ref[c : c + 1, :] == j) for c in range(2)]
    width = x_ref.shape[1]
    out_ref[0, :, 0:width] = dot((picks[0] + picks[1]).astype(BF), rows[...]).astype(BF)
    out_ref[0, :, width:] = (
        dot(picks[0].astype(BF), side_ref[0]) + dot(picks[1].astype(BF), side_ref[1])
    ).astype(BF)


def pack_first(x, tail, lp, side, experts, slots, base):
    rows, width = x.shape
    padded = lp.shape[1]
    return pl.pallas_call(
        functools.partial(pack_first_kernel, slots, base),
        grid=(experts,),
        in_specs=[whole((rows, width), True), whole((16, width)), whole(lp.shape), whole(side.shape)],
        out_specs=image(slots, width + LANES),
        out_shape=jax.ShapeDtypeStruct((experts, slots, width + LANES), BF),
        scratch_shapes=[pltpu.VMEM((padded, width), BF)],
        compiler_params=params(),
        cost_estimate=cost(3 * experts * slots * padded * width, 2 * rows * width),
        name="pack_cotangent",
    )(x, tail, lp, side)


def pack_kernel(slots, base, count, *refs):
    lp_ref, out_ref = refs[count], refs[count + 1]
    total = None
    for p in range(count):
        j = base + pl.program_id(0) * slots + iota(slots, refs[p].shape[0], 0)
        picks = flag((lp_ref[p, 0:1, :] == j) | (lp_ref[p, 1:2, :] == j)).astype(BF)
        part = dot(picks, refs[p][...])
        total = part if total is None else total + part
    out_ref[0] = total.astype(BF)


def pack(pieces, lp, experts, slots, base):
    rows, width = pieces[0].shape
    count = len(pieces)
    return pl.pallas_call(
        functools.partial(pack_kernel, slots, base, count),
        grid=(experts,),
        in_specs=[whole((rows, width), True)] * count + [whole(lp.shape)],
        out_specs=image(slots, width),
        out_shape=jax.ShapeDtypeStruct((experts, slots, width), BF),
        compiler_params=params(),
        cost_estimate=cost(3 * experts * slots * rows * count * width, 2 * rows * count * width),
        name="pack_rows",
    )(*pieces, lp)


def unpack_kernel(count, slots, per, graded, lp_ref, *refs):
    row_refs, (low_ref, high_ref) = refs[:count], refs[count:]
    lp = lp_ref[0]
    height = lp.shape[0]
    rows, width = row_refs[0].shape
    total = jnp.zeros((height, width), F32)
    lanes = up_to(slots, LANES)
    extra = [jnp.zeros((height, lanes), F32) for _ in range(2)]
    for n in range(count):
        j = n * rows + iota(1, rows, 1)
        hits = (lp[:, 0:1] == j) | (lp[:, 1:2] == j)
        total += dot(flag(hits).astype(BF), row_refs[n][...])
        if graded:
            j = iota(1, lanes, 1)
            for e in range(rows // slots):
                spare = row_refs[n][(e + 1) * slots - 16 : (e + 1) * slots, 0 : 2 * lanes].astype(F32)
                spare = spare[per + 16 - slots : per + 17 - slots, :]
                values = spare[:, :lanes] + spare[:, lanes:]
                for c in range(2):
                    hit = lp[:, c : c + 1] - (n * rows + e * slots) == j
                    extra[c] += jnp.where(hit, values, 0.0)
    value = total.astype(BF)
    if graded:
        lane = iota(1, LANES, 1)
        tail = jnp.zeros((height, LANES), F32)
        for c in range(2):
            grad = jnp.sum(extra[c], -1, keepdims=True)
            high = grad.astype(BF).astype(F32)
            tail = jnp.where(lane == c, high, tail)
            tail = jnp.where(lane == 2 + c, grad - high, tail)
        value = jnp.concatenate([value, tail.astype(BF)], 1)
    store_half(low_ref, high_ref, value)


def unpack(lp, rows, slots, per, graded):
    image_slots, height, _ = lp.shape
    count = len(rows)
    width = rows[0].shape[1]
    specs, shapes = halves(image_slots, (height, width + (LANES if graded else 0)), BF)
    return pl.pallas_call(
        functools.partial(unpack_kernel, count, slots, per, graded),
        grid=(image_slots,),
        in_specs=[image(height, 2)] + [whole(item.shape, True) for item in rows],
        out_specs=specs,
        out_shape=shapes,
        compiler_params=params(),
        cost_estimate=cost(3 * image_slots * height * count * rows[0].size, 4 * count * rows[0].size),
        name="unpack_rows",
    )(lp, *rows)


def to_rows_kernel(own, height, count, start_ref, *refs):
    out_ref, rows = refs[count], refs[count + 1]
    b = pl.program_id(0)

    @pl.when(b == 0)
    def _():
        for p in range(count):
            at = pl.multiple_of(start_ref[p], 16)
            rows[pl.ds(at, own * height), :] = refs[p][...]

    tile = out_ref.shape[0]
    window = up_to(tile + 3 * (height - SEQ) + 16, 16)
    lift = height - SEQ
    first = b * tile
    start = (first + lift * (first // SEQ)) // 16 * 16
    start = jnp.minimum(start, rows.shape[0] - window)
    r = first + iota(tile, 1, 0)
    steps = sum(jnp.where(r >= (first // SEQ + n) * SEQ, 1, 0) for n in (1, 2))
    target = r + lift * (first // SEQ + steps) - start
    picks = flag(iota(tile, window, 1) == target).astype(BF)
    out_ref[...] = dot(picks, rows[pl.ds(pl.multiple_of(start, 16), window), :]).astype(out_ref.dtype)


def to_rows(starts, pieces, rows, dtype, height):
    each, width = pieces[0].shape
    count = len(pieces)
    spec = pltpu.PrefetchScalarGridSpec(
        num_scalar_prefetch=1,
        grid=(-(-rows // 208),),
        in_specs=[whole((each, width), True)] * count,
        out_specs=pl.BlockSpec((208, width), lambda i, *_: (i, 0)),
        scratch_shapes=[pltpu.VMEM((each * count, width), BF)],
    )
    return pl.pallas_call(
        functools.partial(to_rows_kernel, each // height, height, count),
        grid_spec=spec,
        out_shape=jax.ShapeDtypeStruct((rows, width), dtype),
        compiler_params=params(),
        cost_estimate=cost(2 * rows * 256 * width, 8 * rows * width),
        name="to_rows",
    )(starts, *pieces)


def middle_kernel(count, *refs):
    mixed_refs, wo_refs = refs[:count], refs[count : 2 * count]
    x_ref, gain_ref, router_ref, ids_ref, noise_ref, mid_ref, second_ref, gates_ref = refs[2 * count :]
    middle = x_ref[0].astype(F32)
    for mixed_ref, wo_ref in zip(mixed_refs, wo_refs):
        middle += dot(mixed_ref[0], wo_ref[...])
    mid_ref[0] = middle
    scaled, _ = norm_parts(middle)
    second = (scaled * gain_ref[...]).astype(BF)
    second_ref[0] = second
    logits = dot(second, router_ref[...])
    lane = iota(1, LANES, 1)
    chosen = [
        jnp.sum(jnp.where(lane == ids_ref[0, :, c : c + 1], logits, 0.0), -1, keepdims=True)
        + noise_ref[0, :, c : c + 1]
        for c in range(2)
    ]
    top = jnp.maximum(chosen[0], chosen[1])
    raw = [jnp.exp(item - top) for item in chosen]
    inverse = 1.0 / (raw[0] + raw[1])
    gates_ref[0] = jnp.where(lane == 0, raw[0] * inverse, 0.0) + jnp.where(lane == 1, raw[1] * inverse, 0.0)


def middle_of(mixed, head_out, x_own, gain, router, ids, noise):
    own, height, cols = mixed[0].shape
    parts = len(mixed)
    width = x_own.shape[2]
    return pl.pallas_call(
        functools.partial(middle_kernel, parts),
        grid=(own,),
        in_specs=[image(height, cols)] * parts
        + [whole((cols, width), True)] * parts
        + [
            image(height, width),
            whole((1, width)),
            whole(router.shape),
            image(height, 2),
            image(height, 2),
        ],
        out_specs=[image(height, width), image(height, width), image(height, LANES)],
        out_shape=[
            jax.ShapeDtypeStruct((own, height, width), F32),
            jax.ShapeDtypeStruct((own, height, width), BF),
            jax.ShapeDtypeStruct((own, height, LANES), F32),
        ],
        compiler_params=params(),
        cost_estimate=cost(4 * own * height * width * width, 24 * own * height * width),
        name="middle",
    )(*mixed, *head_out, x_own, gain, router, ids, noise)


def middle_back_kernel(count, *refs):
    rs_ref, mid_ref, second_ref, gates_ref, ids_ref, up_ref, gain_ref, router_ref = refs[:8]
    mixed_refs, wo_refs = refs[8 : 8 + count], refs[8 + count : 8 + 2 * count]
    mg_ref, hog_ref, rg_ref, ng_ref = refs[8 + 2 * count : 12 + 2 * count]
    dmix_refs, hog_acc = refs[12 + 2 * count : -1], refs[-1]
    i = pl.program_id(0)

    @pl.when(i == 0)
    def _():
        hog_acc[...] = jnp.zeros_like(hog_acc)
        rg_ref[...] = jnp.zeros_like(rg_ref)
        ng_ref[...] = jnp.zeros_like(ng_ref)

    width = up_ref.shape[2]
    lane = iota(1, LANES, 1)
    tail = rs_ref[0, :, width:]
    gates = gates_ref[0]
    gate, grad = [], []
    for c in range(2):
        gate.append(jnp.sum(jnp.where(lane == c, gates, 0.0), -1, keepdims=True))
        grad.append(jnp.sum(jnp.where((lane == c) | (lane == 2 + c), tail, 0.0), -1, keepdims=True))
    mean_term = gate[0] * grad[0] + gate[1] * grad[1]
    logit_grad = jnp.zeros((up_ref.shape[1], LANES), F32)
    for c in range(2):
        logit_grad = jnp.where(lane == ids_ref[0, :, c : c + 1], gate[c] * (grad[c] - mean_term), logit_grad)
    logit_grad = logit_grad.astype(BF)
    second_grad = rs_ref[0, :, 0:width] + dot(logit_grad, router_ref[...], 1, 1)
    rg_ref[...] += dot(logit_grad, second_ref[0], 0, 0)
    scaled, spread = norm_parts(mid_ref[0])
    ng_ref[...] += jnp.sum(second_grad * scaled, 0, keepdims=True)
    middle_grad = up_ref[0].astype(F32) + norm_field_back(second_grad, gain_ref[...], scaled, spread)
    mg_ref[0] = middle_grad
    rounded = middle_grad.astype(BF)
    for t in range(count):
        dmix_refs[t][0] = dot(rounded, wo_refs[t][...], 1, 1).astype(BF)
        hog_acc[t] += dot(mixed_refs[t][0], rounded, 0, 0)

    @pl.when(i == pl.num_programs(0) - 1)
    def _():
        hog_ref[...] = hog_acc[...].astype(BF)


def middle_back(rs, middle, second, gates, ids, up, mixed, head_out, gain, router):
    own, height, cols = mixed[0].shape
    parts = len(mixed)
    width = up.shape[2]
    return pl.pallas_call(
        functools.partial(middle_back_kernel, parts),
        grid=(own,),
        in_specs=[
            image(height, rs.shape[2]),
            image(height, width),
            image(height, width),
            image(height, LANES),
            image(height, 2),
            image(height, width),
            whole((1, width)),
            whole(router.shape),
        ]
        + [image(height, cols)] * parts
        + [whole((cols, width), True)] * parts,
        out_specs=[image(height, width), whole((parts, cols, width)), whole((LANES, width)), whole((1, width))]
        + [image(height, cols)] * parts,
        out_shape=[
            jax.ShapeDtypeStruct((own, height, width), F32),
            jax.ShapeDtypeStruct((parts, cols, width), BF),
            jax.ShapeDtypeStruct((LANES, width), F32),
            jax.ShapeDtypeStruct((1, width), F32),
        ]
        + [jax.ShapeDtypeStruct((own, height, cols), BF)] * parts,
        scratch_shapes=[pltpu.VMEM((parts, cols, width), F32)],
        compiler_params=params(),
        cost_estimate=cost(8 * own * height * width * width, 40 * own * height * width),
        name="middle_back",
    )(rs, middle, second, gates, ids, up, gain, router, *mixed, *head_out)


def input_back_kernel(fg_ref, x_ref, mg_ref, gain_ref, out_ref):
    scaled, spread = norm_parts(x_ref[0].astype(F32))
    out_ref[0] = (mg_ref[0] + norm_field_back(fg_ref[0], gain_ref[...], scaled, spread)).astype(BF)


def input_back(first_grad, x_own, middle_grad, gain):
    own, height, width = x_own.shape
    return pl.pallas_call(
        input_back_kernel,
        grid=(own,),
        in_specs=[image(height, width)] * 3 + [whole((1, width))],
        out_specs=image(height, width),
        out_shape=jax.ShapeDtypeStruct((own, height, width), BF),
        compiler_params=params(),
        cost_estimate=cost(20 * own * height * width, 16 * own * height * width),
        name="input_back",
    )(first_grad, x_own, middle_grad, gain)


def gelu_parts(v):
    x = jnp.abs(v) * 0.7071067811865476
    t = 1.0 / (1.0 + 0.3275911 * x)
    bell = jnp.exp(-x * x)
    poly = ((((1.061405429 * t - 1.453152027) * t + 1.421413741) * t - 0.284496736) * t + 0.254829592) * t
    below = 0.5 * poly * bell
    share = jnp.where(v < 0.0, below, 1.0 - below)
    return v * share, share + v * bell * 0.3989422804014327


def expert_kernel(count, slots, per, x_ref, g_ref, router_ref, *refs):
    w1_refs, w2_refs = refs[:count], refs[count : 2 * count]
    back_ref, act_ref, hg_ref, rg_ref, dx_ref = refs[2 * count :]
    width = x_ref.shape[1]
    rows = x_ref[...]
    lane = iota(1, LANES, 1)
    side = g_ref[:, width:].astype(F32)

    def column(*lanes):
        keep = lane == lanes[0]
        for other in lanes[1:]:
            keep = keep | (lane == other)
        return jnp.sum(jnp.where(keep, side, 0.0), -1, keepdims=True)

    logits = dot(rows, router_ref[...])
    lane_f = lane.astype(F32)
    mine = jnp.sum(jnp.where(lane_f == column(4), logits, 0.0), -1, keepdims=True)
    other = jnp.sum(jnp.where(lane_f == column(0), logits, 0.0), -1, keepdims=True)
    gate = 1.0 / (1.0 + jnp.exp(other - mine - column(1, 2, 3)))
    upstream = g_ref[:, 0:width].astype(F32)
    rows_grad = (gate * upstream).astype(BF)
    rg_ref[...] = rows_grad
    hidden_here = w1_refs[0].shape[1]
    step = min(512, hidden_here)
    for t in range(count):
        for at in range(0, hidden_here, step):
            cols = slice(at, at + step)
            place = slice(t * hidden_here + at, t * hidden_here + at + step)
            hidden = dot(rows, w1_refs[t][:, cols])
            active_grad = dot(rows_grad, w2_refs[t][cols, :], 1, 1)
            active, slope = gelu_parts(hidden)
            act_ref[:, place] = active.astype(BF)
            hg_ref[:, place] = (active_grad * slope).astype(BF)
    out = None
    grad = None
    for t in range(count):
        place = slice(t * hidden_here, (t + 1) * hidden_here)
        part = dot(act_ref[:, place], w2_refs[t][...])
        out = part if out is None else out + part
        part = dot(hg_ref[:, place], w1_refs[t][...], 1, 1)
        grad = part if grad is None else grad + part
    dx_ref[...] = grad.astype(BF)
    back_ref[...] = (gate * out).astype(BF)
    gate_grad = jnp.sum(upstream * out.astype(BF).astype(F32), -1, keepdims=True)
    lanes = up_to(slots, LANES)
    spread = iota(slots, lanes, 0) == iota(slots, lanes, 1)
    spare_row = iota(16, 1, 0) == per + 16 - slots
    for b in range(x_ref.shape[0] // slots):
        end = (b + 1) * slots
        line = jnp.sum(jnp.where(spread, gate_grad[end - slots : end], 0.0), 0, keepdims=True)
        high = line.astype(BF).astype(F32)
        line = jnp.concatenate([high, line - high, jnp.zeros((1, width - 2 * lanes), F32)], 1)
        dx_ref[end - 16 : end, :] = jnp.where(spare_row, line, grad[end - 16 : end]).astype(BF)


def expert(x, g, router, w1, w2, slots, per):
    rows, width = x.shape
    count = len(w1)
    total = count * w1[0].shape[1]
    blocks = rows // slots
    tile = slots * max(n for n in range(1, blocks + 1) if blocks % n == 0 and n * slots <= 448)

    def tiled(cols):
        return pl.BlockSpec((tile, cols), lambda i: (i, 0))

    flops = 8 * rows * width * total
    return pl.pallas_call(
        functools.partial(expert_kernel, count, slots, per),
        grid=(rows // tile,),
        in_specs=[tiled(width), tiled(g.shape[1]), whole(router.shape)]
        + [whole(item.shape, True) for item in w1]
        + [whole(item.shape, True) for item in w2],
        out_specs=[tiled(width), tiled(total), tiled(total), tiled(width), tiled(width)],
        out_shape=[
            jax.ShapeDtypeStruct((rows, width), BF),
            jax.ShapeDtypeStruct((rows, total), BF),
            jax.ShapeDtypeStruct((rows, total), BF),
            jax.ShapeDtypeStruct((rows, width), BF),
            jax.ShapeDtypeStruct((rows, width), BF),
        ],
        compiler_params=params(60),
        cost_estimate=pl.CostEstimate(flops=flops, bytes_accessed=rows * total * 6, transcendentals=rows * total * 2),
        name="expert",
    )(x, g, router, *w1, *w2)


def weight_kernel(count, *refs):
    ins, (low_ref, high_ref) = refs[:-2], refs[-2:]
    total = None
    for n in range(count):
        part = dot(ins[2 * n][...], ins[2 * n + 1][...], 0, 0)
        total = part if total is None else total + part
    store_half(low_ref, high_ref, total.astype(BF))


def weight_grad(columns, rows, parts):
    count = len(columns)
    total = columns[0].shape[1]
    width = rows[0].shape[1]
    here = total // parts
    step = min(512, here)
    specs, args = [], []
    for a, b in zip(columns, rows):
        specs += [pl.BlockSpec((a.shape[0], step), lambda i: (0, i)), whole(b.shape, True)]
        args += [a, b]
    steps = total // step
    out_specs, out_shape = halves(steps, (step, width), BF)
    low, high = pl.pallas_call(
        functools.partial(weight_kernel, count),
        grid=(steps,),
        in_specs=specs,
        out_specs=out_specs,
        out_shape=out_shape,
        compiler_params=params(),
        cost_estimate=pl.CostEstimate(
            flops=2 * sum(b.shape[0] for b in rows) * width * total, bytes_accessed=4 * total * width, transcendentals=0
        ),
        name="weight_grad",
    )(*args)
    return low.reshape(parts // 2, here, width), high.reshape(parts // 2, here, width)


def shards(
    block_in,
    norm_one,
    head_in,
    head_out,
    norm_two,
    router,
    expert_in,
    expert_out,
    expert_ids,
    route_noise,
    cotangent,
):
    rows_here, width = block_in.shape
    parts = lax.axis_size("tensor")
    groups = lax.axis_size("expert")
    me = lax.axis_index("tensor")
    images = rows_here // SEQ
    own = -(-images // parts)
    image_slots = own * parts
    height = up_to(SEQ, 16)
    experts = router.shape[1]
    capacity = (rows_here * 2 * 8 // (5 * experts) + 15) // 16 * 16
    share = -(-capacity // parts)
    per = -(-share // CHUNKS)
    slots = up_to(per + 1, 16)
    chunk_rows = experts * slots
    full = rows_here // 16 * 16

    paired = parts == 4
    order = (0, 2, 1, 3) if paired else tuple(range(parts))
    part_of = [me ^ k if paired else jnp.int32(k) for k in order]

    def cross(x, k):
        return lax.ppermute(x, "tensor", [(n, n ^ k) for n in range(parts)])

    def gathered(x):
        if not paired:
            every = lax.all_gather(x, "tensor", axis=0, tiled=False)
            return [every[p] for p in range(parts)]
        far, near = cross(x, 2), cross(x, 1)
        return [x, far, near, cross(far, 1)]

    def scattered(low, high):
        if not paired:
            both = jnp.concatenate([low, high], 0)
            return lax.psum_scatter(both, "tensor", scatter_dimension=0).astype(F32)
        both = (low.astype(F32) + cross(high, 1).astype(F32)).astype(BF)
        return both[0].astype(F32) + cross(both[1], 2).astype(F32)

    def swapped(pieces):
        if not paired:
            every = lax.all_to_all(jnp.stack(pieces), "tensor", split_axis=0, concat_axis=0, tiled=True)
            return [every[p] for p in range(parts)]
        return [cross(piece, k) if k else piece for piece, k in zip(pieces, order)]

    def over_experts(x):
        return lax.all_to_all(x, "expert", split_axis=0, concat_axis=0, tiled=True)

    def pinned(*items):
        return lax.optimization_barrier(items)

    def tail_of(x):
        return jnp.pad(x[full:], ((0, 16 - (rows_here - full)), (0, 0)))

    def to_images(x, value):
        x = x.reshape(images, SEQ, x.shape[-1])
        return jnp.pad(
            x, ((0, image_slots - images), (0, height - SEQ), (0, 0)), constant_values=value
        )

    def own_images(x):
        pieces = []
        for n in range(own):
            at = jnp.minimum(me * own + n, images - 1) * SEQ
            piece = lax.dynamic_slice(x, (at, 0), (SEQ, x.shape[1]))
            pieces.append(jnp.pad(piece, ((0, height - SEQ), (0, 0))))
        return jnp.stack(pieces)

    names = jnp.arange(experts, dtype=jnp.int32)
    member = [(expert_ids[:, c : c + 1] == names).astype(jnp.int32) for c in range(2)]
    both = member[0] + member[1]
    earlier = jnp.cumsum(both, 0) - both
    slot = jnp.stack([jnp.sum(earlier * item, -1) for item in member], 1)
    local = slot - me * share
    place = local // per * chunk_rows + expert_ids * slots + local % per
    place = jnp.where((local >= 0) & (local < share), place, -1)
    place_flat = jnp.pad(place.T, ((0, 0), (0, full + 16 - rows_here)), constant_values=-1)
    place_images = to_images(place, -1)
    place_images = jnp.concatenate(
        [lax.dynamic_slice_in_dim(place_images, part * own, own, 0) for part in part_of], 0
    )
    place_lanes = jnp.swapaxes(place_images.reshape(parts, own * height, 2), 1, 2)
    ids_own = lax.dynamic_slice_in_dim(to_images(expert_ids, -1), me * own, own, 0)
    noise_own = lax.dynamic_slice_in_dim(to_images(route_noise, 0.0), me * own, own, 0)
    image_order = jnp.concatenate([part * own + jnp.arange(own, dtype=jnp.int32) for part in part_of])
    row_starts = jnp.stack([part * (own * height) for part in part_of]).astype(jnp.int32)

    sides = []
    for c in range(2):
        gap = route_noise[:, c] - route_noise[:, 1 - c]
        high = gap.astype(BF)
        left = gap - high.astype(F32)
        mid = left.astype(BF)
        low = (left - mid.astype(F32)).astype(BF)
        columns = [expert_ids[:, 1 - c].astype(BF), high, mid, low, expert_ids[:, c].astype(BF)]
        sides.append(jnp.stack(columns, 1))
    side = jnp.pad(jnp.stack(sides), ((0, 0), (0, full + 16 - rows_here), (0, LANES - 5)))

    router_wide = jnp.pad(router, ((0, 0), (0, LANES - experts)))
    gain_one, gain_two = norm_one[None, :], norm_two[None, :]
    head_out_all = gathered(head_out)
    w1 = gathered(expert_in[0])

    tail = tail_of(cotangent)
    packed = [
        pack_first(cotangent, tail, place_flat, side, experts, slots, n * chunk_rows) for n in range(CHUNKS)
    ]
    block_rows, *packed = pinned(block_in, *packed)
    signals = [over_experts(item) for item in packed]

    mixed, first_in, qkv, logs = attend(
        image_order, block_rows, tail_of(block_in), gain_one, head_in, images, image_slots, height
    )
    mixed = swapped([mixed[p * own : (p + 1) * own] for p in range(parts)])
    *mixed, signals[0] = pinned(*mixed, signals[0])
    x_own = own_images(block_in)
    valid = (me * own + jnp.arange(own) < images)[:, None, None]
    up_own = jnp.where(valid, own_images(cotangent), 0)
    middle, second_in, gates = middle_of(
        mixed, head_out_all, x_own, gain_two, router_wide, ids_own, noise_own
    )
    *second_all, late_out, signals[-1] = pinned(*gathered(second_in), expert_out[0], signals[-1])
    w2 = gathered(late_out)
    second_all = [item.reshape(own * height, width) for item in second_all]

    outgoing = [pack(second_all, place_lanes, experts, slots, n * chunk_rows) for n in range(CHUNKS)]
    backs, actives, hidden_grads, rows_grads, arrived, returned = [], [], [], [], [], []
    x = over_experts(outgoing[0])
    for n in range(CHUNKS):
        coming = None
        if n + 1 < CHUNKS:
            x, ready = pinned(x, outgoing[n + 1])
            coming = over_experts(ready)
        x = x.reshape(groups * slots, width)
        signal = signals[n].reshape(groups * slots, width + LANES)
        back, active, hidden_grad, rows_grad, row_grad = expert(x, signal, router_wide, w1, w2, slots, per)
        arrived.append(x)
        actives.append(active)
        hidden_grads.append(hidden_grad)
        rows_grads.append(rows_grad)
        backs.append(back)
        if coming is not None:
            x, row_grad = pinned(coming, row_grad)
        returned.append(over_experts(row_grad.reshape(experts, slots, width)))

    out_low, out_high = weight_grad(actives, rows_grads, parts)
    in_low, in_high = weight_grad(hidden_grads, arrived, parts)
    *returned, in_low, in_high, out_low, out_high = pinned(*returned, in_low, in_high, out_low, out_high)
    out_grad = scattered(out_low, out_high)

    def whole_rows(items):
        return [item.reshape(chunk_rows, width) for item in items]

    def by_part(x):
        return x.reshape((parts // 2, own) + x.shape[1:])

    low, high = unpack(place_images, whole_rows(returned), slots, per, True)
    second_sum = scattered(by_part(low), by_part(high))
    combined = [over_experts(item.reshape(experts, slots, width)) for item in backs]
    second_sum, combined[0] = pinned(second_sum, combined[0])
    middle_grad, head_out_part, router_part, norm_two_part, *mixed_grad = middle_back(
        second_sum, middle, second_in, gates, ids_own, up_own, mixed, head_out_all, gain_two, router_wide
    )
    *mixed_grad, in_low, in_high = pinned(*swapped(mixed_grad), in_low, in_high)
    in_grad = scattered(in_low, in_high)
    first_low, first_high, head_in_part, norm_one_part = attend_back(
        jnp.concatenate(mixed_grad, 0), qkv, logs, first_in, jnp.swapaxes(head_in, 1, 2), gain_one
    )
    first_low, first_high, combined[-1] = pinned(first_low, first_high, combined[-1])
    first_grad = scattered(by_part(first_low), by_part(first_high))
    input_part = input_back(first_grad, x_own, middle_grad, gain_one)

    def finished(x, dtype):
        pieces = [item.reshape(own * height, width) for item in gathered(x)]
        return to_rows(row_starts, pieces, rows_here, dtype, height)

    low, high = unpack(place_images, whole_rows(combined), slots, per, False)
    block_own = (middle + scattered(by_part(low), by_part(high))).astype(BF)
    input_grad = finished(input_part, F32)
    block_out = finished(block_own, BF)

    cols = head_in.shape[2]
    half = parts // 2
    head_out_part = scattered(head_out_part[:half], head_out_part[half:]).astype(BF)
    small = jnp.concatenate([norm_one_part, norm_two_part, router_part[:experts]], 0).astype(BF)
    count = 4 * cols + 2 + experts
    total = up_to(count, 16 * groups)
    heads = jnp.concatenate(
        [head_in_part.reshape(3 * cols, width), head_out_part, jnp.pad(small, ((0, total - count), (0, 0)))], 0
    )
    heads = jnp.sum(over_experts(heads.reshape(groups, total // groups, width)).astype(F32), 0).astype(BF)
    heads = lax.all_gather(heads, "expert", axis=0, tiled=True)
    head_in_grad = jnp.swapaxes(heads[: 3 * cols].reshape(3, cols, width), 1, 2).astype(F32)
    head_out_grad = heads[3 * cols : 4 * cols].astype(F32)
    small = heads[4 * cols : count].astype(F32)
    if paired:
        small = small + cross(small, 1)
        small = small + cross(small, 2)
    else:
        small = lax.psum(small, "tensor")
    return (
        block_out,
        input_grad,
        small[0],
        head_in_grad,
        head_out_grad,
        small[1],
        small[2:].T,
        in_grad.T[None],
        out_grad[None],
    )


def solution(mesh):
    in_specs = (
        P("expert", None),
        P(),
        P(None, None, "tensor"),
        P("tensor", None),
        P(),
        P(),
        P("expert", None, "tensor"),
        P("expert", "tensor", None),
        P("expert", None),
        P("expert", None),
        P("expert", None),
    )
    out_specs = (
        P("expert", None),
        P("expert", None),
        P(),
        P(None, None, "tensor"),
        P("tensor", None),
        P(),
        P(),
        P("expert", None, "tensor"),
        P("expert", "tensor", None),
    )
    return jax.shard_map(shards, mesh=mesh, in_specs=in_specs, out_specs=out_specs, check_vma=False)
```

```python
import functools

import jax
import jax.numpy as jnp
from jax import lax
from jax.experimental import pallas as pl
from jax.experimental.pallas import tpu as pltpu
from jax.sharding import PartitionSpec as P

HD = 64
SEQ = 197
LANES = 128
EPSILON = 1e-06
CHUNKS = 2
BF = jnp.bfloat16
F32 = jnp.float32


def up_to(value, unit):
    return -(-value // unit) * unit


def params(mib=48):
    return pltpu.CompilerParams(vmem_limit_bytes=mib * 1024 * 1024)


def dot(a, b, da=1, db=0):
    return lax.dot_general(a, b, (((da,), (db,)), ((), ())), preferred_element_type=F32)


def iota(rows, cols, dim):
    return lax.broadcasted_iota(jnp.int32, (rows, cols), dim)


def flag(mask):
    return jnp.where(mask, 1.0, 0.0)


def whole(shape, once=False):
    zeros = (0,) * len(shape)
    mode = pl.Buffered(1) if once else None
    return pl.BlockSpec(shape, lambda *_: zeros, pipeline_mode=mode)


def image(*shape):
    return pl.BlockSpec((1,) + shape, lambda i, *_: (i,) + (0,) * len(shape))


def fill(x_ref, tail_ref, rows_ref):
    full = x_ref.shape[0] // 16 * 16
    rows_ref[0:full, :] = x_ref[0:full, :]
    rows_ref[full : full + 16, :] = tail_ref[...]
    rest = rows_ref.shape[0] - full - 16
    if rest:
        rows_ref[full + 16 :, :] = jnp.zeros((rest, rows_ref.shape[1]), BF)


def norm_parts(field):
    centre = field - jnp.mean(field, -1, keepdims=True)
    spread = lax.rsqrt(jnp.mean(centre * centre, -1, keepdims=True) + EPSILON)
    return centre * spread, spread


def norm_field_back(upstream, gain, scaled, spread):
    weighted = upstream * gain
    return spread * (
        weighted
        - jnp.mean(weighted, -1, keepdims=True)
        - scaled * jnp.mean(weighted * scaled, -1, keepdims=True)
    )


def cost(flops, size):
    return pl.CostEstimate(flops=flops, bytes_accessed=size, transcendentals=0)


def halves(steps, tail, dtype):
    half = steps // 2
    shape = jax.ShapeDtypeStruct((half,) + tail, dtype)
    zeros = (0,) * len(tail)
    specs = [
        pl.BlockSpec((1,) + tail, lambda i, *_: (jnp.minimum(i, half - 1),) + zeros),
        pl.BlockSpec((1,) + tail, lambda i, *_: (jnp.maximum(i - half, 0),) + zeros),
    ]
    return specs, [shape, shape]


def store_half(low_ref, high_ref, value):
    early = pl.program_id(0) < pl.num_programs(0) // 2

    @pl.when(early)
    def _():
        low_ref[0] = value

    @pl.when(jnp.logical_not(early))
    def _():
        high_ref[0] = value


def head_masks():
    lane = iota(1, LANES, 1)
    return [(flag(lane // HD == h)).astype(BF) for h in range(2)]


def attend_kernel(images, order_ref, x_ref, tail_ref, gain_ref, w_ref, mixed_ref, first_ref, qkv_ref, log_ref, rows):
    @pl.when(pl.program_id(0) == 0)
    def _():
        fill(x_ref, tail_ref, rows)

    i = order_ref[pl.program_id(0)]
    height = first_ref.shape[1]
    window = height + 16
    start = jnp.minimum(i, images - 1) * SEQ
    aligned = start // 16 * 16
    r, c = iota(height, window, 0), iota(height, window, 1)
    limit = jnp.where(i < images, SEQ, 0)
    shift = flag((c == r + (start - aligned)) & (r < limit)).astype(BF)
    field = dot(shift, rows[pl.ds(pl.multiple_of(aligned, 16), window), :])
    scaled, _ = norm_parts(field)
    first = (scaled * gain_ref[...]).astype(BF)
    first_ref[0] = first
    for k in range(3):
        qkv_ref[k, 0] = dot(first, w_ref[k]).astype(BF)
    masks = head_masks()
    lane = iota(1, LANES, 1)
    key_lane = iota(1, height, 1)
    logs = jnp.zeros((height, LANES), F32)
    for pair in range(mixed_ref.shape[2] // LANES):
        cols = slice(pair * LANES, (pair + 1) * LANES)
        queries, keys, values = (qkv_ref[k, 0, :, cols] for k in range(3))
        total = jnp.zeros((height, LANES), F32)
        for h in range(2):
            scores = dot(queries * masks[h], keys, 1, 1) * HD ** (-0.5)
            scores = jnp.where(key_lane < SEQ, scores, -1e30)
            highest = jnp.max(scores, -1, keepdims=True)
            weights = jnp.exp(scores - highest)
            sums = jnp.sum(weights, -1, keepdims=True)
            probs = (weights * (1.0 / sums)).astype(BF)
            total += dot(probs, values * masks[h])
            logs = jnp.where(lane == pair * 2 + h, highest + jnp.log(sums), logs)
        mixed_ref[0, :, cols] = total.astype(BF)
    log_ref[0] = logs


def attend(order, block_in, tail, gain, head_in, images, image_slots, height):
    rows, width = block_in.shape
    cols = head_in.shape[2]
    spec = pltpu.PrefetchScalarGridSpec(
        num_scalar_prefetch=1,
        grid=(image_slots,),
        in_specs=[whole((rows, width), True), whole((16, width)), whole((1, width)), whole(head_in.shape, True)],
        out_specs=[
            image(height, cols),
            image(height, width),
            pl.BlockSpec((3, 1, height, cols), lambda i, *_: (0, i, 0, 0)),
            image(height, LANES),
        ],
        scratch_shapes=[pltpu.VMEM((rows // 16 * 16 + 48, width), BF)],
    )
    return pl.pallas_call(
        functools.partial(attend_kernel, images),
        grid_spec=spec,
        out_shape=[
            jax.ShapeDtypeStruct((image_slots, height, cols), BF),
            jax.ShapeDtypeStruct((image_slots, height, width), BF),
            jax.ShapeDtypeStruct((3, image_slots, height, cols), BF),
            jax.ShapeDtypeStruct((image_slots, height, LANES), F32),
        ],
        compiler_params=params(),
        cost_estimate=cost(16 * image_slots * height * width * cols, 16 * rows * width),
        name="attend",
    )(order, block_in, tail, gain, head_in)


def attend_back_kernel(
    dmix_ref, qkv_ref, log_ref, first_ref, wt_ref, gain_ref, low_ref, high_ref, hg_ref, ng_ref, acc, grads
):
    i = pl.program_id(0)
    height = first_ref.shape[1]
    masks = head_masks()
    lane = iota(1, LANES, 1)
    key_lane = iota(1, height, 1)
    scale = HD ** (-0.5)
    logs = log_ref[0]
    for pair in range(dmix_ref.shape[2] // LANES):
        cols = slice(pair * LANES, (pair + 1) * LANES)
        queries, keys, values = (qkv_ref[k, 0, :, cols] for k in range(3))
        out_grad = dmix_ref[0, :, cols]
        dq = jnp.zeros((height, LANES), F32)
        dk = jnp.zeros((height, LANES), F32)
        dv = jnp.zeros((height, LANES), F32)
        for h in range(2):
            q_h = queries * masks[h]
            o_h = out_grad * masks[h]
            log_h = jnp.sum(jnp.where(lane == pair * 2 + h, logs, 0.0), -1, keepdims=True)
            probs = jnp.exp(dot(q_h, keys, 1, 1) * scale - log_h)
            probs = jnp.where(key_lane < SEQ, probs, 0.0)
            prob_grad = dot(o_h, values, 1, 1)
            dv += dot(probs.astype(BF), o_h, 0, 0)
            delta = jnp.sum(probs * prob_grad, -1, keepdims=True)
            score_grad = (probs * (prob_grad - delta)).astype(BF)
            dq += dot(score_grad, keys * masks[h])
            dk += dot(score_grad, q_h, 0, 0)
        grads[0, :, cols] = (dq * scale).astype(BF)
        grads[1, :, cols] = (dk * scale).astype(BF)
        grads[2, :, cols] = dv.astype(BF)

    @pl.when(i == 0)
    def _():
        acc[...] = jnp.zeros_like(acc)

    first = first_ref[0]
    total = None
    for k in range(3):
        part = dot(grads[k], wt_ref[k])
        total = part if total is None else total + part
        acc[k] += dot(grads[k], first, 0, 0)
    store_half(low_ref, high_ref, total.astype(BF))

    @pl.when(i == pl.num_programs(0) - 1)
    def _():
        hg_ref[...] = acc[...].astype(BF)
        gain_grad = jnp.zeros_like(ng_ref)
        for k in range(3):
            gain_grad += jnp.sum(acc[k] * wt_ref[k].astype(F32), 0, keepdims=True)
        ng_ref[...] = gain_grad / gain_ref[...]


def attend_back(dmix, qkv, logs, first, head_in_t, gain):
    image_slots, height, cols = dmix.shape
    width = first.shape[2]
    specs, shapes = halves(image_slots, (height, width), BF)
    return pl.pallas_call(
        attend_back_kernel,
        grid=(image_slots,),
        in_specs=[
            image(height, cols),
            pl.BlockSpec((3, 1, height, cols), lambda i: (0, i, 0, 0)),
            image(height, LANES),
            image(height, width),
            whole(head_in_t.shape, True),
            whole((1, width)),
        ],
        out_specs=specs + [whole(head_in_t.shape), whole((1, width))],
        out_shape=shapes
        + [jax.ShapeDtypeStruct(head_in_t.shape, BF), jax.ShapeDtypeStruct((1, width), F32)],
        scratch_shapes=[pltpu.VMEM(head_in_t.shape, F32), pltpu.VMEM((3, height, cols), BF)],
        compiler_params=params(),
        cost_estimate=cost(24 * image_slots * height * width * cols, 20 * image_slots * height * width),
        name="attend_back",
    )(dmix, qkv, logs, first, head_in_t, gain)


def pack_first_kernel(slots, base, x_ref, tail_ref, lp_ref, side_ref, out_ref, rows):
    e = pl.program_id(0)

    @pl.when(e == 0)
    def _():
        fill(x_ref, tail_ref, rows)

    j = base + e * slots + iota(slots, rows.shape[0], 0)
    picks = [flag(lp_ref[c : c + 1, :] == j) for c in range(2)]
    width = x_ref.shape[1]
    out_ref[0, :, 0:width] = dot((picks[0] + picks[1]).astype(BF), rows[...]).astype(BF)
    out_ref[0, :, width:] = (
        dot(picks[0].astype(BF), side_ref[0]) + dot(picks[1].astype(BF), side_ref[1])
    ).astype(BF)


def pack_first(x, tail, lp, side, experts, slots, base):
    rows, width = x.shape
    padded = lp.shape[1]
    return pl.pallas_call(
        functools.partial(pack_first_kernel, slots, base),
        grid=(experts,),
        in_specs=[whole((rows, width), True), whole((16, width)), whole(lp.shape), whole(side.shape)],
        out_specs=image(slots, width + LANES),
        out_shape=jax.ShapeDtypeStruct((experts, slots, width + LANES), BF),
        scratch_shapes=[pltpu.VMEM((padded, width), BF)],
        compiler_params=params(),
        cost_estimate=cost(3 * experts * slots * padded * width, 2 * rows * width),
        name="pack_cotangent",
    )(x, tail, lp, side)


def pack_kernel(slots, base, count, *refs):
    lp_ref, out_ref = refs[count], refs[count + 1]
    total = None
    for p in range(count):
        j = base + pl.program_id(0) * slots + iota(slots, refs[p].shape[0], 0)
        picks = flag((lp_ref[p, 0:1, :] == j) | (lp_ref[p, 1:2, :] == j)).astype(BF)
        part = dot(picks, refs[p][...])
        total = part if total is None else total + part
    out_ref[0] = total.astype(BF)


def pack(pieces, lp, experts, slots, base):
    rows, width = pieces[0].shape
    count = len(pieces)
    return pl.pallas_call(
        functools.partial(pack_kernel, slots, base, count),
        grid=(experts,),
        in_specs=[whole((rows, width), True)] * count + [whole(lp.shape)],
        out_specs=image(slots, width),
        out_shape=jax.ShapeDtypeStruct((experts, slots, width), BF),
        compiler_params=params(),
        cost_estimate=cost(3 * experts * slots * rows * count * width, 2 * rows * count * width),
        name="pack_rows",
    )(*pieces, lp)


def unpack_kernel(count, slots, per, graded, lp_ref, *refs):
    row_refs, (low_ref, high_ref) = refs[:count], refs[count:]
    lp = lp_ref[0]
    height = lp.shape[0]
    rows, width = row_refs[0].shape
    total = jnp.zeros((height, width), F32)
    lanes = up_to(slots, LANES)
    extra = [jnp.zeros((height, lanes), F32) for _ in range(2)]
    for n in range(count):
        j = n * rows + iota(1, rows, 1)
        hits = (lp[:, 0:1] == j) | (lp[:, 1:2] == j)
        total += dot(flag(hits).astype(BF), row_refs[n][...])
        if graded:
            j = iota(1, lanes, 1)
            for e in range(rows // slots):
                spare = row_refs[n][(e + 1) * slots - 16 : (e + 1) * slots, 0 : 2 * lanes].astype(F32)
                spare = spare[per + 16 - slots : per + 17 - slots, :]
                values = spare[:, :lanes] + spare[:, lanes:]
                for c in range(2):
                    hit = lp[:, c : c + 1] - (n * rows + e * slots) == j
                    extra[c] += jnp.where(hit, values, 0.0)
    value = total.astype(BF)
    if graded:
        lane = iota(1, LANES, 1)
        tail = jnp.zeros((height, LANES), F32)
        for c in range(2):
            grad = jnp.sum(extra[c], -1, keepdims=True)
            high = grad.astype(BF).astype(F32)
            tail = jnp.where(lane == c, high, tail)
            tail = jnp.where(lane == 2 + c, grad - high, tail)
        value = jnp.concatenate([value, tail.astype(BF)], 1)
    store_half(low_ref, high_ref, value)


def unpack(lp, rows, slots, per, graded):
    image_slots, height, _ = lp.shape
    count = len(rows)
    width = rows[0].shape[1]
    specs, shapes = halves(image_slots, (height, width + (LANES if graded else 0)), BF)
    return pl.pallas_call(
        functools.partial(unpack_kernel, count, slots, per, graded),
        grid=(image_slots,),
        in_specs=[image(height, 2)] + [whole(item.shape, True) for item in rows],
        out_specs=specs,
        out_shape=shapes,
        compiler_params=params(),
        cost_estimate=cost(3 * image_slots * height * count * rows[0].size, 4 * count * rows[0].size),
        name="unpack_rows",
    )(lp, *rows)


def to_rows_kernel(own, height, count, start_ref, *refs):
    out_ref, rows = refs[count], refs[count + 1]
    b = pl.program_id(0)

    @pl.when(b == 0)
    def _():
        for p in range(count):
            at = pl.multiple_of(start_ref[p], 16)
            rows[pl.ds(at, own * height), :] = refs[p][...]

    tile = out_ref.shape[0]
    window = up_to(tile + 3 * (height - SEQ) + 16, 16)
    lift = height - SEQ
    first = b * tile
    start = (first + lift * (first // SEQ)) // 16 * 16
    start = jnp.minimum(start, rows.shape[0] - window)
    r = first + iota(tile, 1, 0)
    steps = sum(jnp.where(r >= (first // SEQ + n) * SEQ, 1, 0) for n in (1, 2))
    target = r + lift * (first // SEQ + steps) - start
    picks = flag(iota(tile, window, 1) == target).astype(BF)
    out_ref[...] = dot(picks, rows[pl.ds(pl.multiple_of(start, 16), window), :]).astype(out_ref.dtype)


def to_rows(starts, pieces, rows, dtype, height):
    each, width = pieces[0].shape
    count = len(pieces)
    spec = pltpu.PrefetchScalarGridSpec(
        num_scalar_prefetch=1,
        grid=(-(-rows // 208),),
        in_specs=[whole((each, width), True)] * count,
        out_specs=pl.BlockSpec((208, width), lambda i, *_: (i, 0)),
        scratch_shapes=[pltpu.VMEM((each * count, width), BF)],
    )
    return pl.pallas_call(
        functools.partial(to_rows_kernel, each // height, height, count),
        grid_spec=spec,
        out_shape=jax.ShapeDtypeStruct((rows, width), dtype),
        compiler_params=params(),
        cost_estimate=cost(2 * rows * 256 * width, 8 * rows * width),
        name="to_rows",
    )(starts, *pieces)


def middle_kernel(count, *refs):
    mixed_refs, wo_refs = refs[:count], refs[count : 2 * count]
    x_ref, gain_ref, router_ref, ids_ref, noise_ref, mid_ref, second_ref, gates_ref = refs[2 * count :]
    middle = x_ref[0].astype(F32)
    for mixed_ref, wo_ref in zip(mixed_refs, wo_refs):
        middle += dot(mixed_ref[0], wo_ref[...])
    mid_ref[0] = middle
    scaled, _ = norm_parts(middle)
    second = (scaled * gain_ref[...]).astype(BF)
    second_ref[0] = second
    logits = dot(second, router_ref[...])
    lane = iota(1, LANES, 1)
    chosen = [
        jnp.sum(jnp.where(lane == ids_ref[0, :, c : c + 1], logits, 0.0), -1, keepdims=True)
        + noise_ref[0, :, c : c + 1]
        for c in range(2)
    ]
    top = jnp.maximum(chosen[0], chosen[1])
    raw = [jnp.exp(item - top) for item in chosen]
    inverse = 1.0 / (raw[0] + raw[1])
    gates_ref[0] = jnp.where(lane == 0, raw[0] * inverse, 0.0) + jnp.where(lane == 1, raw[1] * inverse, 0.0)


def middle_of(mixed, head_out, x_own, gain, router, ids, noise):
    own, height, cols = mixed[0].shape
    parts = len(mixed)
    width = x_own.shape[2]
    return pl.pallas_call(
        functools.partial(middle_kernel, parts),
        grid=(own,),
        in_specs=[image(height, cols)] * parts
        + [whole((cols, width), True)] * parts
        + [
            image(height, width),
            whole((1, width)),
            whole(router.shape),
            image(height, 2),
            image(height, 2),
        ],
        out_specs=[image(height, width), image(height, width), image(height, LANES)],
        out_shape=[
            jax.ShapeDtypeStruct((own, height, width), F32),
            jax.ShapeDtypeStruct((own, height, width), BF),
            jax.ShapeDtypeStruct((own, height, LANES), F32),
        ],
        compiler_params=params(),
        cost_estimate=cost(4 * own * height * width * width, 24 * own * height * width),
        name="middle",
    )(*mixed, *head_out, x_own, gain, router, ids, noise)


def middle_back_kernel(count, *refs):
    rs_ref, mid_ref, second_ref, gates_ref, ids_ref, up_ref, gain_ref, router_ref = refs[:8]
    mixed_refs, wo_refs = refs[8 : 8 + count], refs[8 + count : 8 + 2 * count]
    mg_ref, hog_ref, rg_ref, ng_ref = refs[8 + 2 * count : 12 + 2 * count]
    dmix_refs, hog_acc = refs[12 + 2 * count : -1], refs[-1]
    i = pl.program_id(0)

    @pl.when(i == 0)
    def _():
        hog_acc[...] = jnp.zeros_like(hog_acc)
        rg_ref[...] = jnp.zeros_like(rg_ref)
        ng_ref[...] = jnp.zeros_like(ng_ref)

    width = up_ref.shape[2]
    lane = iota(1, LANES, 1)
    tail = rs_ref[0, :, width:]
    gates = gates_ref[0]
    gate, grad = [], []
    for c in range(2):
        gate.append(jnp.sum(jnp.where(lane == c, gates, 0.0), -1, keepdims=True))
        grad.append(jnp.sum(jnp.where((lane == c) | (lane == 2 + c), tail, 0.0), -1, keepdims=True))
    mean_term = gate[0] * grad[0] + gate[1] * grad[1]
    logit_grad = jnp.zeros((up_ref.shape[1], LANES), F32)
    for c in range(2):
        logit_grad = jnp.where(lane == ids_ref[0, :, c : c + 1], gate[c] * (grad[c] - mean_term), logit_grad)
    logit_grad = logit_grad.astype(BF)
    second_grad = rs_ref[0, :, 0:width] + dot(logit_grad, router_ref[...], 1, 1)
    rg_ref[...] += dot(logit_grad, second_ref[0], 0, 0)
    scaled, spread = norm_parts(mid_ref[0])
    ng_ref[...] += jnp.sum(second_grad * scaled, 0, keepdims=True)
    middle_grad = up_ref[0].astype(F32) + norm_field_back(second_grad, gain_ref[...], scaled, spread)
    mg_ref[0] = middle_grad
    rounded = middle_grad.astype(BF)
    for t in range(count):
        dmix_refs[t][0] = dot(rounded, wo_refs[t][...], 1, 1).astype(BF)
        hog_acc[t] += dot(mixed_refs[t][0], rounded, 0, 0)

    @pl.when(i == pl.num_programs(0) - 1)
    def _():
        hog_ref[...] = hog_acc[...].astype(BF)


def middle_back(rs, middle, second, gates, ids, up, mixed, head_out, gain, router):
    own, height, cols = mixed[0].shape
    parts = len(mixed)
    width = up.shape[2]
    return pl.pallas_call(
        functools.partial(middle_back_kernel, parts),
        grid=(own,),
        in_specs=[
            image(height, rs.shape[2]),
            image(height, width),
            image(height, width),
            image(height, LANES),
            image(height, 2),
            image(height, width),
            whole((1, width)),
            whole(router.shape),
        ]
        + [image(height, cols)] * parts
        + [whole((cols, width), True)] * parts,
        out_specs=[image(height, width), whole((parts, cols, width)), whole((LANES, width)), whole((1, width))]
        + [image(height, cols)] * parts,
        out_shape=[
            jax.ShapeDtypeStruct((own, height, width), F32),
            jax.ShapeDtypeStruct((parts, cols, width), BF),
            jax.ShapeDtypeStruct((LANES, width), F32),
            jax.ShapeDtypeStruct((1, width), F32),
        ]
        + [jax.ShapeDtypeStruct((own, height, cols), BF)] * parts,
        scratch_shapes=[pltpu.VMEM((parts, cols, width), F32)],
        compiler_params=params(),
        cost_estimate=cost(8 * own * height * width * width, 40 * own * height * width),
        name="middle_back",
    )(rs, middle, second, gates, ids, up, gain, router, *mixed, *head_out)


def input_back_kernel(fg_ref, x_ref, mg_ref, gain_ref, out_ref):
    scaled, spread = norm_parts(x_ref[0].astype(F32))
    out_ref[0] = (mg_ref[0] + norm_field_back(fg_ref[0], gain_ref[...], scaled, spread)).astype(BF)


def input_back(first_grad, x_own, middle_grad, gain):
    own, height, width = x_own.shape
    return pl.pallas_call(
        input_back_kernel,
        grid=(own,),
        in_specs=[image(height, width)] * 3 + [whole((1, width))],
        out_specs=image(height, width),
        out_shape=jax.ShapeDtypeStruct((own, height, width), BF),
        compiler_params=params(),
        cost_estimate=cost(20 * own * height * width, 16 * own * height * width),
        name="input_back",
    )(first_grad, x_own, middle_grad, gain)


def gelu_parts(v):
    x = jnp.abs(v) * 0.7071067811865476
    t = 1.0 / (1.0 + 0.3275911 * x)
    bell = jnp.exp(-x * x)
    poly = ((((1.061405429 * t - 1.453152027) * t + 1.421413741) * t - 0.284496736) * t + 0.254829592) * t
    below = 0.5 * poly * bell
    share = jnp.where(v < 0.0, below, 1.0 - below)
    return v * share, share + v * bell * 0.3989422804014327


def expert_kernel(count, slots, per, x_ref, g_ref, router_ref, *refs):
    w1_refs, w2_refs = refs[:count], refs[count : 2 * count]
    back_ref, act_ref, hg_ref, rg_ref, dx_ref = refs[2 * count :]
    width = x_ref.shape[1]
    rows = x_ref[...]
    lane = iota(1, LANES, 1)
    side = g_ref[:, width:].astype(F32)

    def column(*lanes):
        keep = lane == lanes[0]
        for other in lanes[1:]:
            keep = keep | (lane == other)
        return jnp.sum(jnp.where(keep, side, 0.0), -1, keepdims=True)

    logits = dot(rows, router_ref[...])
    lane_f = lane.astype(F32)
    mine = jnp.sum(jnp.where(lane_f == column(4), logits, 0.0), -1, keepdims=True)
    other = jnp.sum(jnp.where(lane_f == column(0), logits, 0.0), -1, keepdims=True)
    gate = 1.0 / (1.0 + jnp.exp(other - mine - column(1, 2, 3)))
    upstream = g_ref[:, 0:width].astype(F32)
    rows_grad = (gate * upstream).astype(BF)
    rg_ref[...] = rows_grad
    hidden_here = w1_refs[0].shape[1]
    step = min(512, hidden_here)
    for t in range(count):
        for at in range(0, hidden_here, step):
            cols = slice(at, at + step)
            place = slice(t * hidden_here + at, t * hidden_here + at + step)
            hidden = dot(rows, w1_refs[t][:, cols])
            active_grad = dot(rows_grad, w2_refs[t][cols, :], 1, 1)
            active, slope = gelu_parts(hidden)
            act_ref[:, place] = active.astype(BF)
            hg_ref[:, place] = (active_grad * slope).astype(BF)
    out = None
    grad = None
    for t in range(count):
        place = slice(t * hidden_here, (t + 1) * hidden_here)
        part = dot(act_ref[:, place], w2_refs[t][...])
        out = part if out is None else out + part
        part = dot(hg_ref[:, place], w1_refs[t][...], 1, 1)
        grad = part if grad is None else grad + part
    dx_ref[...] = grad.astype(BF)
    back_ref[...] = (gate * out).astype(BF)
    gate_grad = jnp.sum(upstream * out.astype(BF).astype(F32), -1, keepdims=True)
    lanes = up_to(slots, LANES)
    spread = iota(slots, lanes, 0) == iota(slots, lanes, 1)
    spare_row = iota(16, 1, 0) == per + 16 - slots
    for b in range(x_ref.shape[0] // slots):
        end = (b + 1) * slots
        line = jnp.sum(jnp.where(spread, gate_grad[end - slots : end], 0.0), 0, keepdims=True)
        high = line.astype(BF).astype(F32)
        line = jnp.concatenate([high, line - high, jnp.zeros((1, width - 2 * lanes), F32)], 1)
        dx_ref[end - 16 : end, :] = jnp.where(spare_row, line, grad[end - 16 : end]).astype(BF)


def expert(x, g, router, w1, w2, slots, per):
    rows, width = x.shape
    count = len(w1)
    total = count * w1[0].shape[1]
    blocks = rows // slots
    tile = slots * max(n for n in range(1, blocks + 1) if blocks % n == 0 and n * slots <= 448)

    def tiled(cols):
        return pl.BlockSpec((tile, cols), lambda i: (i, 0))

    flops = 8 * rows * width * total
    return pl.pallas_call(
        functools.partial(expert_kernel, count, slots, per),
        grid=(rows // tile,),
        in_specs=[tiled(width), tiled(g.shape[1]), whole(router.shape)]
        + [whole(item.shape, True) for item in w1]
        + [whole(item.shape, True) for item in w2],
        out_specs=[tiled(width), tiled(total), tiled(total), tiled(width), tiled(width)],
        out_shape=[
            jax.ShapeDtypeStruct((rows, width), BF),
            jax.ShapeDtypeStruct((rows, total), BF),
            jax.ShapeDtypeStruct((rows, total), BF),
            jax.ShapeDtypeStruct((rows, width), BF),
            jax.ShapeDtypeStruct((rows, width), BF),
        ],
        compiler_params=params(60),
        cost_estimate=pl.CostEstimate(flops=flops, bytes_accessed=rows * total * 6, transcendentals=rows * total * 2),
        name="expert",
    )(x, g, router, *w1, *w2)


def weight_kernel(count, *refs):
    ins, (low_ref, high_ref) = refs[:-2], refs[-2:]
    total = None
    for n in range(count):
        part = dot(ins[2 * n][...], ins[2 * n + 1][...], 0, 0)
        total = part if total is None else total + part
    store_half(low_ref, high_ref, total.astype(BF))


def weight_grad(columns, rows, parts):
    count = len(columns)
    total = columns[0].shape[1]
    width = rows[0].shape[1]
    here = total // parts
    step = min(512, here)
    specs, args = [], []
    for a, b in zip(columns, rows):
        specs += [pl.BlockSpec((a.shape[0], step), lambda i: (0, i)), whole(b.shape, True)]
        args += [a, b]
    steps = total // step
    out_specs, out_shape = halves(steps, (step, width), BF)
    low, high = pl.pallas_call(
        functools.partial(weight_kernel, count),
        grid=(steps,),
        in_specs=specs,
        out_specs=out_specs,
        out_shape=out_shape,
        compiler_params=params(),
        cost_estimate=pl.CostEstimate(
            flops=2 * sum(b.shape[0] for b in rows) * width * total, bytes_accessed=4 * total * width, transcendentals=0
        ),
        name="weight_grad",
    )(*args)
    return low.reshape(parts // 2, here, width), high.reshape(parts // 2, here, width)


def shards(
    block_in,
    norm_one,
    head_in,
    head_out,
    norm_two,
    router,
    expert_in,
    expert_out,
    expert_ids,
    route_noise,
    cotangent,
):
    rows_here, width = block_in.shape
    parts = lax.axis_size("tensor")
    groups = lax.axis_size("expert")
    me = lax.axis_index("tensor")
    images = rows_here // SEQ
    own = -(-images // parts)
    image_slots = own * parts
    height = up_to(SEQ, 16)
    experts = router.shape[1]
    capacity = (rows_here * 2 * 8 // (5 * experts) + 15) // 16 * 16
    share = -(-capacity // parts)
    per = -(-share // CHUNKS)
    slots = up_to(per + 1, 16)
    chunk_rows = experts * slots
    full = rows_here // 16 * 16

    paired = parts == 4
    order = (0, 2, 1, 3) if paired else tuple(range(parts))
    part_of = [me ^ k if paired else jnp.int32(k) for k in order]

    def cross(x, k):
        return lax.ppermute(x, "tensor", [(n, n ^ k) for n in range(parts)])

    def gathered(x):
        if not paired:
            every = lax.all_gather(x, "tensor", axis=0, tiled=False)
            return [every[p] for p in range(parts)]
        far, near = cross(x, 2), cross(x, 1)
        return [x, far, near, cross(far, 1)]

    def near_hop(high):
        return cross(high, 1) if paired else high

    def near_sum(low, came):
        if not paired:
            return jnp.concatenate([low, came], 0)
        return (low.astype(F32) + came.astype(F32)).astype(BF)

    def far_hop(both):
        if not paired:
            return lax.psum_scatter(both, "tensor", scatter_dimension=0)
        return cross(both[1], 2)

    def far_sum(both, came):
        return both[0].astype(F32) + came.astype(F32) if paired else came.astype(F32)

    def scattered(low, high):
        both = near_sum(low, near_hop(high))
        return far_sum(both, far_hop(both))

    def far_part(x):
        return cross(x, 2) if paired else x

    def gathered_from(x, far):
        return [x, far, cross(x, 1), cross(far, 1)] if paired else gathered(x)

    def swapped(pieces):
        if not paired:
            every = lax.all_to_all(jnp.stack(pieces), "tensor", split_axis=0, concat_axis=0, tiled=True)
            return [every[p] for p in range(parts)]
        return [cross(piece, k) if k else piece for piece, k in zip(pieces, order)]

    def over_experts(x):
        return lax.all_to_all(x, "expert", split_axis=0, concat_axis=0, tiled=True)

    def pinned(*items):
        return lax.optimization_barrier(items)

    def tail_of(x):
        return jnp.pad(x[full:], ((0, 16 - (rows_here - full)), (0, 0)))

    def to_images(x, value):
        x = x.reshape(images, SEQ, x.shape[-1])
        return jnp.pad(
            x, ((0, image_slots - images), (0, height - SEQ), (0, 0)), constant_values=value
        )

    def own_images(x):
        pieces = []
        for n in range(own):
            at = jnp.minimum(me * own + n, images - 1) * SEQ
            piece = lax.dynamic_slice(x, (at, 0), (SEQ, x.shape[1]))
            pieces.append(jnp.pad(piece, ((0, height - SEQ), (0, 0))))
        return jnp.stack(pieces)

    names = jnp.arange(experts, dtype=jnp.int32)
    member = [(expert_ids[:, c : c + 1] == names).astype(jnp.int32) for c in range(2)]
    both = member[0] + member[1]
    earlier = jnp.cumsum(both, 0) - both
    slot = jnp.stack([jnp.sum(earlier * item, -1) for item in member], 1)
    local = slot - me * share
    place = local // per * chunk_rows + expert_ids * slots + local % per
    place = jnp.where((local >= 0) & (local < share), place, -1)
    place_flat = jnp.pad(place.T, ((0, 0), (0, full + 16 - rows_here)), constant_values=-1)
    place_images = to_images(place, -1)
    place_images = jnp.concatenate(
        [lax.dynamic_slice_in_dim(place_images, part * own, own, 0) for part in part_of], 0
    )
    place_lanes = jnp.swapaxes(place_images.reshape(parts, own * height, 2), 1, 2)
    ids_own = lax.dynamic_slice_in_dim(to_images(expert_ids, -1), me * own, own, 0)
    noise_own = lax.dynamic_slice_in_dim(to_images(route_noise, 0.0), me * own, own, 0)
    image_order = jnp.concatenate([part * own + jnp.arange(own, dtype=jnp.int32) for part in part_of])
    row_starts = jnp.stack([part * (own * height) for part in part_of]).astype(jnp.int32)

    sides = []
    for c in range(2):
        gap = route_noise[:, c] - route_noise[:, 1 - c]
        high = gap.astype(BF)
        left = gap - high.astype(F32)
        mid = left.astype(BF)
        low = (left - mid.astype(F32)).astype(BF)
        columns = [expert_ids[:, 1 - c].astype(BF), high, mid, low, expert_ids[:, c].astype(BF)]
        sides.append(jnp.stack(columns, 1))
    side = jnp.pad(jnp.stack(sides), ((0, 0), (0, full + 16 - rows_here), (0, LANES - 5)))

    router_wide = jnp.pad(router, ((0, 0), (0, LANES - experts)))
    gain_one, gain_two = norm_one[None, :], norm_two[None, :]
    head_out_all = gathered(head_out)
    w1_far = far_part(expert_in[0])

    tail = tail_of(cotangent)
    packed = [
        pack_first(cotangent, tail, place_flat, side, experts, slots, n * chunk_rows) for n in range(CHUNKS)
    ]
    block_rows, *packed = pinned(block_in, *packed)
    signals = [over_experts(item) for item in packed]

    mixed, first_in, qkv, logs = attend(
        image_order, block_rows, tail_of(block_in), gain_one, head_in, images, image_slots, height
    )
    mixed, w1_far, late_out = pinned(mixed, w1_far, expert_out[0])
    w1 = gathered_from(expert_in[0], w1_far)
    w2_far = far_part(late_out)
    mixed = swapped([mixed[p * own : (p + 1) * own] for p in range(parts)])
    x_own = own_images(block_in)
    valid = (me * own + jnp.arange(own) < images)[:, None, None]
    up_own = jnp.where(valid, own_images(cotangent), 0)
    middle, second_in, gates = middle_of(
        mixed, head_out_all, x_own, gain_two, router_wide, ids_own, noise_own
    )
    second_in, signals[0] = pinned(second_in, signals[0])
    *second_all, signals[-1], w2_far = pinned(*gathered(second_in), signals[-1], w2_far)
    w2 = gathered_from(expert_out[0], w2_far)
    second_all = [item.reshape(own * height, width) for item in second_all]

    outgoing = [pack(second_all, place_lanes, experts, slots, n * chunk_rows) for n in range(CHUNKS)]
    backs, actives, hidden_grads, rows_grads, arrived, returned = [], [], [], [], [], []
    x, *ready = pinned(over_experts(outgoing[0]), *w1, *w2)
    w1, w2 = ready[:parts], ready[parts:]
    for n in range(CHUNKS):
        coming = None
        if n + 1 < CHUNKS:
            x, ready = pinned(x, outgoing[n + 1])
            coming = over_experts(ready)
        x = x.reshape(groups * slots, width)
        signal = signals[n].reshape(groups * slots, width + LANES)
        back, active, hidden_grad, rows_grad, row_grad = expert(x, signal, router_wide, w1, w2, slots, per)
        arrived.append(x)
        actives.append(active)
        hidden_grads.append(hidden_grad)
        rows_grads.append(rows_grad)
        backs.append(back)
        if coming is not None:
            x, row_grad = pinned(coming, row_grad)
        returned.append(over_experts(row_grad.reshape(experts, slots, width)))

    out_low, out_high = weight_grad(actives, rows_grads, parts)
    in_low, in_high = weight_grad(hidden_grads, arrived, parts)
    out_came, in_low, in_high = pinned(near_hop(out_high), in_low, in_high)
    out_both = near_sum(out_low, out_came)
    *returned, in_low, in_high, out_both = pinned(*returned, in_low, in_high, out_both)
    out_far = far_hop(out_both)
    in_came = near_hop(in_high)

    def whole_rows(items):
        return [item.reshape(chunk_rows, width) for item in items]

    def by_part(x):
        return x.reshape((parts // 2, own) + x.shape[1:])

    low, high = unpack(place_images, whole_rows(returned), slots, per, True)
    low, high, in_came = pinned(low, high, in_came)
    in_both = near_sum(in_low, in_came)
    second_sum, in_both = pinned(scattered(by_part(low), by_part(high)), in_both)
    in_far = far_hop(in_both)
    combined = [over_experts(item.reshape(experts, slots, width)) for item in backs]
    middle_grad, head_out_part, router_part, norm_two_part, *mixed_grad = middle_back(
        second_sum, middle, second_in, gates, ids_own, up_own, mixed, head_out_all, gain_two, router_wide
    )
    *mixed_grad, combined[0], out_far = pinned(*mixed_grad, combined[0], out_far)
    out_grad = far_sum(out_both, out_far)
    mixed_grad = swapped(mixed_grad)
    first_low, first_high, head_in_part, norm_one_part = attend_back(
        jnp.concatenate(mixed_grad, 0), qkv, logs, first_in, jnp.swapaxes(head_in, 1, 2), gain_one
    )
    first_low, first_high, combined[-1], in_far = pinned(first_low, first_high, combined[-1], in_far)
    in_grad = far_sum(in_both, in_far)
    first_grad = scattered(by_part(first_low), by_part(first_high))
    input_part = input_back(first_grad, x_own, middle_grad, gain_one)

    def finished(x, dtype):
        pieces = [item.reshape(own * height, width) for item in gathered(x)]
        return to_rows(row_starts, pieces, rows_here, dtype, height)

    low, high = unpack(place_images, whole_rows(combined), slots, per, False)
    block_own = (middle + scattered(by_part(low), by_part(high))).astype(BF)
    input_grad = finished(input_part, F32)
    block_out = finished(block_own, BF)

    cols = head_in.shape[2]
    half = parts // 2
    head_out_part = scattered(head_out_part[:half], head_out_part[half:]).astype(BF)
    small = jnp.concatenate([norm_one_part, norm_two_part, router_part[:experts]], 0).astype(BF)
    count = 4 * cols + 2 + experts
    total = up_to(count, 16 * groups)
    heads = jnp.concatenate(
        [head_in_part.reshape(3 * cols, width), head_out_part, jnp.pad(small, ((0, total - count), (0, 0)))], 0
    )
    heads = jnp.sum(over_experts(heads.reshape(groups, total // groups, width)).astype(F32), 0).astype(BF)
    heads = lax.all_gather(heads, "expert", axis=0, tiled=True)
    head_in_grad = jnp.swapaxes(heads[: 3 * cols].reshape(3, cols, width), 1, 2).astype(F32)
    head_out_grad = heads[3 * cols : 4 * cols].astype(F32)
    small = heads[4 * cols : count].astype(F32)
    if paired:
        small = small + cross(small, 1)
        small = small + cross(small, 2)
    else:
        small = lax.psum(small, "tensor")
    return (
        block_out,
        input_grad,
        small[0],
        head_in_grad,
        head_out_grad,
        small[1],
        small[2:].T,
        in_grad.T[None],
        out_grad[None],
    )


def solution(mesh):
    in_specs = (
        P("expert", None),
        P(),
        P(None, None, "tensor"),
        P("tensor", None),
        P(),
        P(),
        P("expert", None, "tensor"),
        P("expert", "tensor", None),
        P("expert", None),
        P("expert", None),
        P("expert", None),
    )
    out_specs = (
        P("expert", None),
        P("expert", None),
        P(),
        P(None, None, "tensor"),
        P("tensor", None),
        P(),
        P(),
        P("expert", None, "tensor"),
        P("expert", "tensor", None),
    )
    return jax.shard_map(shards, mesh=mesh, in_specs=in_specs, out_specs=out_specs, check_vma=False)
```

```python
import functools

import jax
import jax.numpy as jnp
from jax import lax
from jax.experimental import pallas as pl
from jax.experimental.pallas import tpu as pltpu
from jax.sharding import PartitionSpec as P

HD = 64
SEQ = 197
LANES = 128
EPSILON = 1e-06
CHUNKS = 2
BF = jnp.bfloat16
F32 = jnp.float32


def up_to(value, unit):
    return -(-value // unit) * unit


def params(mib=48):
    return pltpu.CompilerParams(vmem_limit_bytes=mib * 1024 * 1024)


def dot(a, b, da=1, db=0):
    return lax.dot_general(a, b, (((da,), (db,)), ((), ())), preferred_element_type=F32)


def iota(rows, cols, dim):
    return lax.broadcasted_iota(jnp.int32, (rows, cols), dim)


def flag(mask):
    return jnp.where(mask, 1.0, 0.0)


def whole(shape, once=False):
    zeros = (0,) * len(shape)
    mode = pl.Buffered(1) if once else None
    return pl.BlockSpec(shape, lambda *_: zeros, pipeline_mode=mode)


def image(*shape):
    return pl.BlockSpec((1,) + shape, lambda i, *_: (i,) + (0,) * len(shape))


def fill(x_ref, tail_ref, rows_ref):
    full = x_ref.shape[0] // 16 * 16
    rows_ref[0:full, :] = x_ref[0:full, :]
    rows_ref[full : full + 16, :] = tail_ref[...]
    rest = rows_ref.shape[0] - full - 16
    if rest:
        rows_ref[full + 16 :, :] = jnp.zeros((rest, rows_ref.shape[1]), BF)


def norm_parts(field):
    centre = field - jnp.mean(field, -1, keepdims=True)
    spread = lax.rsqrt(jnp.mean(centre * centre, -1, keepdims=True) + EPSILON)
    return centre * spread, spread


def norm_field_back(upstream, gain, scaled, spread):
    weighted = upstream * gain
    return spread * (
        weighted
        - jnp.mean(weighted, -1, keepdims=True)
        - scaled * jnp.mean(weighted * scaled, -1, keepdims=True)
    )


def cost(flops, size):
    return pl.CostEstimate(flops=flops, bytes_accessed=size, transcendentals=0)


def by_piece(count, steps, block, shape, dtype):
    def spec(p):
        def place(i, *_):
            return (jnp.clip(i - p * steps, 0, steps - 1), 0)

        return pl.BlockSpec(block, place)

    return [spec(p) for p in range(count)], [jax.ShapeDtypeStruct(shape, dtype)] * count


def store_piece(refs, steps, value):
    for p, ref in enumerate(refs):

        @pl.when(pl.program_id(0) // steps == p)
        def _():
            ref[...] = value


def rows_spec(tile, width):
    return pl.BlockSpec((tile, width), lambda i, *_: (i, 0))


def own_spec(tile, width):
    return pl.BlockSpec((tile, width), lambda i, at: (at[0] + i, 0))


def window_of(i, height, back=False):
    start = i * SEQ
    aligned = start // 16 * 16
    window = height + 16
    shape = (window, height) if back else (height, window)
    r, c = iota(*shape, 1 if back else 0), iota(*shape, 0 if back else 1)
    match = flag((c == r + (start - aligned)) & (r < SEQ)).astype(BF)
    return match, pl.ds(pl.multiple_of(aligned, 16), window)


def head_masks():
    lane = iota(1, LANES, 1)
    return [(flag(lane // HD == h)).astype(BF) for h in range(2)]


def attend_kernel(count, starts_ref, x_ref, tail_ref, gain_ref, w_ref, first_ref, qkv_ref, log_ref, *refs):
    piece_refs, rows, mixed = refs[:count], refs[count], refs[count + 1]
    i = pl.program_id(0)
    height = first_ref.shape[1]
    cols = mixed.shape[1]

    @pl.when(i == 0)
    def _():
        fill(x_ref, tail_ref, rows)
        mixed[...] = jnp.zeros_like(mixed)

    match, place = window_of(i, height)
    field = dot(match, rows[place, :])
    scaled, _ = norm_parts(field)
    first = (scaled * gain_ref[...]).astype(BF)
    first_ref[0] = first
    for k in range(3):
        qkv_ref[k, 0] = dot(first, w_ref[k]).astype(BF)
    masks = head_masks()
    lane = iota(1, LANES, 1)
    key_lane = iota(1, height, 1)
    logs = jnp.zeros((height, LANES), F32)
    back, _ = window_of(i, height, True)
    for pair in range(cols // LANES):
        part = slice(pair * LANES, (pair + 1) * LANES)
        queries, keys, values = (qkv_ref[k, 0, :, part] for k in range(3))
        total = jnp.zeros((height, LANES), F32)
        for h in range(2):
            scores = dot(queries * masks[h], keys, 1, 1) * HD ** (-0.5)
            scores = jnp.where(key_lane < SEQ, scores, -1e30)
            highest = jnp.max(scores, -1, keepdims=True)
            weights = jnp.exp(scores - highest)
            sums = jnp.sum(weights, -1, keepdims=True)
            probs = (weights * (1.0 / sums)).astype(BF)
            total += dot(probs, values * masks[h])
            logs = jnp.where(lane == pair * 2 + h, highest + jnp.log(sums), logs)
        mixed[place, part] = (mixed[place, part].astype(F32) + dot(back, total.astype(BF))).astype(BF)
    log_ref[0] = logs

    @pl.when(i == pl.num_programs(0) - 1)
    def _():
        for p in range(count):
            at = pl.multiple_of(starts_ref[p], 16)
            piece_refs[p][...] = mixed[pl.ds(at, piece_refs[p].shape[0]), :]


def attend(starts, block_in, tail, gain, head_in, images, height, each, count):
    rows, width = block_in.shape
    cols = head_in.shape[2]
    scratch_rows = max(rows // 16 * 16 + 48, each * count)
    spec = pltpu.PrefetchScalarGridSpec(
        num_scalar_prefetch=1,
        grid=(images,),
        in_specs=[whole((rows, width), True), whole((16, width)), whole((1, width)), whole(head_in.shape, True)],
        out_specs=[
            image(height, width),
            pl.BlockSpec((3, 1, height, cols), lambda i, *_: (0, i, 0, 0)),
            image(height, LANES),
        ]
        + [whole((each, cols))] * count,
        scratch_shapes=[pltpu.VMEM((scratch_rows, width), BF), pltpu.VMEM((scratch_rows, cols), BF)],
    )
    return pl.pallas_call(
        functools.partial(attend_kernel, count),
        grid_spec=spec,
        out_shape=[
            jax.ShapeDtypeStruct((images, height, width), BF),
            jax.ShapeDtypeStruct((3, images, height, cols), BF),
            jax.ShapeDtypeStruct((images, height, LANES), F32),
        ]
        + [jax.ShapeDtypeStruct((each, cols), BF)] * count,
        compiler_params=params(),
        cost_estimate=cost(16 * images * height * width * cols, 16 * rows * width),
        name="attend",
    )(starts, block_in, tail, gain, head_in)


def attend_back_kernel(count, starts_ref, qkv_ref, log_ref, first_ref, wt_ref, gain_ref, *refs):
    dmix_refs, piece_refs = refs[:count], refs[count : 2 * count]
    hg_ref, ng_ref, acc, grads, dmix, field = refs[2 * count :]
    i = pl.program_id(0)
    height = first_ref.shape[1]
    each = dmix_refs[0].shape[0]

    @pl.when(i == 0)
    def _():
        acc[...] = jnp.zeros_like(acc)
        field[...] = jnp.zeros_like(field)
        rest = dmix.shape[0] - each * count
        if rest:
            dmix[each * count :, :] = jnp.zeros((rest, dmix.shape[1]), BF)
        for p in range(count):
            dmix[pl.ds(pl.multiple_of(starts_ref[p], 16), each), :] = dmix_refs[p][...]

    match, place = window_of(i, height)
    back, _ = window_of(i, height, True)
    out_grads = dot(match, dmix[place, :]).astype(BF)
    masks = head_masks()
    lane = iota(1, LANES, 1)
    key_lane = iota(1, height, 1)
    scale = HD ** (-0.5)
    logs = log_ref[0]
    for pair in range(dmix.shape[1] // LANES):
        cols = slice(pair * LANES, (pair + 1) * LANES)
        queries, keys, values = (qkv_ref[k, 0, :, cols] for k in range(3))
        out_grad = out_grads[:, cols]
        dq = jnp.zeros((height, LANES), F32)
        dk = jnp.zeros((height, LANES), F32)
        dv = jnp.zeros((height, LANES), F32)
        for h in range(2):
            q_h = queries * masks[h]
            o_h = out_grad * masks[h]
            log_h = jnp.sum(jnp.where(lane == pair * 2 + h, logs, 0.0), -1, keepdims=True)
            probs = jnp.exp(dot(q_h, keys, 1, 1) * scale - log_h)
            probs = jnp.where(key_lane < SEQ, probs, 0.0)
            prob_grad = dot(o_h, values, 1, 1)
            dv += dot(probs.astype(BF), o_h, 0, 0)
            delta = jnp.sum(probs * prob_grad, -1, keepdims=True)
            score_grad = (probs * (prob_grad - delta)).astype(BF)
            dq += dot(score_grad, keys * masks[h])
            dk += dot(score_grad, q_h, 0, 0)
        grads[0, :, cols] = (dq * scale).astype(BF)
        grads[1, :, cols] = (dk * scale).astype(BF)
        grads[2, :, cols] = dv.astype(BF)

    first = first_ref[0]
    total = None
    for k in range(3):
        part = dot(grads[k], wt_ref[k])
        total = part if total is None else total + part
        acc[k] += dot(grads[k], first, 0, 0)
    field[place, :] = (field[place, :].astype(F32) + dot(back, total.astype(BF))).astype(BF)

    @pl.when(i == pl.num_programs(0) - 1)
    def _():
        for p in range(count):
            piece_refs[p][...] = field[pl.ds(pl.multiple_of(starts_ref[p], 16), each), :]
        hg_ref[...] = acc[...].astype(BF)
        gain_grad = jnp.zeros_like(ng_ref)
        for k in range(3):
            gain_grad += jnp.sum(acc[k] * wt_ref[k].astype(F32), 0, keepdims=True)
        ng_ref[...] = gain_grad / gain_ref[...]


def attend_back(starts, dmix, qkv, logs, first, head_in_t, gain):
    images, height, width = first.shape
    each, cols = dmix[0].shape
    count = len(dmix)
    scratch_rows = max(images * SEQ // 16 * 16 + 48, each * count)
    spec = pltpu.PrefetchScalarGridSpec(
        num_scalar_prefetch=1,
        grid=(images,),
        in_specs=[
            pl.BlockSpec((3, 1, height, cols), lambda i, *_: (0, i, 0, 0)),
            image(height, LANES),
            image(height, width),
            whole(head_in_t.shape, True),
            whole((1, width)),
        ]
        + [whole((each, cols), True)] * count,
        out_specs=[whole((each, width))] * count + [whole(head_in_t.shape), whole((1, width))],
        scratch_shapes=[
            pltpu.VMEM(head_in_t.shape, F32),
            pltpu.VMEM((3, height, cols), BF),
            pltpu.VMEM((scratch_rows, cols), BF),
            pltpu.VMEM((scratch_rows, width), BF),
        ],
    )
    return pl.pallas_call(
        functools.partial(attend_back_kernel, count),
        grid_spec=spec,
        out_shape=[jax.ShapeDtypeStruct((each, width), BF)] * count
        + [jax.ShapeDtypeStruct(head_in_t.shape, BF), jax.ShapeDtypeStruct((1, width), F32)],
        compiler_params=params(),
        cost_estimate=cost(24 * images * height * width * cols, 20 * images * height * width),
        name="attend_back",
    )(starts, qkv, logs, first, head_in_t, gain, *dmix)


def block_count(blocks, slots):
    return max(n for n in range(1, blocks + 1) if blocks % n == 0 and n * slots <= 448)


def pack_first_kernel(x_ref, tail_ref, lp_ref, side_ref, out_ref, rows):
    i, n = pl.program_id(0), pl.program_id(1)

    @pl.when((i == 0) & (n == 0))
    def _():
        fill(x_ref, tail_ref, rows)

    blocks, _, slots, _ = out_ref.shape
    tile = blocks * slots
    j = (n * pl.num_programs(0) + i) * tile + iota(tile, rows.shape[0], 0)
    picks = [flag(lp_ref[c : c + 1, :] == j) for c in range(2)]
    width = x_ref.shape[1]
    main = dot((picks[0] + picks[1]).astype(BF), rows[...]).astype(BF)
    out_ref[:, 0, :, 0:width] = main.reshape(blocks, slots, width)
    extra = dot(picks[0].astype(BF), side_ref[0]) + dot(picks[1].astype(BF), side_ref[1])
    out_ref[:, 0, :, width:] = extra.astype(BF).reshape(blocks, slots, LANES)


def pack_first(x, tail, lp, side, experts, slots):
    rows, width = x.shape
    padded = lp.shape[1]
    blocks = block_count(experts, slots)
    return pl.pallas_call(
        pack_first_kernel,
        grid=(experts // blocks, CHUNKS),
        in_specs=[whole((rows, width), True), whole((16, width)), whole(lp.shape), whole(side.shape)],
        out_specs=pl.BlockSpec((blocks, 1, slots, width + LANES), lambda i, n: (i, n, 0, 0)),
        out_shape=jax.ShapeDtypeStruct((experts, CHUNKS, slots, width + LANES), BF),
        scratch_shapes=[pltpu.VMEM((padded, width), BF)],
        compiler_params=params(),
        cost_estimate=cost(3 * CHUNKS * experts * slots * padded * width, 2 * rows * width),
        name="pack_cotangent",
    )(x, tail, lp, side)


def pack_kernel(base, count, part_ref, *refs):
    lp_ref, out_ref = refs[count], refs[count + 1]
    total = None
    tile = out_ref.shape[0]
    for p in range(count):
        j = base + pl.program_id(0) * tile + iota(tile, refs[p].shape[0], 0)
        lp = lp_ref[part_ref[p]]
        picks = flag((lp[0:1, :] == j) | (lp[1:2, :] == j)).astype(BF)
        part = dot(picks, refs[p][...])
        total = part if total is None else total + part
    out_ref[...] = total.astype(BF)


def pack(part_of, pieces, lp, experts, slots, base):
    rows, width = pieces[0].shape
    count = len(pieces)
    tile = slots * block_count(experts, slots)
    spec = pltpu.PrefetchScalarGridSpec(
        num_scalar_prefetch=1,
        grid=(experts * slots // tile,),
        in_specs=[whole((rows, width), True)] * count + [whole(lp.shape)],
        out_specs=rows_spec(tile, width),
    )
    return pl.pallas_call(
        functools.partial(pack_kernel, base, count),
        grid_spec=spec,
        out_shape=jax.ShapeDtypeStruct((experts * slots, width), BF),
        compiler_params=params(),
        cost_estimate=cost(3 * experts * slots * rows * count * width, 2 * rows * count * width),
        name="pack_rows",
    )(part_of, *pieces, lp)


def unpack_kernel(count, slots, per, graded, part_ref, lp_ref, *refs):
    row_refs, out_refs = refs[:count], refs[count:]
    lp = lp_ref[...]
    height = lp.shape[0]
    rows, width = row_refs[0].shape
    total = jnp.zeros((height, width), F32)
    lanes = up_to(slots, LANES)
    extra = [jnp.zeros((height, lanes), F32) for _ in range(2)]
    for n in range(count):
        j = n * rows + iota(1, rows, 1)
        hits = (lp[:, 0:1] == j) | (lp[:, 1:2] == j)
        total += dot(flag(hits).astype(BF), row_refs[n][...])
        if graded:
            j = iota(1, lanes, 1)
            for e in range(rows // slots):
                spare = row_refs[n][(e + 1) * slots - 16 : (e + 1) * slots, 0 : 2 * lanes].astype(F32)
                spare = spare[per + 16 - slots : per + 17 - slots, :]
                values = spare[:, :lanes] + spare[:, lanes:]
                for c in range(2):
                    hit = lp[:, c : c + 1] - (n * rows + e * slots) == j
                    extra[c] += jnp.where(hit, values, 0.0)
    value = total.astype(BF)
    if graded:
        lane = iota(1, LANES, 1)
        tail = jnp.zeros((height, LANES), F32)
        for c in range(2):
            grad = jnp.sum(extra[c], -1, keepdims=True)
            high = grad.astype(BF).astype(F32)
            tail = jnp.where(lane == c, high, tail)
            tail = jnp.where(lane == 2 + c, grad - high, tail)
        value = jnp.concatenate([value, tail.astype(BF)], 1)
    store_piece(out_refs, 1, value)


def unpack(part_of, lp, rows, slots, per, each, graded):
    parts = lp.shape[0] // each
    count = len(rows)
    width = rows[0].shape[1] + (LANES if graded else 0)
    out_specs, out_shape = by_piece(parts, 1, (each, width), (each, width), BF)
    spec = pltpu.PrefetchScalarGridSpec(
        num_scalar_prefetch=1,
        grid=(parts,),
        in_specs=[pl.BlockSpec((each, 2), lambda i, at: (at[i], 0))] + [whole(item.shape, True) for item in rows],
        out_specs=out_specs,
    )
    return pl.pallas_call(
        functools.partial(unpack_kernel, count, slots, per, graded),
        grid_spec=spec,
        out_shape=out_shape,
        compiler_params=params(),
        cost_estimate=cost(3 * lp.shape[0] * count * rows[0].size, 4 * count * rows[0].size),
        name="unpack_rows",
    )(part_of, lp, *rows)


def assemble_kernel(count, steps, part_ref, *refs):
    out_ref = refs[count]
    for p in range(count):

        @pl.when(pl.program_id(0) // steps == p)
        def _():
            out_ref[...] = refs[p][...].astype(out_ref.dtype)


def assemble(part_of, pieces, rows, dtype):
    each, width = pieces[0].shape
    count = len(pieces)
    tile = each // 2 if each % 32 == 0 else each
    steps = each // tile
    in_specs, _ = by_piece(count, steps, (tile, width), (each, width), BF)
    spec = pltpu.PrefetchScalarGridSpec(
        num_scalar_prefetch=1,
        grid=(count * steps,),
        in_specs=in_specs,
        out_specs=pl.BlockSpec((tile, width), lambda i, at: (at[i // steps] * steps + i % steps, 0)),
    )
    return pl.pallas_call(
        functools.partial(assemble_kernel, count, steps),
        grid_spec=spec,
        out_shape=jax.ShapeDtypeStruct((rows, width), dtype),
        compiler_params=params(),
        cost_estimate=cost(2 * rows * width, 8 * rows * width),
        name="assemble",
    )(part_of, *pieces)


def sum_turned_kernel(a_ref, b_ref, out_ref):
    out_ref[...] = (a_ref[...].astype(F32) + b_ref[...].astype(F32)).T


def sum_turned(a, b):
    rows, width = a.shape
    tile = min(256, rows)
    return pl.pallas_call(
        sum_turned_kernel,
        grid=(rows // tile,),
        in_specs=[rows_spec(tile, width)] * 2,
        out_specs=pl.BlockSpec((width, tile), lambda i: (0, i)),
        out_shape=jax.ShapeDtypeStruct((width, rows), F32),
        compiler_params=params(),
        cost_estimate=cost(rows * width, 8 * rows * width),
        name="sum_turned",
    )(a, b)


def middle_kernel(count, limit, at_ref, *refs):
    mixed_refs, wo_refs = refs[:count], refs[count : 2 * count]
    x_ref, gain_ref, router_ref, ids_ref, noise_ref, mid_ref, second_ref, gates_ref = refs[2 * count :]
    tile = x_ref.shape[0]
    valid = (at_ref[0] + pl.program_id(0)) * tile + iota(tile, 1, 0) < limit
    middle = jnp.where(valid, x_ref[...].astype(F32), 0.0)
    for mixed_ref, wo_ref in zip(mixed_refs, wo_refs):
        middle += dot(mixed_ref[...], wo_ref[...])
    mid_ref[...] = middle
    scaled, _ = norm_parts(middle)
    second = (scaled * gain_ref[...]).astype(BF)
    second_ref[...] = second
    logits = dot(second, router_ref[...])
    lane = iota(1, LANES, 1)
    chosen = [
        jnp.sum(jnp.where(lane == ids_ref[:, c : c + 1], logits, 0.0), -1, keepdims=True)
        + noise_ref[:, c : c + 1]
        for c in range(2)
    ]
    top = jnp.maximum(chosen[0], chosen[1])
    raw = [jnp.exp(item - top) for item in chosen]
    inverse = 1.0 / (raw[0] + raw[1])
    gates = jnp.where(lane == 0, raw[0] * inverse, 0.0) + jnp.where(lane == 1, raw[1] * inverse, 0.0)
    gates_ref[...] = jnp.where(valid, gates, 0.0)


def half_tile(each):
    return each // 2 if each % 32 == 0 else each


def middle_of(at, mixed, head_out, x, gain, router, ids, noise):
    each, cols = mixed[0].shape
    parts = len(mixed)
    rows, width = x.shape
    tile = half_tile(each)
    spec = pltpu.PrefetchScalarGridSpec(
        num_scalar_prefetch=1,
        grid=(each // tile,),
        in_specs=[rows_spec(tile, cols)] * parts
        + [whole((cols, width), True)] * parts
        + [
            own_spec(tile, width),
            whole((1, width)),
            whole(router.shape),
            own_spec(tile, 2),
            own_spec(tile, 2),
        ],
        out_specs=[rows_spec(tile, width), rows_spec(tile, width), rows_spec(tile, LANES)],
    )
    return pl.pallas_call(
        functools.partial(middle_kernel, parts, rows),
        grid_spec=spec,
        out_shape=[
            jax.ShapeDtypeStruct((each, width), F32),
            jax.ShapeDtypeStruct((each, width), BF),
            jax.ShapeDtypeStruct((each, LANES), F32),
        ],
        compiler_params=params(),
        cost_estimate=cost(4 * each * width * width, 24 * each * width),
        name="middle",
    )(at, *mixed, *head_out, x, gain, router, ids, noise)


def middle_back_kernel(count, limit, at_ref, *refs):
    keep_ref, far_ref, mid_ref, second_ref, gates_ref, ids_ref, up_ref, gain_ref, router_ref = refs[:9]
    mixed_refs, wo_refs = refs[9 : 9 + count], refs[9 + count : 9 + 2 * count]
    mg_ref, rg_ref, ng_ref = refs[9 + 2 * count : 12 + 2 * count]
    hog_refs, dmix_refs, hog_acc = refs[12 + 2 * count : 12 + 3 * count], refs[12 + 3 * count : -1], refs[-1]
    i = pl.program_id(0)

    @pl.when(i == 0)
    def _():
        hog_acc[...] = jnp.zeros_like(hog_acc)
        rg_ref[...] = jnp.zeros_like(rg_ref)
        ng_ref[...] = jnp.zeros_like(ng_ref)

    tile, width = up_ref.shape
    valid = (at_ref[0] + i) * tile + iota(tile, 1, 0) < limit
    lane = iota(1, LANES, 1)
    tail = keep_ref[:, width:].astype(F32) + far_ref[:, width:].astype(F32)
    gates = gates_ref[...]
    gate, grad = [], []
    for c in range(2):
        gate.append(jnp.sum(jnp.where(lane == c, gates, 0.0), -1, keepdims=True))
        grad.append(jnp.sum(jnp.where((lane == c) | (lane == 2 + c), tail, 0.0), -1, keepdims=True))
    mean_term = gate[0] * grad[0] + gate[1] * grad[1]
    logit_grad = jnp.zeros((tile, LANES), F32)
    for c in range(2):
        hit = (lane == ids_ref[:, c : c + 1]) & valid
        logit_grad = jnp.where(hit, gate[c] * (grad[c] - mean_term), logit_grad)
    logit_grad = logit_grad.astype(BF)
    routed = keep_ref[:, 0:width].astype(F32) + far_ref[:, 0:width].astype(F32)
    second_grad = routed + dot(logit_grad, router_ref[...], 1, 1)
    rg_ref[...] += dot(logit_grad, second_ref[...], 0, 0)
    scaled, spread = norm_parts(mid_ref[...])
    ng_ref[...] += jnp.sum(second_grad * scaled, 0, keepdims=True)
    upstream = jnp.where(valid, up_ref[...].astype(F32), 0.0)
    middle_grad = upstream + norm_field_back(second_grad, gain_ref[...], scaled, spread)
    mg_ref[...] = middle_grad
    rounded = middle_grad.astype(BF)
    for t in range(count):
        dmix_refs[t][...] = dot(rounded, wo_refs[t][...], 1, 1).astype(BF)
        hog_acc[t] += dot(mixed_refs[t][...], rounded, 0, 0)

    @pl.when(i == pl.num_programs(0) - 1)
    def _():
        for t in range(count):
            hog_refs[t][...] = hog_acc[t].astype(BF)


def middle_back(at, keep, far, middle, second, gates, ids, up, mixed, head_out, gain, router):
    each, cols = mixed[0].shape
    parts = len(mixed)
    rows, width = up.shape
    tile = half_tile(each)
    spec = pltpu.PrefetchScalarGridSpec(
        num_scalar_prefetch=1,
        grid=(each // tile,),
        in_specs=[
            rows_spec(tile, keep.shape[1]),
            rows_spec(tile, keep.shape[1]),
            rows_spec(tile, width),
            rows_spec(tile, width),
            rows_spec(tile, LANES),
            own_spec(tile, 2),
            own_spec(tile, width),
            whole((1, width)),
            whole(router.shape),
        ]
        + [rows_spec(tile, cols)] * parts
        + [whole((cols, width), True)] * parts,
        out_specs=[rows_spec(tile, width), whole((LANES, width)), whole((1, width))]
        + [whole((cols, width))] * parts
        + [rows_spec(tile, cols)] * parts,
        scratch_shapes=[pltpu.VMEM((parts, cols, width), F32)],
    )
    return pl.pallas_call(
        functools.partial(middle_back_kernel, parts, rows),
        grid_spec=spec,
        out_shape=[
            jax.ShapeDtypeStruct((each, width), F32),
            jax.ShapeDtypeStruct((LANES, width), F32),
            jax.ShapeDtypeStruct((1, width), F32),
        ]
        + [jax.ShapeDtypeStruct((cols, width), BF)] * parts
        + [jax.ShapeDtypeStruct((each, cols), BF)] * parts,
        compiler_params=params(),
        cost_estimate=cost(8 * each * width * width, 40 * each * width),
        name="middle_back",
    )(at, keep, far, middle, second, gates, ids, up, gain, router, *mixed, *head_out)


def input_back_kernel(limit, at_ref, keep_ref, far_ref, x_ref, mg_ref, gain_ref, out_ref):
    tile = x_ref.shape[0]
    valid = (at_ref[0] + pl.program_id(0)) * tile + iota(tile, 1, 0) < limit
    scaled, spread = norm_parts(jnp.where(valid, x_ref[...].astype(F32), 0.0))
    first_grad = keep_ref[...].astype(F32) + far_ref[...].astype(F32)
    out_ref[...] = (mg_ref[...] + norm_field_back(first_grad, gain_ref[...], scaled, spread)).astype(BF)


def input_back(at, keep, far, x, middle_grad, gain):
    each, width = middle_grad.shape
    tile = half_tile(each)
    spec = pltpu.PrefetchScalarGridSpec(
        num_scalar_prefetch=1,
        grid=(each // tile,),
        in_specs=[rows_spec(tile, width), rows_spec(tile, width), own_spec(tile, width), rows_spec(tile, width), whole((1, width))],
        out_specs=rows_spec(tile, width),
    )
    return pl.pallas_call(
        functools.partial(input_back_kernel, x.shape[0]),
        grid_spec=spec,
        out_shape=jax.ShapeDtypeStruct((each, width), BF),
        compiler_params=params(),
        cost_estimate=cost(20 * each * width, 16 * each * width),
        name="input_back",
    )(at, keep, far, x, middle_grad, gain)


def gelu_parts(v):
    x = jnp.abs(v) * 0.7071067811865476
    t = 1.0 / (1.0 + 0.3275911 * x)
    bell = jnp.exp(-x * x)
    poly = ((((1.061405429 * t - 1.453152027) * t + 1.421413741) * t - 0.284496736) * t + 0.254829592) * t
    below = 0.5 * poly * bell
    share = jnp.where(v < 0.0, below, 1.0 - below)
    return v * share, share + v * bell * 0.3989422804014327


def expert_kernel(count, slots, per, x_ref, g_ref, router_ref, *refs):
    w1_hbm, w2_hbm = refs[: 2 * count], refs[2 * count : 3 * count]
    back_ref, act_ref, hg_ref, rg_ref, dx_ref, w1, w2, sems = refs[3 * count :]
    rows, width = x_ref[...], x_ref.shape[1]
    half = width // 2
    copies = []
    for t in range(count):
        copies.append(
            [
                pltpu.make_async_copy(w1_hbm[2 * t], w1.at[t, pl.ds(0, half)], sems.at[3 * t]),
                pltpu.make_async_copy(w1_hbm[2 * t + 1], w1.at[t, pl.ds(half, half)], sems.at[3 * t + 1]),
                pltpu.make_async_copy(w2_hbm[t], w2.at[t], sems.at[3 * t + 2]),
            ]
        )

    @pl.when(pl.program_id(0) == 0)
    def _():
        for group in copies:
            for item in group:
                item.start()

    lane = iota(1, LANES, 1)
    signal = g_ref[:, 0].reshape(rows.shape[0], width + LANES)
    side = signal[:, width:].astype(F32)

    def column(*lanes):
        keep = lane == lanes[0]
        for other in lanes[1:]:
            keep = keep | (lane == other)
        return jnp.sum(jnp.where(keep, side, 0.0), -1, keepdims=True)

    logits = dot(rows, router_ref[...])
    lane_f = lane.astype(F32)
    mine = jnp.sum(jnp.where(lane_f == column(4), logits, 0.0), -1, keepdims=True)
    other = jnp.sum(jnp.where(lane_f == column(0), logits, 0.0), -1, keepdims=True)
    gate = 1.0 / (1.0 + jnp.exp(other - mine - column(1, 2, 3)))
    upstream = signal[:, 0:width].astype(F32)
    rows_grad = (gate * upstream).astype(BF)
    rg_ref[...] = rows_grad
    hidden_here = w1.shape[2]
    step = min(512, hidden_here)
    for t in range(count):

        @pl.when(pl.program_id(0) == 0)
        def _():
            for item in copies[t]:
                item.wait()

        for at in range(0, hidden_here, step):
            cols = slice(at, at + step)
            place = slice(t * hidden_here + at, t * hidden_here + at + step)
            hidden = dot(rows, w1[t, :, cols])
            active_grad = dot(rows_grad, w2[t, cols, :], 1, 1)
            active, slope = gelu_parts(hidden)
            act_ref[:, place] = active.astype(BF)
            hg_ref[:, place] = (active_grad * slope).astype(BF)
    out = None
    grad = None
    for t in range(count):
        place = slice(t * hidden_here, (t + 1) * hidden_here)
        part = dot(act_ref[:, place], w2[t])
        out = part if out is None else out + part
        part = dot(hg_ref[:, place], w1[t], 1, 1)
        grad = part if grad is None else grad + part
    dx_ref[...] = grad.astype(BF)
    back_ref[...] = (gate * out).astype(BF)
    gate_grad = jnp.sum(upstream * out.astype(BF).astype(F32), -1, keepdims=True)
    lanes = up_to(slots, LANES)
    spread = iota(slots, lanes, 0) == iota(slots, lanes, 1)
    spare_row = iota(16, 1, 0) == per + 16 - slots
    for b in range(x_ref.shape[0] // slots):
        end = (b + 1) * slots
        line = jnp.sum(jnp.where(spread, gate_grad[end - slots : end], 0.0), 0, keepdims=True)
        high = line.astype(BF).astype(F32)
        line = jnp.concatenate([high, line - high, jnp.zeros((1, width - 2 * lanes), F32)], 1)
        dx_ref[end - 16 : end, :] = jnp.where(spare_row, line, grad[end - 16 : end]).astype(BF)


def expert(x, g, chunk, router, w1, w2, slots, per):
    rows, width = x.shape
    count = len(w2)
    here = w2[0].shape[0]
    total = count * here
    blocks = block_count(rows // slots, slots)
    tile = slots * blocks

    def tiled(cols):
        return pl.BlockSpec((tile, cols), lambda i: (i, 0))

    flops = 8 * rows * width * total
    return pl.pallas_call(
        functools.partial(expert_kernel, count, slots, per),
        grid=(rows // tile,),
        in_specs=[
            tiled(width),
            pl.BlockSpec((blocks, 1, slots, g.shape[3]), lambda i: (i, chunk, 0, 0)),
            whole(router.shape),
        ]
        + [pl.BlockSpec(memory_space=pl.ANY)] * (3 * count),
        out_specs=[tiled(width), tiled(total), tiled(total), tiled(width), tiled(width)],
        out_shape=[
            jax.ShapeDtypeStruct((rows, width), BF),
            jax.ShapeDtypeStruct((rows, total), BF),
            jax.ShapeDtypeStruct((rows, total), BF),
            jax.ShapeDtypeStruct((rows, width), BF),
            jax.ShapeDtypeStruct((rows, width), BF),
        ],
        scratch_shapes=[
            pltpu.VMEM((count, width, here), BF),
            pltpu.VMEM((count, here, width), BF),
            pltpu.SemaphoreType.DMA((3 * count,)),
        ],
        compiler_params=params(60),
        cost_estimate=pl.CostEstimate(flops=flops, bytes_accessed=rows * total * 6, transcendentals=rows * total * 2),
        name="expert",
    )(x, g, router, *w1, *w2)


def weight_kernel(count, steps, *refs):
    ins, outs = refs[: 2 * count], refs[2 * count :]
    total = None
    for n in range(count):
        part = dot(ins[2 * n][...], ins[2 * n + 1][...], 0, 0)
        total = part if total is None else total + part
    store_piece(outs, steps, total.astype(BF))


def weight_grad(columns, rows, first, here):
    count = len(columns)
    width = rows[0].shape[1]
    step = min(512, here)
    steps = here // step
    offset = first * steps
    specs, args = [], []
    for a, b in zip(columns, rows):
        specs += [pl.BlockSpec((a.shape[0], step), lambda i: (0, i + offset)), whole(b.shape, True)]
        args += [a, b]
    out_specs, out_shape = by_piece(2, steps, (step, width), (here, width), BF)
    return pl.pallas_call(
        functools.partial(weight_kernel, count, steps),
        grid=(2 * steps,),
        in_specs=specs,
        out_specs=out_specs,
        out_shape=out_shape,
        compiler_params=params(),
        cost_estimate=cost(4 * sum(b.shape[0] for b in rows) * width * here, 8 * here * width),
        name="weight_grad",
    )(*args)


def shards(
    block_in,
    norm_one,
    head_in,
    head_out,
    norm_two,
    router,
    expert_in,
    expert_out,
    expert_ids,
    route_noise,
    cotangent,
):
    rows_here, width = block_in.shape
    parts = lax.axis_size("tensor")
    groups = lax.axis_size("expert")
    me = lax.axis_index("tensor")
    images = rows_here // SEQ
    height = up_to(SEQ, 16)
    each = up_to(-(-rows_here // parts), 16)
    experts = router.shape[1]
    capacity = (rows_here * 2 * 8 // (5 * experts) + 15) // 16 * 16
    share = -(-capacity // parts)
    per = -(-share // CHUNKS)
    slots = up_to(per + 1, 16)
    chunk_rows = experts * slots
    full = rows_here // 16 * 16
    here = expert_out.shape[1]

    paired = parts == 4
    order = (0, 2, 1, 3) if paired else tuple(range(parts))
    part_of = jnp.stack([me ^ k if paired else jnp.int32(k) for k in order]).astype(jnp.int32)
    starts = part_of * each
    own_block = (me * (each // half_tile(each)))[None].astype(jnp.int32)

    def cross(x, k):
        return lax.ppermute(x, "tensor", [(n, n ^ k) for n in range(parts)])

    def far_part(x):
        return cross(x, 2) if paired else x

    def gathered_from(x, far):
        if not paired:
            every = lax.all_gather(x, "tensor", axis=0, tiled=False)
            return [every[p] for p in range(parts)]
        return [x, far, cross(x, 1), cross(far, 1)]

    def gathered(x):
        return gathered_from(x, far_part(x))

    def near_hop(pieces):
        return [cross(piece, 1) for piece in pieces[2:]] if paired else pieces

    def near_sum(pieces, came):
        if not paired:
            return lax.psum_scatter(jnp.stack(pieces), "tensor", scatter_dimension=0), None
        kept, other = ((a.astype(F32) + b.astype(F32)).astype(BF) for a, b in zip(pieces, came))
        return kept, other

    def far_hop(kept, other):
        return cross(other, 2) if paired else jnp.zeros_like(kept)

    def scattered(pieces):
        kept, other = near_sum(pieces, near_hop(pieces))
        return kept, far_hop(kept, other)

    def swapped(pieces):
        if not paired:
            every = lax.all_to_all(jnp.stack(pieces), "tensor", split_axis=0, concat_axis=0, tiled=True)
            return [every[p] for p in range(parts)]
        return [cross(piece, k) if k else piece for piece, k in zip(pieces, order)]

    def over_experts(x):
        return lax.all_to_all(x, "expert", split_axis=0, concat_axis=0, tiled=True)

    def pinned(*items):
        return lax.optimization_barrier(items)

    def tail_of(x):
        return jnp.pad(x[full:], ((0, 16 - (rows_here - full)), (0, 0)))

    names = jnp.arange(experts, dtype=jnp.int32)
    member = [(expert_ids[:, c : c + 1] == names).astype(jnp.int32) for c in range(2)]
    both = member[0] + member[1]
    earlier = jnp.cumsum(both, 0) - both
    slot = jnp.stack([jnp.sum(earlier * item, -1) for item in member], 1)
    local = slot - me * share
    place = local // per * chunk_rows + expert_ids * slots + local % per
    place = jnp.where((local >= 0) & (local < share), place, -1)
    place = jnp.pad(place, ((0, each * parts - rows_here), (0, 0)), constant_values=-1)
    place_lanes = place.T
    place_parts = jnp.swapaxes(place_lanes.reshape(2, parts, each), 0, 1)

    sides = []
    for c in range(2):
        gap = route_noise[:, c] - route_noise[:, 1 - c]
        high = gap.astype(BF)
        left = gap - high.astype(F32)
        mid = left.astype(BF)
        low = (left - mid.astype(F32)).astype(BF)
        columns = [expert_ids[:, 1 - c].astype(BF), high, mid, low, expert_ids[:, c].astype(BF)]
        sides.append(jnp.stack(columns, 1))
    side = jnp.pad(jnp.stack(sides), ((0, 0), (0, each * parts - rows_here), (0, LANES - 5)))

    router_wide = jnp.pad(router, ((0, 0), (0, LANES - experts)))
    gain_one, gain_two = norm_one[None, :], norm_two[None, :]
    head_out_all = gathered(head_out)
    w1_own = [expert_in[0, : width // 2], expert_in[0, width // 2 :]]
    w1_far = [far_part(item) for item in w1_own]

    packed = pack_first(cotangent, tail_of(cotangent), place_lanes, side, experts, slots)
    block_rows, packed, w1_far[0] = pinned(block_in, packed, w1_far[0])
    signal = over_experts(packed)

    first_in, qkv, logs, *mixed = attend(
        starts, block_rows, tail_of(block_in), gain_one, head_in, images, height, each, parts
    )
    *mixed, w1_far[1] = pinned(*mixed, w1_far[1])
    mixed = swapped(mixed)
    middle, second_in, gates = middle_of(
        own_block, mixed, head_out_all, block_in, gain_two, router_wide, expert_ids, route_noise
    )
    *second_all, signal, late_out = pinned(*gathered(second_in), signal, expert_out[0])
    w1 = [gathered_from(a, b) for a, b in zip(w1_own, w1_far)]
    w1 = [w1[h][p] for p in range(parts) for h in range(2)]

    def packed_rows(n):
        return pack(part_of, second_all, place_parts, experts, slots, n * chunk_rows)

    def sent(x):
        return over_experts(x.reshape(experts, slots, width)).reshape(chunk_rows, width)

    x = sent(packed_rows(0))
    w2_far, *outgoing = pinned(far_part(late_out), *[packed_rows(n) for n in range(1, CHUNKS)])
    w2 = gathered_from(expert_out[0], w2_far)
    backs, actives, hidden_grads, rows_grads, arrived, returned = [], [], [], [], [], []
    for n in range(CHUNKS):
        coming = None
        if n + 1 < CHUNKS:
            x, ready = pinned(x, outgoing[n])
            coming = sent(ready)
        if n == 0:
            x, *ready = pinned(x, *w1, *w2)
            w1, w2 = ready[: 2 * parts], ready[2 * parts :]
        back, active, hidden_grad, rows_grad, row_grad = expert(
            x, signal, n, router_wide, w1, w2, slots, per
        )
        if returned:
            row_grad, returned[-1] = pinned(row_grad, returned[-1])
        arrived.append(x)
        actives.append(active)
        hidden_grads.append(hidden_grad)
        rows_grads.append(rows_grad)
        backs.append(back)
        if coming is not None:
            x, row_grad = pinned(coming, row_grad)
        returned.append(sent(row_grad))

    def weight_parts(columns, rows):
        pairs = [weight_grad(columns, rows, p, here) for p in range(parts - 2, -1, -2)]
        return [item for pair in pairs[::-1] for item in pair]

    out_parts = weight_parts(actives, rows_grads)
    out_kept, out_other = near_sum(out_parts, near_hop(out_parts))
    out_kept, *hidden_grads = pinned(out_kept, *hidden_grads)
    out_far = far_hop(out_kept, out_other)
    in_parts = weight_parts(hidden_grads, arrived)
    in_came = near_hop(in_parts)
    *returned, in_first = pinned(*returned, in_parts[0])
    in_parts[0] = in_first

    second_pieces = unpack(part_of, place, returned, slots, per, each, True)
    *second_pieces, out_far = pinned(*second_pieces, out_far)
    out_grad = out_kept.astype(F32) + out_far.astype(F32)
    second_kept, second_far = scattered(second_pieces)
    in_kept, in_other = near_sum(in_parts, in_came)
    second_far, in_kept = pinned(second_far, in_kept)
    if paired:
        second_far, in_other = pinned(second_far, in_other)
    in_far = far_hop(in_kept, in_other)
    combined = [sent(item) for item in backs]
    middle_grad, router_part, norm_two_part, *pieces = middle_back(
        own_block, second_kept, second_far, middle, second_in, gates, expert_ids, cotangent, mixed, head_out_all,
        gain_two, router_wide,
    )
    head_out_parts, mixed_grad = pieces[:parts], pieces[parts:]
    *mixed_grad, combined[0] = pinned(*mixed_grad, combined[0])
    mixed_grad = swapped(mixed_grad)
    head_out_kept, head_out_far = scattered(head_out_parts)
    *pieces, head_in_part, norm_one_part = attend_back(
        starts, mixed_grad, qkv, logs, first_in, jnp.swapaxes(head_in, 1, 2), gain_one
    )
    *pieces, combined[-1], in_far, head_out_far = pinned(*pieces, combined[-1], in_far, head_out_far)
    in_grad = sum_turned(in_kept, in_far)
    first_kept, first_far = scattered(pieces)
    block_pieces = unpack(part_of, place, combined, slots, per, each, False)
    first_far, *block_pieces = pinned(first_far, *block_pieces)
    input_part = input_back(own_block, first_kept, first_far, block_in, middle_grad, gain_one)
    block_kept, block_far = scattered(block_pieces)
    block_own = (middle + block_kept.astype(F32) + block_far.astype(F32)).astype(BF)

    cols = head_in.shape[2]
    head_out_part = (head_out_kept.astype(F32) + head_out_far.astype(F32)).astype(BF)
    small = jnp.concatenate([norm_one_part, norm_two_part, router_part[:experts]], 0).astype(BF)
    count = 4 * cols + 2 + experts
    total = up_to(count, 16 * groups)
    heads = jnp.concatenate(
        [head_in_part.reshape(3 * cols, width), head_out_part, jnp.pad(small, ((0, total - count), (0, 0)))], 0
    )
    heads = over_experts(heads.reshape(groups, total // groups, width))
    heads, block_own = pinned(heads, block_own)
    input_grad = assemble(part_of, gathered(input_part), rows_here, F32)
    block_out = assemble(part_of, gathered(block_own), rows_here, BF)
    heads = jnp.sum(heads.astype(F32), 0).astype(BF)
    heads = lax.all_gather(heads, "expert", axis=0, tiled=True)
    head_in_grad = jnp.swapaxes(heads[: 3 * cols].reshape(3, cols, width), 1, 2).astype(F32)
    head_out_grad = heads[3 * cols : 4 * cols].astype(F32)
    small = heads[4 * cols : count].astype(F32)
    if paired:
        small = small + cross(small, 1)
        small = small + cross(small, 2)
    else:
        small = lax.psum(small, "tensor")
    return (
        block_out,
        input_grad,
        small[0],
        head_in_grad,
        head_out_grad,
        small[1],
        small[2:].T,
        in_grad[None],
        out_grad[None],
    )


def solution(mesh):
    in_specs = (
        P("expert", None),
        P(),
        P(None, None, "tensor"),
        P("tensor", None),
        P(),
        P(),
        P("expert", None, "tensor"),
        P("expert", "tensor", None),
        P("expert", None),
        P("expert", None),
        P("expert", None),
    )
    out_specs = (
        P("expert", None),
        P("expert", None),
        P(),
        P(None, None, "tensor"),
        P("tensor", None),
        P(),
        P(),
        P("expert", None, "tensor"),
        P("expert", "tensor", None),
    )
    return jax.shard_map(shards, mesh=mesh, in_specs=in_specs, out_specs=out_specs, check_vma=False)
```

```python
import functools

import jax
import jax.numpy as jnp
from jax import lax
from jax.experimental import pallas as pl
from jax.experimental.pallas import tpu as pltpu
from jax.sharding import PartitionSpec as P

HD = 64
SEQ = 197
LANES = 128
EPSILON = 1e-06
CHUNKS = 2
BF = jnp.bfloat16
F32 = jnp.float32


def up_to(value, unit):
    return -(-value // unit) * unit


def params(mib=60):
    return pltpu.CompilerParams(vmem_limit_bytes=mib * 1024 * 1024)


def dot(a, b, da=1, db=0):
    return lax.dot_general(a, b, (((da,), (db,)), ((), ())), preferred_element_type=F32)


def iota(rows, cols, dim):
    return lax.broadcasted_iota(jnp.int32, (rows, cols), dim)


def flag(mask):
    return jnp.where(mask, 1.0, 0.0)


def whole(shape, once=False):
    zeros = (0,) * len(shape)
    mode = pl.Buffered(1) if once else None
    return pl.BlockSpec(shape, lambda *_: zeros, pipeline_mode=mode)


def image(*shape):
    return pl.BlockSpec((1,) + shape, lambda i, *_: (i,) + (0,) * len(shape))


def fill(x_ref, tail_ref, rows_ref):
    full = x_ref.shape[0] // 16 * 16
    rows_ref[0:full, :] = x_ref[0:full, :]
    rows_ref[full : full + 16, :] = tail_ref[...]
    rest = rows_ref.shape[0] - full - 16
    if rest:
        rows_ref[full + 16 :, :] = jnp.zeros((rest, rows_ref.shape[1]), BF)


def norm_parts(field):
    centre = field - jnp.mean(field, -1, keepdims=True)
    spread = lax.rsqrt(jnp.mean(centre * centre, -1, keepdims=True) + EPSILON)
    return centre * spread, spread


def norm_field_back(upstream, gain, scaled, spread):
    weighted = upstream * gain
    return spread * (
        weighted
        - jnp.mean(weighted, -1, keepdims=True)
        - scaled * jnp.mean(weighted * scaled, -1, keepdims=True)
    )


def cost(flops, size):
    return pl.CostEstimate(flops=flops, bytes_accessed=size, transcendentals=0)


def by_piece(count, steps, block, shape, dtype):
    def spec(p):
        def place(i, *_):
            return (jnp.clip(i - p * steps, 0, steps - 1), 0)

        return pl.BlockSpec(block, place)

    return [spec(p) for p in range(count)], [jax.ShapeDtypeStruct(shape, dtype)] * count


def store_piece(refs, steps, value):
    for p, ref in enumerate(refs):

        @pl.when(pl.program_id(0) // steps == p)
        def _():
            ref[...] = value


def rows_spec(tile, width):
    return pl.BlockSpec((tile, width), lambda i, *_: (i, 0))


def own_spec(tile, width):
    return pl.BlockSpec((tile, width), lambda i, at: (at[0] + i, 0))


def window_of(i, height, back=False):
    start = i * SEQ
    aligned = start // 16 * 16
    window = height + 16
    shape = (window, height) if back else (height, window)
    r, c = iota(*shape, 1 if back else 0), iota(*shape, 0 if back else 1)
    match = flag((c == r + (start - aligned)) & (r < SEQ)).astype(BF)
    return match, pl.ds(pl.multiple_of(aligned, 16), window)


def head_masks():
    lane = iota(1, LANES, 1)
    return [(flag(lane // HD == h)).astype(BF) for h in range(2)]


def attend_kernel(count, starts_ref, x_ref, tail_ref, gain_ref, w_ref, first_ref, qkv_ref, log_ref, *refs):
    piece_refs, rows, mixed = refs[:count], refs[count], refs[count + 1]
    i = pl.program_id(0)
    height = first_ref.shape[1]
    cols = mixed.shape[1]

    @pl.when(i == 0)
    def _():
        fill(x_ref, tail_ref, rows)
        mixed[...] = jnp.zeros_like(mixed)

    match, place = window_of(i, height)
    field = dot(match, rows[place, :])
    scaled, _ = norm_parts(field)
    first = (scaled * gain_ref[...]).astype(BF)
    first_ref[0] = first
    for k in range(3):
        qkv_ref[k, 0] = dot(first, w_ref[k]).astype(BF)
    masks = head_masks()
    lane = iota(1, LANES, 1)
    key_lane = iota(1, height, 1)
    logs = jnp.zeros((height, LANES), F32)
    back, _ = window_of(i, height, True)
    for pair in range(cols // LANES):
        part = slice(pair * LANES, (pair + 1) * LANES)
        queries, keys, values = (qkv_ref[k, 0, :, part] for k in range(3))
        total = jnp.zeros((height, LANES), F32)
        for h in range(2):
            scores = dot(queries * masks[h], keys, 1, 1) * HD ** (-0.5)
            scores = jnp.where(key_lane < SEQ, scores, -1e30)
            highest = jnp.max(scores, -1, keepdims=True)
            weights = jnp.exp(scores - highest)
            sums = jnp.sum(weights, -1, keepdims=True)
            probs = (weights * (1.0 / sums)).astype(BF)
            total += dot(probs, values * masks[h])
            logs = jnp.where(lane == pair * 2 + h, highest + jnp.log(sums), logs)
        mixed[place, part] = (mixed[place, part].astype(F32) + dot(back, total.astype(BF))).astype(BF)
    log_ref[0] = logs

    @pl.when(i == pl.num_programs(0) - 1)
    def _():
        for p in range(count):
            at = pl.multiple_of(starts_ref[p], 16)
            piece_refs[p][...] = mixed[pl.ds(at, piece_refs[p].shape[0]), :]


def attend(starts, block_in, tail, gain, head_in, images, height, each, count):
    rows, width = block_in.shape
    cols = head_in.shape[2]
    scratch_rows = max(rows // 16 * 16 + 48, each * count)
    spec = pltpu.PrefetchScalarGridSpec(
        num_scalar_prefetch=1,
        grid=(images,),
        in_specs=[whole((rows, width), True), whole((16, width)), whole((1, width)), whole(head_in.shape, True)],
        out_specs=[
            image(height, width),
            pl.BlockSpec((3, 1, height, cols), lambda i, *_: (0, i, 0, 0)),
            image(height, LANES),
        ]
        + [whole((each, cols))] * count,
        scratch_shapes=[pltpu.VMEM((scratch_rows, width), BF), pltpu.VMEM((scratch_rows, cols), BF)],
    )
    return pl.pallas_call(
        functools.partial(attend_kernel, count),
        grid_spec=spec,
        out_shape=[
            jax.ShapeDtypeStruct((images, height, width), BF),
            jax.ShapeDtypeStruct((3, images, height, cols), BF),
            jax.ShapeDtypeStruct((images, height, LANES), F32),
        ]
        + [jax.ShapeDtypeStruct((each, cols), BF)] * count,
        compiler_params=params(),
        cost_estimate=cost(16 * images * height * width * cols, 16 * rows * width),
        name="attend",
    )(starts, block_in, tail, gain, head_in)


def attend_back_kernel(count, starts_ref, qkv_ref, log_ref, first_ref, wt_ref, gain_ref, *refs):
    dmix_refs, piece_refs = refs[:count], refs[count : 2 * count]
    hg_ref, ng_ref, acc, grads, dmix, field = refs[2 * count :]
    i = pl.program_id(0)
    height = first_ref.shape[1]
    each = dmix_refs[0].shape[0]

    @pl.when(i == 0)
    def _():
        acc[...] = jnp.zeros_like(acc)
        field[...] = jnp.zeros_like(field)
        rest = dmix.shape[0] - each * count
        if rest:
            dmix[each * count :, :] = jnp.zeros((rest, dmix.shape[1]), BF)
        for p in range(count):
            dmix[pl.ds(pl.multiple_of(starts_ref[p], 16), each), :] = dmix_refs[p][...]

    match, place = window_of(i, height)
    back, _ = window_of(i, height, True)
    out_grads = dot(match, dmix[place, :]).astype(BF)
    masks = head_masks()
    lane = iota(1, LANES, 1)
    key_lane = iota(1, height, 1)
    scale = HD ** (-0.5)
    logs = log_ref[0]
    for pair in range(dmix.shape[1] // LANES):
        cols = slice(pair * LANES, (pair + 1) * LANES)
        queries, keys, values = (qkv_ref[k, 0, :, cols] for k in range(3))
        out_grad = out_grads[:, cols]
        dq = jnp.zeros((height, LANES), F32)
        dk = jnp.zeros((height, LANES), F32)
        dv = jnp.zeros((height, LANES), F32)
        for h in range(2):
            q_h = queries * masks[h]
            o_h = out_grad * masks[h]
            log_h = jnp.sum(jnp.where(lane == pair * 2 + h, logs, 0.0), -1, keepdims=True)
            probs = jnp.exp(dot(q_h, keys, 1, 1) * scale - log_h)
            probs = jnp.where(key_lane < SEQ, probs, 0.0)
            prob_grad = dot(o_h, values, 1, 1)
            dv += dot(probs.astype(BF), o_h, 0, 0)
            delta = jnp.sum(probs * prob_grad, -1, keepdims=True)
            score_grad = (probs * (prob_grad - delta)).astype(BF)
            dq += dot(score_grad, keys * masks[h])
            dk += dot(score_grad, q_h, 0, 0)
        grads[0, :, cols] = (dq * scale).astype(BF)
        grads[1, :, cols] = (dk * scale).astype(BF)
        grads[2, :, cols] = dv.astype(BF)

    first = first_ref[0]
    total = None
    for k in range(3):
        part = dot(grads[k], wt_ref[k])
        total = part if total is None else total + part
        acc[k] += dot(grads[k], first, 0, 0)
    field[place, :] = (field[place, :].astype(F32) + dot(back, total.astype(BF))).astype(BF)

    @pl.when(i == pl.num_programs(0) - 1)
    def _():
        for p in range(count):
            piece_refs[p][...] = field[pl.ds(pl.multiple_of(starts_ref[p], 16), each), :]
        hg_ref[...] = acc[...].astype(BF)
        gain_grad = jnp.zeros_like(ng_ref)
        for k in range(3):
            gain_grad += jnp.sum(acc[k] * wt_ref[k].astype(F32), 0, keepdims=True)
        ng_ref[...] = gain_grad / gain_ref[...]


def attend_back(starts, dmix, qkv, logs, first, head_in_t, gain):
    images, height, width = first.shape
    each, cols = dmix[0].shape
    count = len(dmix)
    scratch_rows = max(images * SEQ // 16 * 16 + 48, each * count)
    spec = pltpu.PrefetchScalarGridSpec(
        num_scalar_prefetch=1,
        grid=(images,),
        in_specs=[
            pl.BlockSpec((3, 1, height, cols), lambda i, *_: (0, i, 0, 0)),
            image(height, LANES),
            image(height, width),
            whole(head_in_t.shape, True),
            whole((1, width)),
        ]
        + [whole((each, cols), True)] * count,
        out_specs=[whole((each, width))] * count + [whole(head_in_t.shape), whole((1, width))],
        scratch_shapes=[
            pltpu.VMEM(head_in_t.shape, F32),
            pltpu.VMEM((3, height, cols), BF),
            pltpu.VMEM((scratch_rows, cols), BF),
            pltpu.VMEM((scratch_rows, width), BF),
        ],
    )
    return pl.pallas_call(
        functools.partial(attend_back_kernel, count),
        grid_spec=spec,
        out_shape=[jax.ShapeDtypeStruct((each, width), BF)] * count
        + [jax.ShapeDtypeStruct(head_in_t.shape, BF), jax.ShapeDtypeStruct((1, width), F32)],
        compiler_params=params(),
        cost_estimate=cost(24 * images * height * width * cols, 20 * images * height * width),
        name="attend_back",
    )(starts, qkv, logs, first, head_in_t, gain, *dmix)


def block_count(blocks, slots):
    return max(n for n in range(1, blocks + 1) if blocks % n == 0 and n * slots <= 448)


def pack_first_kernel(x_ref, tail_ref, lp_ref, side_ref, out_ref, rows):
    i, n = pl.program_id(0), pl.program_id(1)

    @pl.when((i == 0) & (n == 0))
    def _():
        fill(x_ref, tail_ref, rows)

    blocks, _, slots, _ = out_ref.shape
    tile = blocks * slots
    j = (n * pl.num_programs(0) + i) * tile + iota(tile, rows.shape[0], 0)
    picks = [flag(lp_ref[c : c + 1, :] == j) for c in range(2)]
    width = x_ref.shape[1]
    main = dot((picks[0] + picks[1]).astype(BF), rows[...]).astype(BF)
    out_ref[:, 0, :, 0:width] = main.reshape(blocks, slots, width)
    extra = dot(picks[0].astype(BF), side_ref[0]) + dot(picks[1].astype(BF), side_ref[1])
    out_ref[:, 0, :, width:] = extra.astype(BF).reshape(blocks, slots, LANES)


def pack_first(x, tail, lp, side, experts, slots):
    rows, width = x.shape
    padded = lp.shape[1]
    blocks = block_count(experts, slots)
    return pl.pallas_call(
        pack_first_kernel,
        grid=(experts // blocks, CHUNKS),
        in_specs=[whole((rows, width), True), whole((16, width)), whole(lp.shape), whole(side.shape)],
        out_specs=pl.BlockSpec((blocks, 1, slots, width + LANES), lambda i, n: (i, n, 0, 0)),
        out_shape=jax.ShapeDtypeStruct((experts, CHUNKS, slots, width + LANES), BF),
        scratch_shapes=[pltpu.VMEM((padded, width), BF)],
        compiler_params=params(),
        cost_estimate=cost(3 * CHUNKS * experts * slots * padded * width, 2 * rows * width),
        name="pack_cotangent",
    )(x, tail, lp, side)


def pack_kernel(base, count, part_ref, *refs):
    lp_ref, out_ref = refs[count], refs[count + 1]
    total = None
    tile = out_ref.shape[0]
    for p in range(count):
        j = base + pl.program_id(0) * tile + iota(tile, refs[p].shape[0], 0)
        lp = lp_ref[part_ref[p]]
        picks = flag((lp[0:1, :] == j) | (lp[1:2, :] == j)).astype(BF)
        part = dot(picks, refs[p][...])
        total = part if total is None else total + part
    out_ref[...] = total.astype(BF)


def pack(part_of, pieces, lp, experts, slots, base):
    rows, width = pieces[0].shape
    count = len(pieces)
    tile = slots * block_count(experts, slots)
    spec = pltpu.PrefetchScalarGridSpec(
        num_scalar_prefetch=1,
        grid=(experts * slots // tile,),
        in_specs=[whole((rows, width), True)] * count + [whole(lp.shape)],
        out_specs=rows_spec(tile, width),
    )
    return pl.pallas_call(
        functools.partial(pack_kernel, base, count),
        grid_spec=spec,
        out_shape=jax.ShapeDtypeStruct((experts * slots, width), BF),
        compiler_params=params(),
        cost_estimate=cost(3 * experts * slots * rows * count * width, 2 * rows * count * width),
        name="pack_rows",
    )(part_of, *pieces, lp)


def unpack_kernel(count, slots, per, graded, part_ref, lp_ref, *refs):
    row_refs, out_refs = refs[:count], refs[count:]
    lp = lp_ref[...]
    height = lp.shape[0]
    rows, width = row_refs[0].shape
    total = jnp.zeros((height, width), F32)
    lanes = up_to(slots, LANES)
    extra = [jnp.zeros((height, lanes), F32) for _ in range(2)]
    for n in range(count):
        j = n * rows + iota(1, rows, 1)
        hits = (lp[:, 0:1] == j) | (lp[:, 1:2] == j)
        total += dot(flag(hits).astype(BF), row_refs[n][...])
        if graded:
            j = iota(1, lanes, 1)
            for e in range(rows // slots):
                spare = row_refs[n][(e + 1) * slots - 16 : (e + 1) * slots, 0 : 2 * lanes].astype(F32)
                spare = spare[per + 16 - slots : per + 17 - slots, :]
                values = spare[:, :lanes] + spare[:, lanes:]
                for c in range(2):
                    hit = lp[:, c : c + 1] - (n * rows + e * slots) == j
                    extra[c] += jnp.where(hit, values, 0.0)
    value = total.astype(BF)
    if graded:
        lane = iota(1, LANES, 1)
        tail = jnp.zeros((height, LANES), F32)
        for c in range(2):
            grad = jnp.sum(extra[c], -1, keepdims=True)
            high = grad.astype(BF).astype(F32)
            tail = jnp.where(lane == c, high, tail)
            tail = jnp.where(lane == 2 + c, grad - high, tail)
        value = jnp.concatenate([value, tail.astype(BF)], 1)
    store_piece(out_refs, 1, value)


def unpack(part_of, lp, rows, slots, per, each, graded):
    parts = lp.shape[0] // each
    count = len(rows)
    width = rows[0].shape[1] + (LANES if graded else 0)
    out_specs, out_shape = by_piece(parts, 1, (each, width), (each, width), BF)
    spec = pltpu.PrefetchScalarGridSpec(
        num_scalar_prefetch=1,
        grid=(parts,),
        in_specs=[pl.BlockSpec((each, 2), lambda i, at: (at[i], 0))] + [whole(item.shape, True) for item in rows],
        out_specs=out_specs,
    )
    return pl.pallas_call(
        functools.partial(unpack_kernel, count, slots, per, graded),
        grid_spec=spec,
        out_shape=out_shape,
        compiler_params=params(),
        cost_estimate=cost(3 * lp.shape[0] * count * rows[0].size, 4 * count * rows[0].size),
        name="unpack_rows",
    )(part_of, lp, *rows)


def assemble_kernel(count, steps, part_ref, *refs):
    out_ref = refs[count]
    for p in range(count):

        @pl.when(pl.program_id(0) // steps == p)
        def _():
            out_ref[...] = refs[p][...].astype(out_ref.dtype)


def assemble(part_of, pieces, rows, dtype):
    each, width = pieces[0].shape
    count = len(pieces)
    tile, steps = each, 1
    in_specs, _ = by_piece(count, steps, (tile, width), (each, width), BF)
    spec = pltpu.PrefetchScalarGridSpec(
        num_scalar_prefetch=1,
        grid=(count * steps,),
        in_specs=in_specs,
        out_specs=pl.BlockSpec((tile, width), lambda i, at: (at[i // steps] * steps + i % steps, 0)),
    )
    return pl.pallas_call(
        functools.partial(assemble_kernel, count, steps),
        grid_spec=spec,
        out_shape=jax.ShapeDtypeStruct((rows, width), dtype),
        compiler_params=params(),
        cost_estimate=cost(2 * rows * width, 8 * rows * width),
        name="assemble",
    )(part_of, *pieces)


def sum_turned_kernel(a_ref, b_ref, out_ref):
    out_ref[...] = (a_ref[...].astype(F32) + b_ref[...].astype(F32)).T


def sum_turned(a, b):
    rows, width = a.shape
    tile = min(256, rows)
    return pl.pallas_call(
        sum_turned_kernel,
        grid=(rows // tile,),
        in_specs=[rows_spec(tile, width)] * 2,
        out_specs=pl.BlockSpec((width, tile), lambda i: (0, i)),
        out_shape=jax.ShapeDtypeStruct((width, rows), F32),
        compiler_params=params(),
        cost_estimate=cost(rows * width, 8 * rows * width),
        name="sum_turned",
    )(a, b)


def middle_kernel(count, limit, at_ref, *refs):
    mixed_refs, wo_refs = refs[:count], refs[count : 2 * count]
    x_ref, gain_ref, router_ref, ids_ref, noise_ref, mid_ref, second_ref, gates_ref = refs[2 * count :]
    tile = x_ref.shape[0]
    valid = (at_ref[0] + pl.program_id(0)) * tile + iota(tile, 1, 0) < limit
    middle = jnp.where(valid, x_ref[...].astype(F32), 0.0)
    for mixed_ref, wo_ref in zip(mixed_refs, wo_refs):
        middle += dot(mixed_ref[...], wo_ref[...])
    mid_ref[...] = middle
    scaled, _ = norm_parts(middle)
    second = (scaled * gain_ref[...]).astype(BF)
    second_ref[...] = second
    logits = dot(second, router_ref[...])
    lane = iota(1, LANES, 1)
    chosen = [
        jnp.sum(jnp.where(lane == ids_ref[:, c : c + 1], logits, 0.0), -1, keepdims=True)
        + noise_ref[:, c : c + 1]
        for c in range(2)
    ]
    top = jnp.maximum(chosen[0], chosen[1])
    raw = [jnp.exp(item - top) for item in chosen]
    inverse = 1.0 / (raw[0] + raw[1])
    gates = jnp.where(lane == 0, raw[0] * inverse, 0.0) + jnp.where(lane == 1, raw[1] * inverse, 0.0)
    gates_ref[...] = jnp.where(valid, gates, 0.0)


def half_tile(each):
    return each // 2 if each % 32 == 0 else each


def middle_of(at, mixed, head_out, x, gain, router, ids, noise):
    each, cols = mixed[0].shape
    parts = len(mixed)
    rows, width = x.shape
    tile = half_tile(each)
    spec = pltpu.PrefetchScalarGridSpec(
        num_scalar_prefetch=1,
        grid=(each // tile,),
        in_specs=[rows_spec(tile, cols)] * parts
        + [whole((cols, width), True)] * parts
        + [
            own_spec(tile, width),
            whole((1, width)),
            whole(router.shape),
            own_spec(tile, 2),
            own_spec(tile, 2),
        ],
        out_specs=[rows_spec(tile, width), rows_spec(tile, width), rows_spec(tile, LANES)],
    )
    return pl.pallas_call(
        functools.partial(middle_kernel, parts, rows),
        grid_spec=spec,
        out_shape=[
            jax.ShapeDtypeStruct((each, width), F32),
            jax.ShapeDtypeStruct((each, width), BF),
            jax.ShapeDtypeStruct((each, LANES), F32),
        ],
        compiler_params=params(),
        cost_estimate=cost(4 * each * width * width, 24 * each * width),
        name="middle",
    )(at, *mixed, *head_out, x, gain, router, ids, noise)


def middle_back_kernel(count, limit, at_ref, *refs):
    keep_ref, far_ref, mid_ref, second_ref, gates_ref, ids_ref, up_ref, gain_ref, router_ref = refs[:9]
    mixed_refs, wo_refs = refs[9 : 9 + count], refs[9 + count : 9 + 2 * count]
    mg_ref, rg_ref, ng_ref = refs[9 + 2 * count : 12 + 2 * count]
    hog_refs, dmix_refs, hog_acc = refs[12 + 2 * count : 12 + 3 * count], refs[12 + 3 * count : -1], refs[-1]
    i = pl.program_id(0)

    @pl.when(i == 0)
    def _():
        hog_acc[...] = jnp.zeros_like(hog_acc)
        rg_ref[...] = jnp.zeros_like(rg_ref)
        ng_ref[...] = jnp.zeros_like(ng_ref)

    tile, width = up_ref.shape
    valid = (at_ref[0] + i) * tile + iota(tile, 1, 0) < limit
    lane = iota(1, LANES, 1)
    tail = keep_ref[:, width:].astype(F32) + far_ref[:, width:].astype(F32)
    gates = gates_ref[...]
    gate, grad = [], []
    for c in range(2):
        gate.append(jnp.sum(jnp.where(lane == c, gates, 0.0), -1, keepdims=True))
        grad.append(jnp.sum(jnp.where((lane == c) | (lane == 2 + c), tail, 0.0), -1, keepdims=True))
    mean_term = gate[0] * grad[0] + gate[1] * grad[1]
    logit_grad = jnp.zeros((tile, LANES), F32)
    for c in range(2):
        hit = (lane == ids_ref[:, c : c + 1]) & valid
        logit_grad = jnp.where(hit, gate[c] * (grad[c] - mean_term), logit_grad)
    logit_grad = logit_grad.astype(BF)
    routed = keep_ref[:, 0:width].astype(F32) + far_ref[:, 0:width].astype(F32)
    second_grad = routed + dot(logit_grad, router_ref[...], 1, 1)
    rg_ref[...] += dot(logit_grad, second_ref[...], 0, 0)
    scaled, spread = norm_parts(mid_ref[...])
    ng_ref[...] += jnp.sum(second_grad * scaled, 0, keepdims=True)
    upstream = jnp.where(valid, up_ref[...].astype(F32), 0.0)
    middle_grad = upstream + norm_field_back(second_grad, gain_ref[...], scaled, spread)
    mg_ref[...] = middle_grad
    rounded = middle_grad.astype(BF)
    for t in range(count):
        dmix_refs[t][...] = dot(rounded, wo_refs[t][...], 1, 1).astype(BF)
        hog_acc[t] += dot(mixed_refs[t][...], rounded, 0, 0)

    @pl.when(i == pl.num_programs(0) - 1)
    def _():
        for t in range(count):
            hog_refs[t][...] = hog_acc[t].astype(BF)


def middle_back(at, keep, far, middle, second, gates, ids, up, mixed, head_out, gain, router):
    each, cols = mixed[0].shape
    parts = len(mixed)
    rows, width = up.shape
    tile = half_tile(each)
    spec = pltpu.PrefetchScalarGridSpec(
        num_scalar_prefetch=1,
        grid=(each // tile,),
        in_specs=[
            rows_spec(tile, keep.shape[1]),
            rows_spec(tile, keep.shape[1]),
            rows_spec(tile, width),
            rows_spec(tile, width),
            rows_spec(tile, LANES),
            own_spec(tile, 2),
            own_spec(tile, width),
            whole((1, width)),
            whole(router.shape),
        ]
        + [rows_spec(tile, cols)] * parts
        + [whole((cols, width), True)] * parts,
        out_specs=[rows_spec(tile, width), whole((LANES, width)), whole((1, width))]
        + [whole((cols, width))] * parts
        + [rows_spec(tile, cols)] * parts,
        scratch_shapes=[pltpu.VMEM((parts, cols, width), F32)],
    )
    return pl.pallas_call(
        functools.partial(middle_back_kernel, parts, rows),
        grid_spec=spec,
        out_shape=[
            jax.ShapeDtypeStruct((each, width), F32),
            jax.ShapeDtypeStruct((LANES, width), F32),
            jax.ShapeDtypeStruct((1, width), F32),
        ]
        + [jax.ShapeDtypeStruct((cols, width), BF)] * parts
        + [jax.ShapeDtypeStruct((each, cols), BF)] * parts,
        compiler_params=params(),
        cost_estimate=cost(8 * each * width * width, 40 * each * width),
        name="middle_back",
    )(at, keep, far, middle, second, gates, ids, up, gain, router, *mixed, *head_out)


def input_back_kernel(limit, at_ref, keep_ref, far_ref, x_ref, mg_ref, gain_ref, out_ref):
    tile = x_ref.shape[0]
    valid = (at_ref[0] + pl.program_id(0)) * tile + iota(tile, 1, 0) < limit
    scaled, spread = norm_parts(jnp.where(valid, x_ref[...].astype(F32), 0.0))
    first_grad = keep_ref[...].astype(F32) + far_ref[...].astype(F32)
    out_ref[...] = (mg_ref[...] + norm_field_back(first_grad, gain_ref[...], scaled, spread)).astype(BF)


def input_back(at, keep, far, x, middle_grad, gain):
    each, width = middle_grad.shape
    tile = half_tile(each)
    spec = pltpu.PrefetchScalarGridSpec(
        num_scalar_prefetch=1,
        grid=(each // tile,),
        in_specs=[rows_spec(tile, width), rows_spec(tile, width), own_spec(tile, width), rows_spec(tile, width), whole((1, width))],
        out_specs=rows_spec(tile, width),
    )
    return pl.pallas_call(
        functools.partial(input_back_kernel, x.shape[0]),
        grid_spec=spec,
        out_shape=jax.ShapeDtypeStruct((each, width), BF),
        compiler_params=params(),
        cost_estimate=cost(20 * each * width, 16 * each * width),
        name="input_back",
    )(at, keep, far, x, middle_grad, gain)


def gelu_parts(v):
    x = jnp.abs(v) * 0.7071067811865476
    t = 1.0 / (1.0 + 0.3275911 * x)
    bell = jnp.exp(-x * x)
    poly = ((((1.061405429 * t - 1.453152027) * t + 1.421413741) * t - 0.284496736) * t + 0.254829592) * t
    below = 0.5 * poly * bell
    share = jnp.where(v < 0.0, below, 1.0 - below)
    return v * share, share + v * bell * 0.3989422804014327


def expert_kernel(count, slots, per, x_ref, g_ref, router_ref, *refs):
    w1_hbm, w2_hbm = refs[: 2 * count], refs[2 * count : 3 * count]
    back_ref, act_ref, hg_ref, rg_ref, dx_ref, w1, w2, sems = refs[3 * count :]
    rows, width = x_ref[...], x_ref.shape[1]
    half = width // 2
    copies = []
    for t in range(count):
        copies.append(
            [
                pltpu.make_async_copy(w1_hbm[2 * t], w1.at[t, pl.ds(0, half)], sems.at[3 * t]),
                pltpu.make_async_copy(w1_hbm[2 * t + 1], w1.at[t, pl.ds(half, half)], sems.at[3 * t + 1]),
                pltpu.make_async_copy(w2_hbm[t], w2.at[t], sems.at[3 * t + 2]),
            ]
        )

    @pl.when(pl.program_id(0) == 0)
    def _():
        for group in copies:
            for item in group:
                item.start()

    lane = iota(1, LANES, 1)
    signal = g_ref[:, 0].reshape(rows.shape[0], width + LANES)
    side = signal[:, width:].astype(F32)

    def column(*lanes):
        keep = lane == lanes[0]
        for other in lanes[1:]:
            keep = keep | (lane == other)
        return jnp.sum(jnp.where(keep, side, 0.0), -1, keepdims=True)

    logits = dot(rows, router_ref[...])
    lane_f = lane.astype(F32)
    mine = jnp.sum(jnp.where(lane_f == column(4), logits, 0.0), -1, keepdims=True)
    other = jnp.sum(jnp.where(lane_f == column(0), logits, 0.0), -1, keepdims=True)
    gate = 1.0 / (1.0 + jnp.exp(other - mine - column(1, 2, 3)))
    upstream = signal[:, 0:width].astype(F32)
    rows_grad = (gate * upstream).astype(BF)
    rg_ref[...] = rows_grad
    hidden_here = w1.shape[2]
    step = min(512, hidden_here)

    def wait(groups):
        @pl.when(pl.program_id(0) == 0)
        def _():
            for group in groups:
                for item in group:
                    item.wait()

    def first_products(t):
        parts = []
        for at in range(0, hidden_here, step):
            cols = slice(at, at + step)
            parts.append((at, dot(rows, w1[t, :, cols]), dot(rows_grad, w2[t, cols, :], 1, 1)))
        return parts

    wait(copies[:1])
    ready = first_products(0)
    wait(copies[1:])
    out = None
    grad = None
    for t in range(count):
        parts = ready
        if t + 1 < count:
            ready = first_products(t + 1)
        for at, hidden, active_grad in parts:
            place = slice(t * hidden_here + at, t * hidden_here + at + step)
            active, slope = gelu_parts(hidden)
            act_ref[:, place] = active.astype(BF)
            hg_ref[:, place] = (active_grad * slope).astype(BF)
        place = slice(t * hidden_here, (t + 1) * hidden_here)
        part = dot(act_ref[:, place], w2[t])
        out = part if out is None else out + part
        part = dot(hg_ref[:, place], w1[t], 1, 1)
        grad = part if grad is None else grad + part
    dx_ref[...] = grad.astype(BF)
    back_ref[...] = (gate * out).astype(BF)
    gate_grad = jnp.sum(upstream * out.astype(BF).astype(F32), -1, keepdims=True)
    lanes = up_to(slots, LANES)
    spread = iota(slots, lanes, 0) == iota(slots, lanes, 1)
    spare_row = iota(16, 1, 0) == per + 16 - slots
    for b in range(x_ref.shape[0] // slots):
        end = (b + 1) * slots
        line = jnp.sum(jnp.where(spread, gate_grad[end - slots : end], 0.0), 0, keepdims=True)
        high = line.astype(BF).astype(F32)
        line = jnp.concatenate([high, line - high, jnp.zeros((1, width - 2 * lanes), F32)], 1)
        dx_ref[end - 16 : end, :] = jnp.where(spare_row, line, grad[end - 16 : end]).astype(BF)


def expert(x, g, chunk, router, w1, w2, slots, per):
    rows, width = x.shape
    count = len(w2)
    here = w2[0].shape[0]
    total = count * here
    blocks = block_count(rows // slots, slots)
    tile = slots * blocks

    def tiled(cols):
        return pl.BlockSpec((tile, cols), lambda i: (i, 0))

    flops = 8 * rows * width * total
    return pl.pallas_call(
        functools.partial(expert_kernel, count, slots, per),
        grid=(rows // tile,),
        in_specs=[
            tiled(width),
            pl.BlockSpec((blocks, 1, slots, g.shape[3]), lambda i: (i, chunk, 0, 0)),
            whole(router.shape),
        ]
        + [pl.BlockSpec(memory_space=pl.ANY)] * (3 * count),
        out_specs=[tiled(width), tiled(total), tiled(total), tiled(width), tiled(width)],
        out_shape=[
            jax.ShapeDtypeStruct((rows, width), BF),
            jax.ShapeDtypeStruct((rows, total), BF),
            jax.ShapeDtypeStruct((rows, total), BF),
            jax.ShapeDtypeStruct((rows, width), BF),
            jax.ShapeDtypeStruct((rows, width), BF),
        ],
        scratch_shapes=[
            pltpu.VMEM((count, width, here), BF),
            pltpu.VMEM((count, here, width), BF),
            pltpu.SemaphoreType.DMA((3 * count,)),
        ],
        compiler_params=params(),
        cost_estimate=pl.CostEstimate(flops=flops, bytes_accessed=rows * total * 6, transcendentals=rows * total * 2),
        name="expert",
    )(x, g, router, *w1, *w2)


def weight_kernel(count, steps, *refs):
    ins, outs = refs[: 2 * count], refs[2 * count :]
    total = None
    for n in range(count):
        part = dot(ins[2 * n][...], ins[2 * n + 1][...], 0, 0)
        total = part if total is None else total + part
    store_piece(outs, steps, total.astype(BF))


def weight_grad(columns, rows, first, here):
    count = len(columns)
    width = rows[0].shape[1]
    step = min(512, here)
    steps = here // step
    offset = first * steps
    specs, args = [], []
    for a, b in zip(columns, rows):
        specs += [pl.BlockSpec((a.shape[0], step), lambda i: (0, i + offset)), whole(b.shape, True)]
        args += [a, b]
    out_specs, out_shape = by_piece(2, steps, (step, width), (here, width), BF)
    return pl.pallas_call(
        functools.partial(weight_kernel, count, steps),
        grid=(2 * steps,),
        in_specs=specs,
        out_specs=out_specs,
        out_shape=out_shape,
        compiler_params=params(),
        cost_estimate=cost(4 * sum(b.shape[0] for b in rows) * width * here, 8 * here * width),
        name="weight_grad",
    )(*args)


def shards(
    block_in,
    norm_one,
    head_in,
    head_out,
    norm_two,
    router,
    expert_in,
    expert_out,
    expert_ids,
    route_noise,
    cotangent,
):
    rows_here, width = block_in.shape
    parts = lax.axis_size("tensor")
    groups = lax.axis_size("expert")
    me = lax.axis_index("tensor")
    images = rows_here // SEQ
    height = up_to(SEQ, 16)
    each = up_to(-(-rows_here // parts), 16)
    experts = router.shape[1]
    capacity = (rows_here * 2 * 8 // (5 * experts) + 15) // 16 * 16
    share = -(-capacity // parts)
    per = -(-share // CHUNKS)
    slots = up_to(per + 1, 16)
    chunk_rows = experts * slots
    full = rows_here // 16 * 16
    here = expert_out.shape[1]

    paired = parts == 4
    order = (0, 2, 1, 3) if paired else tuple(range(parts))
    part_of = jnp.stack([me ^ k if paired else jnp.int32(k) for k in order]).astype(jnp.int32)
    starts = part_of * each
    own_block = (me * (each // half_tile(each)))[None].astype(jnp.int32)

    def cross(x, k):
        return lax.ppermute(x, "tensor", [(n, n ^ k) for n in range(parts)])

    def far_part(x):
        return cross(x, 2) if paired else x

    def gathered_from(x, far):
        if not paired:
            every = lax.all_gather(x, "tensor", axis=0, tiled=False)
            return [every[p] for p in range(parts)]
        return [x, far, cross(x, 1), cross(far, 1)]

    def gathered(x):
        return gathered_from(x, far_part(x))

    def near_hop(pieces):
        return pinned(*[cross(piece, 1) for piece in pieces[2:]]) if paired else pieces

    def near_sum(pieces, came):
        if not paired:
            return lax.psum_scatter(jnp.stack(pieces), "tensor", scatter_dimension=0), None
        kept, other = ((a.astype(F32) + b.astype(F32)).astype(BF) for a, b in zip(pieces, came))
        return kept, other

    def far_hop(kept, other):
        return cross(other, 2) if paired else jnp.zeros_like(kept)

    def scattered(pieces):
        kept, other = near_sum(pieces, near_hop(pieces))
        return kept, far_hop(kept, other)

    def swapped(pieces):
        if not paired:
            every = lax.all_to_all(jnp.stack(pieces), "tensor", split_axis=0, concat_axis=0, tiled=True)
            return [every[p] for p in range(parts)]
        return [cross(piece, k) if k else piece for piece, k in zip(pieces, order)]

    def over_experts(x):
        return lax.all_to_all(x, "expert", split_axis=0, concat_axis=0, tiled=True)

    def pinned(*items):
        return lax.optimization_barrier(items)

    def tail_of(x):
        return jnp.pad(x[full:], ((0, 16 - (rows_here - full)), (0, 0)))

    names = jnp.arange(experts, dtype=jnp.int32)
    member = [(expert_ids[:, c : c + 1] == names).astype(jnp.int32) for c in range(2)]
    both = member[0] + member[1]
    earlier = jnp.cumsum(both, 0) - both
    slot = jnp.stack([jnp.sum(earlier * item, -1) for item in member], 1)
    local = slot - me * share
    place = local // per * chunk_rows + expert_ids * slots + local % per
    place = jnp.where((local >= 0) & (local < share), place, -1)
    place = jnp.pad(place, ((0, each * parts - rows_here), (0, 0)), constant_values=-1)
    place_lanes = place.T
    place_parts = jnp.swapaxes(place_lanes.reshape(2, parts, each), 0, 1)

    sides = []
    for c in range(2):
        gap = route_noise[:, c] - route_noise[:, 1 - c]
        high = gap.astype(BF)
        left = gap - high.astype(F32)
        mid = left.astype(BF)
        low = (left - mid.astype(F32)).astype(BF)
        columns = [expert_ids[:, 1 - c].astype(BF), high, mid, low, expert_ids[:, c].astype(BF)]
        sides.append(jnp.stack(columns, 1))
    side = jnp.pad(jnp.stack(sides), ((0, 0), (0, each * parts - rows_here), (0, LANES - 5)))

    router_wide = jnp.pad(router, ((0, 0), (0, LANES - experts)))
    gain_one, gain_two = norm_one[None, :], norm_two[None, :]
    head_out_far = far_part(head_out)
    w1_own = [expert_in[0, : width // 2], expert_in[0, width // 2 :]]
    w1_far = [far_part(item) for item in w1_own]

    packed = pack_first(cotangent, tail_of(cotangent), place_lanes, side, experts, slots)
    block_rows, packed, w1_far[0] = pinned(block_in, packed, w1_far[0])
    signal = over_experts(packed)

    first_in, qkv, logs, *mixed = attend(
        starts, block_rows, tail_of(block_in), gain_one, head_in, images, height, each, parts
    )
    *mixed, w1_far[1], head_out_far = pinned(*mixed, w1_far[1], head_out_far)
    head_out_all = gathered_from(head_out, head_out_far)
    mixed = swapped(mixed)
    middle, second_in, gates = middle_of(
        own_block, mixed, head_out_all, block_in, gain_two, router_wide, expert_ids, route_noise
    )
    *second_all, signal, late_out = pinned(*gathered(second_in), signal, expert_out[0])
    w1 = [gathered_from(a, b) for a, b in zip(w1_own, w1_far)]
    w1 = [w1[h][p] for p in range(parts) for h in range(2)]

    def packed_rows(n):
        return pack(part_of, second_all, place_parts, experts, slots, n * chunk_rows)

    def sent(x):
        return over_experts(x.reshape(experts, slots, width)).reshape(chunk_rows, width)

    x = sent(packed_rows(0))
    w2_far, *outgoing = pinned(far_part(late_out), *[packed_rows(n) for n in range(1, CHUNKS)])
    w2 = gathered_from(expert_out[0], w2_far)
    backs, actives, hidden_grads, rows_grads, arrived, returned = [], [], [], [], [], []
    for n in range(CHUNKS):
        coming = None
        if n + 1 < CHUNKS:
            x, ready = pinned(x, outgoing[n])
            coming = sent(ready)
        if n == 0:
            x, *ready = pinned(x, *w1, *w2)
            w1, w2 = ready[: 2 * parts], ready[2 * parts :]
        back, active, hidden_grad, rows_grad, row_grad = expert(
            x, signal, n, router_wide, w1, w2, slots, per
        )
        if returned:
            row_grad, active, returned[-1] = pinned(row_grad, active, returned[-1])
        arrived.append(x)
        actives.append(active)
        hidden_grads.append(hidden_grad)
        rows_grads.append(rows_grad)
        backs.append(back)
        if coming is not None:
            x, row_grad = pinned(coming, row_grad)
        returned.append(sent(row_grad))

    def weight_parts(columns, rows):
        pairs = [weight_grad(columns, rows, p, here) for p in range(parts - 2, -1, -2)]
        return [item for pair in pairs[::-1] for item in pair]

    out_parts = weight_parts(actives, rows_grads)
    out_kept, out_other = near_sum(out_parts, near_hop(out_parts))
    out_far = far_hop(out_kept, out_other)
    *returned, out_kept = pinned(*returned, out_kept)

    second_pieces = unpack(part_of, place, returned, slots, per, each, True)
    second_kept, second_other = near_sum(second_pieces, near_hop(second_pieces))
    second_kept, out_far, *hidden_grads = pinned(second_kept, out_far, *hidden_grads)
    second_far = far_hop(second_kept, second_other)
    in_parts = weight_parts(hidden_grads, arrived)
    in_came = near_hop(in_parts)
    second_far, *in_parts = pinned(second_far, *in_parts)
    combined = [sent(item) for item in backs]
    middle_grad, router_part, norm_two_part, *pieces = middle_back(
        own_block, second_kept, second_far, middle, second_in, gates, expert_ids, cotangent, mixed, head_out_all,
        gain_two, router_wide,
    )
    head_out_parts, mixed_grad = pieces[:parts], pieces[parts:]
    *mixed_grad, combined[0] = pinned(*mixed_grad, combined[0])
    *mixed_grad, in_came = pinned(*swapped(mixed_grad), in_came)
    in_kept, in_other = near_sum(in_parts, in_came)
    in_far = far_hop(in_kept, in_other)
    head_out_kept, head_out_far = scattered(head_out_parts)
    *pieces, head_in_part, norm_one_part = attend_back(
        starts, mixed_grad, qkv, logs, first_in, jnp.swapaxes(head_in, 1, 2), gain_one
    )
    *pieces, combined[-1], in_far, head_out_far = pinned(*pieces, combined[-1], in_far, head_out_far)
    first_kept, first_far = scattered(pieces)
    block_pieces = unpack(part_of, place, combined, slots, per, each, False)
    block_kept, block_other = near_sum(block_pieces, near_hop(block_pieces))
    first_far, block_kept = pinned(first_far, block_kept)
    block_far = far_hop(block_kept, block_other)
    input_part = input_back(own_block, first_kept, first_far, block_in, middle_grad, gain_one)
    out_grad = out_kept.astype(F32) + out_far.astype(F32)
    in_grad = sum_turned(in_kept, in_far)
    input_far, out_grad, in_grad = pinned(far_part(input_part), out_grad, in_grad)
    block_own = (middle + block_kept.astype(F32) + block_far.astype(F32)).astype(BF)

    cols = head_in.shape[2]
    head_out_part = (head_out_kept.astype(F32) + head_out_far.astype(F32)).astype(BF)
    small = jnp.concatenate([norm_one_part, norm_two_part, router_part[:experts]], 0).astype(BF)
    count = 4 * cols + 2 + experts
    total = up_to(count, 16 * groups)
    heads = jnp.concatenate(
        [head_in_part.reshape(3 * cols, width), head_out_part, jnp.pad(small, ((0, total - count), (0, 0)))], 0
    )
    heads = over_experts(heads.reshape(groups, total // groups, width))
    heads, block_own = pinned(heads, block_own)
    input_grad = assemble(part_of, gathered_from(input_part, input_far), rows_here, F32)
    block_out = assemble(part_of, gathered(block_own), rows_here, BF)
    heads = jnp.sum(heads.astype(F32), 0).astype(BF)
    heads = lax.all_gather(heads, "expert", axis=0, tiled=True)
    head_in_grad = jnp.swapaxes(heads[: 3 * cols].reshape(3, cols, width), 1, 2).astype(F32)
    head_out_grad = heads[3 * cols : 4 * cols].astype(F32)
    small = heads[4 * cols : count].astype(F32)
    if paired:
        small = small + cross(small, 1)
        small = small + cross(small, 2)
    else:
        small = lax.psum(small, "tensor")
    return (
        block_out,
        input_grad,
        small[0],
        head_in_grad,
        head_out_grad,
        small[1],
        small[2:].T,
        in_grad[None],
        out_grad[None],
    )


def solution(mesh):
    in_specs = (
        P("expert", None),
        P(),
        P(None, None, "tensor"),
        P("tensor", None),
        P(),
        P(),
        P("expert", None, "tensor"),
        P("expert", "tensor", None),
        P("expert", None),
        P("expert", None),
        P("expert", None),
    )
    out_specs = (
        P("expert", None),
        P("expert", None),
        P(),
        P(None, None, "tensor"),
        P("tensor", None),
        P(),
        P(),
        P("expert", None, "tensor"),
        P("expert", "tensor", None),
    )
    return jax.shard_map(shards, mesh=mesh, in_specs=in_specs, out_specs=out_specs, check_vma=False)
```

```python
import functools

import jax
import jax.numpy as jnp
from jax import lax
from jax.experimental import pallas as pl
from jax.experimental.pallas import tpu as pltpu
from jax.sharding import PartitionSpec as P

HD = 64
SEQ = 197
LANES = 128
EPSILON = 1e-06
CHUNKS = 2
BF = jnp.bfloat16
F32 = jnp.float32


def up_to(value, unit):
    return -(-value // unit) * unit


def params(mib=60):
    return pltpu.CompilerParams(vmem_limit_bytes=mib * 1024 * 1024)


def dot(a, b, da=1, db=0):
    return lax.dot_general(a, b, (((da,), (db,)), ((), ())), preferred_element_type=F32)


def iota(rows, cols, dim):
    return lax.broadcasted_iota(jnp.int32, (rows, cols), dim)


def flag(mask):
    return jnp.where(mask, 1.0, 0.0)


def whole(shape, once=False):
    zeros = (0,) * len(shape)
    mode = pl.Buffered(1) if once else None
    return pl.BlockSpec(shape, lambda *_: zeros, pipeline_mode=mode)


def image(*shape):
    return pl.BlockSpec((1,) + shape, lambda i, *_: (i,) + (0,) * len(shape))


def fill(x_ref, tail_ref, rows_ref):
    full = x_ref.shape[0] // 16 * 16
    rows_ref[0:full, :] = x_ref[0:full, :]
    rows_ref[full : full + 16, :] = tail_ref[...]
    rest = rows_ref.shape[0] - full - 16
    if rest:
        rows_ref[full + 16 :, :] = jnp.zeros((rest, rows_ref.shape[1]), BF)


def norm_parts(field):
    centre = field - jnp.mean(field, -1, keepdims=True)
    spread = lax.rsqrt(jnp.mean(centre * centre, -1, keepdims=True) + EPSILON)
    return centre * spread, spread


def norm_field_back(upstream, gain, scaled, spread):
    weighted = upstream * gain
    return spread * (
        weighted
        - jnp.mean(weighted, -1, keepdims=True)
        - scaled * jnp.mean(weighted * scaled, -1, keepdims=True)
    )


def cost(flops, size):
    return pl.CostEstimate(flops=flops, bytes_accessed=size, transcendentals=0)


def by_piece(count, steps, block, shape, dtype):
    def spec(p):
        def place(i, *_):
            return (jnp.clip(i - p * steps, 0, steps - 1), 0)

        return pl.BlockSpec(block, place)

    return [spec(p) for p in range(count)], [jax.ShapeDtypeStruct(shape, dtype)] * count


def store_piece(refs, steps, value):
    for p, ref in enumerate(refs):

        @pl.when(pl.program_id(0) // steps == p)
        def _():
            ref[...] = value


def rows_spec(tile, width):
    return pl.BlockSpec((tile, width), lambda i, *_: (i, 0))


def own_spec(tile, width):
    return pl.BlockSpec((tile, width), lambda i, at: (at[0] + i, 0))


def window_of(i, height, back=False):
    start = i * SEQ
    aligned = start // 16 * 16
    window = height + 16
    shape = (window, height) if back else (height, window)
    r, c = iota(*shape, 1 if back else 0), iota(*shape, 0 if back else 1)
    match = flag((c == r + (start - aligned)) & (r < SEQ)).astype(BF)
    return match, pl.ds(pl.multiple_of(aligned, 16), window)


def head_masks():
    lane = iota(1, LANES, 1)
    return [(flag(lane // HD == h)).astype(BF) for h in range(2)]


def attend_kernel(count, starts_ref, x_ref, tail_ref, gain_ref, w_ref, first_ref, qkv_ref, log_ref, *refs):
    piece_refs, rows, mixed = refs[:count], refs[count], refs[count + 1]
    i = pl.program_id(0)
    height = first_ref.shape[1]
    cols = mixed.shape[1]

    @pl.when(i == 0)
    def _():
        fill(x_ref, tail_ref, rows)
        mixed[...] = jnp.zeros_like(mixed)

    match, place = window_of(i, height)
    field = dot(match, rows[place, :])
    scaled, _ = norm_parts(field)
    first = (scaled * gain_ref[...]).astype(BF)
    first_ref[0] = first
    for k in range(3):
        qkv_ref[k, 0] = dot(first, w_ref[k]).astype(BF)
    masks = head_masks()
    lane = iota(1, LANES, 1)
    key_lane = iota(1, height, 1)
    logs = jnp.zeros((height, LANES), F32)
    back, _ = window_of(i, height, True)
    for pair in range(cols // LANES):
        part = slice(pair * LANES, (pair + 1) * LANES)
        queries, keys, values = (qkv_ref[k, 0, :, part] for k in range(3))
        total = jnp.zeros((height, LANES), F32)
        for h in range(2):
            scores = dot(queries * masks[h], keys, 1, 1) * HD ** (-0.5)
            scores = jnp.where(key_lane < SEQ, scores, -1e30)
            highest = jnp.max(scores, -1, keepdims=True)
            weights = jnp.exp(scores - highest)
            sums = jnp.sum(weights, -1, keepdims=True)
            probs = (weights * (1.0 / sums)).astype(BF)
            total += dot(probs, values * masks[h])
            logs = jnp.where(lane == pair * 2 + h, highest + jnp.log(sums), logs)
        mixed[place, part] = (mixed[place, part].astype(F32) + dot(back, total.astype(BF))).astype(BF)
    log_ref[0] = logs

    @pl.when(i == pl.num_programs(0) - 1)
    def _():
        for p in range(count):
            at = pl.multiple_of(starts_ref[p], 16)
            piece_refs[p][...] = mixed[pl.ds(at, piece_refs[p].shape[0]), :]


def attend(starts, block_in, tail, gain, head_in, images, height, each, count):
    rows, width = block_in.shape
    cols = head_in.shape[2]
    scratch_rows = max(rows // 16 * 16 + 48, each * count)
    spec = pltpu.PrefetchScalarGridSpec(
        num_scalar_prefetch=1,
        grid=(images,),
        in_specs=[whole((rows, width), True), whole((16, width)), whole((1, width)), whole(head_in.shape, True)],
        out_specs=[
            image(height, width),
            pl.BlockSpec((3, 1, height, cols), lambda i, *_: (0, i, 0, 0)),
            image(height, LANES),
        ]
        + [whole((each, cols))] * count,
        scratch_shapes=[pltpu.VMEM((scratch_rows, width), BF), pltpu.VMEM((scratch_rows, cols), BF)],
    )
    return pl.pallas_call(
        functools.partial(attend_kernel, count),
        grid_spec=spec,
        out_shape=[
            jax.ShapeDtypeStruct((images, height, width), BF),
            jax.ShapeDtypeStruct((3, images, height, cols), BF),
            jax.ShapeDtypeStruct((images, height, LANES), F32),
        ]
        + [jax.ShapeDtypeStruct((each, cols), BF)] * count,
        compiler_params=params(),
        cost_estimate=cost(16 * images * height * width * cols, 16 * rows * width),
        name="attend",
    )(starts, block_in, tail, gain, head_in)


def attend_back_kernel(count, starts_ref, qkv_ref, log_ref, first_ref, wt_ref, gain_ref, *refs):
    dmix_refs, piece_refs = refs[:count], refs[count : 2 * count]
    hg_ref, ng_ref, acc, grads, dmix, field = refs[2 * count :]
    i = pl.program_id(0)
    height = first_ref.shape[1]
    each = dmix_refs[0].shape[0]

    @pl.when(i == 0)
    def _():
        acc[...] = jnp.zeros_like(acc)
        field[...] = jnp.zeros_like(field)
        rest = dmix.shape[0] - each * count
        if rest:
            dmix[each * count :, :] = jnp.zeros((rest, dmix.shape[1]), BF)
        for p in range(count):
            dmix[pl.ds(pl.multiple_of(starts_ref[p], 16), each), :] = dmix_refs[p][...]

    match, place = window_of(i, height)
    back, _ = window_of(i, height, True)
    out_grads = dot(match, dmix[place, :]).astype(BF)
    masks = head_masks()
    lane = iota(1, LANES, 1)
    key_lane = iota(1, height, 1)
    scale = HD ** (-0.5)
    logs = log_ref[0]
    for pair in range(dmix.shape[1] // LANES):
        cols = slice(pair * LANES, (pair + 1) * LANES)
        queries, keys, values = (qkv_ref[k, 0, :, cols] for k in range(3))
        out_grad = out_grads[:, cols]
        dq = jnp.zeros((height, LANES), F32)
        dk = jnp.zeros((height, LANES), F32)
        dv = jnp.zeros((height, LANES), F32)
        for h in range(2):
            q_h = queries * masks[h]
            o_h = out_grad * masks[h]
            log_h = jnp.sum(jnp.where(lane == pair * 2 + h, logs, 0.0), -1, keepdims=True)
            probs = jnp.exp(dot(q_h, keys, 1, 1) * scale - log_h)
            probs = jnp.where(key_lane < SEQ, probs, 0.0)
            prob_grad = dot(o_h, values, 1, 1)
            dv += dot(probs.astype(BF), o_h, 0, 0)
            delta = jnp.sum(probs * prob_grad, -1, keepdims=True)
            score_grad = (probs * (prob_grad - delta)).astype(BF)
            dq += dot(score_grad, keys * masks[h])
            dk += dot(score_grad, q_h, 0, 0)
        grads[0, :, cols] = (dq * scale).astype(BF)
        grads[1, :, cols] = (dk * scale).astype(BF)
        grads[2, :, cols] = dv.astype(BF)

    first = first_ref[0]
    total = None
    for k in range(3):
        part = dot(grads[k], wt_ref[k])
        total = part if total is None else total + part
        acc[k] += dot(grads[k], first, 0, 0)
    field[place, :] = (field[place, :].astype(F32) + dot(back, total.astype(BF))).astype(BF)

    @pl.when(i == pl.num_programs(0) - 1)
    def _():
        for p in range(count):
            piece_refs[p][...] = field[pl.ds(pl.multiple_of(starts_ref[p], 16), each), :]
        hg_ref[...] = acc[...].astype(BF)
        gain_grad = jnp.zeros_like(ng_ref)
        for k in range(3):
            gain_grad += jnp.sum(acc[k] * wt_ref[k].astype(F32), 0, keepdims=True)
        ng_ref[...] = gain_grad / gain_ref[...]


def attend_back(starts, dmix, qkv, logs, first, head_in_t, gain):
    images, height, width = first.shape
    each, cols = dmix[0].shape
    count = len(dmix)
    scratch_rows = max(images * SEQ // 16 * 16 + 48, each * count)
    spec = pltpu.PrefetchScalarGridSpec(
        num_scalar_prefetch=1,
        grid=(images,),
        in_specs=[
            pl.BlockSpec((3, 1, height, cols), lambda i, *_: (0, i, 0, 0)),
            image(height, LANES),
            image(height, width),
            whole(head_in_t.shape, True),
            whole((1, width)),
        ]
        + [whole((each, cols), True)] * count,
        out_specs=[whole((each, width))] * count + [whole(head_in_t.shape), whole((1, width))],
        scratch_shapes=[
            pltpu.VMEM(head_in_t.shape, F32),
            pltpu.VMEM((3, height, cols), BF),
            pltpu.VMEM((scratch_rows, cols), BF),
            pltpu.VMEM((scratch_rows, width), BF),
        ],
    )
    return pl.pallas_call(
        functools.partial(attend_back_kernel, count),
        grid_spec=spec,
        out_shape=[jax.ShapeDtypeStruct((each, width), BF)] * count
        + [jax.ShapeDtypeStruct(head_in_t.shape, BF), jax.ShapeDtypeStruct((1, width), F32)],
        compiler_params=params(),
        cost_estimate=cost(24 * images * height * width * cols, 20 * images * height * width),
        name="attend_back",
    )(starts, qkv, logs, first, head_in_t, gain, *dmix)


def block_count(blocks, slots):
    return max(n for n in range(1, blocks + 1) if blocks % n == 0 and n * slots <= 448)


def pack_first_kernel(x_ref, tail_ref, lp_ref, side_ref, out_ref, rows):
    i, n = pl.program_id(0), pl.program_id(1)

    @pl.when((i == 0) & (n == 0))
    def _():
        fill(x_ref, tail_ref, rows)

    blocks, _, slots, _ = out_ref.shape
    tile = blocks * slots
    j = (n * pl.num_programs(0) + i) * tile + iota(tile, rows.shape[0], 0)
    picks = [flag(lp_ref[c : c + 1, :] == j) for c in range(2)]
    width = x_ref.shape[1]
    main = dot((picks[0] + picks[1]).astype(BF), rows[...]).astype(BF)
    out_ref[:, 0, :, 0:width] = main.reshape(blocks, slots, width)
    extra = dot(picks[0].astype(BF), side_ref[0]) + dot(picks[1].astype(BF), side_ref[1])
    out_ref[:, 0, :, width:] = extra.astype(BF).reshape(blocks, slots, LANES)


def pack_first(x, tail, lp, side, experts, slots):
    rows, width = x.shape
    padded = lp.shape[1]
    blocks = block_count(experts, slots)
    return pl.pallas_call(
        pack_first_kernel,
        grid=(experts // blocks, CHUNKS),
        in_specs=[whole((rows, width), True), whole((16, width)), whole(lp.shape), whole(side.shape)],
        out_specs=pl.BlockSpec((blocks, 1, slots, width + LANES), lambda i, n: (i, n, 0, 0)),
        out_shape=jax.ShapeDtypeStruct((experts, CHUNKS, slots, width + LANES), BF),
        scratch_shapes=[pltpu.VMEM((padded, width), BF)],
        compiler_params=params(),
        cost_estimate=cost(3 * CHUNKS * experts * slots * padded * width, 2 * rows * width),
        name="pack_cotangent",
    )(x, tail, lp, side)


def pack_kernel(base, count, part_ref, *refs):
    lp_ref, out_ref = refs[count], refs[count + 1]
    total = None
    tile = out_ref.shape[0]
    for p in range(count):
        j = base + pl.program_id(0) * tile + iota(tile, refs[p].shape[0], 0)
        lp = lp_ref[part_ref[p]]
        picks = flag((lp[0:1, :] == j) | (lp[1:2, :] == j)).astype(BF)
        part = dot(picks, refs[p][...])
        total = part if total is None else total + part
    out_ref[...] = total.astype(BF)


def pack(part_of, pieces, lp, experts, slots, base):
    rows, width = pieces[0].shape
    count = len(pieces)
    tile = slots * block_count(experts, slots)
    spec = pltpu.PrefetchScalarGridSpec(
        num_scalar_prefetch=1,
        grid=(experts * slots // tile,),
        in_specs=[whole((rows, width), True)] * count + [whole(lp.shape)],
        out_specs=rows_spec(tile, width),
    )
    return pl.pallas_call(
        functools.partial(pack_kernel, base, count),
        grid_spec=spec,
        out_shape=jax.ShapeDtypeStruct((experts * slots, width), BF),
        compiler_params=params(),
        cost_estimate=cost(3 * experts * slots * rows * count * width, 2 * rows * count * width),
        name="pack_rows",
    )(part_of, *pieces, lp)


def unpack_kernel(count, slots, per, graded, part_ref, lp_ref, *refs):
    row_refs, out_refs = refs[:count], refs[count:]
    lp = lp_ref[...]
    height = lp.shape[0]
    rows, width = row_refs[0].shape
    total = jnp.zeros((height, width), F32)
    lanes = up_to(slots, LANES)
    extra = [jnp.zeros((height, lanes), F32) for _ in range(2)]
    for n in range(count):
        j = n * rows + iota(1, rows, 1)
        hits = (lp[:, 0:1] == j) | (lp[:, 1:2] == j)
        total += dot(flag(hits).astype(BF), row_refs[n][...])
        if graded:
            j = iota(1, lanes, 1)
            for e in range(rows // slots):
                spare = row_refs[n][(e + 1) * slots - 16 : (e + 1) * slots, 0 : 2 * lanes].astype(F32)
                spare = spare[per + 16 - slots : per + 17 - slots, :]
                values = spare[:, :lanes] + spare[:, lanes:]
                for c in range(2):
                    hit = lp[:, c : c + 1] - (n * rows + e * slots) == j
                    extra[c] += jnp.where(hit, values, 0.0)
    value = total.astype(BF)
    if graded:
        lane = iota(1, LANES, 1)
        tail = jnp.zeros((height, LANES), F32)
        for c in range(2):
            grad = jnp.sum(extra[c], -1, keepdims=True)
            high = grad.astype(BF).astype(F32)
            tail = jnp.where(lane == c, high, tail)
            tail = jnp.where(lane == 2 + c, grad - high, tail)
        value = jnp.concatenate([value, tail.astype(BF)], 1)
    store_piece(out_refs, 1, value)


def unpack(part_of, lp, rows, slots, per, each, graded):
    parts = lp.shape[0] // each
    count = len(rows)
    width = rows[0].shape[1] + (LANES if graded else 0)
    out_specs, out_shape = by_piece(parts, 1, (each, width), (each, width), BF)
    spec = pltpu.PrefetchScalarGridSpec(
        num_scalar_prefetch=1,
        grid=(parts,),
        in_specs=[pl.BlockSpec((each, 2), lambda i, at: (at[i], 0))] + [whole(item.shape, True) for item in rows],
        out_specs=out_specs,
    )
    return pl.pallas_call(
        functools.partial(unpack_kernel, count, slots, per, graded),
        grid_spec=spec,
        out_shape=out_shape,
        compiler_params=params(),
        cost_estimate=cost(3 * lp.shape[0] * count * rows[0].size, 4 * count * rows[0].size),
        name="unpack_rows",
    )(part_of, lp, *rows)


def assemble_kernel(count, steps, part_ref, *refs):
    out_ref = refs[count]
    for p in range(count):

        @pl.when(pl.program_id(0) // steps == p)
        def _():
            out_ref[...] = refs[p][...].astype(out_ref.dtype)


def assemble(part_of, pieces, rows, dtype):
    each, width = pieces[0].shape
    count = len(pieces)
    tile, steps = each, 1
    in_specs, _ = by_piece(count, steps, (tile, width), (each, width), BF)
    spec = pltpu.PrefetchScalarGridSpec(
        num_scalar_prefetch=1,
        grid=(count * steps,),
        in_specs=in_specs,
        out_specs=pl.BlockSpec((tile, width), lambda i, at: (at[i // steps] * steps + i % steps, 0)),
    )
    return pl.pallas_call(
        functools.partial(assemble_kernel, count, steps),
        grid_spec=spec,
        out_shape=jax.ShapeDtypeStruct((rows, width), dtype),
        compiler_params=params(),
        cost_estimate=cost(2 * rows * width, 8 * rows * width),
        name="assemble",
    )(part_of, *pieces)


def sum_turned_kernel(a_ref, b_ref, out_ref):
    out_ref[...] = (a_ref[...].astype(F32) + b_ref[...].astype(F32)).T


def sum_turned(a, b):
    rows, width = a.shape
    tile = min(256, rows)
    return pl.pallas_call(
        sum_turned_kernel,
        grid=(rows // tile,),
        in_specs=[rows_spec(tile, width)] * 2,
        out_specs=pl.BlockSpec((width, tile), lambda i: (0, i)),
        out_shape=jax.ShapeDtypeStruct((width, rows), F32),
        compiler_params=params(),
        cost_estimate=cost(rows * width, 8 * rows * width),
        name="sum_turned",
    )(a, b)


def middle_kernel(count, limit, at_ref, *refs):
    mixed_refs, wo_refs = refs[:count], refs[count : 2 * count]
    x_ref, gain_ref, router_ref, ids_ref, noise_ref, mid_ref, second_ref, gates_ref = refs[2 * count :]
    tile = x_ref.shape[0]
    valid = (at_ref[0] + pl.program_id(0)) * tile + iota(tile, 1, 0) < limit
    middle = jnp.where(valid, x_ref[...].astype(F32), 0.0)
    for mixed_ref, wo_ref in zip(mixed_refs, wo_refs):
        middle += dot(mixed_ref[...], wo_ref[...])
    mid_ref[...] = middle
    scaled, _ = norm_parts(middle)
    second = (scaled * gain_ref[...]).astype(BF)
    second_ref[...] = second
    logits = dot(second, router_ref[...])
    lane = iota(1, LANES, 1)
    chosen = [
        jnp.sum(jnp.where(lane == ids_ref[:, c : c + 1], logits, 0.0), -1, keepdims=True)
        + noise_ref[:, c : c + 1]
        for c in range(2)
    ]
    top = jnp.maximum(chosen[0], chosen[1])
    raw = [jnp.exp(item - top) for item in chosen]
    inverse = 1.0 / (raw[0] + raw[1])
    gates = jnp.where(lane == 0, raw[0] * inverse, 0.0) + jnp.where(lane == 1, raw[1] * inverse, 0.0)
    gates_ref[...] = jnp.where(valid, gates, 0.0)


def half_tile(each):
    return each // 2 if each % 32 == 0 else each


def middle_of(at, mixed, head_out, x, gain, router, ids, noise):
    each, cols = mixed[0].shape
    parts = len(mixed)
    rows, width = x.shape
    tile = half_tile(each)
    spec = pltpu.PrefetchScalarGridSpec(
        num_scalar_prefetch=1,
        grid=(each // tile,),
        in_specs=[rows_spec(tile, cols)] * parts
        + [whole((cols, width), True)] * parts
        + [
            own_spec(tile, width),
            whole((1, width)),
            whole(router.shape),
            own_spec(tile, 2),
            own_spec(tile, 2),
        ],
        out_specs=[rows_spec(tile, width), rows_spec(tile, width), rows_spec(tile, LANES)],
    )
    return pl.pallas_call(
        functools.partial(middle_kernel, parts, rows),
        grid_spec=spec,
        out_shape=[
            jax.ShapeDtypeStruct((each, width), F32),
            jax.ShapeDtypeStruct((each, width), BF),
            jax.ShapeDtypeStruct((each, LANES), F32),
        ],
        compiler_params=params(),
        cost_estimate=cost(4 * each * width * width, 24 * each * width),
        name="middle",
    )(at, *mixed, *head_out, x, gain, router, ids, noise)


def of_tiles(refs):
    value = refs[0][...].astype(F32)
    for n, ref in enumerate(refs[1:]):
        value = jnp.where(pl.program_id(0) > n, ref[...].astype(F32), value)
    return value


def middle_back_kernel(count, limit, tiles, at_ref, *refs):
    far_refs, refs = refs[:tiles], refs[tiles:]
    keep_ref, mid_ref, second_ref, gates_ref, ids_ref, up_ref, gain_ref, router_ref = refs[:8]
    mixed_refs, wo_refs = refs[8 : 8 + count], refs[8 + count : 8 + 2 * count]
    mg_ref, rg_ref, ng_ref = refs[8 + 2 * count : 11 + 2 * count]
    hog_refs, dmix_refs, hog_acc = refs[11 + 2 * count : 11 + 3 * count], refs[11 + 3 * count : -1], refs[-1]
    i = pl.program_id(0)

    @pl.when(i == 0)
    def _():
        hog_acc[...] = jnp.zeros_like(hog_acc)
        rg_ref[...] = jnp.zeros_like(rg_ref)
        ng_ref[...] = jnp.zeros_like(ng_ref)

    tile, width = up_ref.shape
    valid = (at_ref[0] + i) * tile + iota(tile, 1, 0) < limit
    lane = iota(1, LANES, 1)
    both = keep_ref[...].astype(F32) + of_tiles(far_refs)
    tail = both[:, width:]
    gates = gates_ref[...]
    gate, grad = [], []
    for c in range(2):
        gate.append(jnp.sum(jnp.where(lane == c, gates, 0.0), -1, keepdims=True))
        grad.append(jnp.sum(jnp.where((lane == c) | (lane == 2 + c), tail, 0.0), -1, keepdims=True))
    mean_term = gate[0] * grad[0] + gate[1] * grad[1]
    logit_grad = jnp.zeros((tile, LANES), F32)
    for c in range(2):
        hit = (lane == ids_ref[:, c : c + 1]) & valid
        logit_grad = jnp.where(hit, gate[c] * (grad[c] - mean_term), logit_grad)
    logit_grad = logit_grad.astype(BF)
    second_grad = both[:, 0:width] + dot(logit_grad, router_ref[...], 1, 1)
    rg_ref[...] += dot(logit_grad, second_ref[...], 0, 0)
    scaled, spread = norm_parts(mid_ref[...])
    ng_ref[...] += jnp.sum(second_grad * scaled, 0, keepdims=True)
    upstream = jnp.where(valid, up_ref[...].astype(F32), 0.0)
    middle_grad = upstream + norm_field_back(second_grad, gain_ref[...], scaled, spread)
    mg_ref[...] = middle_grad
    rounded = middle_grad.astype(BF)
    for t in range(count):
        dmix_refs[t][...] = dot(rounded, wo_refs[t][...], 1, 1).astype(BF)
        hog_acc[t] += dot(mixed_refs[t][...], rounded, 0, 0)

    @pl.when(i == pl.num_programs(0) - 1)
    def _():
        for t in range(count):
            hog_refs[t][...] = hog_acc[t].astype(BF)


def middle_back(at, keep, far, middle, second, gates, ids, up, mixed, head_out, gain, router):
    each, cols = mixed[0].shape
    parts = len(mixed)
    rows, width = up.shape
    tile = half_tile(each)
    spec = pltpu.PrefetchScalarGridSpec(
        num_scalar_prefetch=1,
        grid=(each // tile,),
        in_specs=[whole((tile, keep.shape[1]))] * len(far)
        + [
            rows_spec(tile, keep.shape[1]),
            rows_spec(tile, width),
            rows_spec(tile, width),
            rows_spec(tile, LANES),
            own_spec(tile, 2),
            own_spec(tile, width),
            whole((1, width)),
            whole(router.shape),
        ]
        + [rows_spec(tile, cols)] * parts
        + [whole((cols, width), True)] * parts,
        out_specs=[rows_spec(tile, width), whole((LANES, width)), whole((1, width))]
        + [whole((cols, width))] * parts
        + [rows_spec(tile, cols)] * parts,
        scratch_shapes=[pltpu.VMEM((parts, cols, width), F32)],
    )
    return pl.pallas_call(
        functools.partial(middle_back_kernel, parts, rows, len(far)),
        grid_spec=spec,
        out_shape=[
            jax.ShapeDtypeStruct((each, width), F32),
            jax.ShapeDtypeStruct((LANES, width), F32),
            jax.ShapeDtypeStruct((1, width), F32),
        ]
        + [jax.ShapeDtypeStruct((cols, width), BF)] * parts
        + [jax.ShapeDtypeStruct((each, cols), BF)] * parts,
        compiler_params=params(),
        cost_estimate=cost(8 * each * width * width, 40 * each * width),
        name="middle_back",
    )(at, *far, keep, middle, second, gates, ids, up, gain, router, *mixed, *head_out)


def input_back_kernel(limit, tiles, at_ref, *refs):
    far_refs, (keep_ref, x_ref, mg_ref, gain_ref, out_ref) = refs[:tiles], refs[tiles:]
    tile = x_ref.shape[0]
    valid = (at_ref[0] + pl.program_id(0)) * tile + iota(tile, 1, 0) < limit
    scaled, spread = norm_parts(jnp.where(valid, x_ref[...].astype(F32), 0.0))
    first_grad = keep_ref[...].astype(F32) + of_tiles(far_refs)
    out_ref[...] = (mg_ref[...] + norm_field_back(first_grad, gain_ref[...], scaled, spread)).astype(BF)


def input_back(at, keep, far, x, middle_grad, gain):
    each, width = middle_grad.shape
    tile = half_tile(each)
    spec = pltpu.PrefetchScalarGridSpec(
        num_scalar_prefetch=1,
        grid=(each // tile,),
        in_specs=[whole((tile, width))] * len(far)
        + [rows_spec(tile, width), own_spec(tile, width), rows_spec(tile, width), whole((1, width))],
        out_specs=rows_spec(tile, width),
    )
    return pl.pallas_call(
        functools.partial(input_back_kernel, x.shape[0], len(far)),
        grid_spec=spec,
        out_shape=jax.ShapeDtypeStruct((each, width), BF),
        compiler_params=params(),
        cost_estimate=cost(20 * each * width, 16 * each * width),
        name="input_back",
    )(at, *far, keep, x, middle_grad, gain)


def gelu_parts(v):
    x = jnp.abs(v) * 0.7071067811865476
    t = 1.0 / (1.0 + 0.3275911 * x)
    bell = jnp.exp(-x * x)
    poly = ((((1.061405429 * t - 1.453152027) * t + 1.421413741) * t - 0.284496736) * t + 0.254829592) * t
    below = 0.5 * poly * bell
    share = jnp.where(v < 0.0, below, 1.0 - below)
    return v * share, share + v * bell * 0.3989422804014327


def expert_kernel(count, slots, per, x_ref, g_ref, router_ref, *refs):
    w1_hbm, w2_hbm = refs[: 2 * count], refs[2 * count : 3 * count]
    back_ref, act_ref, hg_ref, rg_ref, dx_ref, w1, w2, sems = refs[3 * count :]
    rows, width = x_ref[...], x_ref.shape[1]
    half = width // 2
    copies = []
    for t in range(count):
        copies.append(
            [
                pltpu.make_async_copy(w1_hbm[2 * t], w1.at[t, pl.ds(0, half)], sems.at[3 * t]),
                pltpu.make_async_copy(w1_hbm[2 * t + 1], w1.at[t, pl.ds(half, half)], sems.at[3 * t + 1]),
                pltpu.make_async_copy(w2_hbm[t], w2.at[t], sems.at[3 * t + 2]),
            ]
        )

    @pl.when(pl.program_id(0) == 0)
    def _():
        for group in copies:
            for item in group:
                item.start()

    lane = iota(1, LANES, 1)
    signal = g_ref[:, 0].reshape(rows.shape[0], width + LANES)
    side = signal[:, width:].astype(F32)

    def column(*lanes):
        keep = lane == lanes[0]
        for other in lanes[1:]:
            keep = keep | (lane == other)
        return jnp.sum(jnp.where(keep, side, 0.0), -1, keepdims=True)

    logits = dot(rows, router_ref[...])
    lane_f = lane.astype(F32)
    mine = jnp.sum(jnp.where(lane_f == column(4), logits, 0.0), -1, keepdims=True)
    other = jnp.sum(jnp.where(lane_f == column(0), logits, 0.0), -1, keepdims=True)
    gate = 1.0 / (1.0 + jnp.exp(other - mine - column(1, 2, 3)))
    upstream = signal[:, 0:width].astype(F32)
    rows_grad = (gate * upstream).astype(BF)
    rg_ref[...] = rows_grad
    hidden_here = w1.shape[2]
    step = min(512, hidden_here)

    def wait(groups):
        @pl.when(pl.program_id(0) == 0)
        def _():
            for group in groups:
                for item in group:
                    item.wait()

    def first_products(t):
        parts = []
        for at in range(0, hidden_here, step):
            cols = slice(at, at + step)
            parts.append((at, dot(rows, w1[t, :, cols]), dot(rows_grad, w2[t, cols, :], 1, 1)))
        return parts

    wait(copies[:1])
    ready = first_products(0)
    wait(copies[1:])
    out = None
    grad = None
    for t in range(count):
        parts = ready
        if t + 1 < count:
            ready = first_products(t + 1)
        for at, hidden, active_grad in parts:
            place = slice(t * hidden_here + at, t * hidden_here + at + step)
            active, slope = gelu_parts(hidden)
            act_ref[:, place] = active.astype(BF)
            hg_ref[:, place] = (active_grad * slope).astype(BF)
        place = slice(t * hidden_here, (t + 1) * hidden_here)
        part = dot(act_ref[:, place], w2[t])
        out = part if out is None else out + part
        part = dot(hg_ref[:, place], w1[t], 1, 1)
        grad = part if grad is None else grad + part
    dx_ref[...] = grad.astype(BF)
    back_ref[...] = (gate * out).astype(BF)
    gate_grad = jnp.sum(upstream * out.astype(BF).astype(F32), -1, keepdims=True)
    lanes = up_to(slots, LANES)
    spread = iota(slots, lanes, 0) == iota(slots, lanes, 1)
    spare_row = iota(16, 1, 0) == per + 16 - slots
    for b in range(x_ref.shape[0] // slots):
        end = (b + 1) * slots
        line = jnp.sum(jnp.where(spread, gate_grad[end - slots : end], 0.0), 0, keepdims=True)
        high = line.astype(BF).astype(F32)
        line = jnp.concatenate([high, line - high, jnp.zeros((1, width - 2 * lanes), F32)], 1)
        dx_ref[end - 16 : end, :] = jnp.where(spare_row, line, grad[end - 16 : end]).astype(BF)


def expert(x, g, chunk, router, w1, w2, slots, per):
    rows, width = x.shape
    count = len(w2)
    here = w2[0].shape[0]
    total = count * here
    blocks = block_count(rows // slots, slots)
    tile = slots * blocks

    def tiled(cols):
        return pl.BlockSpec((tile, cols), lambda i: (i, 0))

    flops = 8 * rows * width * total
    return pl.pallas_call(
        functools.partial(expert_kernel, count, slots, per),
        grid=(rows // tile,),
        in_specs=[
            tiled(width),
            pl.BlockSpec((blocks, 1, slots, g.shape[3]), lambda i: (i, chunk, 0, 0)),
            whole(router.shape),
        ]
        + [pl.BlockSpec(memory_space=pl.ANY)] * (3 * count),
        out_specs=[tiled(width), tiled(total), tiled(total), tiled(width), tiled(width)],
        out_shape=[
            jax.ShapeDtypeStruct((rows, width), BF),
            jax.ShapeDtypeStruct((rows, total), BF),
            jax.ShapeDtypeStruct((rows, total), BF),
            jax.ShapeDtypeStruct((rows, width), BF),
            jax.ShapeDtypeStruct((rows, width), BF),
        ],
        scratch_shapes=[
            pltpu.VMEM((count, width, here), BF),
            pltpu.VMEM((count, here, width), BF),
            pltpu.SemaphoreType.DMA((3 * count,)),
        ],
        compiler_params=params(),
        cost_estimate=pl.CostEstimate(flops=flops, bytes_accessed=rows * total * 6, transcendentals=rows * total * 2),
        name="expert",
    )(x, g, router, *w1, *w2)


def weight_kernel(count, steps, *refs):
    ins, outs = refs[: 2 * count], refs[2 * count :]
    total = None
    for n in range(count):
        part = dot(ins[2 * n][...], ins[2 * n + 1][...], 0, 0)
        total = part if total is None else total + part
    store_piece(outs, steps, total.astype(BF))


def weight_grad(columns, rows, first, here):
    count = len(columns)
    width = rows[0].shape[1]
    step = min(512, here)
    steps = here // step
    offset = first * steps
    specs, args = [], []
    for a, b in zip(columns, rows):
        specs += [pl.BlockSpec((a.shape[0], step), lambda i: (0, i + offset)), whole(b.shape, True)]
        args += [a, b]
    out_specs, out_shape = by_piece(2, steps, (step, width), (here, width), BF)
    return pl.pallas_call(
        functools.partial(weight_kernel, count, steps),
        grid=(2 * steps,),
        in_specs=specs,
        out_specs=out_specs,
        out_shape=out_shape,
        compiler_params=params(),
        cost_estimate=cost(4 * sum(b.shape[0] for b in rows) * width * here, 8 * here * width),
        name="weight_grad",
    )(*args)


def shards(
    block_in,
    norm_one,
    head_in,
    head_out,
    norm_two,
    router,
    expert_in,
    expert_out,
    expert_ids,
    route_noise,
    cotangent,
):
    rows_here, width = block_in.shape
    parts = lax.axis_size("tensor")
    groups = lax.axis_size("expert")
    me = lax.axis_index("tensor")
    images = rows_here // SEQ
    height = up_to(SEQ, 16)
    each = up_to(-(-rows_here // parts), 16)
    experts = router.shape[1]
    capacity = (rows_here * 2 * 8 // (5 * experts) + 15) // 16 * 16
    share = -(-capacity // parts)
    per = -(-share // CHUNKS)
    slots = up_to(per + 1, 16)
    chunk_rows = experts * slots
    full = rows_here // 16 * 16
    here = expert_out.shape[1]

    paired = parts == 4
    order = (0, 2, 1, 3) if paired else tuple(range(parts))
    part_of = jnp.stack([me ^ k if paired else jnp.int32(k) for k in order]).astype(jnp.int32)
    starts = part_of * each
    own_block = (me * (each // half_tile(each)))[None].astype(jnp.int32)

    def cross(x, k):
        return lax.ppermute(x, "tensor", [(n, n ^ k) for n in range(parts)])

    def far_part(x):
        return cross(x, 2) if paired else x

    def gathered_from(x, far):
        if not paired:
            every = lax.all_gather(x, "tensor", axis=0, tiled=False)
            return [every[p] for p in range(parts)]
        return [x, far, cross(x, 1), cross(far, 1)]

    def gathered(x):
        return gathered_from(x, far_part(x))

    def near_hop(pieces):
        return pinned(*[cross(piece, 1) for piece in pieces[2:]]) if paired else pieces

    def near_sum(pieces, came):
        if not paired:
            return lax.psum_scatter(jnp.stack(pieces), "tensor", scatter_dimension=0), None
        kept, other = ((a.astype(F32) + b.astype(F32)).astype(BF) for a, b in zip(pieces, came))
        return kept, other

    def far_hop(kept, other):
        return cross(other, 2) if paired else jnp.zeros_like(kept)

    def far_tiles(kept, other):
        tile = half_tile(each)
        source = other if paired else jnp.zeros_like(kept)
        tiles = [source[at : at + tile] for at in range(0, each, tile)]
        return [cross(item, 2) for item in tiles] if paired else tiles

    def scattered(pieces):
        kept, other = near_sum(pieces, near_hop(pieces))
        return kept, far_hop(kept, other)

    def swapped(pieces):
        if not paired:
            every = lax.all_to_all(jnp.stack(pieces), "tensor", split_axis=0, concat_axis=0, tiled=True)
            return [every[p] for p in range(parts)]
        return [cross(piece, k) if k else piece for piece, k in zip(pieces, order)]

    def over_experts(x):
        return lax.all_to_all(x, "expert", split_axis=0, concat_axis=0, tiled=True)

    def pinned(*items):
        return lax.optimization_barrier(items)

    def tail_of(x):
        return jnp.pad(x[full:], ((0, 16 - (rows_here - full)), (0, 0)))

    names = jnp.arange(experts, dtype=jnp.int32)
    member = [(expert_ids[:, c : c + 1] == names).astype(jnp.int32) for c in range(2)]
    both = member[0] + member[1]
    earlier = jnp.cumsum(both, 0) - both
    slot = jnp.stack([jnp.sum(earlier * item, -1) for item in member], 1)
    local = slot - me * share
    place = local // per * chunk_rows + expert_ids * slots + local % per
    place = jnp.where((local >= 0) & (local < share), place, -1)
    place = jnp.pad(place, ((0, each * parts - rows_here), (0, 0)), constant_values=-1)
    place_lanes = place.T
    place_parts = jnp.swapaxes(place_lanes.reshape(2, parts, each), 0, 1)

    sides = []
    for c in range(2):
        gap = route_noise[:, c] - route_noise[:, 1 - c]
        high = gap.astype(BF)
        left = gap - high.astype(F32)
        mid = left.astype(BF)
        low = (left - mid.astype(F32)).astype(BF)
        columns = [expert_ids[:, 1 - c].astype(BF), high, mid, low, expert_ids[:, c].astype(BF)]
        sides.append(jnp.stack(columns, 1))
    side = jnp.pad(jnp.stack(sides), ((0, 0), (0, each * parts - rows_here), (0, LANES - 5)))

    router_wide = jnp.pad(router, ((0, 0), (0, LANES - experts)))
    gain_one, gain_two = norm_one[None, :], norm_two[None, :]
    head_out_far = far_part(head_out)
    w1_own = [expert_in[0, : width // 2], expert_in[0, width // 2 :]]
    w1_far = [far_part(item) for item in w1_own]

    packed = pack_first(cotangent, tail_of(cotangent), place_lanes, side, experts, slots)
    block_rows, packed, w1_far[0] = pinned(block_in, packed, w1_far[0])
    signal = over_experts(packed)

    first_in, qkv, logs, *mixed = attend(
        starts, block_rows, tail_of(block_in), gain_one, head_in, images, height, each, parts
    )
    *mixed, w1_far[1], head_out_far = pinned(*mixed, w1_far[1], head_out_far)
    head_out_all = gathered_from(head_out, head_out_far)
    mixed = swapped(mixed)
    middle, second_in, gates = middle_of(
        own_block, mixed, head_out_all, block_in, gain_two, router_wide, expert_ids, route_noise
    )
    *second_all, late_out = pinned(*gathered(second_in), expert_out[0])
    w1 = [gathered_from(a, b) for a, b in zip(w1_own, w1_far)]
    w1 = [w1[h][p] for p in range(parts) for h in range(2)]

    def packed_rows(n):
        return pack(part_of, second_all, place_parts, experts, slots, n * chunk_rows)

    def sent(x):
        return over_experts(x.reshape(experts, slots, width)).reshape(chunk_rows, width)

    x = sent(packed_rows(0))
    w2_far, head_in_t, signal, *outgoing = pinned(
        far_part(late_out), jnp.swapaxes(head_in, 1, 2), signal, *[packed_rows(n) for n in range(1, CHUNKS)]
    )
    w2 = gathered_from(expert_out[0], w2_far)
    backs, actives, hidden_grads, rows_grads, arrived, returned = [], [], [], [], [], []
    for n in range(CHUNKS):
        coming = None
        if n + 1 < CHUNKS:
            x, ready = pinned(x, outgoing[n])
            coming = sent(ready)
        if n == 0:
            x, *ready = pinned(x, *w1, *w2)
            w1, w2 = ready[: 2 * parts], ready[2 * parts :]
        back, active, hidden_grad, rows_grad, row_grad = expert(
            x, signal, n, router_wide, w1, w2, slots, per
        )
        if returned:
            row_grad, active, returned[-1] = pinned(row_grad, active, returned[-1])
        arrived.append(x)
        actives.append(active)
        hidden_grads.append(hidden_grad)
        rows_grads.append(rows_grad)
        backs.append(back)
        if coming is not None:
            x, row_grad = pinned(coming, row_grad)
        returned.append(sent(row_grad))

    def weight_parts(columns, rows):
        pairs = [weight_grad(columns, rows, p, here) for p in range(parts - 2, -1, -2)]
        return [item for pair in pairs[::-1] for item in pair]

    out_parts = weight_parts(actives, rows_grads)
    out_kept, out_other = near_sum(out_parts, near_hop(out_parts))
    out_far = far_hop(out_kept, out_other)
    *returned, out_kept = pinned(*returned, out_kept)

    second_pieces = unpack(part_of, place, returned, slots, per, each, True)
    second_kept, second_other = near_sum(second_pieces, near_hop(second_pieces))
    if paired:
        second_other, *hidden_grads = pinned(second_other, *hidden_grads)
    second_far = far_tiles(second_kept, second_other)
    in_parts = []
    for p in range(parts - 2, -1, -2):
        *hidden_grads, pair = pinned(*hidden_grads, weight_grad(hidden_grads, arrived, p, here))
        in_parts = list(pair) + in_parts
        if p == parts - 2:
            in_came = near_hop([None] * p + list(pair)) if paired else ()
            second_far[0], pair = pinned(second_far[0], pair)
    second_far[-1], out_far, *in_parts = pinned(second_far[-1], out_far, *in_parts)
    combined = [sent(item) for item in backs]
    middle_grad, router_part, norm_two_part, *pieces = middle_back(
        own_block, second_kept, second_far, middle, second_in, gates, expert_ids, cotangent, mixed, head_out_all,
        gain_two, router_wide,
    )
    head_out_parts, mixed_grad = pieces[:parts], pieces[parts:]
    *mixed_grad, combined[0] = pinned(*mixed_grad, combined[0])
    mixed_grad = swapped(mixed_grad)
    head_out_kept, head_out_far = scattered(head_out_parts)
    in_kept, in_other = near_sum(in_parts, in_came)
    if paired:
        in_other = pinned(in_other, head_out_far, *mixed_grad)[0]
    in_far = far_hop(in_kept, in_other)
    *pieces, head_in_part, norm_one_part = attend_back(
        starts, mixed_grad, qkv, logs, first_in, head_in_t, gain_one
    )
    *pieces, combined[-1] = pinned(*pieces, combined[-1])
    first_kept, first_other = near_sum(pieces, near_hop(pieces))
    if paired:
        first_other, first_kept, *combined = pinned(first_other, first_kept, *combined)
    first_far = far_tiles(first_kept, first_other)
    block_pieces = unpack(part_of, place, combined, slots, per, each, False)
    first_far[0], *block_pieces = pinned(first_far[0], *block_pieces)
    block_kept, block_other = near_sum(block_pieces, near_hop(block_pieces))
    if paired:
        first_far[-1], block_other = pinned(first_far[-1], block_other)
    block_far = far_hop(block_kept, block_other)
    input_part = input_back(own_block, first_kept, first_far, block_in, middle_grad, gain_one)
    out_grad = out_kept.astype(F32) + out_far.astype(F32)
    in_grad = sum_turned(in_kept, in_far)
    input_far, out_grad, in_grad, block_far = pinned(far_part(input_part), out_grad, in_grad, block_far)
    block_own = (middle + block_kept.astype(F32) + block_far.astype(F32)).astype(BF)

    cols = head_in.shape[2]
    head_out_part = (head_out_kept.astype(F32) + head_out_far.astype(F32)).astype(BF)
    small = jnp.concatenate([norm_one_part, norm_two_part, router_part[:experts]], 0).astype(BF)
    count = 4 * cols + 2 + experts
    total = up_to(count, 16 * groups)
    heads = jnp.concatenate(
        [head_in_part.reshape(3 * cols, width), head_out_part, jnp.pad(small, ((0, total - count), (0, 0)))], 0
    )
    heads = over_experts(heads.reshape(groups, total // groups, width))
    heads, block_own = pinned(heads, block_own)
    input_grad = assemble(part_of, gathered_from(input_part, input_far), rows_here, F32)
    block_out = assemble(part_of, gathered(block_own), rows_here, BF)
    heads = jnp.sum(heads.astype(F32), 0).astype(BF)
    heads = lax.all_gather(heads, "expert", axis=0, tiled=True)
    head_in_grad = jnp.swapaxes(heads[: 3 * cols].reshape(3, cols, width), 1, 2).astype(F32)
    head_out_grad = heads[3 * cols : 4 * cols].astype(F32)
    small = heads[4 * cols : count].astype(F32)
    if paired:
        small = small + cross(small, 1)
        small = small + cross(small, 2)
    else:
        small = lax.psum(small, "tensor")
    return (
        block_out,
        input_grad,
        small[0],
        head_in_grad,
        head_out_grad,
        small[1],
        small[2:].T,
        in_grad[None],
        out_grad[None],
    )


def solution(mesh):
    in_specs = (
        P("expert", None),
        P(),
        P(None, None, "tensor"),
        P("tensor", None),
        P(),
        P(),
        P("expert", None, "tensor"),
        P("expert", "tensor", None),
        P("expert", None),
        P("expert", None),
        P("expert", None),
    )
    out_specs = (
        P("expert", None),
        P("expert", None),
        P(),
        P(None, None, "tensor"),
        P("tensor", None),
        P(),
        P(),
        P("expert", None, "tensor"),
        P("expert", "tensor", None),
    )
    return jax.shard_map(shards, mesh=mesh, in_specs=in_specs, out_specs=out_specs, check_vma=False)
```

```python
import functools

import jax
import jax.numpy as jnp
from jax import lax
from jax.experimental import pallas as pl
from jax.experimental.pallas import tpu as pltpu
from jax.sharding import PartitionSpec as P

HD = 64
SEQ = 197
LANES = 128
EPSILON = 1e-06
CHUNKS = 2
BF = jnp.bfloat16
F32 = jnp.float32


def up_to(value, unit):
    return -(-value // unit) * unit


def params(mib=60):
    return pltpu.CompilerParams(vmem_limit_bytes=mib * 1024 * 1024)


def dot(a, b, da=1, db=0):
    return lax.dot_general(a, b, (((da,), (db,)), ((), ())), preferred_element_type=F32)


def iota(rows, cols, dim):
    return lax.broadcasted_iota(jnp.int32, (rows, cols), dim)


def flag(mask):
    return jnp.where(mask, 1.0, 0.0)


def whole(shape, once=False):
    zeros = (0,) * len(shape)
    mode = pl.Buffered(1) if once else None
    return pl.BlockSpec(shape, lambda *_: zeros, pipeline_mode=mode)


def image(*shape):
    return pl.BlockSpec((1,) + shape, lambda i, *_: (i,) + (0,) * len(shape))


def fill(x_ref, tail_ref, rows_ref):
    full = x_ref.shape[0] // 16 * 16
    rows_ref[0:full, :] = x_ref[0:full, :]
    rows_ref[full : full + 16, :] = tail_ref[...]
    rest = rows_ref.shape[0] - full - 16
    if rest:
        rows_ref[full + 16 :, :] = jnp.zeros((rest, rows_ref.shape[1]), BF)


def norm_parts(field):
    centre = field - jnp.mean(field, -1, keepdims=True)
    spread = lax.rsqrt(jnp.mean(centre * centre, -1, keepdims=True) + EPSILON)
    return centre * spread, spread


def norm_field_back(upstream, gain, scaled, spread):
    weighted = upstream * gain
    return spread * (
        weighted
        - jnp.mean(weighted, -1, keepdims=True)
        - scaled * jnp.mean(weighted * scaled, -1, keepdims=True)
    )


def cost(flops, size):
    return pl.CostEstimate(flops=flops, bytes_accessed=size, transcendentals=0)


def by_piece(count, steps, block, shape, dtype):
    def spec(p):
        def place(i, *_):
            return (jnp.clip(i - p * steps, 0, steps - 1), 0)

        return pl.BlockSpec(block, place)

    return [spec(p) for p in range(count)], [jax.ShapeDtypeStruct(shape, dtype)] * count


def store_piece(refs, steps, value):
    for p, ref in enumerate(refs):

        @pl.when(pl.program_id(0) // steps == p)
        def _():
            ref[...] = value


def rows_spec(tile, width):
    return pl.BlockSpec((tile, width), lambda i, *_: (i, 0))


def own_spec(tile, width):
    return pl.BlockSpec((tile, width), lambda i, at: (at[0] + i, 0))


def window_of(i, height, back=False):
    start = i * SEQ
    aligned = start // 16 * 16
    window = height + 16
    shape = (window, height) if back else (height, window)
    r, c = iota(*shape, 1 if back else 0), iota(*shape, 0 if back else 1)
    match = flag((c == r + (start - aligned)) & (r < SEQ)).astype(BF)
    return match, pl.ds(pl.multiple_of(aligned, 16), window)


def head_masks():
    lane = iota(1, LANES, 1)
    return [(flag(lane // HD == h)).astype(BF) for h in range(2)]


def attend_kernel(count, starts_ref, x_ref, tail_ref, gain_ref, w_ref, first_ref, qkv_ref, log_ref, *refs):
    piece_refs, rows, mixed = refs[:count], refs[count], refs[count + 1]
    i = pl.program_id(0)
    height = first_ref.shape[1]
    cols = mixed.shape[1]

    @pl.when(i == 0)
    def _():
        fill(x_ref, tail_ref, rows)
        mixed[...] = jnp.zeros_like(mixed)

    match, place = window_of(i, height)
    field = dot(match, rows[place, :])
    scaled, _ = norm_parts(field)
    first = (scaled * gain_ref[...]).astype(BF)
    first_ref[0] = first
    for k in range(3):
        qkv_ref[k, 0] = dot(first, w_ref[k]).astype(BF)
    masks = head_masks()
    lane = iota(1, LANES, 1)
    key_lane = iota(1, height, 1)
    logs = jnp.zeros((height, LANES), F32)
    back, _ = window_of(i, height, True)
    for pair in range(cols // LANES):
        part = slice(pair * LANES, (pair + 1) * LANES)
        queries, keys, values = (qkv_ref[k, 0, :, part] for k in range(3))
        total = jnp.zeros((height, LANES), F32)
        for h in range(2):
            scores = dot(queries * masks[h], keys, 1, 1) * HD ** (-0.5)
            scores = jnp.where(key_lane < SEQ, scores, -1e30)
            highest = jnp.max(scores, -1, keepdims=True)
            weights = jnp.exp(scores - highest)
            sums = jnp.sum(weights, -1, keepdims=True)
            probs = (weights * (1.0 / sums)).astype(BF)
            total += dot(probs, values * masks[h])
            logs = jnp.where(lane == pair * 2 + h, highest + jnp.log(sums), logs)
        mixed[place, part] = (mixed[place, part].astype(F32) + dot(back, total.astype(BF))).astype(BF)
    log_ref[0] = logs

    @pl.when(i == pl.num_programs(0) - 1)
    def _():
        for p in range(count):
            at = pl.multiple_of(starts_ref[p], 16)
            piece_refs[p][...] = mixed[pl.ds(at, piece_refs[p].shape[0]), :]


def attend(starts, block_in, tail, gain, head_in, images, height, each, count):
    rows, width = block_in.shape
    cols = head_in.shape[2]
    scratch_rows = max(rows // 16 * 16 + 48, each * count)
    spec = pltpu.PrefetchScalarGridSpec(
        num_scalar_prefetch=1,
        grid=(images,),
        in_specs=[whole((rows, width), True), whole((16, width)), whole((1, width)), whole(head_in.shape, True)],
        out_specs=[
            image(height, width),
            pl.BlockSpec((3, 1, height, cols), lambda i, *_: (0, i, 0, 0)),
            image(height, LANES),
        ]
        + [whole((each, cols))] * count,
        scratch_shapes=[pltpu.VMEM((scratch_rows, width), BF), pltpu.VMEM((scratch_rows, cols), BF)],
    )
    return pl.pallas_call(
        functools.partial(attend_kernel, count),
        grid_spec=spec,
        out_shape=[
            jax.ShapeDtypeStruct((images, height, width), BF),
            jax.ShapeDtypeStruct((3, images, height, cols), BF),
            jax.ShapeDtypeStruct((images, height, LANES), F32),
        ]
        + [jax.ShapeDtypeStruct((each, cols), BF)] * count,
        compiler_params=params(),
        cost_estimate=cost(16 * images * height * width * cols, 16 * rows * width),
        name="attend",
    )(starts, block_in, tail, gain, head_in)


def attend_back_kernel(count, starts_ref, qkv_ref, log_ref, first_ref, wt_ref, gain_ref, *refs):
    dmix_refs, piece_refs = refs[:count], refs[count : 2 * count]
    hg_ref, ng_ref, acc, grads, dmix, field = refs[2 * count :]
    i = pl.program_id(0)
    height = first_ref.shape[1]
    each = dmix_refs[0].shape[0]

    @pl.when(i == 0)
    def _():
        acc[...] = jnp.zeros_like(acc)
        field[...] = jnp.zeros_like(field)
        rest = dmix.shape[0] - each * count
        if rest:
            dmix[each * count :, :] = jnp.zeros((rest, dmix.shape[1]), BF)
        for p in range(count):
            dmix[pl.ds(pl.multiple_of(starts_ref[p], 16), each), :] = dmix_refs[p][...]

    match, place = window_of(i, height)
    back, _ = window_of(i, height, True)
    out_grads = dot(match, dmix[place, :]).astype(BF)
    masks = head_masks()
    lane = iota(1, LANES, 1)
    key_lane = iota(1, height, 1)
    scale = HD ** (-0.5)
    logs = log_ref[0]
    for pair in range(dmix.shape[1] // LANES):
        cols = slice(pair * LANES, (pair + 1) * LANES)
        queries, keys, values = (qkv_ref[k, 0, :, cols] for k in range(3))
        out_grad = out_grads[:, cols]
        dq = jnp.zeros((height, LANES), F32)
        dk = jnp.zeros((height, LANES), F32)
        dv = jnp.zeros((height, LANES), F32)
        for h in range(2):
            q_h = queries * masks[h]
            o_h = out_grad * masks[h]
            log_h = jnp.sum(jnp.where(lane == pair * 2 + h, logs, 0.0), -1, keepdims=True)
            probs = jnp.exp(dot(q_h, keys, 1, 1) * scale - log_h)
            probs = jnp.where(key_lane < SEQ, probs, 0.0)
            prob_grad = dot(o_h, values, 1, 1)
            dv += dot(probs.astype(BF), o_h, 0, 0)
            delta = jnp.sum(probs * prob_grad, -1, keepdims=True)
            score_grad = (probs * (prob_grad - delta)).astype(BF)
            dq += dot(score_grad, keys * masks[h])
            dk += dot(score_grad, q_h, 0, 0)
        grads[0, :, cols] = (dq * scale).astype(BF)
        grads[1, :, cols] = (dk * scale).astype(BF)
        grads[2, :, cols] = dv.astype(BF)

    first = first_ref[0]
    total = None
    for k in range(3):
        part = dot(grads[k], wt_ref[k])
        total = part if total is None else total + part
        acc[k] += dot(grads[k], first, 0, 0)
    field[place, :] = (field[place, :].astype(F32) + dot(back, total.astype(BF))).astype(BF)

    @pl.when(i == pl.num_programs(0) - 1)
    def _():
        for p in range(count):
            piece_refs[p][...] = field[pl.ds(pl.multiple_of(starts_ref[p], 16), each), :]
        hg_ref[...] = acc[...].astype(BF)
        gain_grad = jnp.zeros_like(ng_ref)
        for k in range(3):
            gain_grad += jnp.sum(acc[k] * wt_ref[k].astype(F32), 0, keepdims=True)
        ng_ref[...] = gain_grad / gain_ref[...]


def attend_back(starts, dmix, qkv, logs, first, head_in_t, gain):
    images, height, width = first.shape
    each, cols = dmix[0].shape
    count = len(dmix)
    scratch_rows = max(images * SEQ // 16 * 16 + 48, each * count)
    spec = pltpu.PrefetchScalarGridSpec(
        num_scalar_prefetch=1,
        grid=(images,),
        in_specs=[
            pl.BlockSpec((3, 1, height, cols), lambda i, *_: (0, i, 0, 0)),
            image(height, LANES),
            image(height, width),
            whole(head_in_t.shape, True),
            whole((1, width)),
        ]
        + [whole((each, cols), True)] * count,
        out_specs=[whole((each, width))] * count + [whole(head_in_t.shape), whole((1, width))],
        scratch_shapes=[
            pltpu.VMEM(head_in_t.shape, F32),
            pltpu.VMEM((3, height, cols), BF),
            pltpu.VMEM((scratch_rows, cols), BF),
            pltpu.VMEM((scratch_rows, width), BF),
        ],
    )
    return pl.pallas_call(
        functools.partial(attend_back_kernel, count),
        grid_spec=spec,
        out_shape=[jax.ShapeDtypeStruct((each, width), BF)] * count
        + [jax.ShapeDtypeStruct(head_in_t.shape, BF), jax.ShapeDtypeStruct((1, width), F32)],
        compiler_params=params(),
        cost_estimate=cost(24 * images * height * width * cols, 20 * images * height * width),
        name="attend_back",
    )(starts, qkv, logs, first, head_in_t, gain, *dmix)


def block_count(blocks, slots):
    return max(n for n in range(1, blocks + 1) if blocks % n == 0 and n * slots <= 448)


def pack_first_kernel(x_ref, tail_ref, lp_ref, side_ref, out_ref, rows):
    i, n = pl.program_id(0), pl.program_id(1)

    @pl.when((i == 0) & (n == 0))
    def _():
        fill(x_ref, tail_ref, rows)

    blocks, _, slots, _ = out_ref.shape
    tile = blocks * slots
    j = (n * pl.num_programs(0) + i) * tile + iota(tile, rows.shape[0], 0)
    picks = [flag(lp_ref[c : c + 1, :] == j) for c in range(2)]
    width = x_ref.shape[1]
    main = dot((picks[0] + picks[1]).astype(BF), rows[...]).astype(BF)
    out_ref[:, 0, :, 0:width] = main.reshape(blocks, slots, width)
    extra = dot(picks[0].astype(BF), side_ref[0]) + dot(picks[1].astype(BF), side_ref[1])
    out_ref[:, 0, :, width:] = extra.astype(BF).reshape(blocks, slots, LANES)


def pack_first(x, tail, lp, side, experts, slots):
    rows, width = x.shape
    padded = lp.shape[1]
    blocks = block_count(experts, slots)
    return pl.pallas_call(
        pack_first_kernel,
        grid=(experts // blocks, CHUNKS),
        in_specs=[whole((rows, width), True), whole((16, width)), whole(lp.shape), whole(side.shape)],
        out_specs=pl.BlockSpec((blocks, 1, slots, width + LANES), lambda i, n: (i, n, 0, 0)),
        out_shape=jax.ShapeDtypeStruct((experts, CHUNKS, slots, width + LANES), BF),
        scratch_shapes=[pltpu.VMEM((padded, width), BF)],
        compiler_params=params(),
        cost_estimate=cost(3 * CHUNKS * experts * slots * padded * width, 2 * rows * width),
        name="pack_cotangent",
    )(x, tail, lp, side)


def pack_kernel(base, count, part_ref, *refs):
    lp_ref, out_ref = refs[count], refs[count + 1]
    total = None
    tile = out_ref.shape[0]
    for p in range(count):
        j = base + pl.program_id(0) * tile + iota(tile, refs[p].shape[0], 0)
        lp = lp_ref[part_ref[p]]
        picks = flag((lp[0:1, :] == j) | (lp[1:2, :] == j)).astype(BF)
        part = dot(picks, refs[p][...])
        total = part if total is None else total + part
    out_ref[...] = total.astype(BF)


def pack(part_of, pieces, lp, experts, slots, base):
    rows, width = pieces[0].shape
    count = len(pieces)
    tile = slots * block_count(experts, slots)
    spec = pltpu.PrefetchScalarGridSpec(
        num_scalar_prefetch=1,
        grid=(experts * slots // tile,),
        in_specs=[whole((rows, width), True)] * count + [whole(lp.shape)],
        out_specs=rows_spec(tile, width),
    )
    return pl.pallas_call(
        functools.partial(pack_kernel, base, count),
        grid_spec=spec,
        out_shape=jax.ShapeDtypeStruct((experts * slots, width), BF),
        compiler_params=params(),
        cost_estimate=cost(3 * experts * slots * rows * count * width, 2 * rows * count * width),
        name="pack_rows",
    )(part_of, *pieces, lp)


def unpack_kernel(count, slots, per, graded, part_ref, lp_ref, *refs):
    row_refs, out_refs = refs[:count], refs[count:]
    lp = lp_ref[...]
    height = lp.shape[0]
    rows, width = row_refs[0].shape
    total = jnp.zeros((height, width), F32)
    lanes = up_to(slots, LANES)
    extra = [jnp.zeros((height, lanes), F32) for _ in range(2)]
    for n in range(count):
        j = n * rows + iota(1, rows, 1)
        hits = (lp[:, 0:1] == j) | (lp[:, 1:2] == j)
        total += dot(flag(hits).astype(BF), row_refs[n][...])
        if graded:
            j = iota(1, lanes, 1)
            for e in range(rows // slots):
                spare = row_refs[n][(e + 1) * slots - 16 : (e + 1) * slots, 0 : 2 * lanes].astype(F32)
                spare = spare[per + 16 - slots : per + 17 - slots, :]
                values = spare[:, :lanes] + spare[:, lanes:]
                for c in range(2):
                    hit = lp[:, c : c + 1] - (n * rows + e * slots) == j
                    extra[c] += jnp.where(hit, values, 0.0)
    value = total.astype(BF)
    if graded:
        lane = iota(1, LANES, 1)
        tail = jnp.zeros((height, LANES), F32)
        for c in range(2):
            grad = jnp.sum(extra[c], -1, keepdims=True)
            high = grad.astype(BF).astype(F32)
            tail = jnp.where(lane == c, high, tail)
            tail = jnp.where(lane == 2 + c, grad - high, tail)
        value = jnp.concatenate([value, tail.astype(BF)], 1)
    store_piece(out_refs, 1, value)


def unpack(part_of, lp, rows, slots, per, each, graded):
    parts = lp.shape[0] // each
    count = len(rows)
    width = rows[0].shape[1] + (LANES if graded else 0)
    out_specs, out_shape = by_piece(parts, 1, (each, width), (each, width), BF)
    spec = pltpu.PrefetchScalarGridSpec(
        num_scalar_prefetch=1,
        grid=(parts,),
        in_specs=[pl.BlockSpec((each, 2), lambda i, at: (at[i], 0))] + [whole(item.shape, True) for item in rows],
        out_specs=out_specs,
    )
    return pl.pallas_call(
        functools.partial(unpack_kernel, count, slots, per, graded),
        grid_spec=spec,
        out_shape=out_shape,
        compiler_params=params(),
        cost_estimate=cost(3 * lp.shape[0] * count * rows[0].size, 4 * count * rows[0].size),
        name="unpack_rows",
    )(part_of, lp, *rows)


def assemble_kernel(count, steps, part_ref, *refs):
    out_ref = refs[count]
    for p in range(count):

        @pl.when(pl.program_id(0) // steps == p)
        def _():
            out_ref[...] = refs[p][...].astype(out_ref.dtype)


def assemble(part_of, pieces, rows, dtype):
    each, width = pieces[0].shape
    count = len(pieces)
    tile, steps = each, 1
    in_specs, _ = by_piece(count, steps, (tile, width), (each, width), BF)
    spec = pltpu.PrefetchScalarGridSpec(
        num_scalar_prefetch=1,
        grid=(count * steps,),
        in_specs=in_specs,
        out_specs=pl.BlockSpec((tile, width), lambda i, at: (at[i // steps] * steps + i % steps, 0)),
    )
    return pl.pallas_call(
        functools.partial(assemble_kernel, count, steps),
        grid_spec=spec,
        out_shape=jax.ShapeDtypeStruct((rows, width), dtype),
        compiler_params=params(),
        cost_estimate=cost(2 * rows * width, 8 * rows * width),
        name="assemble",
    )(part_of, *pieces)


def of_tiles(refs):
    value = refs[0][...].astype(F32)
    for n, ref in enumerate(refs[1:]):
        value = jnp.where(pl.program_id(0) > n, ref[...].astype(F32), value)
    return value


def sum_far_kernel(turned, *refs):
    far_refs, keep_ref, out_ref = refs[:-2], refs[-2], refs[-1]
    total = keep_ref[...].astype(F32) + of_tiles(far_refs)
    out_ref[...] = total.T if turned else total


def sum_far(keep, far, turned):
    rows, width = keep.shape
    tile = rows // len(far)
    return pl.pallas_call(
        functools.partial(sum_far_kernel, turned),
        grid=(len(far),),
        in_specs=[whole((tile, width))] * len(far) + [rows_spec(tile, width)],
        out_specs=pl.BlockSpec((width, tile), lambda i: (0, i)) if turned else rows_spec(tile, width),
        out_shape=jax.ShapeDtypeStruct((width, rows) if turned else (rows, width), F32),
        compiler_params=params(),
        cost_estimate=cost(rows * width, 8 * rows * width),
        name="sum_far",
    )(*far, keep)


def middle_kernel(count, limit, at_ref, *refs):
    mixed_refs, wo_refs = refs[:count], refs[count : 2 * count]
    x_ref, gain_ref, router_ref, ids_ref, noise_ref, mid_ref, second_ref, gates_ref = refs[2 * count :]
    tile = x_ref.shape[0]
    valid = (at_ref[0] + pl.program_id(0)) * tile + iota(tile, 1, 0) < limit
    middle = jnp.where(valid, x_ref[...].astype(F32), 0.0)
    for mixed_ref, wo_ref in zip(mixed_refs, wo_refs):
        middle += dot(mixed_ref[...], wo_ref[...])
    mid_ref[...] = middle
    scaled, _ = norm_parts(middle)
    second = (scaled * gain_ref[...]).astype(BF)
    second_ref[...] = second
    logits = dot(second, router_ref[...])
    lane = iota(1, LANES, 1)
    chosen = [
        jnp.sum(jnp.where(lane == ids_ref[:, c : c + 1], logits, 0.0), -1, keepdims=True)
        + noise_ref[:, c : c + 1]
        for c in range(2)
    ]
    top = jnp.maximum(chosen[0], chosen[1])
    raw = [jnp.exp(item - top) for item in chosen]
    inverse = 1.0 / (raw[0] + raw[1])
    gates = jnp.where(lane == 0, raw[0] * inverse, 0.0) + jnp.where(lane == 1, raw[1] * inverse, 0.0)
    gates_ref[...] = jnp.where(valid, gates, 0.0)


def half_tile(each):
    return each // 2 if each % 32 == 0 else each


def middle_of(at, mixed, head_out, x, gain, router, ids, noise):
    each, cols = mixed[0].shape
    parts = len(mixed)
    rows, width = x.shape
    tile = half_tile(each)
    spec = pltpu.PrefetchScalarGridSpec(
        num_scalar_prefetch=1,
        grid=(each // tile,),
        in_specs=[rows_spec(tile, cols)] * parts
        + [whole((cols, width), True)] * parts
        + [
            own_spec(tile, width),
            whole((1, width)),
            whole(router.shape),
            own_spec(tile, 2),
            own_spec(tile, 2),
        ],
        out_specs=[rows_spec(tile, width), rows_spec(tile, width), rows_spec(tile, LANES)],
    )
    return pl.pallas_call(
        functools.partial(middle_kernel, parts, rows),
        grid_spec=spec,
        out_shape=[
            jax.ShapeDtypeStruct((each, width), F32),
            jax.ShapeDtypeStruct((each, width), BF),
            jax.ShapeDtypeStruct((each, LANES), F32),
        ],
        compiler_params=params(),
        cost_estimate=cost(4 * each * width * width, 24 * each * width),
        name="middle",
    )(at, *mixed, *head_out, x, gain, router, ids, noise)


def middle_back_kernel(count, limit, tiles, at_ref, *refs):
    far_refs, refs = refs[:tiles], refs[tiles:]
    keep_ref, mid_ref, second_ref, gates_ref, ids_ref, up_ref, gain_ref, router_ref = refs[:8]
    mixed_refs, wo_refs = refs[8 : 8 + count], refs[8 + count : 8 + 2 * count]
    mg_ref, rg_ref, ng_ref = refs[8 + 2 * count : 11 + 2 * count]
    hog_refs, dmix_refs, hog_acc = refs[11 + 2 * count : 11 + 3 * count], refs[11 + 3 * count : -1], refs[-1]
    i = pl.program_id(0)

    @pl.when(i == 0)
    def _():
        hog_acc[...] = jnp.zeros_like(hog_acc)
        rg_ref[...] = jnp.zeros_like(rg_ref)
        ng_ref[...] = jnp.zeros_like(ng_ref)

    tile, width = up_ref.shape
    valid = (at_ref[0] + i) * tile + iota(tile, 1, 0) < limit
    lane = iota(1, LANES, 1)
    both = keep_ref[...].astype(F32) + of_tiles(far_refs)
    tail = both[:, width:]
    gates = gates_ref[...]
    gate, grad = [], []
    for c in range(2):
        gate.append(jnp.sum(jnp.where(lane == c, gates, 0.0), -1, keepdims=True))
        grad.append(jnp.sum(jnp.where((lane == c) | (lane == 2 + c), tail, 0.0), -1, keepdims=True))
    mean_term = gate[0] * grad[0] + gate[1] * grad[1]
    logit_grad = jnp.zeros((tile, LANES), F32)
    for c in range(2):
        hit = (lane == ids_ref[:, c : c + 1]) & valid
        logit_grad = jnp.where(hit, gate[c] * (grad[c] - mean_term), logit_grad)
    logit_grad = logit_grad.astype(BF)
    second_grad = both[:, 0:width] + dot(logit_grad, router_ref[...], 1, 1)
    rg_ref[...] += dot(logit_grad, second_ref[...], 0, 0)
    scaled, spread = norm_parts(mid_ref[...])
    ng_ref[...] += jnp.sum(second_grad * scaled, 0, keepdims=True)
    upstream = jnp.where(valid, up_ref[...].astype(F32), 0.0)
    middle_grad = upstream + norm_field_back(second_grad, gain_ref[...], scaled, spread)
    mg_ref[...] = middle_grad
    rounded = middle_grad.astype(BF)
    for t in range(count):
        dmix_refs[t][...] = dot(rounded, wo_refs[t][...], 1, 1).astype(BF)
        hog_acc[t] += dot(mixed_refs[t][...], rounded, 0, 0)

    @pl.when(i == pl.num_programs(0) - 1)
    def _():
        for t in range(count):
            hog_refs[t][...] = hog_acc[t].astype(BF)


def middle_back(at, keep, far, middle, second, gates, ids, up, mixed, head_out, gain, router):
    each, cols = mixed[0].shape
    parts = len(mixed)
    rows, width = up.shape
    tile = half_tile(each)
    spec = pltpu.PrefetchScalarGridSpec(
        num_scalar_prefetch=1,
        grid=(each // tile,),
        in_specs=[whole((tile, keep.shape[1]))] * len(far)
        + [
            rows_spec(tile, keep.shape[1]),
            rows_spec(tile, width),
            rows_spec(tile, width),
            rows_spec(tile, LANES),
            own_spec(tile, 2),
            own_spec(tile, width),
            whole((1, width)),
            whole(router.shape),
        ]
        + [rows_spec(tile, cols)] * parts
        + [whole((cols, width), True)] * parts,
        out_specs=[rows_spec(tile, width), whole((LANES, width)), whole((1, width))]
        + [whole((cols, width))] * parts
        + [rows_spec(tile, cols)] * parts,
        scratch_shapes=[pltpu.VMEM((parts, cols, width), F32)],
    )
    return pl.pallas_call(
        functools.partial(middle_back_kernel, parts, rows, len(far)),
        grid_spec=spec,
        out_shape=[
            jax.ShapeDtypeStruct((each, width), F32),
            jax.ShapeDtypeStruct((LANES, width), F32),
            jax.ShapeDtypeStruct((1, width), F32),
        ]
        + [jax.ShapeDtypeStruct((cols, width), BF)] * parts
        + [jax.ShapeDtypeStruct((each, cols), BF)] * parts,
        compiler_params=params(),
        cost_estimate=cost(8 * each * width * width, 40 * each * width),
        name="middle_back",
    )(at, *far, keep, middle, second, gates, ids, up, gain, router, *mixed, *head_out)


def input_back_kernel(limit, tiles, at_ref, *refs):
    far_refs, (keep_ref, x_ref, mg_ref, gain_ref, out_ref) = refs[:tiles], refs[tiles:]
    tile = x_ref.shape[0]
    valid = (at_ref[0] + pl.program_id(0)) * tile + iota(tile, 1, 0) < limit
    scaled, spread = norm_parts(jnp.where(valid, x_ref[...].astype(F32), 0.0))
    first_grad = keep_ref[...].astype(F32) + of_tiles(far_refs)
    out_ref[...] = (mg_ref[...] + norm_field_back(first_grad, gain_ref[...], scaled, spread)).astype(BF)


def input_back(at, keep, far, x, middle_grad, gain):
    each, width = middle_grad.shape
    tile = half_tile(each)
    spec = pltpu.PrefetchScalarGridSpec(
        num_scalar_prefetch=1,
        grid=(each // tile,),
        in_specs=[whole((tile, width))] * len(far)
        + [rows_spec(tile, width), own_spec(tile, width), rows_spec(tile, width), whole((1, width))],
        out_specs=rows_spec(tile, width),
    )
    return pl.pallas_call(
        functools.partial(input_back_kernel, x.shape[0], len(far)),
        grid_spec=spec,
        out_shape=jax.ShapeDtypeStruct((each, width), BF),
        compiler_params=params(),
        cost_estimate=cost(20 * each * width, 16 * each * width),
        name="input_back",
    )(at, *far, keep, x, middle_grad, gain)


def gelu_parts(v):
    x = jnp.abs(v) * 0.7071067811865476
    t = 1.0 / (1.0 + 0.3275911 * x)
    bell = jnp.exp(-x * x)
    poly = ((((1.061405429 * t - 1.453152027) * t + 1.421413741) * t - 0.284496736) * t + 0.254829592) * t
    below = 0.5 * poly * bell
    share = jnp.where(v < 0.0, below, 1.0 - below)
    return v * share, share + v * bell * 0.3989422804014327


def expert_kernel(count, slots, per, x_ref, g_ref, router_ref, *refs):
    w1_hbm, w2_hbm = refs[: 2 * count], refs[2 * count : 3 * count]
    back_ref, act_ref, hg_ref, rg_ref, dx_ref, w1, w2, sems = refs[3 * count :]
    rows, width = x_ref[...], x_ref.shape[1]
    half = width // 2
    copies = []
    for t in range(count):
        copies.append(
            [
                pltpu.make_async_copy(w1_hbm[2 * t], w1.at[t, pl.ds(0, half)], sems.at[3 * t]),
                pltpu.make_async_copy(w1_hbm[2 * t + 1], w1.at[t, pl.ds(half, half)], sems.at[3 * t + 1]),
                pltpu.make_async_copy(w2_hbm[t], w2.at[t], sems.at[3 * t + 2]),
            ]
        )

    @pl.when(pl.program_id(0) == 0)
    def _():
        for group in copies:
            for item in group:
                item.start()

    lane = iota(1, LANES, 1)
    signal = g_ref[:, 0].reshape(rows.shape[0], width + LANES)
    side = signal[:, width:].astype(F32)

    def column(*lanes):
        keep = lane == lanes[0]
        for other in lanes[1:]:
            keep = keep | (lane == other)
        return jnp.sum(jnp.where(keep, side, 0.0), -1, keepdims=True)

    logits = dot(rows, router_ref[...])
    lane_f = lane.astype(F32)
    mine = jnp.sum(jnp.where(lane_f == column(4), logits, 0.0), -1, keepdims=True)
    other = jnp.sum(jnp.where(lane_f == column(0), logits, 0.0), -1, keepdims=True)
    gate = 1.0 / (1.0 + jnp.exp(other - mine - column(1, 2, 3)))
    upstream = signal[:, 0:width].astype(F32)
    rows_grad = (gate * upstream).astype(BF)
    rg_ref[...] = rows_grad
    hidden_here = w1.shape[2]
    step = min(512, hidden_here)

    def wait(groups):
        @pl.when(pl.program_id(0) == 0)
        def _():
            for group in groups:
                for item in group:
                    item.wait()

    def first_products(t):
        parts = []
        for at in range(0, hidden_here, step):
            cols = slice(at, at + step)
            parts.append((at, dot(rows, w1[t, :, cols]), dot(rows_grad, w2[t, cols, :], 1, 1)))
        return parts

    wait(copies[:1])
    ready = first_products(0)
    wait(copies[1:])
    out = None
    grad = None
    for t in range(count):
        parts = ready
        if t + 1 < count:
            ready = first_products(t + 1)
        for at, hidden, active_grad in parts:
            place = slice(t * hidden_here + at, t * hidden_here + at + step)
            active, slope = gelu_parts(hidden)
            act_ref[:, place] = active.astype(BF)
            hg_ref[:, place] = (active_grad * slope).astype(BF)
        place = slice(t * hidden_here, (t + 1) * hidden_here)
        part = dot(act_ref[:, place], w2[t])
        out = part if out is None else out + part
        part = dot(hg_ref[:, place], w1[t], 1, 1)
        grad = part if grad is None else grad + part
    dx_ref[...] = grad.astype(BF)
    back_ref[...] = (gate * out).astype(BF)
    gate_grad = jnp.sum(upstream * out.astype(BF).astype(F32), -1, keepdims=True)
    lanes = up_to(slots, LANES)
    spread = iota(slots, lanes, 0) == iota(slots, lanes, 1)
    spare_row = iota(16, 1, 0) == per + 16 - slots
    for b in range(x_ref.shape[0] // slots):
        end = (b + 1) * slots
        line = jnp.sum(jnp.where(spread, gate_grad[end - slots : end], 0.0), 0, keepdims=True)
        high = line.astype(BF).astype(F32)
        line = jnp.concatenate([high, line - high, jnp.zeros((1, width - 2 * lanes), F32)], 1)
        dx_ref[end - 16 : end, :] = jnp.where(spare_row, line, grad[end - 16 : end]).astype(BF)


def expert(x, g, chunk, router, w1, w2, slots, per):
    rows, width = x.shape
    count = len(w2)
    here = w2[0].shape[0]
    total = count * here
    blocks = block_count(rows // slots, slots)
    tile = slots * blocks

    def tiled(cols):
        return pl.BlockSpec((tile, cols), lambda i: (i, 0))

    flops = 8 * rows * width * total
    return pl.pallas_call(
        functools.partial(expert_kernel, count, slots, per),
        grid=(rows // tile,),
        in_specs=[
            tiled(width),
            pl.BlockSpec((blocks, 1, slots, g.shape[3]), lambda i: (i, chunk, 0, 0)),
            whole(router.shape),
        ]
        + [pl.BlockSpec(memory_space=pl.ANY)] * (3 * count),
        out_specs=[tiled(width), tiled(total), tiled(total), tiled(width), tiled(width)],
        out_shape=[
            jax.ShapeDtypeStruct((rows, width), BF),
            jax.ShapeDtypeStruct((rows, total), BF),
            jax.ShapeDtypeStruct((rows, total), BF),
            jax.ShapeDtypeStruct((rows, width), BF),
            jax.ShapeDtypeStruct((rows, width), BF),
        ],
        scratch_shapes=[
            pltpu.VMEM((count, width, here), BF),
            pltpu.VMEM((count, here, width), BF),
            pltpu.SemaphoreType.DMA((3 * count,)),
        ],
        compiler_params=params(),
        cost_estimate=pl.CostEstimate(flops=flops, bytes_accessed=rows * total * 6, transcendentals=rows * total * 2),
        name="expert",
    )(x, g, router, *w1, *w2)


def weight_kernel(count, steps, *refs):
    ins, outs = refs[: 2 * count], refs[2 * count :]
    total = None
    for n in range(count):
        part = dot(ins[2 * n][...], ins[2 * n + 1][...], 0, 0)
        total = part if total is None else total + part
    store_piece(outs, steps, total.astype(BF))


def weight_grad(columns, rows, first, here):
    count = len(columns)
    width = rows[0].shape[1]
    step = min(512, here)
    steps = here // step
    offset = first * steps
    specs, args = [], []
    for a, b in zip(columns, rows):
        specs += [pl.BlockSpec((a.shape[0], step), lambda i: (0, i + offset)), whole(b.shape, True)]
        args += [a, b]
    out_specs, out_shape = by_piece(2, steps, (step, width), (here, width), BF)
    return pl.pallas_call(
        functools.partial(weight_kernel, count, steps),
        grid=(2 * steps,),
        in_specs=specs,
        out_specs=out_specs,
        out_shape=out_shape,
        compiler_params=params(),
        cost_estimate=cost(4 * sum(b.shape[0] for b in rows) * width * here, 8 * here * width),
        name="weight_grad",
    )(*args)


def shards(
    block_in,
    norm_one,
    head_in,
    head_out,
    norm_two,
    router,
    expert_in,
    expert_out,
    expert_ids,
    route_noise,
    cotangent,
):
    rows_here, width = block_in.shape
    parts = lax.axis_size("tensor")
    groups = lax.axis_size("expert")
    me = lax.axis_index("tensor")
    images = rows_here // SEQ
    height = up_to(SEQ, 16)
    each = up_to(-(-rows_here // parts), 16)
    experts = router.shape[1]
    capacity = (rows_here * 2 * 8 // (5 * experts) + 15) // 16 * 16
    share = -(-capacity // parts)
    per = -(-share // CHUNKS)
    slots = up_to(per + 1, 16)
    chunk_rows = experts * slots
    full = rows_here // 16 * 16
    here = expert_out.shape[1]

    paired = parts == 4
    order = (0, 2, 1, 3) if paired else tuple(range(parts))
    part_of = jnp.stack([me ^ k if paired else jnp.int32(k) for k in order]).astype(jnp.int32)
    starts = part_of * each
    own_block = (me * (each // half_tile(each)))[None].astype(jnp.int32)

    def cross(x, k):
        return lax.ppermute(x, "tensor", [(n, n ^ k) for n in range(parts)])

    def far_part(x):
        return cross(x, 2) if paired else x

    def gathered_from(x, far):
        if not paired:
            every = lax.all_gather(x, "tensor", axis=0, tiled=False)
            return [every[p] for p in range(parts)]
        return [x, far, cross(x, 1), cross(far, 1)]

    def gathered(x):
        return gathered_from(x, far_part(x))

    def near_hop(pieces):
        return pinned(*[cross(piece, 1) for piece in pieces[2:]]) if paired else pieces

    def near_sum(pieces, came):
        if not paired:
            return lax.psum_scatter(jnp.stack(pieces), "tensor", scatter_dimension=0), None
        kept, other = ((a.astype(F32) + b.astype(F32)).astype(BF) for a, b in zip(pieces, came))
        return kept, other

    def far_hop(kept, other):
        return cross(other, 2) if paired else jnp.zeros_like(kept)

    def far_tile(kept, other, n, tile):
        if not paired:
            return jnp.zeros_like(kept[n * tile : (n + 1) * tile])
        return cross(other[n * tile : (n + 1) * tile], 2)

    def after(x, *items):
        return x if x is None else pinned(x, *items)[0]

    def scattered(pieces):
        kept, other = near_sum(pieces, near_hop(pieces))
        return kept, far_hop(kept, other)

    def swapped(pieces):
        if not paired:
            every = lax.all_to_all(jnp.stack(pieces), "tensor", split_axis=0, concat_axis=0, tiled=True)
            return [every[p] for p in range(parts)]
        return [cross(piece, k) if k else piece for piece, k in zip(pieces, order)]

    def over_experts(x):
        return lax.all_to_all(x, "expert", split_axis=0, concat_axis=0, tiled=True)

    def pinned(*items):
        return lax.optimization_barrier(items)

    def tail_of(x):
        return jnp.pad(x[full:], ((0, 16 - (rows_here - full)), (0, 0)))

    names = jnp.arange(experts, dtype=jnp.int32)
    member = [(expert_ids[:, c : c + 1] == names).astype(jnp.int32) for c in range(2)]
    both = member[0] + member[1]
    earlier = jnp.cumsum(both, 0) - both
    slot = jnp.stack([jnp.sum(earlier * item, -1) for item in member], 1)
    local = slot - me * share
    place = local // per * chunk_rows + expert_ids * slots + local % per
    place = jnp.where((local >= 0) & (local < share), place, -1)
    place = jnp.pad(place, ((0, each * parts - rows_here), (0, 0)), constant_values=-1)
    place_lanes = place.T
    place_parts = jnp.swapaxes(place_lanes.reshape(2, parts, each), 0, 1)

    sides = []
    for c in range(2):
        gap = route_noise[:, c] - route_noise[:, 1 - c]
        high = gap.astype(BF)
        left = gap - high.astype(F32)
        mid = left.astype(BF)
        low = (left - mid.astype(F32)).astype(BF)
        columns = [expert_ids[:, 1 - c].astype(BF), high, mid, low, expert_ids[:, c].astype(BF)]
        sides.append(jnp.stack(columns, 1))
    side = jnp.pad(jnp.stack(sides), ((0, 0), (0, each * parts - rows_here), (0, LANES - 5)))

    router_wide = jnp.pad(router, ((0, 0), (0, LANES - experts)))
    gain_one, gain_two = norm_one[None, :], norm_two[None, :]
    head_out_far = far_part(head_out)
    w1_own = [expert_in[0, : width // 2], expert_in[0, width // 2 :]]
    w1_far = [far_part(item) for item in w1_own]

    packed = pack_first(cotangent, tail_of(cotangent), place_lanes, side, experts, slots)
    block_rows, packed, w1_far[0] = pinned(block_in, packed, w1_far[0])
    signal = over_experts(packed)

    first_in, qkv, logs, *mixed = attend(
        starts, block_rows, tail_of(block_in), gain_one, head_in, images, height, each, parts
    )
    *mixed, w1_far[1], head_out_far = pinned(*mixed, w1_far[1], head_out_far)
    head_out_all = gathered_from(head_out, head_out_far)
    mixed = swapped(mixed)
    middle, second_in, gates = middle_of(
        own_block, mixed, head_out_all, block_in, gain_two, router_wide, expert_ids, route_noise
    )
    *second_all, late_out = pinned(*gathered(second_in), expert_out[0])
    w1 = [gathered_from(a, b) for a, b in zip(w1_own, w1_far)]
    w1 = [w1[h][p] for p in range(parts) for h in range(2)]

    def packed_rows(n):
        return pack(part_of, second_all, place_parts, experts, slots, n * chunk_rows)

    def sent(x):
        return over_experts(x.reshape(experts, slots, width)).reshape(chunk_rows, width)

    x = sent(packed_rows(0))
    w2_far, head_in_t, signal, *outgoing = pinned(
        far_part(late_out), jnp.swapaxes(head_in, 1, 2), signal, *[packed_rows(n) for n in range(1, CHUNKS)]
    )
    w2 = gathered_from(expert_out[0], w2_far)
    backs, actives, hidden_grads, rows_grads, arrived, returned = [], [], [], [], [], []
    for n in range(CHUNKS):
        coming = None
        if n + 1 < CHUNKS:
            x, ready = pinned(x, outgoing[n])
            coming = sent(ready)
        if n == 0:
            x, *ready = pinned(x, *w1, *w2)
            w1, w2 = ready[: 2 * parts], ready[2 * parts :]
        back, active, hidden_grad, rows_grad, row_grad = expert(
            x, signal, n, router_wide, w1, w2, slots, per
        )
        if returned:
            row_grad, active, returned[-1] = pinned(row_grad, active, returned[-1])
        arrived.append(x)
        actives.append(active)
        hidden_grads.append(hidden_grad)
        rows_grads.append(rows_grad)
        backs.append(back)
        if coming is not None:
            x, row_grad = pinned(coming, row_grad)
        returned.append(sent(row_grad))

    def weight_parts(columns, rows):
        pairs = [weight_grad(columns, rows, p, here) for p in range(parts - 2, -1, -2)]
        return [item for pair in pairs[::-1] for item in pair]

    out_parts = weight_parts(actives, rows_grads)
    out_kept, out_other = near_sum(out_parts, near_hop(out_parts))
    quarter = here // 4
    tile = half_tile(each)
    tiles = each // tile
    out_far = [far_tile(out_kept, out_other, n, quarter) for n in range(2)]
    *returned, out_kept, out_far[0] = pinned(*returned, out_kept, out_far[0])

    second_pieces = unpack(part_of, place, returned, slots, per, each, True)
    *second_pieces, out_far[1] = pinned(*second_pieces, out_far[1])
    out_far += [far_tile(out_kept, out_other, n, quarter) for n in range(2, 4)]
    second_kept, second_other = near_sum(second_pieces, near_hop(second_pieces))
    second_kept, out_far[2] = pinned(second_kept, out_far[2])
    second_other = after(second_other, second_kept)
    *hidden_grads, second_kept = pinned(*hidden_grads, second_kept)
    second_far = [far_tile(second_kept, second_other, n, tile) for n in range(tiles)]
    in_parts = []
    for p in range(parts - 2, -1, -2):
        *hidden_grads, pair = pinned(*hidden_grads, weight_grad(hidden_grads, arrived, p, here))
        in_parts = list(pair) + in_parts
        if p == parts - 2:
            in_came = near_hop([None] * p + list(pair)) if paired else ()
            second_far[0], out_far[3], pair = pinned(second_far[0], out_far[3], pair)
    in_kept, in_other = near_sum(in_parts, in_came)
    second_far[-1], in_kept = pinned(second_far[-1], in_kept)
    in_other = after(in_other, in_kept)
    in_far = [far_tile(in_kept, in_other, 0, quarter)]
    combined = [sent(item) for item in backs]
    middle_grad, router_part, norm_two_part, *pieces = middle_back(
        own_block, second_kept, second_far, middle, second_in, gates, expert_ids, cotangent, mixed, head_out_all,
        gain_two, router_wide,
    )
    head_out_parts, mixed_grad = pieces[:parts], pieces[parts:]
    *mixed_grad, combined[0], in_far[0] = pinned(*mixed_grad, combined[0], in_far[0])
    mixed_grad = swapped(mixed_grad)
    head_out_kept, head_out_far = scattered(head_out_parts)
    in_other = after(in_other, *mixed_grad)
    in_far += [far_tile(in_kept, in_other, n, quarter) for n in (1, 2)]
    *pieces, head_in_part, norm_one_part = attend_back(
        starts, mixed_grad, qkv, logs, first_in, head_in_t, gain_one
    )
    *pieces, combined[-1], in_far[1], in_far[2], head_out_far = pinned(
        *pieces, combined[-1], in_far[1], in_far[2], head_out_far
    )
    first_kept, first_other = near_sum(pieces, near_hop(pieces))
    first_kept, head_in_part, head_out_far, *combined = pinned(first_kept, head_in_part, head_out_far, *combined)
    first_other = after(first_other, first_kept)
    first_far = [far_tile(first_kept, first_other, n, tile) for n in range(tiles)]
    block_pieces = unpack(part_of, place, combined, slots, per, each, False)
    first_far, block_pieces = pinned(first_far, block_pieces)
    in_far.append(far_tile(in_kept, after(in_other, block_pieces[0]), 3, quarter))
    block_kept, block_other = near_sum(block_pieces, near_hop(block_pieces))
    input_part = input_back(own_block, first_kept, first_far, block_in, middle_grad, gain_one)
    input_part, block_kept, in_far[3] = pinned(input_part, block_kept, in_far[3])
    block_far = far_hop(block_kept, after(block_other, block_kept))
    out_grad = sum_far(out_kept, out_far, False)
    in_grad = sum_far(in_kept, in_far, True)
    input_far, out_grad, in_grad, block_far = pinned(far_part(input_part), out_grad, in_grad, block_far)
    block_own = (middle + block_kept.astype(F32) + block_far.astype(F32)).astype(BF)

    cols = head_in.shape[2]
    head_out_part = (head_out_kept.astype(F32) + head_out_far.astype(F32)).astype(BF)
    small = jnp.concatenate([norm_one_part, norm_two_part, router_part[:experts]], 0).astype(BF)
    count = 4 * cols + 2 + experts
    total = up_to(count, 16 * groups)
    heads = jnp.concatenate(
        [head_in_part.reshape(3 * cols, width), head_out_part, jnp.pad(small, ((0, total - count), (0, 0)))], 0
    )
    heads = over_experts(heads.reshape(groups, total // groups, width))
    heads, input_part = pinned(heads, input_part)
    input_grad = assemble(part_of, gathered_from(input_part, input_far), rows_here, F32)
    block_out = assemble(part_of, gathered(block_own), rows_here, BF)
    heads = jnp.sum(heads.astype(F32), 0).astype(BF)
    heads = lax.all_gather(heads, "expert", axis=0, tiled=True)
    head_in_grad = jnp.swapaxes(heads[: 3 * cols].reshape(3, cols, width), 1, 2).astype(F32)
    head_out_grad = heads[3 * cols : 4 * cols].astype(F32)
    small = heads[4 * cols : count].astype(F32)
    if paired:
        small = small + cross(small, 1)
        small = small + cross(small, 2)
    else:
        small = lax.psum(small, "tensor")
    return (
        block_out,
        input_grad,
        small[0],
        head_in_grad,
        head_out_grad,
        small[1],
        small[2:].T,
        in_grad[None],
        out_grad[None],
    )


def solution(mesh):
    in_specs = (
        P("expert", None),
        P(),
        P(None, None, "tensor"),
        P("tensor", None),
        P(),
        P(),
        P("expert", None, "tensor"),
        P("expert", "tensor", None),
        P("expert", None),
        P("expert", None),
        P("expert", None),
    )
    out_specs = (
        P("expert", None),
        P("expert", None),
        P(),
        P(None, None, "tensor"),
        P("tensor", None),
        P(),
        P(),
        P("expert", None, "tensor"),
        P("expert", "tensor", None),
    )
    return jax.shard_map(shards, mesh=mesh, in_specs=in_specs, out_specs=out_specs, check_vma=False)
```

```python
import functools

import jax
import jax.numpy as jnp
from jax import lax
from jax.experimental import pallas as pl
from jax.experimental.pallas import tpu as pltpu
from jax.sharding import PartitionSpec as P

HD = 64
SEQ = 197
LANES = 128
EPSILON = 1e-06
CHUNKS = 2
BF = jnp.bfloat16
F32 = jnp.float32


def up_to(value, unit):
    return -(-value // unit) * unit


def params(mib=60):
    return pltpu.CompilerParams(vmem_limit_bytes=mib * 1024 * 1024)


def dot(a, b, da=1, db=0):
    return lax.dot_general(a, b, (((da,), (db,)), ((), ())), preferred_element_type=F32)


def iota(rows, cols, dim):
    return lax.broadcasted_iota(jnp.int32, (rows, cols), dim)


def flag(mask):
    return jnp.where(mask, 1.0, 0.0)


def whole(shape, once=False):
    zeros = (0,) * len(shape)
    mode = pl.Buffered(1) if once else None
    return pl.BlockSpec(shape, lambda *_: zeros, pipeline_mode=mode)


def image(*shape):
    return pl.BlockSpec((1,) + shape, lambda i, *_: (i,) + (0,) * len(shape))


def fill(x_ref, tail_ref, rows_ref):
    full = x_ref.shape[0] // 16 * 16
    rows_ref[0:full, :] = x_ref[0:full, :]
    rows_ref[full : full + 16, :] = tail_ref[...]
    rest = rows_ref.shape[0] - full - 16
    if rest:
        rows_ref[full + 16 :, :] = jnp.zeros((rest, rows_ref.shape[1]), BF)


def norm_parts(field):
    centre = field - jnp.mean(field, -1, keepdims=True)
    spread = lax.rsqrt(jnp.mean(centre * centre, -1, keepdims=True) + EPSILON)
    return centre * spread, spread


def norm_field_back(upstream, gain, scaled, spread):
    weighted = upstream * gain
    return spread * (
        weighted
        - jnp.mean(weighted, -1, keepdims=True)
        - scaled * jnp.mean(weighted * scaled, -1, keepdims=True)
    )


def cost(flops, size):
    return pl.CostEstimate(flops=flops, bytes_accessed=size, transcendentals=0)


def by_piece(count, steps, block, shape, dtype):
    def spec(p):
        def place(i, *_):
            return (jnp.clip(i - p * steps, 0, steps - 1), 0)

        return pl.BlockSpec(block, place)

    return [spec(p) for p in range(count)], [jax.ShapeDtypeStruct(shape, dtype)] * count


def store_piece(refs, steps, value):
    for p, ref in enumerate(refs):

        @pl.when(pl.program_id(0) // steps == p)
        def _():
            ref[...] = value


def rows_spec(tile, width):
    return pl.BlockSpec((tile, width), lambda i, *_: (i, 0))


def own_spec(tile, width):
    return pl.BlockSpec((tile, width), lambda i, at: (at[0] + i, 0))


def window_of(i, height, back=False):
    start = i * SEQ
    aligned = start // 16 * 16
    window = height + 16
    shape = (window, height) if back else (height, window)
    r, c = iota(*shape, 1 if back else 0), iota(*shape, 0 if back else 1)
    match = flag((c == r + (start - aligned)) & (r < SEQ)).astype(BF)
    return match, pl.ds(pl.multiple_of(aligned, 16), window)


def head_masks():
    lane = iota(1, LANES, 1)
    return [(flag(lane // HD == h)).astype(BF) for h in range(2)]


def attend_kernel(count, starts_ref, x_ref, tail_ref, gain_ref, w_ref, first_ref, qkv_ref, log_ref, *refs):
    piece_refs, rows, mixed = refs[:count], refs[count], refs[count + 1]
    i = pl.program_id(0)
    height = first_ref.shape[1]
    cols = mixed.shape[1]

    @pl.when(i == 0)
    def _():
        fill(x_ref, tail_ref, rows)
        mixed[...] = jnp.zeros_like(mixed)

    match, place = window_of(i, height)
    field = dot(match, rows[place, :])
    scaled, _ = norm_parts(field)
    first = (scaled * gain_ref[...]).astype(BF)
    first_ref[0] = first
    for k in range(3):
        qkv_ref[k, 0] = dot(first, w_ref[k]).astype(BF)
    masks = head_masks()
    lane = iota(1, LANES, 1)
    key_lane = iota(1, height, 1)
    logs = jnp.zeros((height, LANES), F32)
    back, _ = window_of(i, height, True)
    for pair in range(cols // LANES):
        part = slice(pair * LANES, (pair + 1) * LANES)
        queries, keys, values = (qkv_ref[k, 0, :, part] for k in range(3))
        total = jnp.zeros((height, LANES), F32)
        for h in range(2):
            scores = dot(queries * masks[h], keys, 1, 1) * HD ** (-0.5)
            scores = jnp.where(key_lane < SEQ, scores, -1e30)
            highest = jnp.max(scores, -1, keepdims=True)
            weights = jnp.exp(scores - highest)
            sums = jnp.sum(weights, -1, keepdims=True)
            probs = (weights * (1.0 / sums)).astype(BF)
            total += dot(probs, values * masks[h])
            logs = jnp.where(lane == pair * 2 + h, highest + jnp.log(sums), logs)
        mixed[place, part] = (mixed[place, part].astype(F32) + dot(back, total.astype(BF))).astype(BF)
    log_ref[0] = logs

    @pl.when(i == pl.num_programs(0) - 1)
    def _():
        for p in range(count):
            at = pl.multiple_of(starts_ref[p], 16)
            piece_refs[p][...] = mixed[pl.ds(at, piece_refs[p].shape[0]), :]


def attend(starts, block_in, tail, gain, head_in, images, height, each, count):
    rows, width = block_in.shape
    cols = head_in.shape[2]
    scratch_rows = max(rows // 16 * 16 + 48, each * count)
    spec = pltpu.PrefetchScalarGridSpec(
        num_scalar_prefetch=1,
        grid=(images,),
        in_specs=[whole((rows, width), True), whole((16, width)), whole((1, width)), whole(head_in.shape, True)],
        out_specs=[
            image(height, width),
            pl.BlockSpec((3, 1, height, cols), lambda i, *_: (0, i, 0, 0)),
            image(height, LANES),
        ]
        + [whole((each, cols))] * count,
        scratch_shapes=[pltpu.VMEM((scratch_rows, width), BF), pltpu.VMEM((scratch_rows, cols), BF)],
    )
    return pl.pallas_call(
        functools.partial(attend_kernel, count),
        grid_spec=spec,
        out_shape=[
            jax.ShapeDtypeStruct((images, height, width), BF),
            jax.ShapeDtypeStruct((3, images, height, cols), BF),
            jax.ShapeDtypeStruct((images, height, LANES), F32),
        ]
        + [jax.ShapeDtypeStruct((each, cols), BF)] * count,
        compiler_params=params(),
        cost_estimate=cost(16 * images * height * width * cols, 16 * rows * width),
        name="attend",
    )(starts, block_in, tail, gain, head_in)


def attend_back_kernel(count, starts_ref, qkv_ref, log_ref, first_ref, wt_ref, gain_ref, *refs):
    dmix_refs, piece_refs = refs[:count], refs[count : 2 * count]
    hg_ref, ng_ref, acc, grads, dmix, field = refs[2 * count :]
    i = pl.program_id(0)
    height = first_ref.shape[1]
    each = dmix_refs[0].shape[0]

    @pl.when(i == 0)
    def _():
        acc[...] = jnp.zeros_like(acc)
        field[...] = jnp.zeros_like(field)
        rest = dmix.shape[0] - each * count
        if rest:
            dmix[each * count :, :] = jnp.zeros((rest, dmix.shape[1]), BF)
        for p in range(count):
            dmix[pl.ds(pl.multiple_of(starts_ref[p], 16), each), :] = dmix_refs[p][...]

    match, place = window_of(i, height)
    back, _ = window_of(i, height, True)
    out_grads = dot(match, dmix[place, :]).astype(BF)
    masks = head_masks()
    lane = iota(1, LANES, 1)
    key_lane = iota(1, height, 1)
    scale = HD ** (-0.5)
    logs = log_ref[0]
    for pair in range(dmix.shape[1] // LANES):
        cols = slice(pair * LANES, (pair + 1) * LANES)
        queries, keys, values = (qkv_ref[k, 0, :, cols] for k in range(3))
        out_grad = out_grads[:, cols]
        dq = jnp.zeros((height, LANES), F32)
        dk = jnp.zeros((height, LANES), F32)
        dv = jnp.zeros((height, LANES), F32)
        for h in range(2):
            q_h = queries * masks[h]
            o_h = out_grad * masks[h]
            log_h = jnp.sum(jnp.where(lane == pair * 2 + h, logs, 0.0), -1, keepdims=True)
            probs = jnp.exp(dot(q_h, keys, 1, 1) * scale - log_h)
            probs = jnp.where(key_lane < SEQ, probs, 0.0)
            prob_grad = dot(o_h, values, 1, 1)
            dv += dot(probs.astype(BF), o_h, 0, 0)
            delta = jnp.sum(probs * prob_grad, -1, keepdims=True)
            score_grad = (probs * (prob_grad - delta)).astype(BF)
            dq += dot(score_grad, keys * masks[h])
            dk += dot(score_grad, q_h, 0, 0)
        grads[0, :, cols] = (dq * scale).astype(BF)
        grads[1, :, cols] = (dk * scale).astype(BF)
        grads[2, :, cols] = dv.astype(BF)

    first = first_ref[0]
    total = None
    for k in range(3):
        part = dot(grads[k], wt_ref[k])
        total = part if total is None else total + part
        acc[k] += dot(grads[k], first, 0, 0)
    field[place, :] = (field[place, :].astype(F32) + dot(back, total.astype(BF))).astype(BF)

    @pl.when(i == pl.num_programs(0) - 1)
    def _():
        for p in range(count):
            piece_refs[p][...] = field[pl.ds(pl.multiple_of(starts_ref[p], 16), each), :]
        hg_ref[...] = acc[...].astype(BF)
        gain_grad = jnp.zeros_like(ng_ref)
        for k in range(3):
            gain_grad += jnp.sum(acc[k] * wt_ref[k].astype(F32), 0, keepdims=True)
        ng_ref[...] = gain_grad / gain_ref[...]


def attend_back(starts, dmix, qkv, logs, first, head_in_t, gain):
    images, height, width = first.shape
    each, cols = dmix[0].shape
    count = len(dmix)
    scratch_rows = max(images * SEQ // 16 * 16 + 48, each * count)
    spec = pltpu.PrefetchScalarGridSpec(
        num_scalar_prefetch=1,
        grid=(images,),
        in_specs=[
            pl.BlockSpec((3, 1, height, cols), lambda i, *_: (0, i, 0, 0)),
            image(height, LANES),
            image(height, width),
            whole(head_in_t.shape, True),
            whole((1, width)),
        ]
        + [whole((each, cols), True)] * count,
        out_specs=[whole((each, width))] * count + [whole(head_in_t.shape), whole((1, width))],
        scratch_shapes=[
            pltpu.VMEM(head_in_t.shape, F32),
            pltpu.VMEM((3, height, cols), BF),
            pltpu.VMEM((scratch_rows, cols), BF),
            pltpu.VMEM((scratch_rows, width), BF),
        ],
    )
    return pl.pallas_call(
        functools.partial(attend_back_kernel, count),
        grid_spec=spec,
        out_shape=[jax.ShapeDtypeStruct((each, width), BF)] * count
        + [jax.ShapeDtypeStruct(head_in_t.shape, BF), jax.ShapeDtypeStruct((1, width), F32)],
        compiler_params=params(),
        cost_estimate=cost(24 * images * height * width * cols, 20 * images * height * width),
        name="attend_back",
    )(starts, qkv, logs, first, head_in_t, gain, *dmix)


def block_count(blocks, slots):
    return max(n for n in range(1, blocks + 1) if blocks % n == 0 and n * slots <= 448)


def pack_first_kernel(x_ref, tail_ref, lp_ref, side_ref, out_ref, rows):
    i, n = pl.program_id(0), pl.program_id(1)

    @pl.when((i == 0) & (n == 0))
    def _():
        fill(x_ref, tail_ref, rows)

    blocks, _, slots, _ = out_ref.shape
    tile = blocks * slots
    j = (n * pl.num_programs(0) + i) * tile + iota(tile, rows.shape[0], 0)
    picks = [flag(lp_ref[c : c + 1, :] == j) for c in range(2)]
    width = x_ref.shape[1]
    main = dot((picks[0] + picks[1]).astype(BF), rows[...]).astype(BF)
    out_ref[:, 0, :, 0:width] = main.reshape(blocks, slots, width)
    extra = dot(picks[0].astype(BF), side_ref[0]) + dot(picks[1].astype(BF), side_ref[1])
    out_ref[:, 0, :, width:] = extra.astype(BF).reshape(blocks, slots, LANES)


def pack_first(x, tail, lp, side, experts, slots):
    rows, width = x.shape
    padded = lp.shape[1]
    blocks = block_count(experts, slots)
    return pl.pallas_call(
        pack_first_kernel,
        grid=(experts // blocks, CHUNKS),
        in_specs=[whole((rows, width), True), whole((16, width)), whole(lp.shape), whole(side.shape)],
        out_specs=pl.BlockSpec((blocks, 1, slots, width + LANES), lambda i, n: (i, n, 0, 0)),
        out_shape=jax.ShapeDtypeStruct((experts, CHUNKS, slots, width + LANES), BF),
        scratch_shapes=[pltpu.VMEM((padded, width), BF)],
        compiler_params=params(),
        cost_estimate=cost(3 * CHUNKS * experts * slots * padded * width, 2 * rows * width),
        name="pack_cotangent",
    )(x, tail, lp, side)


def pack_kernel(base, count, part_ref, *refs):
    lp_ref, out_ref = refs[count], refs[count + 1]
    total = None
    tile = out_ref.shape[0]
    for p in range(count):
        j = base + pl.program_id(0) * tile + iota(tile, refs[p].shape[0], 0)
        lp = lp_ref[part_ref[p]]
        picks = flag((lp[0:1, :] == j) | (lp[1:2, :] == j)).astype(BF)
        part = dot(picks, refs[p][...])
        total = part if total is None else total + part
    out_ref[...] = total.astype(BF)


def pack(part_of, pieces, lp, experts, slots, base):
    rows, width = pieces[0].shape
    count = len(pieces)
    tile = slots * block_count(experts, slots)
    spec = pltpu.PrefetchScalarGridSpec(
        num_scalar_prefetch=1,
        grid=(experts * slots // tile,),
        in_specs=[whole((rows, width), True)] * count + [whole(lp.shape)],
        out_specs=rows_spec(tile, width),
    )
    return pl.pallas_call(
        functools.partial(pack_kernel, base, count),
        grid_spec=spec,
        out_shape=jax.ShapeDtypeStruct((experts * slots, width), BF),
        compiler_params=params(),
        cost_estimate=cost(3 * experts * slots * rows * count * width, 2 * rows * count * width),
        name="pack_rows",
    )(part_of, *pieces, lp)


def unpack_kernel(count, slots, per, graded, part_ref, lp_ref, *refs):
    row_refs, out_refs = refs[:count], refs[count:]
    lp = lp_ref[...]
    height = lp.shape[0]
    rows, width = row_refs[0].shape
    total = jnp.zeros((height, width), F32)
    lanes = up_to(slots, LANES)
    extra = [jnp.zeros((height, lanes), F32) for _ in range(2)]
    for n in range(count):
        j = n * rows + iota(1, rows, 1)
        hits = (lp[:, 0:1] == j) | (lp[:, 1:2] == j)
        total += dot(flag(hits).astype(BF), row_refs[n][...])
        if graded:
            j = iota(1, lanes, 1)
            for e in range(rows // slots):
                spare = row_refs[n][(e + 1) * slots - 16 : (e + 1) * slots, 0 : 2 * lanes].astype(F32)
                spare = spare[per + 16 - slots : per + 17 - slots, :]
                values = spare[:, :lanes] + spare[:, lanes:]
                for c in range(2):
                    hit = lp[:, c : c + 1] - (n * rows + e * slots) == j
                    extra[c] += jnp.where(hit, values, 0.0)
    value = total.astype(BF)
    if graded:
        lane = iota(1, LANES, 1)
        tail = jnp.zeros((height, LANES), F32)
        for c in range(2):
            grad = jnp.sum(extra[c], -1, keepdims=True)
            high = grad.astype(BF).astype(F32)
            tail = jnp.where(lane == c, high, tail)
            tail = jnp.where(lane == 2 + c, grad - high, tail)
        value = jnp.concatenate([value, tail.astype(BF)], 1)
    store_piece(out_refs, 1, value)


def unpack(part_of, lp, rows, slots, per, each, graded):
    parts = lp.shape[0] // each
    count = len(rows)
    width = rows[0].shape[1] + (LANES if graded else 0)
    out_specs, out_shape = by_piece(parts, 1, (each, width), (each, width), BF)
    spec = pltpu.PrefetchScalarGridSpec(
        num_scalar_prefetch=1,
        grid=(parts,),
        in_specs=[pl.BlockSpec((each, 2), lambda i, at: (at[i], 0))] + [whole(item.shape, True) for item in rows],
        out_specs=out_specs,
    )
    return pl.pallas_call(
        functools.partial(unpack_kernel, count, slots, per, graded),
        grid_spec=spec,
        out_shape=out_shape,
        compiler_params=params(),
        cost_estimate=cost(3 * lp.shape[0] * count * rows[0].size, 4 * count * rows[0].size),
        name="unpack_rows",
    )(part_of, lp, *rows)


def assemble_kernel(count, steps, part_ref, *refs):
    out_ref = refs[count]
    for p in range(count):

        @pl.when(pl.program_id(0) // steps == p)
        def _():
            out_ref[...] = refs[p][...].astype(out_ref.dtype)


def assemble(part_of, pieces, rows, dtype):
    each, width = pieces[0].shape
    count = len(pieces)
    tile, steps = each, 1
    in_specs, _ = by_piece(count, steps, (tile, width), (each, width), BF)
    spec = pltpu.PrefetchScalarGridSpec(
        num_scalar_prefetch=1,
        grid=(count * steps,),
        in_specs=in_specs,
        out_specs=pl.BlockSpec((tile, width), lambda i, at: (at[i // steps] * steps + i % steps, 0)),
    )
    return pl.pallas_call(
        functools.partial(assemble_kernel, count, steps),
        grid_spec=spec,
        out_shape=jax.ShapeDtypeStruct((rows, width), dtype),
        compiler_params=params(),
        cost_estimate=cost(2 * rows * width, 8 * rows * width),
        name="assemble",
    )(part_of, *pieces)


def of_tiles(refs):
    value = refs[0][...].astype(F32)
    for n, ref in enumerate(refs[1:]):
        value = jnp.where(pl.program_id(0) > n, ref[...].astype(F32), value)
    return value


def sum_far_kernel(turned, *refs):
    far_refs, keep_ref, out_ref = refs[:-2], refs[-2], refs[-1]
    total = keep_ref[...].astype(F32) + of_tiles(far_refs)
    out_ref[...] = total.T if turned else total


def sum_far(keep, far, turned):
    rows, width = keep.shape
    tile = rows // len(far)
    return pl.pallas_call(
        functools.partial(sum_far_kernel, turned),
        grid=(len(far),),
        in_specs=[whole((tile, width))] * len(far) + [rows_spec(tile, width)],
        out_specs=pl.BlockSpec((width, tile), lambda i: (0, i)) if turned else rows_spec(tile, width),
        out_shape=jax.ShapeDtypeStruct((width, rows) if turned else (rows, width), F32),
        compiler_params=params(),
        cost_estimate=cost(rows * width, 8 * rows * width),
        name="sum_far",
    )(*far, keep)


def middle_kernel(count, limit, at_ref, *refs):
    mixed_refs, wo_refs = refs[:count], refs[count : 2 * count]
    x_ref, gain_ref, router_ref, ids_ref, noise_ref, mid_ref, second_ref, gates_ref = refs[2 * count :]
    tile = x_ref.shape[0]
    valid = (at_ref[0] + pl.program_id(0)) * tile + iota(tile, 1, 0) < limit
    middle = jnp.where(valid, x_ref[...].astype(F32), 0.0)
    for mixed_ref, wo_ref in zip(mixed_refs, wo_refs):
        middle += dot(mixed_ref[...], wo_ref[...])
    mid_ref[...] = middle
    scaled, _ = norm_parts(middle)
    second = (scaled * gain_ref[...]).astype(BF)
    second_ref[...] = second
    logits = dot(second, router_ref[...])
    lane = iota(1, LANES, 1)
    chosen = [
        jnp.sum(jnp.where(lane == ids_ref[:, c : c + 1], logits, 0.0), -1, keepdims=True)
        + noise_ref[:, c : c + 1]
        for c in range(2)
    ]
    top = jnp.maximum(chosen[0], chosen[1])
    raw = [jnp.exp(item - top) for item in chosen]
    inverse = 1.0 / (raw[0] + raw[1])
    gates = jnp.where(lane == 0, raw[0] * inverse, 0.0) + jnp.where(lane == 1, raw[1] * inverse, 0.0)
    gates_ref[...] = jnp.where(valid, gates, 0.0)


def half_tile(each):
    return each // 2 if each % 32 == 0 else each


def middle_of(at, mixed, head_out, x, gain, router, ids, noise):
    each, cols = mixed[0].shape
    parts = len(mixed)
    rows, width = x.shape
    tile = half_tile(each)
    spec = pltpu.PrefetchScalarGridSpec(
        num_scalar_prefetch=1,
        grid=(each // tile,),
        in_specs=[rows_spec(tile, cols)] * parts
        + [whole((cols, width), True)] * parts
        + [
            own_spec(tile, width),
            whole((1, width)),
            whole(router.shape),
            own_spec(tile, 2),
            own_spec(tile, 2),
        ],
        out_specs=[rows_spec(tile, width), rows_spec(tile, width), rows_spec(tile, LANES)],
    )
    return pl.pallas_call(
        functools.partial(middle_kernel, parts, rows),
        grid_spec=spec,
        out_shape=[
            jax.ShapeDtypeStruct((each, width), F32),
            jax.ShapeDtypeStruct((each, width), BF),
            jax.ShapeDtypeStruct((each, LANES), F32),
        ],
        compiler_params=params(),
        cost_estimate=cost(4 * each * width * width, 24 * each * width),
        name="middle",
    )(at, *mixed, *head_out, x, gain, router, ids, noise)


def middle_back_kernel(count, limit, tiles, at_ref, *refs):
    far_refs, refs = refs[:tiles], refs[tiles:]
    keep_ref, mid_ref, second_ref, gates_ref, ids_ref, up_ref, gain_ref, router_ref = refs[:8]
    mixed_refs, wo_refs = refs[8 : 8 + count], refs[8 + count : 8 + 2 * count]
    mg_ref, rg_ref, ng_ref = refs[8 + 2 * count : 11 + 2 * count]
    hog_refs, dmix_refs, hog_acc = refs[11 + 2 * count : 11 + 3 * count], refs[11 + 3 * count : -1], refs[-1]
    i = pl.program_id(0)

    @pl.when(i == 0)
    def _():
        hog_acc[...] = jnp.zeros_like(hog_acc)
        rg_ref[...] = jnp.zeros_like(rg_ref)
        ng_ref[...] = jnp.zeros_like(ng_ref)

    tile, width = up_ref.shape
    valid = (at_ref[0] + i) * tile + iota(tile, 1, 0) < limit
    lane = iota(1, LANES, 1)
    both = keep_ref[...].astype(F32) + of_tiles(far_refs)
    tail = both[:, width:]
    gates = gates_ref[...]
    gate, grad = [], []
    for c in range(2):
        gate.append(jnp.sum(jnp.where(lane == c, gates, 0.0), -1, keepdims=True))
        grad.append(jnp.sum(jnp.where((lane == c) | (lane == 2 + c), tail, 0.0), -1, keepdims=True))
    mean_term = gate[0] * grad[0] + gate[1] * grad[1]
    logit_grad = jnp.zeros((tile, LANES), F32)
    for c in range(2):
        hit = (lane == ids_ref[:, c : c + 1]) & valid
        logit_grad = jnp.where(hit, gate[c] * (grad[c] - mean_term), logit_grad)
    logit_grad = logit_grad.astype(BF)
    second_grad = both[:, 0:width] + dot(logit_grad, router_ref[...], 1, 1)
    rg_ref[...] += dot(logit_grad, second_ref[...], 0, 0)
    scaled, spread = norm_parts(mid_ref[...])
    ng_ref[...] += jnp.sum(second_grad * scaled, 0, keepdims=True)
    upstream = jnp.where(valid, up_ref[...].astype(F32), 0.0)
    middle_grad = upstream + norm_field_back(second_grad, gain_ref[...], scaled, spread)
    mg_ref[...] = middle_grad
    rounded = middle_grad.astype(BF)
    for t in range(count):
        dmix_refs[t][...] = dot(rounded, wo_refs[t][...], 1, 1).astype(BF)
        hog_acc[t] += dot(mixed_refs[t][...], rounded, 0, 0)

    @pl.when(i == pl.num_programs(0) - 1)
    def _():
        for t in range(count):
            hog_refs[t][...] = hog_acc[t].astype(BF)


def middle_back(at, keep, far, middle, second, gates, ids, up, mixed, head_out, gain, router):
    each, cols = mixed[0].shape
    parts = len(mixed)
    rows, width = up.shape
    tile = half_tile(each)
    spec = pltpu.PrefetchScalarGridSpec(
        num_scalar_prefetch=1,
        grid=(each // tile,),
        in_specs=[whole((tile, keep.shape[1]))] * len(far)
        + [
            rows_spec(tile, keep.shape[1]),
            rows_spec(tile, width),
            rows_spec(tile, width),
            rows_spec(tile, LANES),
            own_spec(tile, 2),
            own_spec(tile, width),
            whole((1, width)),
            whole(router.shape),
        ]
        + [rows_spec(tile, cols)] * parts
        + [whole((cols, width), True)] * parts,
        out_specs=[rows_spec(tile, width), whole((LANES, width)), whole((1, width))]
        + [whole((cols, width))] * parts
        + [rows_spec(tile, cols)] * parts,
        scratch_shapes=[pltpu.VMEM((parts, cols, width), F32)],
    )
    return pl.pallas_call(
        functools.partial(middle_back_kernel, parts, rows, len(far)),
        grid_spec=spec,
        out_shape=[
            jax.ShapeDtypeStruct((each, width), F32),
            jax.ShapeDtypeStruct((LANES, width), F32),
            jax.ShapeDtypeStruct((1, width), F32),
        ]
        + [jax.ShapeDtypeStruct((cols, width), BF)] * parts
        + [jax.ShapeDtypeStruct((each, cols), BF)] * parts,
        compiler_params=params(),
        cost_estimate=cost(8 * each * width * width, 40 * each * width),
        name="middle_back",
    )(at, *far, keep, middle, second, gates, ids, up, gain, router, *mixed, *head_out)


def input_back_kernel(limit, tiles, at_ref, *refs):
    far_refs, (keep_ref, x_ref, mg_ref, gain_ref, out_ref) = refs[:tiles], refs[tiles:]
    tile = x_ref.shape[0]
    valid = (at_ref[0] + pl.program_id(0)) * tile + iota(tile, 1, 0) < limit
    scaled, spread = norm_parts(jnp.where(valid, x_ref[...].astype(F32), 0.0))
    first_grad = keep_ref[...].astype(F32) + of_tiles(far_refs)
    out_ref[...] = (mg_ref[...] + norm_field_back(first_grad, gain_ref[...], scaled, spread)).astype(BF)


def input_back(at, keep, far, x, middle_grad, gain):
    each, width = middle_grad.shape
    tile = half_tile(each)
    spec = pltpu.PrefetchScalarGridSpec(
        num_scalar_prefetch=1,
        grid=(each // tile,),
        in_specs=[whole((tile, width))] * len(far)
        + [rows_spec(tile, width), own_spec(tile, width), rows_spec(tile, width), whole((1, width))],
        out_specs=rows_spec(tile, width),
    )
    return pl.pallas_call(
        functools.partial(input_back_kernel, x.shape[0], len(far)),
        grid_spec=spec,
        out_shape=jax.ShapeDtypeStruct((each, width), BF),
        compiler_params=params(),
        cost_estimate=cost(20 * each * width, 16 * each * width),
        name="input_back",
    )(at, *far, keep, x, middle_grad, gain)


def gelu_parts(v):
    x = jnp.abs(v) * 0.7071067811865476
    t = 1.0 / (1.0 + 0.3275911 * x)
    bell = jnp.exp(-x * x)
    poly = ((((1.061405429 * t - 1.453152027) * t + 1.421413741) * t - 0.284496736) * t + 0.254829592) * t
    below = 0.5 * poly * bell
    share = jnp.where(v < 0.0, below, 1.0 - below)
    return v * share, share + v * bell * 0.3989422804014327


def expert_kernel(count, slots, per, x_ref, g_ref, router_ref, *refs):
    w1_hbm, w2_hbm = refs[: 2 * count], refs[2 * count : 3 * count]
    back_ref, act_ref, hg_ref, rg_ref, dx_ref, w1, w2, sems = refs[3 * count :]
    rows, width = x_ref[...], x_ref.shape[1]
    half = width // 2
    copies = []
    for t in range(count):
        copies.append(
            [
                pltpu.make_async_copy(w1_hbm[2 * t], w1.at[t, pl.ds(0, half)], sems.at[3 * t]),
                pltpu.make_async_copy(w1_hbm[2 * t + 1], w1.at[t, pl.ds(half, half)], sems.at[3 * t + 1]),
                pltpu.make_async_copy(w2_hbm[t], w2.at[t], sems.at[3 * t + 2]),
            ]
        )

    @pl.when(pl.program_id(0) == 0)
    def _():
        for group in copies:
            for item in group:
                item.start()

    lane = iota(1, LANES, 1)
    signal = g_ref[:, 0].reshape(rows.shape[0], width + LANES)
    side = signal[:, width:].astype(F32)

    def column(*lanes):
        keep = lane == lanes[0]
        for other in lanes[1:]:
            keep = keep | (lane == other)
        return jnp.sum(jnp.where(keep, side, 0.0), -1, keepdims=True)

    logits = dot(rows, router_ref[...])
    lane_f = lane.astype(F32)
    mine = jnp.sum(jnp.where(lane_f == column(4), logits, 0.0), -1, keepdims=True)
    other = jnp.sum(jnp.where(lane_f == column(0), logits, 0.0), -1, keepdims=True)
    gate = 1.0 / (1.0 + jnp.exp(other - mine - column(1, 2, 3)))
    upstream = signal[:, 0:width].astype(F32)
    rows_grad = (gate * upstream).astype(BF)
    rg_ref[...] = rows_grad
    hidden_here = w1.shape[2]
    step = min(512, hidden_here)

    def wait(groups):
        @pl.when(pl.program_id(0) == 0)
        def _():
            for group in groups:
                for item in group:
                    item.wait()

    def first_products(t):
        parts = []
        for at in range(0, hidden_here, step):
            cols = slice(at, at + step)
            parts.append((at, dot(rows, w1[t, :, cols]), dot(rows_grad, w2[t, cols, :], 1, 1)))
        return parts

    wait(copies[:1])
    ready = first_products(0)
    wait(copies[1:])
    out = None
    grad = None
    for t in range(count):
        parts = ready
        if t + 1 < count:
            ready = first_products(t + 1)
        for at, hidden, active_grad in parts:
            place = slice(t * hidden_here + at, t * hidden_here + at + step)
            active, slope = gelu_parts(hidden)
            act_ref[:, place] = active.astype(BF)
            hg_ref[:, place] = (active_grad * slope).astype(BF)
        place = slice(t * hidden_here, (t + 1) * hidden_here)
        part = dot(act_ref[:, place], w2[t])
        out = part if out is None else out + part
        part = dot(hg_ref[:, place], w1[t], 1, 1)
        grad = part if grad is None else grad + part
    dx_ref[...] = grad.astype(BF)
    back_ref[...] = (gate * out).astype(BF)
    gate_grad = jnp.sum(upstream * out.astype(BF).astype(F32), -1, keepdims=True)
    lanes = up_to(slots, LANES)
    spread = iota(slots, lanes, 0) == iota(slots, lanes, 1)
    spare_row = iota(16, 1, 0) == per + 16 - slots
    for b in range(x_ref.shape[0] // slots):
        end = (b + 1) * slots
        line = jnp.sum(jnp.where(spread, gate_grad[end - slots : end], 0.0), 0, keepdims=True)
        high = line.astype(BF).astype(F32)
        line = jnp.concatenate([high, line - high, jnp.zeros((1, width - 2 * lanes), F32)], 1)
        dx_ref[end - 16 : end, :] = jnp.where(spare_row, line, grad[end - 16 : end]).astype(BF)


def expert(x, g, chunk, router, w1, w2, slots, per):
    rows, width = x.shape
    count = len(w2)
    here = w2[0].shape[0]
    total = count * here
    blocks = block_count(rows // slots, slots)
    tile = slots * blocks

    def tiled(cols):
        return pl.BlockSpec((tile, cols), lambda i: (i, 0))

    flops = 8 * rows * width * total
    return pl.pallas_call(
        functools.partial(expert_kernel, count, slots, per),
        grid=(rows // tile,),
        in_specs=[
            tiled(width),
            pl.BlockSpec((blocks, 1, slots, g.shape[3]), lambda i: (i, chunk, 0, 0)),
            whole(router.shape),
        ]
        + [pl.BlockSpec(memory_space=pl.ANY)] * (3 * count),
        out_specs=[tiled(width), tiled(total), tiled(total), tiled(width), tiled(width)],
        out_shape=[
            jax.ShapeDtypeStruct((rows, width), BF),
            jax.ShapeDtypeStruct((rows, total), BF),
            jax.ShapeDtypeStruct((rows, total), BF),
            jax.ShapeDtypeStruct((rows, width), BF),
            jax.ShapeDtypeStruct((rows, width), BF),
        ],
        scratch_shapes=[
            pltpu.VMEM((count, width, here), BF),
            pltpu.VMEM((count, here, width), BF),
            pltpu.SemaphoreType.DMA((3 * count,)),
        ],
        compiler_params=params(),
        cost_estimate=pl.CostEstimate(flops=flops, bytes_accessed=rows * total * 6, transcendentals=rows * total * 2),
        name="expert",
    )(x, g, router, *w1, *w2)


def weight_kernel(count, steps, *refs):
    ins, outs = refs[: 2 * count], refs[2 * count :]
    total = None
    for n in range(count):
        part = dot(ins[2 * n][...], ins[2 * n + 1][...], 0, 0)
        total = part if total is None else total + part
    store_piece(outs, steps, total.astype(BF))


def weight_grad(columns, rows, first, here):
    count = len(columns)
    width = rows[0].shape[1]
    step = min(512, here)
    steps = here // step
    offset = first * steps
    specs, args = [], []
    for a, b in zip(columns, rows):
        specs += [pl.BlockSpec((a.shape[0], step), lambda i: (0, i + offset)), whole(b.shape, True)]
        args += [a, b]
    out_specs, out_shape = by_piece(2, steps, (step, width), (here, width), BF)
    return pl.pallas_call(
        functools.partial(weight_kernel, count, steps),
        grid=(2 * steps,),
        in_specs=specs,
        out_specs=out_specs,
        out_shape=out_shape,
        compiler_params=params(),
        cost_estimate=cost(4 * sum(b.shape[0] for b in rows) * width * here, 8 * here * width),
        name="weight_grad",
    )(*args)


def shards(
    block_in,
    norm_one,
    head_in,
    head_out,
    norm_two,
    router,
    expert_in,
    expert_out,
    expert_ids,
    route_noise,
    cotangent,
):
    rows_here, width = block_in.shape
    parts = lax.axis_size("tensor")
    groups = lax.axis_size("expert")
    me = lax.axis_index("tensor")
    images = rows_here // SEQ
    height = up_to(SEQ, 16)
    each = up_to(-(-rows_here // parts), 16)
    experts = router.shape[1]
    capacity = (rows_here * 2 * 8 // (5 * experts) + 15) // 16 * 16
    share = -(-capacity // parts)
    per = -(-share // CHUNKS)
    slots = up_to(per + 1, 16)
    chunk_rows = experts * slots
    full = rows_here // 16 * 16
    here = expert_out.shape[1]

    paired = parts == 4
    order = (0, 2, 1, 3) if paired else tuple(range(parts))
    part_of = jnp.stack([me ^ k if paired else jnp.int32(k) for k in order]).astype(jnp.int32)
    starts = part_of * each
    own_block = (me * (each // half_tile(each)))[None].astype(jnp.int32)

    def cross(x, k):
        return lax.ppermute(x, "tensor", [(n, n ^ k) for n in range(parts)])

    def far_part(x):
        return cross(x, 2) if paired else x

    def gathered_from(x, far):
        if not paired:
            every = lax.all_gather(x, "tensor", axis=0, tiled=False)
            return [every[p] for p in range(parts)]
        return [x, far, cross(x, 1), cross(far, 1)]

    def gathered(x):
        return gathered_from(x, far_part(x))

    def near_hop(pieces):
        return pinned(*[cross(piece, 1) for piece in pieces[2:]]) if paired else pieces

    def near_sum(pieces, came):
        if not paired:
            return lax.psum_scatter(jnp.stack(pieces), "tensor", scatter_dimension=0), None
        kept, other = ((a.astype(F32) + b.astype(F32)).astype(BF) for a, b in zip(pieces, came))
        return kept, other

    def far_hop(kept, other):
        return cross(other, 2) if paired else jnp.zeros_like(kept)

    def far_tile(kept, other, n, tile):
        if not paired:
            return jnp.zeros_like(kept[n * tile : (n + 1) * tile])
        return cross(other[n * tile : (n + 1) * tile], 2)

    def after(x, *items):
        return x if x is None else pinned(x, *items)[0]

    def scattered(pieces):
        kept, other = near_sum(pieces, near_hop(pieces))
        return kept, far_hop(kept, other)

    def swapped(pieces):
        if not paired:
            every = lax.all_to_all(jnp.stack(pieces), "tensor", split_axis=0, concat_axis=0, tiled=True)
            return [every[p] for p in range(parts)]
        return [cross(piece, k) if k else piece for piece, k in zip(pieces, order)]

    def over_experts(x):
        return lax.all_to_all(x, "expert", split_axis=0, concat_axis=0, tiled=True)

    def pinned(*items):
        return lax.optimization_barrier(items)

    def tail_of(x):
        return jnp.pad(x[full:], ((0, 16 - (rows_here - full)), (0, 0)))

    names = jnp.arange(experts, dtype=jnp.int32)
    member = [(expert_ids[:, c : c + 1] == names).astype(jnp.int32) for c in range(2)]
    both = member[0] + member[1]
    earlier = jnp.cumsum(both, 0) - both
    slot = jnp.stack([jnp.sum(earlier * item, -1) for item in member], 1)
    local = slot - me * share
    place = local // per * chunk_rows + expert_ids * slots + local % per
    place = jnp.where((local >= 0) & (local < share), place, -1)
    place = jnp.pad(place, ((0, each * parts - rows_here), (0, 0)), constant_values=-1)
    place_lanes = place.T
    place_parts = jnp.swapaxes(place_lanes.reshape(2, parts, each), 0, 1)

    sides = []
    for c in range(2):
        gap = route_noise[:, c] - route_noise[:, 1 - c]
        high = gap.astype(BF)
        left = gap - high.astype(F32)
        mid = left.astype(BF)
        low = (left - mid.astype(F32)).astype(BF)
        columns = [expert_ids[:, 1 - c].astype(BF), high, mid, low, expert_ids[:, c].astype(BF)]
        sides.append(jnp.stack(columns, 1))
    side = jnp.pad(jnp.stack(sides), ((0, 0), (0, each * parts - rows_here), (0, LANES - 5)))

    router_wide = jnp.pad(router, ((0, 0), (0, LANES - experts)))
    gain_one, gain_two = norm_one[None, :], norm_two[None, :]
    head_out_far = far_part(head_out)
    w1_own = [expert_in[0, : width // 2], expert_in[0, width // 2 :]]
    w1_far = [far_part(item) for item in w1_own]

    packed = pack_first(cotangent, tail_of(cotangent), place_lanes, side, experts, slots)
    block_rows, packed, w1_far[0] = pinned(block_in, packed, w1_far[0])
    signal = over_experts(packed)

    first_in, qkv, logs, *mixed = attend(
        starts, block_rows, tail_of(block_in), gain_one, head_in, images, height, each, parts
    )
    *mixed, w1_far[1], head_out_far = pinned(*mixed, w1_far[1], head_out_far)
    head_out_all = gathered_from(head_out, head_out_far)
    mixed = swapped(mixed)
    middle, second_in, gates = middle_of(
        own_block, mixed, head_out_all, block_in, gain_two, router_wide, expert_ids, route_noise
    )
    *second_all, signal, late_out = pinned(*gathered(second_in), signal, expert_out[0])
    w1 = [gathered_from(a, b) for a, b in zip(w1_own, w1_far)]
    w1 = [w1[h][p] for p in range(parts) for h in range(2)]

    def packed_rows(n):
        return pack(part_of, second_all, place_parts, experts, slots, n * chunk_rows)

    def sent(x):
        return over_experts(x.reshape(experts, slots, width)).reshape(chunk_rows, width)

    x = sent(packed_rows(0))
    w2_far, *outgoing = pinned(far_part(late_out), *[packed_rows(n) for n in range(1, CHUNKS)])
    w2 = gathered_from(expert_out[0], w2_far)
    backs, actives, hidden_grads, rows_grads, arrived, returned = [], [], [], [], [], []
    for n in range(CHUNKS):
        coming = None
        if n + 1 < CHUNKS:
            x, ready = pinned(x, outgoing[n])
            coming = sent(ready)
        if n == 0:
            x, *ready = pinned(x, *w1, *w2)
            w1, w2 = ready[: 2 * parts], ready[2 * parts :]
        back, active, hidden_grad, rows_grad, row_grad = expert(
            x, signal, n, router_wide, w1, w2, slots, per
        )
        if returned:
            row_grad, active, returned[-1] = pinned(row_grad, active, returned[-1])
        arrived.append(x)
        actives.append(active)
        hidden_grads.append(hidden_grad)
        rows_grads.append(rows_grad)
        backs.append(back)
        if coming is not None:
            x, row_grad = pinned(coming, row_grad)
        returned.append(sent(row_grad))

    def weight_parts(columns, rows):
        pairs = [weight_grad(columns, rows, p, here) for p in range(parts - 2, -1, -2)]
        return [item for pair in pairs[::-1] for item in pair]

    out_parts = weight_parts(actives, rows_grads)
    out_kept, out_other = near_sum(out_parts, near_hop(out_parts))
    quarter = here // 4
    tile = half_tile(each)
    tiles = each // tile
    out_far = [far_tile(out_kept, out_other, n, here // 2) for n in range(2)]
    *returned, out_kept = pinned(*returned, out_kept)

    second_pieces = unpack(part_of, place, returned, slots, per, each, True)
    second_kept, second_other = near_sum(second_pieces, near_hop(second_pieces))
    second_kept, out_far[0] = pinned(second_kept, out_far[0])
    if paired:
        second_other, second_kept, *hidden_grads = pinned(second_other, second_kept, *hidden_grads)
    second_far = [far_tile(second_kept, second_other, n, tile) for n in range(tiles)]
    in_parts = []
    for p in range(parts - 2, -1, -2):
        *hidden_grads, pair = pinned(*hidden_grads, weight_grad(hidden_grads, arrived, p, here))
        in_parts = list(pair) + in_parts
        if p == parts - 2:
            in_came = near_hop([None] * p + list(pair)) if paired else ()
            second_far[0], out_far[1], pair = pinned(second_far[0], out_far[1], pair)
    in_kept, in_other = near_sum(in_parts, in_came)
    second_far[-1], in_kept = pinned(second_far[-1], in_kept)
    in_other = after(in_other, in_kept)
    in_far = [far_tile(in_kept, in_other, 0, quarter)]
    combined = [sent(item) for item in backs]
    middle_grad, router_part, norm_two_part, *pieces = middle_back(
        own_block, second_kept, second_far, middle, second_in, gates, expert_ids, cotangent, mixed, head_out_all,
        gain_two, router_wide,
    )
    head_out_parts, mixed_grad = pieces[:parts], pieces[parts:]
    *mixed_grad, combined[0], in_far[0] = pinned(*mixed_grad, combined[0], in_far[0])
    mixed_grad = swapped(mixed_grad)
    head_out_kept, head_out_far = scattered(head_out_parts)
    in_other = after(in_other, *mixed_grad)
    in_far += [far_tile(in_kept, in_other, n, quarter) for n in (1, 2)]
    *pieces, head_in_part, norm_one_part = attend_back(
        starts, mixed_grad, qkv, logs, first_in, jnp.swapaxes(head_in, 1, 2), gain_one
    )
    *pieces, combined[-1], in_far[1], in_far[2], head_out_far = pinned(
        *pieces, combined[-1], in_far[1], in_far[2], head_out_far
    )
    first_kept, first_other = near_sum(pieces, near_hop(pieces))
    if paired:
        first_other, first_kept, head_in_part, head_out_far, *combined = pinned(
            first_other, first_kept, head_in_part, head_out_far, *combined
        )
    first_far = [far_tile(first_kept, first_other, n, tile) for n in range(tiles)]
    block_pieces = unpack(part_of, place, combined, slots, per, each, False)
    first_far[0], block_pieces = pinned(first_far[0], block_pieces)
    in_far.append(far_tile(in_kept, after(in_other, block_pieces[0]), 3, quarter))
    block_kept, block_other = near_sum(block_pieces, near_hop(block_pieces))
    input_part = input_back(own_block, first_kept, first_far, block_in, middle_grad, gain_one)
    block_far = far_hop(block_kept, block_other)
    head_out_part = (head_out_kept.astype(F32) + head_out_far.astype(F32)).astype(BF)
    small = jnp.concatenate([norm_one_part, norm_two_part, router_part[:experts]], 0).astype(BF)
    cols = head_in.shape[2]
    count = 4 * cols + 2 + experts
    total = up_to(count, 16 * groups)
    heads = jnp.concatenate(
        [head_in_part.reshape(3 * cols, width), head_out_part, jnp.pad(small, ((0, total - count), (0, 0)))], 0
    )
    heads = over_experts(heads.reshape(groups, total // groups, width))
    input_far = far_part(input_part)
    heads, out_kept = pinned(heads, out_kept)
    out_grad = sum_far(out_kept, out_far, False)
    in_grad = sum_far(in_kept, in_far, True)
    input_far, out_grad, in_grad, block_far = pinned(input_far, out_grad, in_grad, block_far)
    block_own = (middle + block_kept.astype(F32) + block_far.astype(F32)).astype(BF)

    input_grad = assemble(part_of, gathered_from(input_part, input_far), rows_here, F32)
    block_out = assemble(part_of, gathered(block_own), rows_here, BF)
    heads = jnp.sum(heads.astype(F32), 0).astype(BF)
    heads = lax.all_gather(heads, "expert", axis=0, tiled=True)
    head_in_grad = jnp.swapaxes(heads[: 3 * cols].reshape(3, cols, width), 1, 2).astype(F32)
    head_out_grad = heads[3 * cols : 4 * cols].astype(F32)
    small = heads[4 * cols : count].astype(F32)
    if paired:
        small = small + cross(small, 1)
        small = small + cross(small, 2)
    else:
        small = lax.psum(small, "tensor")
    return (
        block_out,
        input_grad,
        small[0],
        head_in_grad,
        head_out_grad,
        small[1],
        small[2:].T,
        in_grad[None],
        out_grad[None],
    )


def solution(mesh):
    in_specs = (
        P("expert", None),
        P(),
        P(None, None, "tensor"),
        P("tensor", None),
        P(),
        P(),
        P("expert", None, "tensor"),
        P("expert", "tensor", None),
        P("expert", None),
        P("expert", None),
        P("expert", None),
    )
    out_specs = (
        P("expert", None),
        P("expert", None),
        P(),
        P(None, None, "tensor"),
        P("tensor", None),
        P(),
        P(),
        P("expert", None, "tensor"),
        P("expert", "tensor", None),
    )
    return jax.shard_map(shards, mesh=mesh, in_specs=in_specs, out_specs=out_specs, check_vma=False)
```

```python
import functools

import jax
import jax.numpy as jnp
from jax import lax
from jax.experimental import pallas as pl
from jax.experimental.pallas import tpu as pltpu
from jax.sharding import PartitionSpec as P

HD = 64
SEQ = 197
LANES = 128
EPSILON = 1e-06
CHUNKS = 2
BF = jnp.bfloat16
F32 = jnp.float32


def up_to(value, unit):
    return -(-value // unit) * unit


def params(mib=60):
    return pltpu.CompilerParams(vmem_limit_bytes=mib * 1024 * 1024)


def dot(a, b, da=1, db=0):
    return lax.dot_general(a, b, (((da,), (db,)), ((), ())), preferred_element_type=F32)


def iota(rows, cols, dim):
    return lax.broadcasted_iota(jnp.int32, (rows, cols), dim)


def flag(mask):
    return jnp.where(mask, 1.0, 0.0)


def whole(shape, once=False):
    zeros = (0,) * len(shape)
    mode = pl.Buffered(1) if once else None
    return pl.BlockSpec(shape, lambda *_: zeros, pipeline_mode=mode)


def image(*shape):
    return pl.BlockSpec((1,) + shape, lambda i, *_: (i,) + (0,) * len(shape))


def fill(x_ref, tail_ref, rows_ref):
    full = x_ref.shape[0] // 16 * 16
    rows_ref[0:full, :] = x_ref[0:full, :]
    rows_ref[full : full + 16, :] = tail_ref[...]
    rest = rows_ref.shape[0] - full - 16
    if rest:
        rows_ref[full + 16 :, :] = jnp.zeros((rest, rows_ref.shape[1]), BF)


def norm_parts(field):
    centre = field - jnp.mean(field, -1, keepdims=True)
    spread = lax.rsqrt(jnp.mean(centre * centre, -1, keepdims=True) + EPSILON)
    return centre * spread, spread


def norm_field_back(upstream, gain, scaled, spread):
    weighted = upstream * gain
    return spread * (
        weighted
        - jnp.mean(weighted, -1, keepdims=True)
        - scaled * jnp.mean(weighted * scaled, -1, keepdims=True)
    )


def cost(flops, size):
    return pl.CostEstimate(flops=flops, bytes_accessed=size, transcendentals=0)


def by_piece(count, steps, block, shape, dtype):
    def spec(p):
        def place(i, *_):
            return (jnp.clip(i - p * steps, 0, steps - 1), 0)

        return pl.BlockSpec(block, place)

    return [spec(p) for p in range(count)], [jax.ShapeDtypeStruct(shape, dtype)] * count


def store_piece(refs, steps, value):
    for p, ref in enumerate(refs):

        @pl.when(pl.program_id(0) // steps == p)
        def _():
            ref[...] = value


def rows_spec(tile, width):
    return pl.BlockSpec((tile, width), lambda i, *_: (i, 0))


def own_spec(tile, width):
    return pl.BlockSpec((tile, width), lambda i, at: (at[0] + i, 0))


def window_of(i, height, back=False):
    start = i * SEQ
    aligned = start // 16 * 16
    window = height + 16
    shape = (window, height) if back else (height, window)
    r, c = iota(*shape, 1 if back else 0), iota(*shape, 0 if back else 1)
    match = flag((c == r + (start - aligned)) & (r < SEQ)).astype(BF)
    return match, pl.ds(pl.multiple_of(aligned, 16), window)


def head_masks():
    lane = iota(1, LANES, 1)
    return [(flag(lane // HD == h)).astype(BF) for h in range(2)]


def attend_kernel(count, starts_ref, x_ref, tail_ref, gain_ref, w_ref, first_ref, qkv_ref, log_ref, *refs):
    piece_refs, rows, mixed = refs[:count], refs[count], refs[count + 1]
    i = pl.program_id(0)
    height = first_ref.shape[1]
    cols = mixed.shape[1]

    @pl.when(i == 0)
    def _():
        fill(x_ref, tail_ref, rows)
        mixed[...] = jnp.zeros_like(mixed)

    match, place = window_of(i, height)
    field = dot(match, rows[place, :])
    scaled, _ = norm_parts(field)
    first = (scaled * gain_ref[...]).astype(BF)
    first_ref[0] = first
    for k in range(3):
        qkv_ref[k, 0] = dot(first, w_ref[k]).astype(BF)
    masks = head_masks()
    lane = iota(1, LANES, 1)
    key_lane = iota(1, height, 1)
    logs = jnp.zeros((height, LANES), F32)
    back, _ = window_of(i, height, True)
    for pair in range(cols // LANES):
        part = slice(pair * LANES, (pair + 1) * LANES)
        queries, keys, values = (qkv_ref[k, 0, :, part] for k in range(3))
        total = jnp.zeros((height, LANES), F32)
        for h in range(2):
            scores = dot(queries * masks[h], keys, 1, 1) * HD ** (-0.5)
            scores = jnp.where(key_lane < SEQ, scores, -1e30)
            highest = jnp.max(scores, -1, keepdims=True)
            weights = jnp.exp(scores - highest)
            sums = jnp.sum(weights, -1, keepdims=True)
            probs = (weights * (1.0 / sums)).astype(BF)
            total += dot(probs, values * masks[h])
            logs = jnp.where(lane == pair * 2 + h, highest + jnp.log(sums), logs)
        mixed[place, part] = (mixed[place, part].astype(F32) + dot(back, total.astype(BF))).astype(BF)
    log_ref[0] = logs

    @pl.when(i == pl.num_programs(0) - 1)
    def _():
        for p in range(count):
            at = pl.multiple_of(starts_ref[p], 16)
            piece_refs[p][...] = mixed[pl.ds(at, piece_refs[p].shape[0]), :]


def attend(starts, block_in, tail, gain, head_in, images, height, each, count):
    rows, width = block_in.shape
    cols = head_in.shape[2]
    scratch_rows = max(rows // 16 * 16 + 48, each * count)
    spec = pltpu.PrefetchScalarGridSpec(
        num_scalar_prefetch=1,
        grid=(images,),
        in_specs=[whole((rows, width), True), whole((16, width)), whole((1, width)), whole(head_in.shape, True)],
        out_specs=[
            image(height, width),
            pl.BlockSpec((3, 1, height, cols), lambda i, *_: (0, i, 0, 0)),
            image(height, LANES),
        ]
        + [whole((each, cols))] * count,
        scratch_shapes=[pltpu.VMEM((scratch_rows, width), BF), pltpu.VMEM((scratch_rows, cols), BF)],
    )
    return pl.pallas_call(
        functools.partial(attend_kernel, count),
        grid_spec=spec,
        out_shape=[
            jax.ShapeDtypeStruct((images, height, width), BF),
            jax.ShapeDtypeStruct((3, images, height, cols), BF),
            jax.ShapeDtypeStruct((images, height, LANES), F32),
        ]
        + [jax.ShapeDtypeStruct((each, cols), BF)] * count,
        compiler_params=params(),
        cost_estimate=cost(16 * images * height * width * cols, 16 * rows * width),
        name="attend",
    )(starts, block_in, tail, gain, head_in)


def attend_back_kernel(count, starts_ref, qkv_ref, log_ref, first_ref, wt_ref, gain_ref, *refs):
    dmix_refs, piece_refs = refs[:count], refs[count : 2 * count]
    hg_ref, ng_ref, acc, grads, dmix, field = refs[2 * count :]
    i = pl.program_id(0)
    height = first_ref.shape[1]
    each = dmix_refs[0].shape[0]

    @pl.when(i == 0)
    def _():
        acc[...] = jnp.zeros_like(acc)
        field[...] = jnp.zeros_like(field)
        rest = dmix.shape[0] - each * count
        if rest:
            dmix[each * count :, :] = jnp.zeros((rest, dmix.shape[1]), BF)
        for p in range(count):
            dmix[pl.ds(pl.multiple_of(starts_ref[p], 16), each), :] = dmix_refs[p][...]

    match, place = window_of(i, height)
    back, _ = window_of(i, height, True)
    out_grads = dot(match, dmix[place, :]).astype(BF)
    masks = head_masks()
    lane = iota(1, LANES, 1)
    key_lane = iota(1, height, 1)
    scale = HD ** (-0.5)
    logs = log_ref[0]
    for pair in range(dmix.shape[1] // LANES):
        cols = slice(pair * LANES, (pair + 1) * LANES)
        queries, keys, values = (qkv_ref[k, 0, :, cols] for k in range(3))
        out_grad = out_grads[:, cols]
        dq = jnp.zeros((height, LANES), F32)
        dk = jnp.zeros((height, LANES), F32)
        dv = jnp.zeros((height, LANES), F32)
        for h in range(2):
            q_h = queries * masks[h]
            o_h = out_grad * masks[h]
            log_h = jnp.sum(jnp.where(lane == pair * 2 + h, logs, 0.0), -1, keepdims=True)
            probs = jnp.exp(dot(q_h, keys, 1, 1) * scale - log_h)
            probs = jnp.where(key_lane < SEQ, probs, 0.0)
            prob_grad = dot(o_h, values, 1, 1)
            dv += dot(probs.astype(BF), o_h, 0, 0)
            delta = jnp.sum(probs * prob_grad, -1, keepdims=True)
            score_grad = (probs * (prob_grad - delta)).astype(BF)
            dq += dot(score_grad, keys * masks[h])
            dk += dot(score_grad, q_h, 0, 0)
        grads[0, :, cols] = (dq * scale).astype(BF)
        grads[1, :, cols] = (dk * scale).astype(BF)
        grads[2, :, cols] = dv.astype(BF)

    first = first_ref[0]
    total = None
    for k in range(3):
        part = dot(grads[k], wt_ref[k])
        total = part if total is None else total + part
        acc[k] += dot(grads[k], first, 0, 0)
    field[place, :] = (field[place, :].astype(F32) + dot(back, total.astype(BF))).astype(BF)

    @pl.when(i == pl.num_programs(0) - 1)
    def _():
        for p in range(count):
            piece_refs[p][...] = field[pl.ds(pl.multiple_of(starts_ref[p], 16), each), :]
        hg_ref[...] = acc[...].astype(BF)
        gain_grad = jnp.zeros_like(ng_ref)
        for k in range(3):
            gain_grad += jnp.sum(acc[k] * wt_ref[k].astype(F32), 0, keepdims=True)
        ng_ref[...] = gain_grad / gain_ref[...]


def attend_back(starts, dmix, qkv, logs, first, head_in_t, gain):
    images, height, width = first.shape
    each, cols = dmix[0].shape
    count = len(dmix)
    scratch_rows = max(images * SEQ // 16 * 16 + 48, each * count)
    spec = pltpu.PrefetchScalarGridSpec(
        num_scalar_prefetch=1,
        grid=(images,),
        in_specs=[
            pl.BlockSpec((3, 1, height, cols), lambda i, *_: (0, i, 0, 0)),
            image(height, LANES),
            image(height, width),
            whole(head_in_t.shape, True),
            whole((1, width)),
        ]
        + [whole((each, cols), True)] * count,
        out_specs=[whole((each, width))] * count + [whole(head_in_t.shape), whole((1, width))],
        scratch_shapes=[
            pltpu.VMEM(head_in_t.shape, F32),
            pltpu.VMEM((3, height, cols), BF),
            pltpu.VMEM((scratch_rows, cols), BF),
            pltpu.VMEM((scratch_rows, width), BF),
        ],
    )
    return pl.pallas_call(
        functools.partial(attend_back_kernel, count),
        grid_spec=spec,
        out_shape=[jax.ShapeDtypeStruct((each, width), BF)] * count
        + [jax.ShapeDtypeStruct(head_in_t.shape, BF), jax.ShapeDtypeStruct((1, width), F32)],
        compiler_params=params(),
        cost_estimate=cost(24 * images * height * width * cols, 20 * images * height * width),
        name="attend_back",
    )(starts, qkv, logs, first, head_in_t, gain, *dmix)


def block_count(blocks, slots):
    return max(n for n in range(1, blocks + 1) if blocks % n == 0 and n * slots <= 448)


def pack_first_kernel(x_ref, tail_ref, lp_ref, side_ref, out_ref, rows):
    i, n = pl.program_id(0), pl.program_id(1)

    @pl.when((i == 0) & (n == 0))
    def _():
        fill(x_ref, tail_ref, rows)

    blocks, _, slots, _ = out_ref.shape
    tile = blocks * slots
    j = (n * pl.num_programs(0) + i) * tile + iota(tile, rows.shape[0], 0)
    picks = [flag(lp_ref[c : c + 1, :] == j) for c in range(2)]
    width = x_ref.shape[1]
    main = dot((picks[0] + picks[1]).astype(BF), rows[...]).astype(BF)
    out_ref[:, 0, :, 0:width] = main.reshape(blocks, slots, width)
    extra = dot(picks[0].astype(BF), side_ref[0]) + dot(picks[1].astype(BF), side_ref[1])
    out_ref[:, 0, :, width:] = extra.astype(BF).reshape(blocks, slots, LANES)


def pack_first(x, tail, lp, side, experts, slots):
    rows, width = x.shape
    padded = lp.shape[1]
    blocks = block_count(experts, slots)
    return pl.pallas_call(
        pack_first_kernel,
        grid=(experts // blocks, CHUNKS),
        in_specs=[whole((rows, width), True), whole((16, width)), whole(lp.shape), whole(side.shape)],
        out_specs=pl.BlockSpec((blocks, 1, slots, width + LANES), lambda i, n: (i, n, 0, 0)),
        out_shape=jax.ShapeDtypeStruct((experts, CHUNKS, slots, width + LANES), BF),
        scratch_shapes=[pltpu.VMEM((padded, width), BF)],
        compiler_params=params(),
        cost_estimate=cost(3 * CHUNKS * experts * slots * padded * width, 2 * rows * width),
        name="pack_cotangent",
    )(x, tail, lp, side)


def pack_kernel(base, count, part_ref, *refs):
    lp_ref, out_ref = refs[count], refs[count + 1]
    total = None
    tile = out_ref.shape[0]
    for p in range(count):
        j = base + pl.program_id(0) * tile + iota(tile, refs[p].shape[0], 0)
        lp = lp_ref[part_ref[p]]
        picks = flag((lp[0:1, :] == j) | (lp[1:2, :] == j)).astype(BF)
        part = dot(picks, refs[p][...])
        total = part if total is None else total + part
    out_ref[...] = total.astype(BF)


def pack(part_of, pieces, lp, experts, slots, base):
    rows, width = pieces[0].shape
    count = len(pieces)
    tile = slots * block_count(experts, slots)
    spec = pltpu.PrefetchScalarGridSpec(
        num_scalar_prefetch=1,
        grid=(experts * slots // tile,),
        in_specs=[whole((rows, width), True)] * count + [whole(lp.shape)],
        out_specs=rows_spec(tile, width),
    )
    return pl.pallas_call(
        functools.partial(pack_kernel, base, count),
        grid_spec=spec,
        out_shape=jax.ShapeDtypeStruct((experts * slots, width), BF),
        compiler_params=params(),
        cost_estimate=cost(3 * experts * slots * rows * count * width, 2 * rows * count * width),
        name="pack_rows",
    )(part_of, *pieces, lp)


def unpack_kernel(count, slots, per, graded, part_ref, lp_ref, *refs):
    row_refs, out_refs = refs[:count], refs[count:]
    lp = lp_ref[...]
    height = lp.shape[0]
    rows, width = row_refs[0].shape
    total = jnp.zeros((height, width), F32)
    lanes = up_to(slots, LANES)
    extra = [jnp.zeros((height, lanes), F32) for _ in range(2)]
    for n in range(count):
        j = n * rows + iota(1, rows, 1)
        hits = (lp[:, 0:1] == j) | (lp[:, 1:2] == j)
        total += dot(flag(hits).astype(BF), row_refs[n][...])
        if graded:
            j = iota(1, lanes, 1)
            for e in range(rows // slots):
                spare = row_refs[n][(e + 1) * slots - 16 : (e + 1) * slots, 0 : 2 * lanes].astype(F32)
                spare = spare[per + 16 - slots : per + 17 - slots, :]
                values = spare[:, :lanes] + spare[:, lanes:]
                for c in range(2):
                    hit = lp[:, c : c + 1] - (n * rows + e * slots) == j
                    extra[c] += jnp.where(hit, values, 0.0)
    value = total.astype(BF)
    if graded:
        lane = iota(1, LANES, 1)
        tail = jnp.zeros((height, LANES), F32)
        for c in range(2):
            grad = jnp.sum(extra[c], -1, keepdims=True)
            high = grad.astype(BF).astype(F32)
            tail = jnp.where(lane == c, high, tail)
            tail = jnp.where(lane == 2 + c, grad - high, tail)
        value = jnp.concatenate([value, tail.astype(BF)], 1)
    store_piece(out_refs, 1, value)


def unpack(part_of, lp, rows, slots, per, each, graded):
    parts = lp.shape[0] // each
    count = len(rows)
    width = rows[0].shape[1] + (LANES if graded else 0)
    out_specs, out_shape = by_piece(parts, 1, (each, width), (each, width), BF)
    spec = pltpu.PrefetchScalarGridSpec(
        num_scalar_prefetch=1,
        grid=(parts,),
        in_specs=[pl.BlockSpec((each, 2), lambda i, at: (at[i], 0))] + [whole(item.shape, True) for item in rows],
        out_specs=out_specs,
    )
    return pl.pallas_call(
        functools.partial(unpack_kernel, count, slots, per, graded),
        grid_spec=spec,
        out_shape=out_shape,
        compiler_params=params(),
        cost_estimate=cost(3 * lp.shape[0] * count * rows[0].size, 4 * count * rows[0].size),
        name="unpack_rows",
    )(part_of, lp, *rows)


def assemble_kernel(count, steps, part_ref, *refs):
    out_ref = refs[count]
    for p in range(count):

        @pl.when(pl.program_id(0) // steps == p)
        def _():
            out_ref[...] = refs[p][...].astype(out_ref.dtype)


def assemble(part_of, pieces, rows, dtype):
    each, width = pieces[0].shape
    count = len(pieces)
    tile, steps = each, 1
    in_specs, _ = by_piece(count, steps, (tile, width), (each, width), BF)
    spec = pltpu.PrefetchScalarGridSpec(
        num_scalar_prefetch=1,
        grid=(count * steps,),
        in_specs=in_specs,
        out_specs=pl.BlockSpec((tile, width), lambda i, at: (at[i // steps] * steps + i % steps, 0)),
    )
    return pl.pallas_call(
        functools.partial(assemble_kernel, count, steps),
        grid_spec=spec,
        out_shape=jax.ShapeDtypeStruct((rows, width), dtype),
        compiler_params=params(),
        cost_estimate=cost(2 * rows * width, 8 * rows * width),
        name="assemble",
    )(part_of, *pieces)


def sum_turned_kernel(a_ref, b_ref, out_ref):
    out_ref[...] = (a_ref[...].astype(F32) + b_ref[...].astype(F32)).T


def sum_turned(a, b):
    rows, width = a.shape
    tile = min(256, rows)
    return pl.pallas_call(
        sum_turned_kernel,
        grid=(rows // tile,),
        in_specs=[rows_spec(tile, width)] * 2,
        out_specs=pl.BlockSpec((width, tile), lambda i: (0, i)),
        out_shape=jax.ShapeDtypeStruct((width, rows), F32),
        compiler_params=params(),
        cost_estimate=cost(rows * width, 8 * rows * width),
        name="sum_turned",
    )(a, b)


def middle_kernel(count, limit, at_ref, *refs):
    mixed_refs, wo_refs = refs[:count], refs[count : 2 * count]
    x_ref, gain_ref, router_ref, ids_ref, noise_ref, mid_ref, second_ref, gates_ref = refs[2 * count :]
    tile = x_ref.shape[0]
    valid = (at_ref[0] + pl.program_id(0)) * tile + iota(tile, 1, 0) < limit
    middle = jnp.where(valid, x_ref[...].astype(F32), 0.0)
    for mixed_ref, wo_ref in zip(mixed_refs, wo_refs):
        middle += dot(mixed_ref[...], wo_ref[...])
    mid_ref[...] = middle
    scaled, _ = norm_parts(middle)
    second = (scaled * gain_ref[...]).astype(BF)
    second_ref[...] = second
    logits = dot(second, router_ref[...])
    lane = iota(1, LANES, 1)
    chosen = [
        jnp.sum(jnp.where(lane == ids_ref[:, c : c + 1], logits, 0.0), -1, keepdims=True)
        + noise_ref[:, c : c + 1]
        for c in range(2)
    ]
    top = jnp.maximum(chosen[0], chosen[1])
    raw = [jnp.exp(item - top) for item in chosen]
    inverse = 1.0 / (raw[0] + raw[1])
    gates = jnp.where(lane == 0, raw[0] * inverse, 0.0) + jnp.where(lane == 1, raw[1] * inverse, 0.0)
    gates_ref[...] = jnp.where(valid, gates, 0.0)


def half_tile(each):
    return each // 2 if each % 32 == 0 else each


def middle_of(at, mixed, head_out, x, gain, router, ids, noise):
    each, cols = mixed[0].shape
    parts = len(mixed)
    rows, width = x.shape
    tile = half_tile(each)
    spec = pltpu.PrefetchScalarGridSpec(
        num_scalar_prefetch=1,
        grid=(each // tile,),
        in_specs=[rows_spec(tile, cols)] * parts
        + [whole((cols, width), True)] * parts
        + [
            own_spec(tile, width),
            whole((1, width)),
            whole(router.shape),
            own_spec(tile, 2),
            own_spec(tile, 2),
        ],
        out_specs=[rows_spec(tile, width), rows_spec(tile, width), rows_spec(tile, LANES)],
    )
    return pl.pallas_call(
        functools.partial(middle_kernel, parts, rows),
        grid_spec=spec,
        out_shape=[
            jax.ShapeDtypeStruct((each, width), F32),
            jax.ShapeDtypeStruct((each, width), BF),
            jax.ShapeDtypeStruct((each, LANES), F32),
        ],
        compiler_params=params(),
        cost_estimate=cost(4 * each * width * width, 24 * each * width),
        name="middle",
    )(at, *mixed, *head_out, x, gain, router, ids, noise)


def middle_back_kernel(count, limit, at_ref, *refs):
    keep_ref, far_ref, mid_ref, second_ref, gates_ref, ids_ref, up_ref, gain_ref, router_ref = refs[:9]
    mixed_refs, wo_refs = refs[9 : 9 + count], refs[9 + count : 9 + 2 * count]
    mg_ref, rg_ref, ng_ref = refs[9 + 2 * count : 12 + 2 * count]
    hog_refs, dmix_refs, hog_acc = refs[12 + 2 * count : 12 + 3 * count], refs[12 + 3 * count : -1], refs[-1]
    i = pl.program_id(0)

    @pl.when(i == 0)
    def _():
        hog_acc[...] = jnp.zeros_like(hog_acc)
        rg_ref[...] = jnp.zeros_like(rg_ref)
        ng_ref[...] = jnp.zeros_like(ng_ref)

    tile, width = up_ref.shape
    valid = (at_ref[0] + i) * tile + iota(tile, 1, 0) < limit
    lane = iota(1, LANES, 1)
    tail = keep_ref[:, width:].astype(F32) + far_ref[:, width:].astype(F32)
    gates = gates_ref[...]
    gate, grad = [], []
    for c in range(2):
        gate.append(jnp.sum(jnp.where(lane == c, gates, 0.0), -1, keepdims=True))
        grad.append(jnp.sum(jnp.where((lane == c) | (lane == 2 + c), tail, 0.0), -1, keepdims=True))
    mean_term = gate[0] * grad[0] + gate[1] * grad[1]
    logit_grad = jnp.zeros((tile, LANES), F32)
    for c in range(2):
        hit = (lane == ids_ref[:, c : c + 1]) & valid
        logit_grad = jnp.where(hit, gate[c] * (grad[c] - mean_term), logit_grad)
    logit_grad = logit_grad.astype(BF)
    routed = keep_ref[:, 0:width].astype(F32) + far_ref[:, 0:width].astype(F32)
    second_grad = routed + dot(logit_grad, router_ref[...], 1, 1)
    rg_ref[...] += dot(logit_grad, second_ref[...], 0, 0)
    scaled, spread = norm_parts(mid_ref[...])
    ng_ref[...] += jnp.sum(second_grad * scaled, 0, keepdims=True)
    upstream = jnp.where(valid, up_ref[...].astype(F32), 0.0)
    middle_grad = upstream + norm_field_back(second_grad, gain_ref[...], scaled, spread)
    mg_ref[...] = middle_grad
    rounded = middle_grad.astype(BF)
    for t in range(count):
        dmix_refs[t][...] = dot(rounded, wo_refs[t][...], 1, 1).astype(BF)
        hog_acc[t] += dot(mixed_refs[t][...], rounded, 0, 0)

    @pl.when(i == pl.num_programs(0) - 1)
    def _():
        for t in range(count):
            hog_refs[t][...] = hog_acc[t].astype(BF)


def middle_back(at, keep, far, middle, second, gates, ids, up, mixed, head_out, gain, router):
    each, cols = mixed[0].shape
    parts = len(mixed)
    rows, width = up.shape
    tile = half_tile(each)
    spec = pltpu.PrefetchScalarGridSpec(
        num_scalar_prefetch=1,
        grid=(each // tile,),
        in_specs=[
            rows_spec(tile, keep.shape[1]),
            rows_spec(tile, keep.shape[1]),
            rows_spec(tile, width),
            rows_spec(tile, width),
            rows_spec(tile, LANES),
            own_spec(tile, 2),
            own_spec(tile, width),
            whole((1, width)),
            whole(router.shape),
        ]
        + [rows_spec(tile, cols)] * parts
        + [whole((cols, width), True)] * parts,
        out_specs=[rows_spec(tile, width), whole((LANES, width)), whole((1, width))]
        + [whole((cols, width))] * parts
        + [rows_spec(tile, cols)] * parts,
        scratch_shapes=[pltpu.VMEM((parts, cols, width), F32)],
    )
    return pl.pallas_call(
        functools.partial(middle_back_kernel, parts, rows),
        grid_spec=spec,
        out_shape=[
            jax.ShapeDtypeStruct((each, width), F32),
            jax.ShapeDtypeStruct((LANES, width), F32),
            jax.ShapeDtypeStruct((1, width), F32),
        ]
        + [jax.ShapeDtypeStruct((cols, width), BF)] * parts
        + [jax.ShapeDtypeStruct((each, cols), BF)] * parts,
        compiler_params=params(),
        cost_estimate=cost(8 * each * width * width, 40 * each * width),
        name="middle_back",
    )(at, keep, far, middle, second, gates, ids, up, gain, router, *mixed, *head_out)


def input_back_kernel(limit, at_ref, keep_ref, far_ref, x_ref, mg_ref, gain_ref, out_ref):
    tile = x_ref.shape[0]
    valid = (at_ref[0] + pl.program_id(0)) * tile + iota(tile, 1, 0) < limit
    scaled, spread = norm_parts(jnp.where(valid, x_ref[...].astype(F32), 0.0))
    first_grad = keep_ref[...].astype(F32) + far_ref[...].astype(F32)
    out_ref[...] = (mg_ref[...] + norm_field_back(first_grad, gain_ref[...], scaled, spread)).astype(BF)


def input_back(at, keep, far, x, middle_grad, gain):
    each, width = middle_grad.shape
    tile = half_tile(each)
    spec = pltpu.PrefetchScalarGridSpec(
        num_scalar_prefetch=1,
        grid=(each // tile,),
        in_specs=[rows_spec(tile, width), rows_spec(tile, width), own_spec(tile, width), rows_spec(tile, width), whole((1, width))],
        out_specs=rows_spec(tile, width),
    )
    return pl.pallas_call(
        functools.partial(input_back_kernel, x.shape[0]),
        grid_spec=spec,
        out_shape=jax.ShapeDtypeStruct((each, width), BF),
        compiler_params=params(),
        cost_estimate=cost(20 * each * width, 16 * each * width),
        name="input_back",
    )(at, keep, far, x, middle_grad, gain)


def gelu_parts(v):
    x = jnp.abs(v) * 0.7071067811865476
    t = 1.0 / (1.0 + 0.3275911 * x)
    bell = jnp.exp(-x * x)
    poly = ((((1.061405429 * t - 1.453152027) * t + 1.421413741) * t - 0.284496736) * t + 0.254829592) * t
    below = 0.5 * poly * bell
    share = jnp.where(v < 0.0, below, 1.0 - below)
    return v * share, share + v * bell * 0.3989422804014327


def expert_kernel(count, slots, per, x_ref, g_ref, router_ref, *refs):
    w1_hbm, w2_hbm = refs[: 2 * count], refs[2 * count : 3 * count]
    back_ref, act_ref, hg_ref, rg_ref, dx_ref, w1, w2, sems = refs[3 * count :]
    rows, width = x_ref[...], x_ref.shape[1]
    half = width // 2
    copies = []
    for t in range(count):
        copies.append(
            [
                pltpu.make_async_copy(w1_hbm[2 * t], w1.at[t, pl.ds(0, half)], sems.at[3 * t]),
                pltpu.make_async_copy(w1_hbm[2 * t + 1], w1.at[t, pl.ds(half, half)], sems.at[3 * t + 1]),
                pltpu.make_async_copy(w2_hbm[t], w2.at[t], sems.at[3 * t + 2]),
            ]
        )

    @pl.when(pl.program_id(0) == 0)
    def _():
        for group in copies:
            for item in group:
                item.start()

    lane = iota(1, LANES, 1)
    signal = g_ref[:, 0].reshape(rows.shape[0], width + LANES)
    side = signal[:, width:].astype(F32)

    def column(*lanes):
        keep = lane == lanes[0]
        for other in lanes[1:]:
            keep = keep | (lane == other)
        return jnp.sum(jnp.where(keep, side, 0.0), -1, keepdims=True)

    logits = dot(rows, router_ref[...])
    lane_f = lane.astype(F32)
    mine = jnp.sum(jnp.where(lane_f == column(4), logits, 0.0), -1, keepdims=True)
    other = jnp.sum(jnp.where(lane_f == column(0), logits, 0.0), -1, keepdims=True)
    gate = 1.0 / (1.0 + jnp.exp(other - mine - column(1, 2, 3)))
    upstream = signal[:, 0:width].astype(F32)
    rows_grad = (gate * upstream).astype(BF)
    rg_ref[...] = rows_grad
    hidden_here = w1.shape[2]
    step = min(512, hidden_here)

    def wait(groups):
        @pl.when(pl.program_id(0) == 0)
        def _():
            for group in groups:
                for item in group:
                    item.wait()

    def first_products(t):
        parts = []
        for at in range(0, hidden_here, step):
            cols = slice(at, at + step)
            parts.append((at, dot(rows, w1[t, :, cols]), dot(rows_grad, w2[t, cols, :], 1, 1)))
        return parts

    wait(copies[:1])
    ready = first_products(0)
    wait(copies[1:])
    out = None
    grad = None
    for t in range(count):
        parts = ready
        if t + 1 < count:
            ready = first_products(t + 1)
        for at, hidden, active_grad in parts:
            place = slice(t * hidden_here + at, t * hidden_here + at + step)
            active, slope = gelu_parts(hidden)
            act_ref[:, place] = active.astype(BF)
            hg_ref[:, place] = (active_grad * slope).astype(BF)
        place = slice(t * hidden_here, (t + 1) * hidden_here)
        part = dot(act_ref[:, place], w2[t])
        out = part if out is None else out + part
        part = dot(hg_ref[:, place], w1[t], 1, 1)
        grad = part if grad is None else grad + part
    dx_ref[...] = grad.astype(BF)
    back_ref[...] = (gate * out).astype(BF)
    gate_grad = jnp.sum(upstream * out.astype(BF).astype(F32), -1, keepdims=True)
    lanes = up_to(slots, LANES)
    spread = iota(slots, lanes, 0) == iota(slots, lanes, 1)
    spare_row = iota(16, 1, 0) == per + 16 - slots
    for b in range(x_ref.shape[0] // slots):
        end = (b + 1) * slots
        line = jnp.sum(jnp.where(spread, gate_grad[end - slots : end], 0.0), 0, keepdims=True)
        high = line.astype(BF).astype(F32)
        line = jnp.concatenate([high, line - high, jnp.zeros((1, width - 2 * lanes), F32)], 1)
        dx_ref[end - 16 : end, :] = jnp.where(spare_row, line, grad[end - 16 : end]).astype(BF)


def expert(x, g, chunk, router, w1, w2, slots, per):
    rows, width = x.shape
    count = len(w2)
    here = w2[0].shape[0]
    total = count * here
    blocks = block_count(rows // slots, slots)
    tile = slots * blocks

    def tiled(cols):
        return pl.BlockSpec((tile, cols), lambda i: (i, 0))

    flops = 8 * rows * width * total
    return pl.pallas_call(
        functools.partial(expert_kernel, count, slots, per),
        grid=(rows // tile,),
        in_specs=[
            tiled(width),
            pl.BlockSpec((blocks, 1, slots, g.shape[3]), lambda i: (i, chunk, 0, 0)),
            whole(router.shape),
        ]
        + [pl.BlockSpec(memory_space=pl.ANY)] * (3 * count),
        out_specs=[tiled(width), tiled(total), tiled(total), tiled(width), tiled(width)],
        out_shape=[
            jax.ShapeDtypeStruct((rows, width), BF),
            jax.ShapeDtypeStruct((rows, total), BF),
            jax.ShapeDtypeStruct((rows, total), BF),
            jax.ShapeDtypeStruct((rows, width), BF),
            jax.ShapeDtypeStruct((rows, width), BF),
        ],
        scratch_shapes=[
            pltpu.VMEM((count, width, here), BF),
            pltpu.VMEM((count, here, width), BF),
            pltpu.SemaphoreType.DMA((3 * count,)),
        ],
        compiler_params=params(),
        cost_estimate=pl.CostEstimate(flops=flops, bytes_accessed=rows * total * 6, transcendentals=rows * total * 2),
        name="expert",
    )(x, g, router, *w1, *w2)


def weight_kernel(count, steps, *refs):
    ins, outs = refs[: 2 * count], refs[2 * count :]
    total = None
    for n in range(count):
        part = dot(ins[2 * n][...], ins[2 * n + 1][...], 0, 0)
        total = part if total is None else total + part
    store_piece(outs, steps, total.astype(BF))


def weight_grad(columns, rows, first, here, parts=2):
    count = len(columns)
    width = rows[0].shape[1]
    step = min(512, here)
    steps = here // step
    offset = first * steps
    specs, args = [], []
    for a, b in zip(columns, rows):
        specs += [pl.BlockSpec((a.shape[0], step), lambda i: (0, i + offset)), whole(b.shape, True)]
        args += [a, b]
    out_specs, out_shape = by_piece(parts, steps, (step, width), (here, width), BF)
    return pl.pallas_call(
        functools.partial(weight_kernel, count, steps),
        grid=(parts * steps,),
        in_specs=specs,
        out_specs=out_specs,
        out_shape=out_shape,
        compiler_params=params(),
        cost_estimate=cost(2 * parts * sum(b.shape[0] for b in rows) * width * here, 4 * parts * here * width),
        name="weight_grad",
    )(*args)


def shards(
    block_in,
    norm_one,
    head_in,
    head_out,
    norm_two,
    router,
    expert_in,
    expert_out,
    expert_ids,
    route_noise,
    cotangent,
):
    rows_here, width = block_in.shape
    parts = lax.axis_size("tensor")
    groups = lax.axis_size("expert")
    me = lax.axis_index("tensor")
    images = rows_here // SEQ
    height = up_to(SEQ, 16)
    each = up_to(-(-rows_here // parts), 16)
    experts = router.shape[1]
    capacity = (rows_here * 2 * 8 // (5 * experts) + 15) // 16 * 16
    share = -(-capacity // parts)
    per = -(-share // CHUNKS)
    slots = up_to(per + 1, 16)
    chunk_rows = experts * slots
    full = rows_here // 16 * 16
    here = expert_out.shape[1]

    paired = parts == 4
    order = (0, 2, 1, 3) if paired else tuple(range(parts))
    part_of = jnp.stack([me ^ k if paired else jnp.int32(k) for k in order]).astype(jnp.int32)
    starts = part_of * each
    own_block = (me * (each // half_tile(each)))[None].astype(jnp.int32)

    def cross(x, k):
        return lax.ppermute(x, "tensor", [(n, n ^ k) for n in range(parts)])

    def far_part(x):
        return cross(x, 2) if paired else x

    def gathered_from(x, far):
        if not paired:
            every = lax.all_gather(x, "tensor", axis=0, tiled=False)
            return [every[p] for p in range(parts)]
        return [x, far, cross(x, 1), cross(far, 1)]

    def gathered(x):
        return gathered_from(x, far_part(x))

    def near_hop(pieces):
        return pinned(*[cross(piece, 1) for piece in pieces[2:]]) if paired else pieces

    def near_sum(pieces, came):
        if not paired:
            return lax.psum_scatter(jnp.stack(pieces), "tensor", scatter_dimension=0), None
        kept, other = ((a.astype(F32) + b.astype(F32)).astype(BF) for a, b in zip(pieces, came))
        return kept, other

    def far_hop(kept, other):
        return cross(other, 2) if paired else jnp.zeros_like(kept)

    def scattered(pieces):
        kept, other = near_sum(pieces, near_hop(pieces))
        return kept, far_hop(kept, other)

    def swapped(pieces):
        if not paired:
            every = lax.all_to_all(jnp.stack(pieces), "tensor", split_axis=0, concat_axis=0, tiled=True)
            return [every[p] for p in range(parts)]
        return [cross(piece, k) if k else piece for piece, k in zip(pieces, order)]

    def over_experts(x):
        return lax.all_to_all(x, "expert", split_axis=0, concat_axis=0, tiled=True)

    def pinned(*items):
        return lax.optimization_barrier(items)

    def tail_of(x):
        return jnp.pad(x[full:], ((0, 16 - (rows_here - full)), (0, 0)))

    names = jnp.arange(experts, dtype=jnp.int32)
    member = [(expert_ids[:, c : c + 1] == names).astype(jnp.int32) for c in range(2)]
    both = member[0] + member[1]
    earlier = jnp.cumsum(both, 0) - both
    slot = jnp.stack([jnp.sum(earlier * item, -1) for item in member], 1)
    local = slot - me * share
    place = local // per * chunk_rows + expert_ids * slots + local % per
    place = jnp.where((local >= 0) & (local < share), place, -1)
    place = jnp.pad(place, ((0, each * parts - rows_here), (0, 0)), constant_values=-1)
    place_lanes = place.T
    place_parts = jnp.swapaxes(place_lanes.reshape(2, parts, each), 0, 1)

    sides = []
    for c in range(2):
        gap = route_noise[:, c] - route_noise[:, 1 - c]
        high = gap.astype(BF)
        left = gap - high.astype(F32)
        mid = left.astype(BF)
        low = (left - mid.astype(F32)).astype(BF)
        columns = [expert_ids[:, 1 - c].astype(BF), high, mid, low, expert_ids[:, c].astype(BF)]
        sides.append(jnp.stack(columns, 1))
    side = jnp.pad(jnp.stack(sides), ((0, 0), (0, each * parts - rows_here), (0, LANES - 5)))

    router_wide = jnp.pad(router, ((0, 0), (0, LANES - experts)))
    gain_one, gain_two = norm_one[None, :], norm_two[None, :]
    head_out_far = far_part(head_out)
    w1_own = [expert_in[0, : width // 2], expert_in[0, width // 2 :]]
    w1_far = [far_part(item) for item in w1_own]

    packed = pack_first(cotangent, tail_of(cotangent), place_lanes, side, experts, slots)
    block_rows, packed, w1_far[0] = pinned(block_in, packed, w1_far[0])
    signal = over_experts(packed)

    first_in, qkv, logs, *mixed = attend(
        starts, block_rows, tail_of(block_in), gain_one, head_in, images, height, each, parts
    )
    *mixed, w1_far[1], head_out_far = pinned(*mixed, w1_far[1], head_out_far)
    head_out_all = gathered_from(head_out, head_out_far)
    mixed = swapped(mixed)
    middle, second_in, gates = middle_of(
        own_block, mixed, head_out_all, block_in, gain_two, router_wide, expert_ids, route_noise
    )
    *second_all, signal, late_out = pinned(*gathered(second_in), signal, expert_out[0])
    w1 = [gathered_from(a, b) for a, b in zip(w1_own, w1_far)]
    w1 = [w1[h][p] for p in range(parts) for h in range(2)]

    def packed_rows(n):
        return pack(part_of, second_all, place_parts, experts, slots, n * chunk_rows)

    def sent(x):
        return over_experts(x.reshape(experts, slots, width)).reshape(chunk_rows, width)

    x = sent(packed_rows(0))
    w2_far, *outgoing = pinned(far_part(late_out), *[packed_rows(n) for n in range(1, CHUNKS)])
    w2 = gathered_from(expert_out[0], w2_far)
    backs, actives, hidden_grads, rows_grads, arrived, returned = [], [], [], [], [], []
    for n in range(CHUNKS):
        coming = None
        if n + 1 < CHUNKS:
            x, ready = pinned(x, outgoing[n])
            coming = sent(ready)
        if n == 0:
            x, *ready = pinned(x, *w1, *w2)
            w1, w2 = ready[: 2 * parts], ready[2 * parts :]
        back, active, hidden_grad, rows_grad, row_grad = expert(
            x, signal, n, router_wide, w1, w2, slots, per
        )
        if returned:
            row_grad, active, returned[-1] = pinned(row_grad, active, returned[-1])
        arrived.append(x)
        actives.append(active)
        hidden_grads.append(hidden_grad)
        rows_grads.append(rows_grad)
        backs.append(back)
        if coming is not None:
            x, row_grad = pinned(coming, row_grad)
        returned.append(sent(row_grad))

    def weight_parts(columns, rows):
        pairs = [weight_grad(columns, rows, p, here) for p in range(parts - 2, -1, -2)]
        return [item for pair in pairs[::-1] for item in pair]

    out_parts = weight_parts(actives, rows_grads)
    out_kept, out_other = near_sum(out_parts, near_hop(out_parts))
    out_far = far_hop(out_kept, out_other)
    *returned, out_kept = pinned(*returned, out_kept)

    second_pieces = unpack(part_of, place, returned, slots, per, each, True)
    second_kept, second_other = near_sum(second_pieces, near_hop(second_pieces))
    if paired:
        second_other, second_kept, out_far, *hidden_grads = pinned(
            second_other, second_kept, out_far, *hidden_grads
        )
    second_far = far_hop(second_kept, second_other)
    in_parts = weight_grad(hidden_grads, arrived, 0, here, parts)
    in_came = near_hop(in_parts)
    second_far, *in_parts = pinned(second_far, *in_parts)
    combined = [sent(item) for item in backs]
    middle_grad, router_part, norm_two_part, *pieces = middle_back(
        own_block, second_kept, second_far, middle, second_in, gates, expert_ids, cotangent, mixed, head_out_all,
        gain_two, router_wide,
    )
    head_out_parts, mixed_grad = pieces[:parts], pieces[parts:]
    *mixed_grad, combined[0] = pinned(*mixed_grad, combined[0])
    *mixed_grad, in_came = pinned(*mixed_grad, in_came)
    mixed_grad = swapped(mixed_grad)
    in_kept, in_other = near_sum(in_parts, in_came)
    if paired:
        in_other = pinned(in_other, *mixed_grad)[0]
    in_far = far_hop(in_kept, in_other)
    head_out_kept, head_out_far = scattered(head_out_parts)
    *pieces, head_in_part, norm_one_part = attend_back(
        starts, mixed_grad, qkv, logs, first_in, jnp.swapaxes(head_in, 1, 2), gain_one
    )
    *pieces, combined[-1] = pinned(*pieces, combined[-1])
    first_kept, first_other = near_sum(pieces, near_hop(pieces))
    if paired:
        first_other, first_kept, in_far, head_in_part, *combined = pinned(
            first_other, first_kept, in_far, head_in_part, *combined
        )
    first_far = far_hop(first_kept, first_other)
    block_pieces = unpack(part_of, place, combined, slots, per, each, False)
    *block_pieces, head_out_far = pinned(*block_pieces, head_out_far)
    block_kept, block_other = near_sum(block_pieces, near_hop(block_pieces))
    first_far, block_kept = pinned(first_far, block_kept)
    block_far = far_hop(block_kept, block_other)
    input_part = input_back(own_block, first_kept, first_far, block_in, middle_grad, gain_one)
    out_grad = out_kept.astype(F32) + out_far.astype(F32)
    in_grad = sum_turned(in_kept, in_far)
    input_far, out_grad, in_grad, block_far = pinned(far_part(input_part), out_grad, in_grad, block_far)
    block_own = (middle + block_kept.astype(F32) + block_far.astype(F32)).astype(BF)

    input_grad = assemble(part_of, gathered_from(input_part, input_far), rows_here, F32)
    block_out = assemble(part_of, gathered(block_own), rows_here, BF)

    head_out_part = (head_out_kept.astype(F32) + head_out_far.astype(F32)).astype(BF)
    small = jnp.concatenate([norm_one_part, norm_two_part, router_part[:experts]], 0).astype(BF)
    cols, count = head_out.shape[0], 2 + experts
    rest = jnp.concatenate([head_out_part, jnp.pad(small, ((0, up_to(count, 16) - count), (0, 0)))], 0)
    head_in_grad, rest = lax.psum((head_in_part, rest), "expert")
    head_in_grad = jnp.swapaxes(head_in_grad, 1, 2).astype(F32)
    head_out_grad = rest[:cols].astype(F32)
    small = rest[cols : cols + count].astype(F32)
    if paired:
        small = small + cross(small, 1)
        small = small + cross(small, 2)
    else:
        small = lax.psum(small, "tensor")
    return (
        block_out,
        input_grad,
        small[0],
        head_in_grad,
        head_out_grad,
        small[1],
        small[2:].T,
        in_grad[None],
        out_grad[None],
    )


def solution(mesh):
    in_specs = (
        P("expert", None),
        P(),
        P(None, None, "tensor"),
        P("tensor", None),
        P(),
        P(),
        P("expert", None, "tensor"),
        P("expert", "tensor", None),
        P("expert", None),
        P("expert", None),
        P("expert", None),
    )
    out_specs = (
        P("expert", None),
        P("expert", None),
        P(),
        P(None, None, "tensor"),
        P("tensor", None),
        P(),
        P(),
        P("expert", None, "tensor"),
        P("expert", "tensor", None),
    )
    return jax.shard_map(shards, mesh=mesh, in_specs=in_specs, out_specs=out_specs, check_vma=False)
```

```python
import functools

import jax
import jax.numpy as jnp
from jax import lax
from jax.experimental import pallas as pl
from jax.experimental.pallas import tpu as pltpu
from jax.sharding import PartitionSpec as P

HD = 64
SEQ = 197
LANES = 128
EPSILON = 1e-06
CHUNKS = 2
BF = jnp.bfloat16
F32 = jnp.float32


def up_to(value, unit):
    return -(-value // unit) * unit


def params(mib=60):
    return pltpu.CompilerParams(vmem_limit_bytes=mib * 1024 * 1024)


def dot(a, b, da=1, db=0):
    return lax.dot_general(a, b, (((da,), (db,)), ((), ())), preferred_element_type=F32)


def iota(rows, cols, dim):
    return lax.broadcasted_iota(jnp.int32, (rows, cols), dim)


def flag(mask):
    return jnp.where(mask, 1.0, 0.0)


def whole(shape, once=False):
    zeros = (0,) * len(shape)
    mode = pl.Buffered(1) if once else None
    return pl.BlockSpec(shape, lambda *_: zeros, pipeline_mode=mode)


def image(*shape):
    return pl.BlockSpec((1,) + shape, lambda i, *_: (i,) + (0,) * len(shape))


def fill(x_ref, tail_ref, rows_ref):
    full = x_ref.shape[0] // 16 * 16
    rows_ref[0:full, :] = x_ref[0:full, :]
    rows_ref[full : full + 16, :] = tail_ref[...]
    rest = rows_ref.shape[0] - full - 16
    if rest:
        rows_ref[full + 16 :, :] = jnp.zeros((rest, rows_ref.shape[1]), BF)


def norm_parts(field):
    centre = field - jnp.mean(field, -1, keepdims=True)
    spread = lax.rsqrt(jnp.mean(centre * centre, -1, keepdims=True) + EPSILON)
    return centre * spread, spread


def norm_field_back(upstream, gain, scaled, spread):
    weighted = upstream * gain
    return spread * (
        weighted
        - jnp.mean(weighted, -1, keepdims=True)
        - scaled * jnp.mean(weighted * scaled, -1, keepdims=True)
    )


def cost(flops, size):
    return pl.CostEstimate(flops=flops, bytes_accessed=size, transcendentals=0)


def by_piece(count, steps, block, shape, dtype):
    def spec(p):
        def place(i, *_):
            return (jnp.clip(i - p * steps, 0, steps - 1), 0)

        return pl.BlockSpec(block, place)

    return [spec(p) for p in range(count)], [jax.ShapeDtypeStruct(shape, dtype)] * count


def store_piece(refs, steps, value):
    for p, ref in enumerate(refs):

        @pl.when(pl.program_id(0) // steps == p)
        def _():
            ref[...] = value


def rows_spec(tile, width):
    return pl.BlockSpec((tile, width), lambda i, *_: (i, 0))


def own_spec(tile, width):
    return pl.BlockSpec((tile, width), lambda i, at: (at[0] + i, 0))


def window_of(i, height, back=False):
    start = i * SEQ
    aligned = start // 16 * 16
    window = height + 16
    shape = (window, height) if back else (height, window)
    r, c = iota(*shape, 1 if back else 0), iota(*shape, 0 if back else 1)
    match = flag((c == r + (start - aligned)) & (r < SEQ)).astype(BF)
    return match, pl.ds(pl.multiple_of(aligned, 16), window)


def head_masks():
    lane = iota(1, LANES, 1)
    return [(flag(lane // HD == h)).astype(BF) for h in range(2)]


def attend_kernel(count, starts_ref, x_ref, tail_ref, gain_ref, w_ref, first_ref, qkv_ref, log_ref, *refs):
    piece_refs, rows, mixed = refs[:count], refs[count], refs[count + 1]
    i = pl.program_id(0)
    height = first_ref.shape[1]
    cols = mixed.shape[1]

    @pl.when(i == 0)
    def _():
        fill(x_ref, tail_ref, rows)
        mixed[...] = jnp.zeros_like(mixed)

    match, place = window_of(i, height)
    field = dot(match, rows[place, :])
    scaled, _ = norm_parts(field)
    first = (scaled * gain_ref[...]).astype(BF)
    first_ref[0] = first
    for k in range(3):
        qkv_ref[k, 0] = dot(first, w_ref[k]).astype(BF)
    masks = head_masks()
    lane = iota(1, LANES, 1)
    key_lane = iota(1, height, 1)
    logs = jnp.zeros((height, LANES), F32)
    back, _ = window_of(i, height, True)
    for pair in range(cols // LANES):
        part = slice(pair * LANES, (pair + 1) * LANES)
        queries, keys, values = (qkv_ref[k, 0, :, part] for k in range(3))
        total = jnp.zeros((height, LANES), F32)
        for h in range(2):
            scores = dot(queries * masks[h], keys, 1, 1) * HD ** (-0.5)
            scores = jnp.where(key_lane < SEQ, scores, -1e30)
            highest = jnp.max(scores, -1, keepdims=True)
            weights = jnp.exp(scores - highest)
            sums = jnp.sum(weights, -1, keepdims=True)
            probs = (weights * (1.0 / sums)).astype(BF)
            total += dot(probs, values * masks[h])
            logs = jnp.where(lane == pair * 2 + h, highest + jnp.log(sums), logs)
        mixed[place, part] = (mixed[place, part].astype(F32) + dot(back, total.astype(BF))).astype(BF)
    log_ref[0] = logs

    @pl.when(i == pl.num_programs(0) - 1)
    def _():
        for p in range(count):
            at = pl.multiple_of(starts_ref[p], 16)
            piece_refs[p][...] = mixed[pl.ds(at, piece_refs[p].shape[0]), :]


def attend(starts, block_in, tail, gain, head_in, images, height, each, count):
    rows, width = block_in.shape
    cols = head_in.shape[2]
    scratch_rows = max(rows // 16 * 16 + 48, each * count)
    spec = pltpu.PrefetchScalarGridSpec(
        num_scalar_prefetch=1,
        grid=(images,),
        in_specs=[whole((rows, width), True), whole((16, width)), whole((1, width)), whole(head_in.shape, True)],
        out_specs=[
            image(height, width),
            pl.BlockSpec((3, 1, height, cols), lambda i, *_: (0, i, 0, 0)),
            image(height, LANES),
        ]
        + [whole((each, cols))] * count,
        scratch_shapes=[pltpu.VMEM((scratch_rows, width), BF), pltpu.VMEM((scratch_rows, cols), BF)],
    )
    return pl.pallas_call(
        functools.partial(attend_kernel, count),
        grid_spec=spec,
        out_shape=[
            jax.ShapeDtypeStruct((images, height, width), BF),
            jax.ShapeDtypeStruct((3, images, height, cols), BF),
            jax.ShapeDtypeStruct((images, height, LANES), F32),
        ]
        + [jax.ShapeDtypeStruct((each, cols), BF)] * count,
        compiler_params=params(),
        cost_estimate=cost(16 * images * height * width * cols, 16 * rows * width),
        name="attend",
    )(starts, block_in, tail, gain, head_in)


def attend_back_kernel(count, starts_ref, qkv_ref, log_ref, first_ref, wt_ref, gain_ref, *refs):
    dmix_refs, piece_refs = refs[:count], refs[count : 2 * count]
    hg_ref, ng_ref, acc, grads, dmix, field = refs[2 * count :]
    i = pl.program_id(0)
    height = first_ref.shape[1]
    each = dmix_refs[0].shape[0]

    @pl.when(i == 0)
    def _():
        acc[...] = jnp.zeros_like(acc)
        field[...] = jnp.zeros_like(field)
        rest = dmix.shape[0] - each * count
        if rest:
            dmix[each * count :, :] = jnp.zeros((rest, dmix.shape[1]), BF)
        for p in range(count):
            dmix[pl.ds(pl.multiple_of(starts_ref[p], 16), each), :] = dmix_refs[p][...]

    match, place = window_of(i, height)
    back, _ = window_of(i, height, True)
    out_grads = dot(match, dmix[place, :]).astype(BF)
    masks = head_masks()
    lane = iota(1, LANES, 1)
    key_lane = iota(1, height, 1)
    scale = HD ** (-0.5)
    logs = log_ref[0]
    for pair in range(dmix.shape[1] // LANES):
        cols = slice(pair * LANES, (pair + 1) * LANES)
        queries, keys, values = (qkv_ref[k, 0, :, cols] for k in range(3))
        out_grad = out_grads[:, cols]
        dq = jnp.zeros((height, LANES), F32)
        dk = jnp.zeros((height, LANES), F32)
        dv = jnp.zeros((height, LANES), F32)
        for h in range(2):
            q_h = queries * masks[h]
            o_h = out_grad * masks[h]
            log_h = jnp.sum(jnp.where(lane == pair * 2 + h, logs, 0.0), -1, keepdims=True)
            probs = jnp.exp(dot(q_h, keys, 1, 1) * scale - log_h)
            probs = jnp.where(key_lane < SEQ, probs, 0.0)
            prob_grad = dot(o_h, values, 1, 1)
            dv += dot(probs.astype(BF), o_h, 0, 0)
            delta = jnp.sum(probs * prob_grad, -1, keepdims=True)
            score_grad = (probs * (prob_grad - delta)).astype(BF)
            dq += dot(score_grad, keys * masks[h])
            dk += dot(score_grad, q_h, 0, 0)
        grads[0, :, cols] = (dq * scale).astype(BF)
        grads[1, :, cols] = (dk * scale).astype(BF)
        grads[2, :, cols] = dv.astype(BF)

    first = first_ref[0]
    total = None
    for k in range(3):
        part = dot(grads[k], wt_ref[k])
        total = part if total is None else total + part
        acc[k] += dot(grads[k], first, 0, 0)
    field[place, :] = (field[place, :].astype(F32) + dot(back, total.astype(BF))).astype(BF)

    @pl.when(i == pl.num_programs(0) - 1)
    def _():
        for p in range(count):
            piece_refs[p][...] = field[pl.ds(pl.multiple_of(starts_ref[p], 16), each), :]
        hg_ref[...] = acc[...].astype(BF)
        gain_grad = jnp.zeros_like(ng_ref)
        for k in range(3):
            gain_grad += jnp.sum(acc[k] * wt_ref[k].astype(F32), 0, keepdims=True)
        ng_ref[...] = gain_grad / gain_ref[...]


def attend_back(starts, dmix, qkv, logs, first, head_in_t, gain):
    images, height, width = first.shape
    each, cols = dmix[0].shape
    count = len(dmix)
    scratch_rows = max(images * SEQ // 16 * 16 + 48, each * count)
    spec = pltpu.PrefetchScalarGridSpec(
        num_scalar_prefetch=1,
        grid=(images,),
        in_specs=[
            pl.BlockSpec((3, 1, height, cols), lambda i, *_: (0, i, 0, 0)),
            image(height, LANES),
            image(height, width),
            whole(head_in_t.shape, True),
            whole((1, width)),
        ]
        + [whole((each, cols), True)] * count,
        out_specs=[whole((each, width))] * count + [whole(head_in_t.shape), whole((1, width))],
        scratch_shapes=[
            pltpu.VMEM(head_in_t.shape, F32),
            pltpu.VMEM((3, height, cols), BF),
            pltpu.VMEM((scratch_rows, cols), BF),
            pltpu.VMEM((scratch_rows, width), BF),
        ],
    )
    return pl.pallas_call(
        functools.partial(attend_back_kernel, count),
        grid_spec=spec,
        out_shape=[jax.ShapeDtypeStruct((each, width), BF)] * count
        + [jax.ShapeDtypeStruct(head_in_t.shape, BF), jax.ShapeDtypeStruct((1, width), F32)],
        compiler_params=params(),
        cost_estimate=cost(24 * images * height * width * cols, 20 * images * height * width),
        name="attend_back",
    )(starts, qkv, logs, first, head_in_t, gain, *dmix)


def block_count(blocks, slots):
    return max(n for n in range(1, blocks + 1) if blocks % n == 0 and n * slots <= 448)


def pack_first_kernel(x_ref, tail_ref, lp_ref, side_ref, out_ref, rows):
    i, n = pl.program_id(0), pl.program_id(1)

    @pl.when((i == 0) & (n == 0))
    def _():
        fill(x_ref, tail_ref, rows)

    blocks, _, slots, _ = out_ref.shape
    tile = blocks * slots
    j = (n * pl.num_programs(0) + i) * tile + iota(tile, rows.shape[0], 0)
    picks = [flag(lp_ref[c : c + 1, :] == j) for c in range(2)]
    width = x_ref.shape[1]
    main = dot((picks[0] + picks[1]).astype(BF), rows[...]).astype(BF)
    out_ref[:, 0, :, 0:width] = main.reshape(blocks, slots, width)
    extra = dot(picks[0].astype(BF), side_ref[0]) + dot(picks[1].astype(BF), side_ref[1])
    out_ref[:, 0, :, width:] = extra.astype(BF).reshape(blocks, slots, LANES)


def pack_first(x, tail, lp, side, experts, slots):
    rows, width = x.shape
    padded = lp.shape[1]
    blocks = block_count(experts, slots)
    return pl.pallas_call(
        pack_first_kernel,
        grid=(experts // blocks, CHUNKS),
        in_specs=[whole((rows, width), True), whole((16, width)), whole(lp.shape), whole(side.shape)],
        out_specs=pl.BlockSpec((blocks, 1, slots, width + LANES), lambda i, n: (i, n, 0, 0)),
        out_shape=jax.ShapeDtypeStruct((experts, CHUNKS, slots, width + LANES), BF),
        scratch_shapes=[pltpu.VMEM((padded, width), BF)],
        compiler_params=params(),
        cost_estimate=cost(3 * CHUNKS * experts * slots * padded * width, 2 * rows * width),
        name="pack_cotangent",
    )(x, tail, lp, side)


def pack_kernel(base, count, part_ref, *refs):
    lp_ref, out_ref = refs[count], refs[count + 1]
    total = None
    tile = out_ref.shape[0]
    for p in range(count):
        j = base + pl.program_id(0) * tile + iota(tile, refs[p].shape[0], 0)
        lp = lp_ref[part_ref[p]]
        picks = flag((lp[0:1, :] == j) | (lp[1:2, :] == j)).astype(BF)
        part = dot(picks, refs[p][...])
        total = part if total is None else total + part
    out_ref[...] = total.astype(BF)


def pack(part_of, pieces, lp, experts, slots, base):
    rows, width = pieces[0].shape
    count = len(pieces)
    tile = slots * block_count(experts, slots)
    spec = pltpu.PrefetchScalarGridSpec(
        num_scalar_prefetch=1,
        grid=(experts * slots // tile,),
        in_specs=[whole((rows, width), True)] * count + [whole(lp.shape)],
        out_specs=rows_spec(tile, width),
    )
    return pl.pallas_call(
        functools.partial(pack_kernel, base, count),
        grid_spec=spec,
        out_shape=jax.ShapeDtypeStruct((experts * slots, width), BF),
        compiler_params=params(),
        cost_estimate=cost(3 * experts * slots * rows * count * width, 2 * rows * count * width),
        name="pack_rows",
    )(part_of, *pieces, lp)


def unpack_kernel(count, slots, per, graded, part_ref, lp_ref, *refs):
    row_refs, out_refs = refs[:count], refs[count:]
    lp = lp_ref[...]
    height = lp.shape[0]
    rows, width = row_refs[0].shape
    total = jnp.zeros((height, width), F32)
    lanes = up_to(slots, LANES)
    extra = [jnp.zeros((height, lanes), F32) for _ in range(2)]
    for n in range(count):
        j = n * rows + iota(1, rows, 1)
        hits = (lp[:, 0:1] == j) | (lp[:, 1:2] == j)
        total += dot(flag(hits).astype(BF), row_refs[n][...])
        if graded:
            j = iota(1, lanes, 1)
            for e in range(rows // slots):
                spare = row_refs[n][(e + 1) * slots - 16 : (e + 1) * slots, 0 : 2 * lanes].astype(F32)
                spare = spare[per + 16 - slots : per + 17 - slots, :]
                values = spare[:, :lanes] + spare[:, lanes:]
                for c in range(2):
                    hit = lp[:, c : c + 1] - (n * rows + e * slots) == j
                    extra[c] += jnp.where(hit, values, 0.0)
    value = total.astype(BF)
    if graded:
        lane = iota(1, LANES, 1)
        tail = jnp.zeros((height, LANES), F32)
        for c in range(2):
            grad = jnp.sum(extra[c], -1, keepdims=True)
            high = grad.astype(BF).astype(F32)
            tail = jnp.where(lane == c, high, tail)
            tail = jnp.where(lane == 2 + c, grad - high, tail)
        value = jnp.concatenate([value, tail.astype(BF)], 1)
    store_piece(out_refs, 1, value)


def unpack(part_of, lp, rows, slots, per, each, graded):
    parts = lp.shape[0] // each
    count = len(rows)
    width = rows[0].shape[1] + (LANES if graded else 0)
    out_specs, out_shape = by_piece(parts, 1, (each, width), (each, width), BF)
    spec = pltpu.PrefetchScalarGridSpec(
        num_scalar_prefetch=1,
        grid=(parts,),
        in_specs=[pl.BlockSpec((each, 2), lambda i, at: (at[i], 0))] + [whole(item.shape, True) for item in rows],
        out_specs=out_specs,
    )
    return pl.pallas_call(
        functools.partial(unpack_kernel, count, slots, per, graded),
        grid_spec=spec,
        out_shape=out_shape,
        compiler_params=params(),
        cost_estimate=cost(3 * lp.shape[0] * count * rows[0].size, 4 * count * rows[0].size),
        name="unpack_rows",
    )(part_of, lp, *rows)


def assemble_kernel(count, steps, part_ref, *refs):
    out_ref = refs[count]
    for p in range(count):

        @pl.when(pl.program_id(0) // steps == p)
        def _():
            out_ref[...] = refs[p][...].astype(out_ref.dtype)


def assemble(part_of, pieces, rows, dtype):
    each, width = pieces[0].shape
    count = len(pieces)
    tile, steps = each, 1
    in_specs, _ = by_piece(count, steps, (tile, width), (each, width), BF)
    spec = pltpu.PrefetchScalarGridSpec(
        num_scalar_prefetch=1,
        grid=(count * steps,),
        in_specs=in_specs,
        out_specs=pl.BlockSpec((tile, width), lambda i, at: (at[i // steps] * steps + i % steps, 0)),
    )
    return pl.pallas_call(
        functools.partial(assemble_kernel, count, steps),
        grid_spec=spec,
        out_shape=jax.ShapeDtypeStruct((rows, width), dtype),
        compiler_params=params(),
        cost_estimate=cost(2 * rows * width, 8 * rows * width),
        name="assemble",
    )(part_of, *pieces)


def sum_turned_kernel(a_ref, b_ref, out_ref):
    out_ref[...] = (a_ref[...].astype(F32) + b_ref[...].astype(F32)).T


def sum_turned(a, b):
    rows, width = a.shape
    tile = min(256, rows)
    return pl.pallas_call(
        sum_turned_kernel,
        grid=(rows // tile,),
        in_specs=[rows_spec(tile, width)] * 2,
        out_specs=pl.BlockSpec((width, tile), lambda i: (0, i)),
        out_shape=jax.ShapeDtypeStruct((width, rows), F32),
        compiler_params=params(),
        cost_estimate=cost(rows * width, 8 * rows * width),
        name="sum_turned",
    )(a, b)


def middle_kernel(count, limit, at_ref, *refs):
    mixed_refs, wo_refs = refs[:count], refs[count : 2 * count]
    x_ref, gain_ref, router_ref, ids_ref, noise_ref, mid_ref, second_ref, gates_ref = refs[2 * count :]
    tile = x_ref.shape[0]
    valid = (at_ref[0] + pl.program_id(0)) * tile + iota(tile, 1, 0) < limit
    middle = jnp.where(valid, x_ref[...].astype(F32), 0.0)
    for mixed_ref, wo_ref in zip(mixed_refs, wo_refs):
        middle += dot(mixed_ref[...], wo_ref[...])
    mid_ref[...] = middle
    scaled, _ = norm_parts(middle)
    second = (scaled * gain_ref[...]).astype(BF)
    second_ref[...] = second
    logits = dot(second, router_ref[...])
    lane = iota(1, LANES, 1)
    chosen = [
        jnp.sum(jnp.where(lane == ids_ref[:, c : c + 1], logits, 0.0), -1, keepdims=True)
        + noise_ref[:, c : c + 1]
        for c in range(2)
    ]
    top = jnp.maximum(chosen[0], chosen[1])
    raw = [jnp.exp(item - top) for item in chosen]
    inverse = 1.0 / (raw[0] + raw[1])
    gates = jnp.where(lane == 0, raw[0] * inverse, 0.0) + jnp.where(lane == 1, raw[1] * inverse, 0.0)
    gates_ref[...] = jnp.where(valid, gates, 0.0)


def half_tile(each):
    return each // 2 if each % 32 == 0 else each


def middle_of(at, mixed, head_out, x, gain, router, ids, noise):
    each, cols = mixed[0].shape
    parts = len(mixed)
    rows, width = x.shape
    tile = half_tile(each)
    spec = pltpu.PrefetchScalarGridSpec(
        num_scalar_prefetch=1,
        grid=(each // tile,),
        in_specs=[rows_spec(tile, cols)] * parts
        + [whole((cols, width), True)] * parts
        + [
            own_spec(tile, width),
            whole((1, width)),
            whole(router.shape),
            own_spec(tile, 2),
            own_spec(tile, 2),
        ],
        out_specs=[rows_spec(tile, width), rows_spec(tile, width), rows_spec(tile, LANES)],
    )
    return pl.pallas_call(
        functools.partial(middle_kernel, parts, rows),
        grid_spec=spec,
        out_shape=[
            jax.ShapeDtypeStruct((each, width), F32),
            jax.ShapeDtypeStruct((each, width), BF),
            jax.ShapeDtypeStruct((each, LANES), F32),
        ],
        compiler_params=params(),
        cost_estimate=cost(4 * each * width * width, 24 * each * width),
        name="middle",
    )(at, *mixed, *head_out, x, gain, router, ids, noise)


def middle_back_kernel(count, limit, at_ref, *refs):
    keep_ref, far_ref, mid_ref, second_ref, gates_ref, ids_ref, up_ref, gain_ref, router_ref = refs[:9]
    mixed_refs, wo_refs = refs[9 : 9 + count], refs[9 + count : 9 + 2 * count]
    mg_ref, rg_ref, ng_ref = refs[9 + 2 * count : 12 + 2 * count]
    hog_refs, dmix_refs, hog_acc = refs[12 + 2 * count : 12 + 3 * count], refs[12 + 3 * count : -1], refs[-1]
    i = pl.program_id(0)

    @pl.when(i == 0)
    def _():
        hog_acc[...] = jnp.zeros_like(hog_acc)
        rg_ref[...] = jnp.zeros_like(rg_ref)
        ng_ref[...] = jnp.zeros_like(ng_ref)

    tile, width = up_ref.shape
    valid = (at_ref[0] + i) * tile + iota(tile, 1, 0) < limit
    lane = iota(1, LANES, 1)
    tail = keep_ref[:, width:].astype(F32) + far_ref[:, width:].astype(F32)
    gates = gates_ref[...]
    gate, grad = [], []
    for c in range(2):
        gate.append(jnp.sum(jnp.where(lane == c, gates, 0.0), -1, keepdims=True))
        grad.append(jnp.sum(jnp.where((lane == c) | (lane == 2 + c), tail, 0.0), -1, keepdims=True))
    mean_term = gate[0] * grad[0] + gate[1] * grad[1]
    logit_grad = jnp.zeros((tile, LANES), F32)
    for c in range(2):
        hit = (lane == ids_ref[:, c : c + 1]) & valid
        logit_grad = jnp.where(hit, gate[c] * (grad[c] - mean_term), logit_grad)
    logit_grad = logit_grad.astype(BF)
    routed = keep_ref[:, 0:width].astype(F32) + far_ref[:, 0:width].astype(F32)
    second_grad = routed + dot(logit_grad, router_ref[...], 1, 1)
    rg_ref[...] += dot(logit_grad, second_ref[...], 0, 0)
    scaled, spread = norm_parts(mid_ref[...])
    ng_ref[...] += jnp.sum(second_grad * scaled, 0, keepdims=True)
    upstream = jnp.where(valid, up_ref[...].astype(F32), 0.0)
    middle_grad = upstream + norm_field_back(second_grad, gain_ref[...], scaled, spread)
    mg_ref[...] = middle_grad
    rounded = middle_grad.astype(BF)
    for t in range(count):
        dmix_refs[t][...] = dot(rounded, wo_refs[t][...], 1, 1).astype(BF)
        hog_acc[t] += dot(mixed_refs[t][...], rounded, 0, 0)

    @pl.when(i == pl.num_programs(0) - 1)
    def _():
        for t in range(count):
            hog_refs[t][...] = hog_acc[t].astype(BF)


def middle_back(at, keep, far, middle, second, gates, ids, up, mixed, head_out, gain, router):
    each, cols = mixed[0].shape
    parts = len(mixed)
    rows, width = up.shape
    tile = half_tile(each)
    spec = pltpu.PrefetchScalarGridSpec(
        num_scalar_prefetch=1,
        grid=(each // tile,),
        in_specs=[
            rows_spec(tile, keep.shape[1]),
            rows_spec(tile, keep.shape[1]),
            rows_spec(tile, width),
            rows_spec(tile, width),
            rows_spec(tile, LANES),
            own_spec(tile, 2),
            own_spec(tile, width),
            whole((1, width)),
            whole(router.shape),
        ]
        + [rows_spec(tile, cols)] * parts
        + [whole((cols, width), True)] * parts,
        out_specs=[rows_spec(tile, width), whole((LANES, width)), whole((1, width))]
        + [whole((cols, width))] * parts
        + [rows_spec(tile, cols)] * parts,
        scratch_shapes=[pltpu.VMEM((parts, cols, width), F32)],
    )
    return pl.pallas_call(
        functools.partial(middle_back_kernel, parts, rows),
        grid_spec=spec,
        out_shape=[
            jax.ShapeDtypeStruct((each, width), F32),
            jax.ShapeDtypeStruct((LANES, width), F32),
            jax.ShapeDtypeStruct((1, width), F32),
        ]
        + [jax.ShapeDtypeStruct((cols, width), BF)] * parts
        + [jax.ShapeDtypeStruct((each, cols), BF)] * parts,
        compiler_params=params(),
        cost_estimate=cost(8 * each * width * width, 40 * each * width),
        name="middle_back",
    )(at, keep, far, middle, second, gates, ids, up, gain, router, *mixed, *head_out)


def input_back_kernel(limit, at_ref, keep_ref, far_ref, x_ref, mg_ref, gain_ref, out_ref):
    tile = x_ref.shape[0]
    valid = (at_ref[0] + pl.program_id(0)) * tile + iota(tile, 1, 0) < limit
    scaled, spread = norm_parts(jnp.where(valid, x_ref[...].astype(F32), 0.0))
    first_grad = keep_ref[...].astype(F32) + far_ref[...].astype(F32)
    out_ref[...] = (mg_ref[...] + norm_field_back(first_grad, gain_ref[...], scaled, spread)).astype(BF)


def input_back(at, keep, far, x, middle_grad, gain):
    each, width = middle_grad.shape
    tile = half_tile(each)
    spec = pltpu.PrefetchScalarGridSpec(
        num_scalar_prefetch=1,
        grid=(each // tile,),
        in_specs=[rows_spec(tile, width), rows_spec(tile, width), own_spec(tile, width), rows_spec(tile, width), whole((1, width))],
        out_specs=rows_spec(tile, width),
    )
    return pl.pallas_call(
        functools.partial(input_back_kernel, x.shape[0]),
        grid_spec=spec,
        out_shape=jax.ShapeDtypeStruct((each, width), BF),
        compiler_params=params(),
        cost_estimate=cost(20 * each * width, 16 * each * width),
        name="input_back",
    )(at, keep, far, x, middle_grad, gain)


def gelu_parts(v):
    x = jnp.abs(v) * 0.7071067811865476
    t = 1.0 / (1.0 + 0.3275911 * x)
    bell = jnp.exp(-x * x)
    poly = ((((1.061405429 * t - 1.453152027) * t + 1.421413741) * t - 0.284496736) * t + 0.254829592) * t
    below = 0.5 * poly * bell
    share = jnp.where(v < 0.0, below, 1.0 - below)
    return v * share, share + v * bell * 0.3989422804014327


def expert_kernel(count, slots, per, x_ref, g_ref, router_ref, *refs):
    w1_hbm, w2_hbm = refs[: 2 * count], refs[2 * count : 3 * count]
    back_ref, act_ref, hg_ref, rg_ref, dx_ref, w1, w2, sems = refs[3 * count :]
    rows, width = x_ref[...], x_ref.shape[1]
    half = width // 2
    copies = []
    for t in range(count):
        copies.append(
            [
                pltpu.make_async_copy(w1_hbm[2 * t], w1.at[t, pl.ds(0, half)], sems.at[3 * t]),
                pltpu.make_async_copy(w1_hbm[2 * t + 1], w1.at[t, pl.ds(half, half)], sems.at[3 * t + 1]),
                pltpu.make_async_copy(w2_hbm[t], w2.at[t], sems.at[3 * t + 2]),
            ]
        )

    @pl.when(pl.program_id(0) == 0)
    def _():
        for group in copies:
            for item in group:
                item.start()

    lane = iota(1, LANES, 1)
    signal = g_ref[:, 0].reshape(rows.shape[0], width + LANES)
    side = signal[:, width:].astype(F32)

    def column(*lanes):
        keep = lane == lanes[0]
        for other in lanes[1:]:
            keep = keep | (lane == other)
        return jnp.sum(jnp.where(keep, side, 0.0), -1, keepdims=True)

    logits = dot(rows, router_ref[...])
    lane_f = lane.astype(F32)
    mine = jnp.sum(jnp.where(lane_f == column(4), logits, 0.0), -1, keepdims=True)
    other = jnp.sum(jnp.where(lane_f == column(0), logits, 0.0), -1, keepdims=True)
    gate = 1.0 / (1.0 + jnp.exp(other - mine - column(1, 2, 3)))
    upstream = signal[:, 0:width].astype(F32)
    rows_grad = (gate * upstream).astype(BF)
    rg_ref[...] = rows_grad
    hidden_here = w1.shape[2]
    step = min(512, hidden_here)

    def wait(groups):
        @pl.when(pl.program_id(0) == 0)
        def _():
            for group in groups:
                for item in group:
                    item.wait()

    def first_products(t):
        parts = []
        for at in range(0, hidden_here, step):
            cols = slice(at, at + step)
            parts.append((at, dot(rows, w1[t, :, cols]), dot(rows_grad, w2[t, cols, :], 1, 1)))
        return parts

    wait(copies[:1])
    ready = first_products(0)
    wait(copies[1:])
    out = None
    grad = None
    for t in range(count):
        parts = ready
        if t + 1 < count:
            ready = first_products(t + 1)
        for at, hidden, active_grad in parts:
            place = slice(t * hidden_here + at, t * hidden_here + at + step)
            active, slope = gelu_parts(hidden)
            act_ref[:, place] = active.astype(BF)
            hg_ref[:, place] = (active_grad * slope).astype(BF)
        place = slice(t * hidden_here, (t + 1) * hidden_here)
        part = dot(act_ref[:, place], w2[t])
        out = part if out is None else out + part
        part = dot(hg_ref[:, place], w1[t], 1, 1)
        grad = part if grad is None else grad + part
    dx_ref[...] = grad.astype(BF)
    back_ref[...] = (gate * out).astype(BF)
    gate_grad = jnp.sum(upstream * out.astype(BF).astype(F32), -1, keepdims=True)
    lanes = up_to(slots, LANES)
    spread = iota(slots, lanes, 0) == iota(slots, lanes, 1)
    spare_row = iota(16, 1, 0) == per + 16 - slots
    for b in range(x_ref.shape[0] // slots):
        end = (b + 1) * slots
        line = jnp.sum(jnp.where(spread, gate_grad[end - slots : end], 0.0), 0, keepdims=True)
        high = line.astype(BF).astype(F32)
        line = jnp.concatenate([high, line - high, jnp.zeros((1, width - 2 * lanes), F32)], 1)
        dx_ref[end - 16 : end, :] = jnp.where(spare_row, line, grad[end - 16 : end]).astype(BF)


def expert(x, g, chunk, router, w1, w2, slots, per):
    rows, width = x.shape
    count = len(w2)
    here = w2[0].shape[0]
    total = count * here
    blocks = block_count(rows // slots, slots)
    tile = slots * blocks

    def tiled(cols):
        return pl.BlockSpec((tile, cols), lambda i: (i, 0))

    flops = 8 * rows * width * total
    return pl.pallas_call(
        functools.partial(expert_kernel, count, slots, per),
        grid=(rows // tile,),
        in_specs=[
            tiled(width),
            pl.BlockSpec((blocks, 1, slots, g.shape[3]), lambda i: (i, chunk, 0, 0)),
            whole(router.shape),
        ]
        + [pl.BlockSpec(memory_space=pl.ANY)] * (3 * count),
        out_specs=[tiled(width), tiled(total), tiled(total), tiled(width), tiled(width)],
        out_shape=[
            jax.ShapeDtypeStruct((rows, width), BF),
            jax.ShapeDtypeStruct((rows, total), BF),
            jax.ShapeDtypeStruct((rows, total), BF),
            jax.ShapeDtypeStruct((rows, width), BF),
            jax.ShapeDtypeStruct((rows, width), BF),
        ],
        scratch_shapes=[
            pltpu.VMEM((count, width, here), BF),
            pltpu.VMEM((count, here, width), BF),
            pltpu.SemaphoreType.DMA((3 * count,)),
        ],
        compiler_params=params(),
        cost_estimate=pl.CostEstimate(flops=flops, bytes_accessed=rows * total * 6, transcendentals=rows * total * 2),
        name="expert",
    )(x, g, router, *w1, *w2)


def weight_kernel(count, steps, *refs):
    ins, outs = refs[: 2 * count], refs[2 * count :]
    total = None
    for n in range(count):
        part = dot(ins[2 * n][...], ins[2 * n + 1][...], 0, 0)
        total = part if total is None else total + part
    store_piece(outs, steps, total.astype(BF))


def weight_grad(columns, rows, first, here):
    count = len(columns)
    width = rows[0].shape[1]
    step = min(512, here)
    steps = here // step
    offset = first * steps
    specs, args = [], []
    for a, b in zip(columns, rows):
        specs += [pl.BlockSpec((a.shape[0], step), lambda i: (0, i + offset)), whole(b.shape, True)]
        args += [a, b]
    out_specs, out_shape = by_piece(2, steps, (step, width), (here, width), BF)
    return pl.pallas_call(
        functools.partial(weight_kernel, count, steps),
        grid=(2 * steps,),
        in_specs=specs,
        out_specs=out_specs,
        out_shape=out_shape,
        compiler_params=params(),
        cost_estimate=cost(4 * sum(b.shape[0] for b in rows) * width * here, 8 * here * width),
        name="weight_grad",
    )(*args)


def shards(
    block_in,
    norm_one,
    head_in,
    head_out,
    norm_two,
    router,
    expert_in,
    expert_out,
    expert_ids,
    route_noise,
    cotangent,
):
    rows_here, width = block_in.shape
    parts = lax.axis_size("tensor")
    groups = lax.axis_size("expert")
    me = lax.axis_index("tensor")
    images = rows_here // SEQ
    height = up_to(SEQ, 16)
    each = up_to(-(-rows_here // parts), 16)
    experts = router.shape[1]
    capacity = (rows_here * 2 * 8 // (5 * experts) + 15) // 16 * 16
    share = -(-capacity // parts)
    per = -(-share // CHUNKS)
    slots = up_to(per + 1, 16)
    chunk_rows = experts * slots
    full = rows_here // 16 * 16
    here = expert_out.shape[1]

    paired = parts == 4
    order = (0, 2, 1, 3) if paired else tuple(range(parts))
    part_of = jnp.stack([me ^ k if paired else jnp.int32(k) for k in order]).astype(jnp.int32)
    starts = part_of * each
    own_block = (me * (each // half_tile(each)))[None].astype(jnp.int32)

    def cross(x, k):
        return lax.ppermute(x, "tensor", [(n, n ^ k) for n in range(parts)])

    def far_part(x):
        return cross(x, 2) if paired else x

    def gathered_from(x, far):
        if not paired:
            every = lax.all_gather(x, "tensor", axis=0, tiled=False)
            return [every[p] for p in range(parts)]
        return [x, far, cross(x, 1), cross(far, 1)]

    def gathered(x):
        return gathered_from(x, far_part(x))

    def near_hop(pieces):
        return pinned(*[cross(piece, 1) for piece in pieces[2:]]) if paired else pieces

    def near_sum(pieces, came):
        if not paired:
            return lax.psum_scatter(jnp.stack(pieces), "tensor", scatter_dimension=0), None
        kept, other = ((a.astype(F32) + b.astype(F32)).astype(BF) for a, b in zip(pieces, came))
        return kept, other

    def far_hop(kept, other):
        return cross(other, 2) if paired else jnp.zeros_like(kept)

    def scattered(pieces):
        kept, other = near_sum(pieces, near_hop(pieces))
        return kept, far_hop(kept, other)

    def swapped(pieces):
        if not paired:
            every = lax.all_to_all(jnp.stack(pieces), "tensor", split_axis=0, concat_axis=0, tiled=True)
            return [every[p] for p in range(parts)]
        return [cross(piece, k) if k else piece for piece, k in zip(pieces, order)]

    def over_experts(x):
        return lax.all_to_all(x, "expert", split_axis=0, concat_axis=0, tiled=True)

    def pinned(*items):
        return lax.optimization_barrier(items)

    def tail_of(x):
        return jnp.pad(x[full:], ((0, 16 - (rows_here - full)), (0, 0)))

    names = jnp.arange(experts, dtype=jnp.int32)
    member = [(expert_ids[:, c : c + 1] == names).astype(jnp.int32) for c in range(2)]
    both = member[0] + member[1]
    earlier = jnp.cumsum(both, 0) - both
    slot = jnp.stack([jnp.sum(earlier * item, -1) for item in member], 1)
    local = slot - me * share
    place = local // per * chunk_rows + expert_ids * slots + local % per
    place = jnp.where((local >= 0) & (local < share), place, -1)
    place = jnp.pad(place, ((0, each * parts - rows_here), (0, 0)), constant_values=-1)
    place_lanes = place.T
    place_parts = jnp.swapaxes(place_lanes.reshape(2, parts, each), 0, 1)

    sides = []
    for c in range(2):
        gap = route_noise[:, c] - route_noise[:, 1 - c]
        high = gap.astype(BF)
        left = gap - high.astype(F32)
        mid = left.astype(BF)
        low = (left - mid.astype(F32)).astype(BF)
        columns = [expert_ids[:, 1 - c].astype(BF), high, mid, low, expert_ids[:, c].astype(BF)]
        sides.append(jnp.stack(columns, 1))
    side = jnp.pad(jnp.stack(sides), ((0, 0), (0, each * parts - rows_here), (0, LANES - 5)))

    router_wide = jnp.pad(router, ((0, 0), (0, LANES - experts)))
    gain_one, gain_two = norm_one[None, :], norm_two[None, :]
    head_out_far = far_part(head_out)
    w1_own = [expert_in[0, : width // 2], expert_in[0, width // 2 :]]
    w1_far = [far_part(item) for item in w1_own]

    packed = pack_first(cotangent, tail_of(cotangent), place_lanes, side, experts, slots)
    block_rows, packed, w1_far[0] = pinned(block_in, packed, w1_far[0])
    signal = over_experts(packed)

    first_in, qkv, logs, *mixed = attend(
        starts, block_rows, tail_of(block_in), gain_one, head_in, images, height, each, parts
    )
    *mixed, w1_far[1], head_out_far = pinned(*mixed, w1_far[1], head_out_far)
    head_out_all = gathered_from(head_out, head_out_far)
    mixed = swapped(mixed)
    middle, second_in, gates = middle_of(
        own_block, mixed, head_out_all, block_in, gain_two, router_wide, expert_ids, route_noise
    )
    *second_all, signal, late_out = pinned(*gathered(second_in), signal, expert_out[0])
    w1 = [gathered_from(a, b) for a, b in zip(w1_own, w1_far)]
    w1 = [w1[h][p] for p in range(parts) for h in range(2)]

    def packed_rows(n):
        return pack(part_of, second_all, place_parts, experts, slots, n * chunk_rows)

    def sent(x):
        return over_experts(x.reshape(experts, slots, width)).reshape(chunk_rows, width)

    x = sent(packed_rows(0))
    w2_far, *outgoing = pinned(far_part(late_out), *[packed_rows(n) for n in range(1, CHUNKS)])
    w2 = gathered_from(expert_out[0], w2_far)
    backs, actives, hidden_grads, rows_grads, arrived, returned = [], [], [], [], [], []
    for n in range(CHUNKS):
        coming = None
        if n + 1 < CHUNKS:
            x, ready = pinned(x, outgoing[n])
            coming = sent(ready)
        if n == 0:
            x, *ready = pinned(x, *w1, *w2)
            w1, w2 = ready[: 2 * parts], ready[2 * parts :]
        back, active, hidden_grad, rows_grad, row_grad = expert(
            x, signal, n, router_wide, w1, w2, slots, per
        )
        if returned:
            row_grad, active, returned[-1] = pinned(row_grad, active, returned[-1])
        arrived.append(x)
        actives.append(active)
        hidden_grads.append(hidden_grad)
        rows_grads.append(rows_grad)
        backs.append(back)
        if coming is not None:
            x, row_grad = pinned(coming, row_grad)
        returned.append(sent(row_grad))

    def weight_parts(columns, rows):
        pairs = [weight_grad(columns, rows, p, here) for p in range(parts - 2, -1, -2)]
        return [item for pair in pairs[::-1] for item in pair]

    out_parts = weight_parts(actives, rows_grads)
    out_kept, out_other = near_sum(out_parts, near_hop(out_parts))
    out_far = far_hop(out_kept, out_other)
    *returned, out_kept = pinned(*returned, out_kept)

    second_pieces = unpack(part_of, place, returned, slots, per, each, True)
    second_kept, second_other = near_sum(second_pieces, near_hop(second_pieces))
    second_kept, out_far, *hidden_grads = pinned(second_kept, out_far, *hidden_grads)
    second_far = far_hop(second_kept, second_other)
    in_parts = weight_parts(hidden_grads, arrived)
    in_came = near_hop(in_parts)
    second_far, *in_parts = pinned(second_far, *in_parts)
    combined = [sent(item) for item in backs]
    middle_grad, router_part, norm_two_part, *pieces = middle_back(
        own_block, second_kept, second_far, middle, second_in, gates, expert_ids, cotangent, mixed, head_out_all,
        gain_two, router_wide,
    )
    head_out_parts, mixed_grad = pieces[:parts], pieces[parts:]
    *mixed_grad, combined[0] = pinned(*mixed_grad, combined[0])
    *mixed_grad, in_came = pinned(*swapped(mixed_grad), in_came)
    in_kept, in_other = near_sum(in_parts, in_came)
    in_far = far_hop(in_kept, in_other)
    head_out_kept, head_out_far = scattered(head_out_parts)
    *pieces, head_in_part, norm_one_part = attend_back(
        starts, mixed_grad, qkv, logs, first_in, jnp.swapaxes(head_in, 1, 2), gain_one
    )
    *pieces, combined[-1] = pinned(*pieces, combined[-1])
    first_kept, first_other = near_sum(pieces, near_hop(pieces))
    if paired:
        first_other, first_kept, in_far, head_in_part, *combined = pinned(
            first_other, first_kept, in_far, head_in_part, *combined
        )
    first_far = far_hop(first_kept, first_other)
    block_pieces = unpack(part_of, place, combined, slots, per, each, False)
    *block_pieces, head_out_far = pinned(*block_pieces, head_out_far)
    block_kept, block_other = near_sum(block_pieces, near_hop(block_pieces))
    first_far, block_kept = pinned(first_far, block_kept)
    block_far = far_hop(block_kept, block_other)
    input_part = input_back(own_block, first_kept, first_far, block_in, middle_grad, gain_one)
    out_grad = out_kept.astype(F32) + out_far.astype(F32)
    in_grad = sum_turned(in_kept, in_far)
    input_far, out_grad, in_grad, block_far = pinned(far_part(input_part), out_grad, in_grad, block_far)
    block_own = (middle + block_kept.astype(F32) + block_far.astype(F32)).astype(BF)

    cols = head_in.shape[2]
    head_out_part = (head_out_kept.astype(F32) + head_out_far.astype(F32)).astype(BF)
    small = jnp.concatenate([norm_one_part, norm_two_part, router_part[:experts]], 0).astype(BF)
    count = 4 * cols + 2 + experts
    total = up_to(count, 16 * groups)
    heads = jnp.concatenate(
        [head_in_part.reshape(3 * cols, width), head_out_part, jnp.pad(small, ((0, total - count), (0, 0)))], 0
    )
    heads = over_experts(heads.reshape(groups, total // groups, width))
    heads, block_own = pinned(heads, block_own)
    input_grad = assemble(part_of, gathered_from(input_part, input_far), rows_here, F32)
    block_out = assemble(part_of, gathered(block_own), rows_here, BF)
    heads = jnp.sum(heads.astype(F32), 0).astype(BF)
    heads = lax.all_gather(heads, "expert", axis=0, tiled=True)
    head_in_grad = jnp.swapaxes(heads[: 3 * cols].reshape(3, cols, width), 1, 2).astype(F32)
    head_out_grad = heads[3 * cols : 4 * cols].astype(F32)
    small = heads[4 * cols : count].astype(F32)
    if paired:
        small = small + cross(small, 1)
        small = small + cross(small, 2)
    else:
        small = lax.psum(small, "tensor")
    return (
        block_out,
        input_grad,
        small[0],
        head_in_grad,
        head_out_grad,
        small[1],
        small[2:].T,
        in_grad[None],
        out_grad[None],
    )


def solution(mesh):
    in_specs = (
        P("expert", None),
        P(),
        P(None, None, "tensor"),
        P("tensor", None),
        P(),
        P(),
        P("expert", None, "tensor"),
        P("expert", "tensor", None),
        P("expert", None),
        P("expert", None),
        P("expert", None),
    )
    out_specs = (
        P("expert", None),
        P("expert", None),
        P(),
        P(None, None, "tensor"),
        P("tensor", None),
        P(),
        P(),
        P("expert", None, "tensor"),
        P("expert", "tensor", None),
    )
    return jax.shard_map(shards, mesh=mesh, in_specs=in_specs, out_specs=out_specs, check_vma=False)
```
